32 devices in a mesh: groups: 2 (over x), curve: 16 (over z, y, core).
Axes of the slice: x: 2, y: 2, z: 4, core: 2. Of those that a mesh axis runs over, the one named last changes fastest.
Arguments:
- fine_latent: bfloat16 [65536, 128], P(('groups', 'curve')), parts along dimension 0, may hold values from -6 to 6
- coarse_latent: bfloat16 [32768, 128], P(('groups', 'curve')), parts along dimension 0, may hold values from -6 to 6
- grad_coarse: bfloat16 [32768, 128], P(('groups', 'curve')), parts along dimension 0, may hold values from -6 to 6
- restrict_weights: bfloat16 [2, 32768], P(None, ('groups', 'curve')), parts along dimension 1, may hold values from 0.25 to 1
- send_rows: int32 [65536], P(('groups', 'curve')), parts along dimension 0, may hold values from 0 to 1024, as said below
- pair_slots: int32 [32768], P(('groups', 'curve')), parts along dimension 0, may hold values from 0 to 2047, as said below
- edge_receivers: int32 [196608], P(('groups', 'curve')), parts along dimension 0, may hold values from 0 to 2047
- edge_offsets: int32 [196608], P(('groups', 'curve')), parts along dimension 0, may hold values from -256 to 256
- edge_weight: bfloat16 [256, 128], replicated, may hold values from -0.375 to 0.375
- node_weight_in: bfloat16 [128, 128], replicated, may hold values from -0.5 to 0.5
- node_weight_out: bfloat16 [128, 128], replicated, may hold values from -0.5 to 0.5
- node_gain: float32 [128], replicated, may hold values from 0.5 to 2
Outputs:
- grad_fine: bfloat16 [65536, 128], P(('groups', 'curve')), parts along dimension 0
- grad_edge: float32 [512, 128], P('groups'), parts along dimension 0
- grad_node_in: float32 [256, 128], P('groups'), parts along dimension 0
- grad_node_out: float32 [256, 128], P('groups'), parts along dimension 0
- grad_gain: float32 [256], P('groups'), parts along dimension 0
The draws below stay inside these ranges and needn't reach their ends.
There are 2 independent parts, one for each index of `groups`. The reference program is written for one: setup_inputs(seed, part) draws one part's arguments, and reference() takes and returns one part's arrays. A program takes and returns all parts, laid end to end along the dimension named above; an argument that names none is the same for every part. Nothing has to cross between parts.
Inputs may be any that keep to these rules, and one draw needn't show every extreme that they name: `send_rows`: in coarse shard d's block, entry s * 128 + t is the local coarse row sent in slot t toward fine shard s, and 1024 marks an empty slot. Every local coarse row is sent once; used slots toward a shard come first; some pair of shards fills all 128 slots. The numbers of used slots from one coarse shard toward the fine shards form the same multiset for every coarse shard, and toward one fine shard from the coarse shards the same multiset again. `pair_slots`: pair k of fine shard s (its fine rows 2 k and 2 k + 1) receives from slot d * 128 + t of coarse shard d's block toward s, the slot that holds its coarse node; each used slot serves exactly one pair.
All inputs are finite; a program needn't handle non-finite values.
Results may differ from the reference program's by a relative error of at most 0.0062.
The reference program's roundings to bfloat16 on the way count: a program that leaves them out, or rounds other values in their place, can miss the bound.
Values may be sent and summed in bfloat16 or wider, within the bound.
No kernel may reach another device: no remote copies, remote signals or barrier semaphores. Data moves between devices by JAX's collectives and lax.ppermute only.
A program may use at most 64 MiB of HBM per device.

```python
import math
import jax
import jax.numpy as jnp
from jax import lax

L = 128
CF = 2048
HB = 256
CC = 1024
E_DEV = 6144
CAP = 128
NF = 32768
NC = 16384
NE = 98304
N_CURVE = 16


def regroup_tables(key):
    shard_count = N_CURVE
    mean_count = CC // shard_count
    keys = jax.random.split(key, 6)
    order = jax.random.permutation(keys[0], shard_count).astype(jnp.int32)
    half_count = shard_count // 2
    delta = jax.random.randint(keys[1], (half_count,), 0, mean_count + 1).astype(jnp.int32)
    delta = delta.at[0].set(mean_count)
    base = jnp.zeros((shard_count,), jnp.int32)
    base = base.at[order[:half_count]].set(mean_count + delta)
    base = base.at[order[half_count:]].set(mean_count - delta)
    row_shift = jax.random.permutation(keys[2], shard_count).astype(jnp.int32)
    col_shift = jax.random.permutation(keys[3], shard_count).astype(jnp.int32)
    counts = base[(row_shift[:, None] + col_shift[None, :]) % shard_count]
    coarse_start = jnp.cumsum(counts, axis=0) - counts
    fine_incl = jnp.cumsum(counts, axis=1)
    fine_start = fine_incl - counts
    coarse_perm = jax.vmap(lambda sub: jax.random.permutation(sub, CC))(jax.random.split(keys[4], shard_count)).astype(jnp.int32)
    fine_perm = jax.vmap(lambda sub: jax.random.permutation(sub, CC))(jax.random.split(keys[5], shard_count)).astype(jnp.int32)
    slot_pos = jnp.arange(CAP, dtype=jnp.int32)
    position = coarse_start.T[:, :, None] + slot_pos[None, None, :]
    valid = slot_pos[None, None, :] < counts.T[:, :, None]
    safe = jnp.minimum(position, CC - 1)
    shard_ids = jnp.arange(shard_count, dtype=jnp.int32)[:, None, None]
    picked = coarse_perm[shard_ids, safe]
    send_rows = jnp.where(valid, picked, CC).reshape(-1).astype(jnp.int32)
    source = jnp.sum((fine_incl[:, None, :] <= fine_perm[:, :, None]).astype(jnp.int32), axis=2)
    start = jnp.take_along_axis(fine_start, source, axis=1)
    pair_slots = (source * CAP + fine_perm - start).reshape(-1).astype(jnp.int32)
    return (send_rows, pair_slots)


def draw_send_rows(key, part):
    tables = regroup_tables(key)
    return tables[0]


def draw_pair_slots(key, part):
    tables = regroup_tables(key)
    return tables[1]


def touch_ends(result, stream_key, low, high):
    shape = result.shape
    spot = [jax.random.randint(jax.random.fold_in(stream_key, axis), (), 0, shape[axis]) for axis in range(len(shape))]
    result = result.at[tuple(spot)].set(low)
    longest = shape.index(max(shape))
    spot[longest] = (spot[longest] + 1) % shape[longest]
    return result.at[tuple(spot)].set(high)


def block_scale(rng, shape, cuts, smallest, high):
    def one(axis_at, parts):
        steps = jax.random.uniform(jax.random.fold_in(jax.random.fold_in(rng, 6), axis_at), (parts,), jnp.float32, smallest / len(cuts), high / len(cuts))
        return jnp.repeat(jnp.exp(steps), shape[axis_at] // parts).reshape((-1,) + (1,) * (len(shape) - axis_at - 1))

    gain = one(*cuts[0])
    for cut in cuts[1:]:
        gain = gain * one(*cut)
    return gain


def bell_draw(stream_key, extent, width, bound, shards=(), kind=jnp.bfloat16):
    loudness = block_scale(stream_key, extent, shards, -0.22, 0.18) if shards else 1.0
    array = jax.random.normal(stream_key, extent, jnp.float32) * width * loudness
    return jnp.minimum(jnp.maximum(array, -bound), bound).astype(kind)


def setup_inputs(seed: int = 0, part: int = 0) -> dict:
    arg_keys = jax.random.split(jax.random.key(seed), 13)
    part_splits = jax.random.split(jax.random.fold_in(arg_keys[12], part), 13)
    fine_latent = bell_draw(part_splits[0], (NF, L), 1.0, 6.0, ((0, 16),))
    coarse_latent = bell_draw(part_splits[1], (NC, L), 1.0, 6.0, ((0, 16),))
    grad_coarse = bell_draw(part_splits[2], (NC, L), 1.0, 6.0, ((0, 16),))
    restrict_weights = jnp.clip(0.25 + 0.75 * jax.random.uniform(part_splits[3], (2, NC), jnp.float32) ** block_scale(part_splits[3], (2, NC), ((1, 16),), -0.2, 0.2), 0.25, 1.0).astype(jnp.bfloat16)
    send_rows = draw_send_rows(jax.random.fold_in(jax.random.fold_in(arg_keys[12], part), 71), part)
    pair_slots = draw_pair_slots(jax.random.fold_in(jax.random.fold_in(arg_keys[12], part), 71), part)
    edge_receivers = touch_ends(jax.random.randint(part_splits[6], (NE,), 0, CF), jax.random.fold_in(part_splits[6], 1), 0, CF - 1).astype(jnp.int32)
    edge_offsets = touch_ends(jax.random.randint(part_splits[7], (NE,), 0 - HB, HB + 1), jax.random.fold_in(part_splits[7], 1), 0 - HB, HB).astype(jnp.int32)
    edge_weight = bell_draw(arg_keys[8], (2 * L, L), (2 * L) ** -0.5, 0.375)
    node_weight_in = bell_draw(arg_keys[9], (L, L), L ** -0.5, 0.5)
    node_weight_out = bell_draw(arg_keys[10], (L, L), L ** -0.5, 0.5)
    node_gain = jnp.clip(jnp.exp(jax.random.uniform(arg_keys[11], (L,), jnp.float32, math.log(0.5), math.log(2.0))), 0.5, 2.0)
    return dict(fine_latent=fine_latent, coarse_latent=coarse_latent, grad_coarse=grad_coarse, restrict_weights=restrict_weights, send_rows=send_rows, pair_slots=pair_slots, edge_receivers=edge_receivers, edge_offsets=edge_offsets, edge_weight=edge_weight, node_weight_in=node_weight_in, node_weight_out=node_weight_out, node_gain=node_gain)


def silu_slope(values):
    sigm = jax.nn.sigmoid(values)
    return sigm * (1.0 + values * (1.0 - sigm))

def coarse_back(coarse_latent, grad_coarse, node_weight_in, node_weight_out, node_gain):
    pre_node = jnp.dot(coarse_latent, node_weight_in, preferred_element_type=jnp.float32)
    hidden = jax.nn.silu(pre_node).astype(jnp.bfloat16)
    mapped = jnp.dot(hidden, node_weight_out, preferred_element_type=jnp.float32)
    centred = mapped - lax.optimization_barrier(jnp.mean(mapped, axis=1, keepdims=True))
    inverse = lax.rsqrt(lax.optimization_barrier(jnp.mean(centred * centred, axis=1, keepdims=True)) + 1e-05)
    normed = centred * inverse
    upstream = grad_coarse.astype(jnp.float32)
    scaled_up = upstream * node_gain
    grad_mapped = (inverse * (scaled_up - lax.optimization_barrier(jnp.mean(scaled_up, axis=1, keepdims=True)) - normed * lax.optimization_barrier(jnp.mean(scaled_up * normed, axis=1, keepdims=True)))).astype(jnp.bfloat16)
    grad_hidden = jnp.dot(grad_mapped, node_weight_out.T, preferred_element_type=jnp.float32)
    grad_pre = (grad_hidden * silu_slope(pre_node)).astype(jnp.bfloat16)
    grad_input = (upstream + jnp.dot(grad_pre, node_weight_in.T, preferred_element_type=jnp.float32)).astype(jnp.bfloat16)
    term_gain = lax.optimization_barrier(jnp.sum(upstream * normed, axis=0))
    contract = (((0,), (0,)), ((), ()))
    term_in = lax.dot_general(coarse_latent, grad_pre, contract, preferred_element_type=jnp.float32)
    term_out = lax.dot_general(hidden, grad_mapped, contract, preferred_element_type=jnp.float32)
    return (grad_input, term_gain, term_in, term_out)

def edge_back(window, receivers, offsets, grad_rows, edge_weight, border):
    send_index = receivers + offsets + border
    recv_index = receivers + border
    inputs = jnp.concatenate([jnp.take(window, send_index, axis=0), jnp.take(window, recv_index, axis=0)], axis=1)
    edge_pre = jnp.dot(inputs, edge_weight, preferred_element_type=jnp.float32)
    edge_grad = (jnp.take(grad_rows, receivers, axis=0).astype(jnp.float32) * silu_slope(edge_pre)).astype(jnp.bfloat16)
    term_edge = lax.dot_general(inputs, edge_grad, (((0,), (0,)), ((), ())), preferred_element_type=jnp.float32)
    input_grad = jnp.dot(edge_grad, edge_weight.T, preferred_element_type=jnp.float32)
    latent_width = grad_rows.shape[1]
    stacked = jnp.concatenate([input_grad[:, :latent_width], input_grad[:, latent_width:]], axis=0)
    targets = jnp.concatenate([send_index, recv_index], axis=0)
    window_grad = jax.ops.segment_sum(stacked, targets, num_segments=window.shape[0])
    return (window_grad, term_edge)

def reference(fine_latent, coarse_latent, grad_coarse, restrict_weights, send_rows, pair_slots, edge_receivers, edge_offsets, edge_weight, node_weight_in, node_weight_out, node_gain):
    grad_input, term_gain, term_in, term_out = coarse_back(coarse_latent, grad_coarse, node_weight_in, node_weight_out, node_gain)
    pair_index = jnp.arange(NC, dtype=jnp.int32)
    fine_shard = (pair_index // CC).astype(jnp.int32)
    source = (pair_slots // CAP).astype(jnp.int32)
    within = (pair_slots % CAP).astype(jnp.int32)
    entry = (source * (N_CURVE * CAP) + fine_shard * CAP + within).astype(jnp.int32)
    coarse_node = (source * CC + jnp.take(send_rows, entry, axis=0)).astype(jnp.int32)
    rows_in = jnp.take(grad_input, coarse_node, axis=0)
    weights_in = jnp.take(restrict_weights.T, coarse_node, axis=0)
    fine_grad = (weights_in.astype(jnp.float32)[:, :, None] * rows_in.astype(jnp.float32)[:, None, :]).astype(jnp.bfloat16).reshape(NF, L)
    padded = jnp.pad(fine_latent, ((HB, HB), (0, 0)))
    receivers_all = edge_receivers.reshape(N_CURVE, E_DEV)
    offsets_all = edge_offsets.reshape(N_CURVE, E_DEV)

    def device_step(carry, item):
        accum, edge_total = carry
        shard, receivers, offsets = item
        start = (shard * CF).astype(jnp.int32)
        window = lax.dynamic_slice_in_dim(padded, start, CF + 2 * HB, 0)
        grad_rows = lax.dynamic_slice_in_dim(fine_grad, start, CF, 0)
        window_grad, term_edge = edge_back(window, receivers, offsets, grad_rows, edge_weight, HB)
        current = lax.dynamic_slice_in_dim(accum, start, CF + 2 * HB, 0)
        accum = lax.dynamic_update_slice_in_dim(accum, current + window_grad, start, 0)
        return ((accum, edge_total + term_edge), None)
    start_carry = (jnp.zeros((NF + 2 * HB, L), jnp.float32), jnp.zeros((2 * L, L), jnp.float32))
    (accum, edge_total), _ = lax.scan(device_step, start_carry, (jnp.arange(N_CURVE, dtype=jnp.int32), receivers_all, offsets_all))
    grad_fine = (fine_grad.astype(jnp.float32) + accum[HB:HB + NF]).astype(jnp.bfloat16)
    coarse_scale = 1.0 / math.sqrt(NC)
    edge_scale = 1.0 / math.sqrt(NE)
    return (grad_fine, edge_total * edge_scale, term_in * coarse_scale, term_out * coarse_scale, term_gain * coarse_scale)
```

```python
import functools
import math

import jax
import jax.numpy as jnp
from jax import lax
from jax.experimental import pallas as pl
from jax.experimental.pallas import tpu as pltpu
from jax.sharding import PartitionSpec as P

HB = 256
LANES = 128
SPAN = 256
EXTRA = 16
TILE = 512

F32 = jnp.float32
BF16 = jnp.bfloat16
NT = (((1,), (1,)), ((), ()))
TN = (((0,), (0,)), ((), ()))


def dot(left, right, dims=(((1,), (0,)), ((), ()))):
    return lax.dot_general(left, right, dims, preferred_element_type=F32)


def silu_slope(values):
    sigm = jax.nn.sigmoid(values)
    return sigm * (1.0 + values * (1.0 - sigm))


def columns(row):
    return jnp.broadcast_to(row, (LANES, LANES)).T


def index_columns(ref, first, count):
    return jnp.concatenate([columns(ref[pl.ds(first + i, 1), :]) for i in range(count)], axis=0)


def small(values):
    return values.astype(F32).astype(BF16)


def place_hot(cols):
    place = small(cols & (SPAN - 1))
    lane = lax.broadcasted_iota(jnp.int32, place.shape, 1)
    one, zero = jnp.ones((), BF16), jnp.zeros((), BF16)
    return jnp.concatenate(
        [jnp.where(place == small(lane + start), one, zero) for start in range(0, SPAN, LANES)],
        axis=1,
    )


def gather_rows(cols, table, width):
    hot = place_hot(cols)
    block = cols // SPAN
    total = table.shape[1]
    step = max(width, 2 * LANES)
    found = [jnp.zeros(cols.shape, F32) for _ in range(width // LANES)]
    for start in range(0, total, step):
        part = dot(hot, table[:, start : start + step])
        for inner in range(0, step, width):
            here = block == (start + inner) // width
            for i in range(len(found)):
                at = inner + i * LANES
                found[i] = jnp.where(here, part[:, at : at + LANES], found[i])
    return found


def two_parts(values):
    high = values.astype(BF16)
    return high, (values - high.astype(F32)).astype(BF16)


def coarse_kernel(
    peers,
    latent_ref,
    grad_ref,
    weights_ref,
    rows_ref,
    w_in_ref,
    w_out_ref,
    gain_ref,
    sent_ref,
    table_ref,
):
    count = latent_ref.shape[0]
    capacity = sent_ref.shape[1] - EXTRA - max(EXTRA, SPAN // peers)
    w_in, w_out, gain = w_in_ref[...], w_out_ref[...], gain_ref[...]
    term_in = jnp.zeros((LANES, LANES), F32)
    term_out = jnp.zeros((LANES, LANES), F32)
    term_gain = jnp.zeros((1, LANES), F32)
    for block in range(count // SPAN):
        rows = pl.ds(block * SPAN, SPAN)
        latent = latent_ref[rows, :]
        pre = dot(latent, w_in)
        sigm = jax.nn.sigmoid(pre)
        hidden = (pre * sigm).astype(BF16)
        slope = sigm * (1.0 + pre * (1.0 - sigm))
        mapped = dot(hidden, w_out)
        centred = mapped - jnp.mean(mapped, axis=1, keepdims=True)
        inverse = lax.rsqrt(jnp.mean(centred * centred, axis=1, keepdims=True) + 1e-05)
        normed = centred * inverse
        upstream = grad_ref[rows, :].astype(F32)
        scaled = upstream * gain
        grad_mapped = (
            inverse
            * (
                scaled
                - jnp.mean(scaled, axis=1, keepdims=True)
                - normed * jnp.mean(scaled * normed, axis=1, keepdims=True)
            )
        ).astype(BF16)
        grad_pre = (dot(grad_mapped, w_out, NT) * slope).astype(BF16)
        grad_in = (upstream + dot(grad_pre, w_in, NT)).astype(BF16)
        term_gain += jnp.sum(upstream * normed, axis=0, keepdims=True)
        term_in += dot(latent, grad_pre, TN)
        term_out += dot(hidden, grad_mapped, TN)
        table_ref[:, block * SPAN : block * SPAN + LANES] = grad_in
        for half in range(SPAN // LANES):
            at = block * SPAN + half * LANES
            pair = weights_ref[:, at : at + LANES].astype(F32)
            square = jnp.concatenate([pair, jnp.zeros((LANES - 2, LANES), F32)], axis=0)
            table_ref[
                half * LANES : (half + 1) * LANES, block * SPAN + LANES : (block + 1) * SPAN
            ] = square.T.astype(BF16)
    gain_high, gain_low = two_parts(term_gain)
    gain_rows = jnp.concatenate([gain_high.astype(F32), gain_low.astype(F32)], axis=0)
    terms = jnp.concatenate([term_in, term_out], axis=0)
    chunk = SPAN // peers
    per_step = 256 // LANES
    for first in range(0, rows_ref.shape[0], per_step):
        cols = index_columns(rows_ref, first, per_step)
        sent, weight = gather_rows(cols, table_ref[...], SPAN)
        for part in range(per_step * LANES // capacity):
            peer = first * LANES // capacity + part
            rows = slice(part * capacity, (part + 1) * capacity)
            sent_ref[peer, 0:capacity, :] = sent[rows].astype(BF16)
            square = weight[rows]
            if capacity < LANES:
                square = jnp.concatenate(
                    [square, jnp.zeros((LANES - capacity, LANES), F32)], axis=0
                )
            extra = jnp.concatenate(
                [square.T[0:2], gain_rows, jnp.zeros((EXTRA - 4, LANES), F32)], axis=0
            )
            sent_ref[peer, capacity : capacity + EXTRA, :] = extra.astype(BF16)
            share = terms[peer * chunk : (peer + 1) * chunk]
            if chunk < EXTRA:
                share = jnp.concatenate([share, jnp.zeros((EXTRA - chunk, LANES), F32)], axis=0)
            sent_ref[peer, capacity + EXTRA :, :] = share.astype(BF16)


def slope_kernel(
    low_ref, fine_ref, high_ref, recv_ref, off_ref, weight_ref, slope_ref, window_table, fine_table
):
    blocks = fine_ref.shape[0] // SPAN
    window_table[:, 0:LANES] = low_ref[...]
    for block in range(blocks):
        rows = fine_ref[block * SPAN : (block + 1) * SPAN, :]
        window_table[:, (block + 1) * LANES : (block + 2) * LANES] = rows
        fine_table[:, block * LANES : (block + 1) * LANES] = rows
    window_table[:, (blocks + 1) * LANES :] = high_ref[...]
    count = TILE // LANES

    def step(tile, carry):
        recv = index_columns(recv_ref, tile * count, count)
        send = recv + index_columns(off_ref, tile * count, count) + HB
        (sender,) = gather_rows(send, window_table, LANES)
        (receiver,) = gather_rows(recv, fine_table, LANES)
        inputs = jnp.concatenate([sender.astype(BF16), receiver.astype(BF16)], axis=1)
        slope_ref[pl.ds(tile * TILE, TILE), :] = silu_slope(dot(inputs, weight_ref[...]))
        return carry

    lax.fori_loop(0, slope_ref.shape[0] // TILE, step, 0)


def edge_kernel(
    arrived_ref,
    slots_ref,
    slope_ref,
    recv_ref,
    off_ref,
    low_ref,
    fine_ref,
    high_ref,
    weight_ref,
    summed_ref,
    to_prev_ref,
    to_next_ref,
    term_ref,
    coarse_ref,
    gain_ref,
    slot_table,
    grad_table,
    grad_rows,
    send_sum,
    recv_sum,
):
    peers = arrived_ref.shape[0]
    share = max(EXTRA, SPAN // peers)
    capacity = arrived_ref.shape[1] - EXTRA - share
    per_block = SPAN // capacity
    coarse = jnp.zeros((share, LANES), F32)
    gain = jnp.zeros((1, LANES), F32)
    for peer in range(peers):
        block, part = divmod(peer, per_block)
        rows = slice(part * capacity, (part + 1) * capacity)
        slot_table[rows, block * SPAN : block * SPAN + LANES] = arrived_ref[peer, 0:capacity, :]
        extra = arrived_ref[peer, capacity : capacity + EXTRA, :].astype(F32)
        square = jnp.concatenate([extra, jnp.zeros((LANES - EXTRA, LANES), F32)], axis=0).T
        slot_table[rows, block * SPAN + LANES : (block + 1) * SPAN] = square[0:capacity].astype(
            BF16
        )
        gain += extra[2:3] + extra[3:4]
        coarse += arrived_ref[peer, capacity + EXTRA :, :].astype(F32)
    coarse_ref[...] = coarse
    gain_ref[...] = gain

    per_step = SPAN // LANES
    for first in range(0, slots_ref.shape[0], per_step):
        cols = index_columns(slots_ref, first, per_step)
        grad, weight = gather_rows(cols, slot_table, SPAN)
        for r in range(2):
            rows = (grad * weight[:, r : r + 1]).astype(BF16).astype(F32)
            grad_rows[pl.ds(2 * first * LANES + r, SPAN, stride=2), :] = rows
    blocks = fine_ref.shape[0] // SPAN
    for block in range(blocks):
        grad_table[:, block * LANES : (block + 1) * LANES] = grad_rows[
            block * SPAN : (block + 1) * SPAN, :
        ].astype(BF16)

    send_sum[...] = jnp.zeros(send_sum.shape, F32)
    recv_sum[...] = jnp.zeros(recv_sum.shape, F32)
    count = TILE // LANES
    one, zero = jnp.ones((), BF16), jnp.zeros((), BF16)

    def add_rows(total, rows, cols, values):
        place = small(rows & (SPAN - 1))
        sub = small(lax.broadcasted_iota(jnp.int32, (SPAN, TILE), 0))
        hot = jnp.where(sub == place, one, zero)
        block = small(cols // SPAN)
        for start in range(0, total.shape[1], 2 * LANES):
            first = start // LANES
            spread = jnp.concatenate(
                [
                    jnp.where(block == jnp.full((), first + i, BF16), values, zero)
                    for i in range(2)
                ],
                axis=1,
            )
            total[:, start : start + 2 * LANES] += dot(hot, spread)

    def step(tile, carry):
        recv_row = jnp.concatenate(
            [recv_ref[pl.ds(tile * count + i, 1), :] for i in range(count)], axis=1
        )
        off_row = jnp.concatenate(
            [off_ref[pl.ds(tile * count + i, 1), :] for i in range(count)], axis=1
        )
        send_row = recv_row + off_row + HB
        recv = index_columns(recv_ref, tile * count, count)
        send = recv + index_columns(off_ref, tile * count, count) + HB
        (upstream,) = gather_rows(recv, grad_table, LANES)
        values = (upstream * slope_ref[pl.ds(tile * TILE, TILE), :]).astype(BF16)
        add_rows(send_sum, send_row, send, values)
        add_rows(recv_sum, recv_row, recv, values)
        return carry

    lax.fori_loop(0, slope_ref.shape[0] // TILE, step, 0)

    weight_send = weight_ref[0:LANES, :]
    weight_recv = weight_ref[LANES:, :]

    def back(values, weight):
        high, low = two_parts(values)
        return dot(high, weight, NT) + dot(low, weight, NT)

    def outer(rows, values):
        high, low = two_parts(values)
        both = dot(rows, jnp.concatenate([high, low], axis=1), TN)
        return both[:, 0:LANES] + both[:, LANES:]

    first = send_sum[:, 0:LANES]
    last = send_sum[:, (blocks + 1) * LANES :]
    to_prev_ref[...] = back(first, weight_send).astype(BF16)
    to_next_ref[...] = back(last, weight_send).astype(BF16)
    term_send = outer(low_ref[...], first) + outer(high_ref[...], last)
    term_recv = jnp.zeros((LANES, LANES), F32)
    for block in range(blocks):
        at = slice(block * SPAN, (block + 1) * SPAN)
        rows = fine_ref[at, :]
        sent = send_sum[:, (block + 1) * LANES : (block + 2) * LANES]
        received = recv_sum[:, block * LANES : (block + 1) * LANES]
        summed_ref[at, :] = grad_rows[at, :] + back(sent, weight_send) + back(received, weight_recv)
        term_send += outer(rows, sent)
        term_recv += outer(rows, received)
    term_ref[0:LANES, :] = term_send.astype(BF16)
    term_ref[LANES:, :] = term_recv.astype(BF16)


def per_device(
    fine_latent,
    coarse_latent,
    grad_coarse,
    restrict_weights,
    send_rows,
    pair_slots,
    edge_receivers,
    edge_offsets,
    edge_weight,
    node_weight_in,
    node_weight_out,
    node_gain,
):
    peers = lax.axis_size("curve")
    coarse_count = coarse_latent.shape[0]
    fine_count = fine_latent.shape[0]
    edge_count = edge_receivers.shape[0]
    capacity = send_rows.shape[0] // peers
    chunk = SPAN // peers
    share = max(EXTRA, chunk)
    payload = capacity + EXTRA + share
    fine_blocks = fine_count // SPAN
    forward = [(i, i + 1) for i in range(peers - 1)]
    backward = [(i + 1, i) for i in range(peers - 1)]
    params = pltpu.CompilerParams(vmem_limit_bytes=50 * 1024 * 1024)

    low = lax.ppermute(fine_latent[fine_count - HB :], "curve", forward)
    high = lax.ppermute(fine_latent[:HB], "curve", backward)

    sent = pl.pallas_call(
        functools.partial(coarse_kernel, peers),
        out_shape=jax.ShapeDtypeStruct((peers, payload, LANES), BF16),
        scratch_shapes=[pltpu.VMEM((SPAN, coarse_count), BF16)],
        compiler_params=params,
        cost_estimate=pl.CostEstimate(
            flops=2_000_000_000, bytes_accessed=2_000_000, transcendentals=400_000
        ),
        name="coarse_block",
    )(
        coarse_latent,
        grad_coarse,
        restrict_weights,
        send_rows.reshape(-1, LANES),
        node_weight_in,
        node_weight_out,
        node_gain.reshape(1, LANES),
    )
    arrived = lax.all_to_all(sent, "curve", split_axis=0, concat_axis=0, tiled=True)

    receivers = edge_receivers.reshape(-1, LANES)
    offsets = edge_offsets.reshape(-1, LANES)
    slope = pl.pallas_call(
        slope_kernel,
        out_shape=jax.ShapeDtypeStruct((edge_count, LANES), F32),
        scratch_shapes=[
            pltpu.VMEM((SPAN, (fine_blocks + 2) * LANES), BF16),
            pltpu.VMEM((SPAN, fine_blocks * LANES), BF16),
        ],
        compiler_params=params,
        cost_estimate=pl.CostEstimate(
            flops=16_000_000_000, bytes_accessed=5_000_000, transcendentals=800_000
        ),
        name="edge_slope",
    )(low, fine_latent, high, receivers, offsets, edge_weight)

    summed, to_prev, to_next, term_edge, coarse_share, term_gain = pl.pallas_call(
        edge_kernel,
        out_shape=(
            jax.ShapeDtypeStruct((fine_count, LANES), F32),
            jax.ShapeDtypeStruct((HB, LANES), BF16),
            jax.ShapeDtypeStruct((HB, LANES), BF16),
            jax.ShapeDtypeStruct((2 * LANES, LANES), BF16),
            jax.ShapeDtypeStruct((share, LANES), F32),
            jax.ShapeDtypeStruct((1, LANES), F32),
        ),
        scratch_shapes=[
            pltpu.VMEM((SPAN, peers * capacity), BF16),
            pltpu.VMEM((SPAN, fine_blocks * LANES), BF16),
            pltpu.VMEM((fine_count, LANES), F32),
            pltpu.VMEM((SPAN, (fine_blocks + 2) * LANES), F32),
            pltpu.VMEM((SPAN, fine_blocks * LANES), F32),
        ],
        compiler_params=params,
        cost_estimate=pl.CostEstimate(
            flops=24_000_000_000, bytes_accessed=8_000_000, transcendentals=0
        ),
        name="edge_back",
    )(
        arrived,
        pair_slots.reshape(-1, LANES),
        slope,
        receivers,
        offsets,
        low,
        fine_latent,
        high,
        edge_weight,
    )
    edge_parts = lax.all_to_all(
        term_edge.reshape(peers, chunk, LANES), "curve", split_axis=0, concat_axis=0, tiled=True
    )
    from_next = lax.ppermute(to_prev, "curve", backward)
    from_prev = lax.ppermute(to_next, "curve", forward)
    edge_share = jnp.sum(edge_parts.astype(F32), axis=0)
    coarse_scale = 1.0 / math.sqrt(coarse_count * peers)
    edge_scale = 1.0 / math.sqrt(edge_count * peers)
    shares = jnp.stack([edge_share * edge_scale, coarse_share[:chunk] * coarse_scale])
    whole = lax.all_to_all(
        jnp.broadcast_to(shares[None], (peers, 2, chunk, LANES)),
        "curve",
        split_axis=0,
        concat_axis=0,
        tiled=True,
    )
    terms = whole.transpose(1, 0, 2, 3).reshape(2, 2 * LANES, LANES)
    grad_fine = jnp.concatenate(
        [
            summed[:HB] + from_prev.astype(F32),
            summed[HB : fine_count - HB],
            summed[fine_count - HB :] + from_next.astype(F32),
        ],
        axis=0,
    ).astype(BF16)
    return (
        grad_fine,
        terms[0],
        terms[1, :LANES],
        terms[1, LANES:],
        term_gain.reshape(LANES) * coarse_scale,
    )


def solution(mesh):
    placed = (
        P(("groups", "curve"), None),
        P(("groups", "curve"), None),
        P(("groups", "curve"), None),
        P(None, ("groups", "curve")),
        P(("groups", "curve")),
        P(("groups", "curve")),
        P(("groups", "curve")),
        P(("groups", "curve")),
        P(),
        P(),
        P(),
        P(),
    )
    return jax.shard_map(
        per_device,
        mesh=mesh,
        in_specs=placed,
        out_specs=(
            P(("groups", "curve"), None),
            P("groups", None),
            P("groups", None),
            P("groups", None),
            P("groups"),
        ),
        check_vma=False,
    )
```

```python
import math

import jax
import jax.numpy as jnp
from jax import lax
from jax.experimental import pallas as pl
from jax.experimental.pallas import tpu as pltpu
from jax.sharding import PartitionSpec as P

HB = 256
LANES = 128
SPAN = 256
EXTRA = 16
TILE = 512

F32 = jnp.float32
BF16 = jnp.bfloat16
NT = (((1,), (1,)), ((), ()))
TN = (((0,), (0,)), ((), ()))


def dot(left, right, dims=(((1,), (0,)), ((), ()))):
    return lax.dot_general(left, right, dims, preferred_element_type=F32)


def silu_slope(values):
    sigm = jax.nn.sigmoid(values)
    return sigm * (1.0 + values * (1.0 - sigm))


def columns(row):
    return jnp.broadcast_to(row, (LANES, LANES)).T


def index_columns(ref, first, count):
    return jnp.concatenate([columns(ref[pl.ds(first + i, 1), :]) for i in range(count)], axis=0)


def small(values):
    return values.astype(F32).astype(BF16)


def place_hot(cols):
    place = small(cols & (SPAN - 1))
    lane = lax.broadcasted_iota(jnp.int32, place.shape, 1)
    one, zero = jnp.ones((), BF16), jnp.zeros((), BF16)
    return jnp.concatenate(
        [jnp.where(place == small(lane + start), one, zero) for start in range(0, SPAN, LANES)],
        axis=1,
    )


def gather_rows(cols, table, width):
    hot = place_hot(cols)
    block = cols // SPAN
    total = table.shape[1]
    step = max(width, 2 * LANES)
    found = [jnp.zeros(cols.shape, F32) for _ in range(width // LANES)]
    for start in range(0, total, step):
        part = dot(hot, table[:, start : start + step])
        for inner in range(0, step, width):
            here = block == (start + inner) // width
            for i in range(len(found)):
                at = inner + i * LANES
                found[i] = jnp.where(here, part[:, at : at + LANES], found[i])
    return found


def two_parts(values):
    high = values.astype(BF16)
    return high, (values - high.astype(F32)).astype(BF16)


def coarse_kernel(
    latent_ref,
    grad_ref,
    weights_ref,
    rows_ref,
    w_in_ref,
    w_out_ref,
    gain_ref,
    sent_ref,
    terms_ref,
    table_ref,
    *held,
):
    *held, arrivals = held
    sources = (latent_ref, grad_ref, weights_ref, rows_ref, w_in_ref, w_out_ref, gain_ref)
    copies = [
        pltpu.make_async_copy(source, target, arrivals.at[i])
        for i, (source, target) in enumerate(zip(sources, held))
    ]
    for copy in copies:
        copy.start()
    for copy in copies:
        copy.wait()
    latent_ref, grad_ref, weights_ref, rows_ref, w_in_ref, w_out_ref, gain_ref = held
    count = latent_ref.shape[0]
    capacity = sent_ref.shape[1] - EXTRA
    w_in, w_out, gain = w_in_ref[...], w_out_ref[...], gain_ref[...]
    term_in = jnp.zeros((LANES, LANES), F32)
    term_out = jnp.zeros((LANES, LANES), F32)
    term_gain = jnp.zeros((1, LANES), F32)
    for block in range(count // SPAN):
        rows = pl.ds(block * SPAN, SPAN)
        latent = latent_ref[rows, :]
        pre = dot(latent, w_in)
        sigm = jax.nn.sigmoid(pre)
        hidden = (pre * sigm).astype(BF16)
        slope = sigm * (1.0 + pre * (1.0 - sigm))
        mapped = dot(hidden, w_out)
        centred = mapped - jnp.mean(mapped, axis=1, keepdims=True)
        inverse = lax.rsqrt(jnp.mean(centred * centred, axis=1, keepdims=True) + 1e-05)
        normed = centred * inverse
        upstream = grad_ref[rows, :].astype(F32)
        scaled = upstream * gain
        grad_mapped = (
            inverse
            * (
                scaled
                - jnp.mean(scaled, axis=1, keepdims=True)
                - normed * jnp.mean(scaled * normed, axis=1, keepdims=True)
            )
        ).astype(BF16)
        grad_pre = (dot(grad_mapped, w_out, NT) * slope).astype(BF16)
        grad_in = (upstream + dot(grad_pre, w_in, NT)).astype(BF16)
        term_gain += jnp.sum(upstream * normed, axis=0, keepdims=True)
        term_in += dot(latent, grad_pre, TN)
        term_out += dot(hidden, grad_mapped, TN)
        table_ref[:, block * SPAN : block * SPAN + LANES] = grad_in
        for half in range(SPAN // LANES):
            at = block * SPAN + half * LANES
            pair = weights_ref[:, at : at + LANES].astype(F32)
            square = jnp.concatenate([pair, jnp.zeros((LANES - 2, LANES), F32)], axis=0)
            table_ref[
                half * LANES : (half + 1) * LANES, block * SPAN + LANES : (block + 1) * SPAN
            ] = square.T.astype(BF16)
    gain_high, gain_low = two_parts(term_gain)
    gain_rows = jnp.concatenate([gain_high.astype(F32), gain_low.astype(F32)], axis=0)
    terms_ref[0:LANES, :] = term_in
    terms_ref[LANES:, :] = term_out
    per_step = 256 // LANES
    for first in range(0, rows_ref.shape[0], per_step):
        cols = index_columns(rows_ref, first, per_step)
        sent, weight = gather_rows(cols, table_ref[...], SPAN)
        for part in range(per_step * LANES // capacity):
            peer = first * LANES // capacity + part
            rows = slice(part * capacity, (part + 1) * capacity)
            sent_ref[peer, 0:capacity, :] = sent[rows].astype(BF16)
            square = weight[rows]
            if capacity < LANES:
                square = jnp.concatenate(
                    [square, jnp.zeros((LANES - capacity, LANES), F32)], axis=0
                )
            extra = jnp.concatenate(
                [square.T[0:2], gain_rows, jnp.zeros((EXTRA - 4, LANES), F32)], axis=0
            )
            sent_ref[peer, capacity:, :] = extra.astype(BF16)


def slope_kernel(
    low_ref, fine_ref, high_ref, recv_ref, off_ref, weight_ref, slope_ref, window_table, fine_table
):
    blocks = fine_ref.shape[0] // SPAN
    window_table[:, 0:LANES] = low_ref[...]
    for block in range(blocks):
        rows = fine_ref[block * SPAN : (block + 1) * SPAN, :]
        window_table[:, (block + 1) * LANES : (block + 2) * LANES] = rows
        fine_table[:, block * LANES : (block + 1) * LANES] = rows
    window_table[:, (blocks + 1) * LANES :] = high_ref[...]
    count = TILE // LANES

    def step(tile, carry):
        recv = index_columns(recv_ref, tile * count, count)
        send = recv + index_columns(off_ref, tile * count, count) + HB
        (sender,) = gather_rows(send, window_table, LANES)
        (receiver,) = gather_rows(recv, fine_table, LANES)
        inputs = jnp.concatenate([sender.astype(BF16), receiver.astype(BF16)], axis=1)
        slope_ref[pl.ds(tile * TILE, TILE), :] = silu_slope(dot(inputs, weight_ref[...]))
        return carry

    lax.fori_loop(0, slope_ref.shape[0] // TILE, step, 0)


def edge_kernel(
    arrived_ref,
    slots_ref,
    slope_ref,
    recv_ref,
    off_ref,
    low_ref,
    fine_ref,
    high_ref,
    weight_ref,
    coarse_terms_ref,
    grad_rows,
    send_sum,
    recv_sum,
    to_prev_ref,
    to_next_ref,
    term_ref,
    gain_ref,
    slot_table,
    grad_table,
):
    peers = arrived_ref.shape[0]
    capacity = arrived_ref.shape[1] - EXTRA
    per_block = SPAN // capacity
    gain = jnp.zeros((1, LANES), F32)
    for peer in range(peers):
        block, part = divmod(peer, per_block)
        rows = slice(part * capacity, (part + 1) * capacity)
        slot_table[rows, block * SPAN : block * SPAN + LANES] = arrived_ref[peer, 0:capacity, :]
        extra = arrived_ref[peer, capacity:, :].astype(F32)
        square = jnp.concatenate([extra, jnp.zeros((LANES - EXTRA, LANES), F32)], axis=0).T
        slot_table[rows, block * SPAN + LANES : (block + 1) * SPAN] = square[0:capacity].astype(
            BF16
        )
        gain += extra[2:3] + extra[3:4]
    gain_ref[...] = gain

    per_step = SPAN // LANES
    for first in range(0, slots_ref.shape[0], per_step):
        cols = index_columns(slots_ref, first, per_step)
        grad, weight = gather_rows(cols, slot_table, SPAN)
        for r in range(2):
            rows = (grad * weight[:, r : r + 1]).astype(BF16).astype(F32)
            grad_rows[pl.ds(2 * first * LANES + r, SPAN, stride=2), :] = rows
    blocks = fine_ref.shape[0] // SPAN
    for block in range(blocks):
        grad_table[:, block * LANES : (block + 1) * LANES] = grad_rows[
            block * SPAN : (block + 1) * SPAN, :
        ].astype(BF16)

    send_sum[...] = jnp.zeros(send_sum.shape, F32)
    recv_sum[...] = jnp.zeros(recv_sum.shape, F32)
    count = TILE // LANES
    one, zero = jnp.ones((), BF16), jnp.zeros((), BF16)

    def add_rows(total, rows, cols, values):
        place = small(rows & (SPAN - 1))
        sub = small(lax.broadcasted_iota(jnp.int32, (SPAN, TILE), 0))
        hot = jnp.where(sub == place, one, zero)
        block = small(cols // SPAN)
        for start in range(0, total.shape[1], 2 * LANES):
            first = start // LANES
            spread = jnp.concatenate(
                [
                    jnp.where(block == jnp.full((), first + i, BF16), values, zero)
                    for i in range(2)
                ],
                axis=1,
            )
            total[:, start : start + 2 * LANES] += dot(hot, spread)

    def step(tile, carry):
        recv_row = jnp.concatenate(
            [recv_ref[pl.ds(tile * count + i, 1), :] for i in range(count)], axis=1
        )
        off_row = jnp.concatenate(
            [off_ref[pl.ds(tile * count + i, 1), :] for i in range(count)], axis=1
        )
        send_row = recv_row + off_row + HB
        recv = index_columns(recv_ref, tile * count, count)
        send = recv + index_columns(off_ref, tile * count, count) + HB
        (upstream,) = gather_rows(recv, grad_table, LANES)
        values = (upstream * slope_ref[pl.ds(tile * TILE, TILE), :]).astype(BF16)
        add_rows(send_sum, send_row, send, values)
        add_rows(recv_sum, recv_row, recv, values)
        return carry

    lax.fori_loop(0, slope_ref.shape[0] // TILE, step, 0)

    weight_send = weight_ref[0:LANES, :]
    first = send_sum[:, 0:LANES]
    last = send_sum[:, (blocks + 1) * LANES :]
    to_prev_ref[...] = back(first, weight_send).astype(BF16)
    to_next_ref[...] = back(last, weight_send).astype(BF16)
    term_send = outer(low_ref[...], first) + outer(high_ref[...], last)
    term_recv = jnp.zeros((LANES, LANES), F32)
    for block in range(blocks):
        rows = fine_ref[block * SPAN : (block + 1) * SPAN, :]
        term_send += outer(rows, send_sum[:, (block + 1) * LANES : (block + 2) * LANES])
        term_recv += outer(rows, recv_sum[:, block * LANES : (block + 1) * LANES])
    term_ref[0:LANES, :] = term_send.astype(BF16)
    term_ref[LANES : 2 * LANES, :] = term_recv.astype(BF16)
    term_ref[2 * LANES :, :] = coarse_terms_ref[...].astype(BF16)


def back(values, weight):
    high, low = two_parts(values)
    return dot(high, weight, NT) + dot(low, weight, NT)


def outer(rows, values):
    high, low = two_parts(values)
    both = dot(rows, jnp.concatenate([high, low], axis=1), TN)
    return both[:, 0:LANES] + both[:, LANES:]


def fine_kernel(grad_rows, send_sum, recv_sum, weight_ref, summed_ref):
    weight_send = weight_ref[0:LANES, :]
    weight_recv = weight_ref[LANES:, :]
    for block in range(grad_rows.shape[0] // SPAN):
        at = slice(block * SPAN, (block + 1) * SPAN)
        sent = send_sum[:, (block + 1) * LANES : (block + 2) * LANES]
        received = recv_sum[:, block * LANES : (block + 1) * LANES]
        summed_ref[at, :] = grad_rows[at, :] + back(sent, weight_send) + back(received, weight_recv)


def per_device(
    fine_latent,
    coarse_latent,
    grad_coarse,
    restrict_weights,
    send_rows,
    pair_slots,
    edge_receivers,
    edge_offsets,
    edge_weight,
    node_weight_in,
    node_weight_out,
    node_gain,
):
    peers = lax.axis_size("curve")
    coarse_count = coarse_latent.shape[0]
    fine_count = fine_latent.shape[0]
    edge_count = edge_receivers.shape[0]
    capacity = send_rows.shape[0] // peers
    payload = capacity + EXTRA
    fine_blocks = fine_count // SPAN
    forward = [(i, i + 1) for i in range(peers - 1)]
    backward = [(i + 1, i) for i in range(peers - 1)]
    params = pltpu.CompilerParams(vmem_limit_bytes=32 * 1024 * 1024)
    alone = pltpu.CompilerParams(vmem_limit_bytes=64 * 1024 * 1024 - 256 * 1024)

    low = lax.ppermute(fine_latent[fine_count - HB :], "curve", forward)
    high = lax.ppermute(fine_latent[:HB], "curve", backward)

    sent, coarse_terms = pl.pallas_call(
        coarse_kernel,
        out_shape=(
            jax.ShapeDtypeStruct((peers, payload, LANES), BF16),
            jax.ShapeDtypeStruct((2 * LANES, LANES), F32),
        ),
        in_specs=[pl.BlockSpec(memory_space=pltpu.HBM)] * 7,
        scratch_shapes=[
            pltpu.VMEM((SPAN, coarse_count), BF16),
            pltpu.VMEM((coarse_count, LANES), BF16),
            pltpu.VMEM((coarse_count, LANES), BF16),
            pltpu.VMEM((2, coarse_count), BF16),
            pltpu.VMEM((peers * capacity // LANES, LANES), jnp.int32),
            pltpu.VMEM((LANES, LANES), BF16),
            pltpu.VMEM((LANES, LANES), BF16),
            pltpu.VMEM((1, LANES), F32),
            pltpu.SemaphoreType.DMA((7,)),
        ],
        compiler_params=alone,
        cost_estimate=pl.CostEstimate(
            flops=2_000_000_000, bytes_accessed=2_000_000, transcendentals=400_000
        ),
        name="coarse_block",
    )(
        coarse_latent,
        grad_coarse,
        restrict_weights,
        send_rows.reshape(-1, LANES),
        node_weight_in,
        node_weight_out,
        node_gain.reshape(1, LANES),
    )
    arrived = lax.all_to_all(sent, "curve", split_axis=0, concat_axis=0, tiled=True)

    receivers = edge_receivers.reshape(-1, LANES)
    offsets = edge_offsets.reshape(-1, LANES)
    slope = pl.pallas_call(
        slope_kernel,
        out_shape=jax.ShapeDtypeStruct((edge_count, LANES), F32),
        scratch_shapes=[
            pltpu.VMEM((SPAN, (fine_blocks + 2) * LANES), BF16),
            pltpu.VMEM((SPAN, fine_blocks * LANES), BF16),
        ],
        compiler_params=params,
        cost_estimate=pl.CostEstimate(
            flops=16_000_000_000, bytes_accessed=5_000_000, transcendentals=800_000
        ),
        name="edge_slope",
    )(low, fine_latent, high, receivers, offsets, edge_weight)

    grad_rows, send_sum, recv_sum, to_prev, to_next, terms, term_gain = pl.pallas_call(
        edge_kernel,
        out_shape=(
            jax.ShapeDtypeStruct((fine_count, LANES), F32),
            jax.ShapeDtypeStruct((SPAN, (fine_blocks + 2) * LANES), F32),
            jax.ShapeDtypeStruct((SPAN, fine_blocks * LANES), F32),
            jax.ShapeDtypeStruct((HB, LANES), BF16),
            jax.ShapeDtypeStruct((HB, LANES), BF16),
            jax.ShapeDtypeStruct((4 * LANES, LANES), BF16),
            jax.ShapeDtypeStruct((1, LANES), F32),
        ),
        scratch_shapes=[
            pltpu.VMEM((SPAN, peers * capacity), BF16),
            pltpu.VMEM((SPAN, fine_blocks * LANES), BF16),
        ],
        compiler_params=params,
        cost_estimate=pl.CostEstimate(
            flops=24_000_000_000, bytes_accessed=8_000_000, transcendentals=0
        ),
        name="edge_back",
    )(
        arrived,
        pair_slots.reshape(-1, LANES),
        slope,
        receivers,
        offsets,
        low,
        fine_latent,
        high,
        edge_weight,
        coarse_terms,
    )
    summed = pl.pallas_call(
        fine_kernel,
        out_shape=jax.ShapeDtypeStruct((fine_count, LANES), F32),
        compiler_params=params,
        cost_estimate=pl.CostEstimate(
            flops=1_000_000_000, bytes_accessed=5_000_000, transcendentals=0
        ),
        name="fine_sums",
    )(grad_rows, send_sum, recv_sum, edge_weight)
    hops = 1
    while hops < peers:
        there = lax.ppermute(terms, "curve", [(i, i ^ hops) for i in range(peers)])
        total = terms.astype(F32) + there.astype(F32)
        terms = total.astype(BF16)
        if hops == 1:
            from_next = lax.ppermute(to_prev, "curve", backward)
            from_prev = lax.ppermute(to_next, "curve", forward)
        hops *= 2
    coarse_scale = 1.0 / math.sqrt(coarse_count * peers)
    edge_scale = 1.0 / math.sqrt(edge_count * peers)
    grad_fine = jnp.concatenate(
        [
            summed[:HB] + from_prev.astype(F32),
            summed[HB : fine_count - HB],
            summed[fine_count - HB :] + from_next.astype(F32),
        ],
        axis=0,
    ).astype(BF16)
    return (
        grad_fine,
        total[: 2 * LANES] * edge_scale,
        total[2 * LANES : 3 * LANES] * coarse_scale,
        total[3 * LANES :] * coarse_scale,
        term_gain.reshape(LANES) * coarse_scale,
    )


def solution(mesh):
    placed = (
        P(("groups", "curve"), None),
        P(("groups", "curve"), None),
        P(("groups", "curve"), None),
        P(None, ("groups", "curve")),
        P(("groups", "curve")),
        P(("groups", "curve")),
        P(("groups", "curve")),
        P(("groups", "curve")),
        P(),
        P(),
        P(),
        P(),
    )
    return jax.shard_map(
        per_device,
        mesh=mesh,
        in_specs=placed,
        out_specs=(
            P(("groups", "curve"), None),
            P("groups", None),
            P("groups", None),
            P("groups", None),
            P("groups"),
        ),
        check_vma=False,
    )
```

```python
import functools
import math

import jax
import jax.numpy as jnp
from jax import lax
from jax.experimental import pallas as pl
from jax.experimental.pallas import tpu as pltpu
from jax.sharding import PartitionSpec as P

HB = 256
LANES = 128
SPAN = 256
EXTRA = 16
TILE = 512
SENDERS = 3

F32 = jnp.float32
BF16 = jnp.bfloat16
NT = (((1,), (1,)), ((), ()))
TN = (((0,), (0,)), ((), ()))


def dot(left, right, dims=(((1,), (0,)), ((), ()))):
    return lax.dot_general(left, right, dims, preferred_element_type=F32)


def silu_slope(values):
    sigm = jax.nn.sigmoid(values)
    return sigm * (1.0 + values * (1.0 - sigm))


def columns(row):
    return jnp.broadcast_to(row, (LANES, LANES)).T


def index_columns(ref, first, count):
    return jnp.concatenate([columns(ref[pl.ds(first + i, 1), :]) for i in range(count)], axis=0)


def small(values):
    return values.astype(F32).astype(BF16)


def place_hot(cols):
    place = small(cols & (SPAN - 1))
    lane = lax.broadcasted_iota(jnp.int32, place.shape, 1)
    one, zero = jnp.ones((), BF16), jnp.zeros((), BF16)
    return jnp.concatenate(
        [jnp.where(place == small(lane + start), one, zero) for start in range(0, SPAN, LANES)],
        axis=1,
    )


def gather_rows(cols, table, width):
    hot = place_hot(cols)
    block = cols // SPAN
    total = table.shape[1]
    step = max(width, 2 * LANES)
    found = [jnp.zeros(cols.shape, F32) for _ in range(width // LANES)]
    for start in range(0, total, step):
        part = dot(hot, table[:, start : start + step])
        for inner in range(0, step, width):
            here = block == (start + inner) // width
            for i in range(len(found)):
                at = inner + i * LANES
                found[i] = jnp.where(here, part[:, at : at + LANES], found[i])
    return found


def two_parts(values):
    high = values.astype(BF16)
    return high, (values - high.astype(F32)).astype(BF16)


def back(values, weight):
    high, low = two_parts(values)
    return dot(high, weight, NT) + dot(low, weight, NT)


def outer(rows, values):
    high, low = two_parts(values)
    both = dot(rows, jnp.concatenate([high, low], axis=1), TN)
    return both[:, 0:LANES] + both[:, LANES:]


def reversed_bits(number, limit):
    result = 0
    while limit > 1:
        result = 2 * result + number % 2
        number //= 2
        limit //= 2
    return result


def fetch(sources, targets, arrivals):
    copies = [
        pltpu.make_async_copy(source, target, arrivals.at[i])
        for i, (source, target) in enumerate(zip(sources, targets))
    ]
    for copy in copies:
        copy.start()
    return copies


def coarse_kernel(
    peers,
    latent_ref,
    grad_ref,
    weights_ref,
    rows_ref,
    w_in_ref,
    w_out_ref,
    gain_ref,
    sent_ref,
    table_ref,
    *held,
):
    *held, arrivals = held
    sources = (latent_ref, grad_ref, weights_ref, rows_ref, w_in_ref, w_out_ref, gain_ref)
    copies = fetch(sources, held, arrivals)
    for copy in copies:
        copy.wait()
    latent_ref, grad_ref, weights_ref, rows_ref, w_in_ref, w_out_ref, gain_ref = held
    count = latent_ref.shape[0]
    chunk = SPAN // peers
    capacity = sent_ref.shape[1] - EXTRA - max(EXTRA, chunk)
    w_in, w_out, gain = w_in_ref[...], w_out_ref[...], gain_ref[...]
    term_in = jnp.zeros((LANES, LANES), F32)
    term_out = jnp.zeros((LANES, LANES), F32)
    term_gain = jnp.zeros((1, LANES), F32)
    for block in range(count // SPAN):
        rows = pl.ds(block * SPAN, SPAN)
        latent = latent_ref[rows, :]
        pre = dot(latent, w_in)
        sigm = jax.nn.sigmoid(pre)
        hidden = (pre * sigm).astype(BF16)
        slope = sigm * (1.0 + pre * (1.0 - sigm))
        mapped = dot(hidden, w_out)
        centred = mapped - jnp.mean(mapped, axis=1, keepdims=True)
        inverse = lax.rsqrt(jnp.mean(centred * centred, axis=1, keepdims=True) + 1e-05)
        normed = centred * inverse
        upstream = grad_ref[rows, :].astype(F32)
        scaled = upstream * gain
        grad_mapped = (
            inverse
            * (
                scaled
                - jnp.mean(scaled, axis=1, keepdims=True)
                - normed * jnp.mean(scaled * normed, axis=1, keepdims=True)
            )
        ).astype(BF16)
        grad_pre = (dot(grad_mapped, w_out, NT) * slope).astype(BF16)
        grad_in = (upstream + dot(grad_pre, w_in, NT)).astype(BF16)
        term_gain += jnp.sum(upstream * normed, axis=0, keepdims=True)
        term_in += dot(latent, grad_pre, TN)
        term_out += dot(hidden, grad_mapped, TN)
        table_ref[:, block * SPAN : block * SPAN + LANES] = grad_in
        for half in range(SPAN // LANES):
            at = block * SPAN + half * LANES
            pair = weights_ref[:, at : at + LANES].astype(F32)
            square = jnp.concatenate([pair, jnp.zeros((LANES - 2, LANES), F32)], axis=0)
            table_ref[
                half * LANES : (half + 1) * LANES, block * SPAN + LANES : (block + 1) * SPAN
            ] = square.T.astype(BF16)
    gain_high, gain_low = two_parts(term_gain)
    gain_rows = jnp.concatenate([gain_high.astype(F32), gain_low.astype(F32)], axis=0)
    terms = jnp.concatenate([term_in, term_out], axis=0)
    per_step = 256 // LANES
    for first in range(0, rows_ref.shape[0], per_step):
        cols = index_columns(rows_ref, first, per_step)
        sent, weight = gather_rows(cols, table_ref[...], SPAN)
        for part in range(per_step * LANES // capacity):
            peer = first * LANES // capacity + part
            rows = slice(part * capacity, (part + 1) * capacity)
            sent_ref[peer, 0:capacity, :] = sent[rows].astype(BF16)
            square = weight[rows]
            if capacity < LANES:
                square = jnp.concatenate(
                    [square, jnp.zeros((LANES - capacity, LANES), F32)], axis=0
                )
            extra = jnp.concatenate(
                [square.T[0:2], gain_rows, jnp.zeros((EXTRA - 4, LANES), F32)], axis=0
            )
            sent_ref[peer, capacity : capacity + EXTRA, :] = extra.astype(BF16)
            first_row = reversed_bits(peer, peers) * chunk
            share = terms[first_row : first_row + chunk]
            if chunk < EXTRA:
                share = jnp.concatenate([share, jnp.zeros((EXTRA - chunk, LANES), F32)], axis=0)
            sent_ref[peer, capacity + EXTRA :, :] = share.astype(BF16)


def order_edges(recv_ref, off_ref, ordered, stats_vmem, wide, counts, fine_count):
    rows = recv_ref.shape[0]
    shift = (fine_count // LANES).bit_length() - 1
    lane = lax.broadcasted_iota(jnp.int32, (LANES, LANES), 1)
    sub = lax.broadcasted_iota(jnp.int32, (LANES, LANES), 0)
    group = 4
    counts[...] = jnp.zeros(counts.shape, F32)

    def count(step, carry):
        for i in range(group):
            row = step * group + i
            recv = columns(recv_ref[pl.ds(row, 1), :])
            wide[pl.ds(row * LANES, LANES), :] = recv
            hot = jnp.where((recv >> shift) == lane, 1.0, 0.0)
            counts[pl.ds(row, 1), :] = jnp.sum(hot, axis=0, keepdims=True)
        return carry

    lax.fori_loop(0, rows // group, count, 0)
    number = counts[...]
    before_row = jnp.where(lane < sub, 1.0, 0.0).astype(BF16)
    before_bucket = jnp.where(sub < lane, 1.0, 0.0).astype(BF16)
    total = jnp.broadcast_to(jnp.sum(number, axis=0, keepdims=True), (8, LANES))
    high = jnp.floor(total * (1.0 / 64.0))
    low = total - 64.0 * high
    start = 64.0 * dot(high.astype(BF16), before_bucket) + dot(low.astype(BF16), before_bucket)
    counts[...] = dot(before_row, number.astype(BF16)) + start[0:1]
    lane_place = small(lane)
    zero = jnp.zeros((), BF16)

    def place(step, moved):
        left, right = [], []
        for i in range(group):
            row = step * group + i
            recv = wide[pl.ds(row * LANES, LANES), :]
            off = columns(off_ref[pl.ds(row, 1), :]) + HB
            bucket = recv >> shift
            same = (bucket == (recv_ref[pl.ds(row, 1), :] >> shift)) & (lane < sub)
            mine = jnp.where(bucket == lane, counts[pl.ds(row, 1), :], 0.0)
            position = jnp.sum(mine + jnp.where(same, 1.0, 0.0), axis=1, keepdims=True)
            position = jnp.broadcast_to(position, (LANES, LANES)).astype(jnp.int32)
            here = (position >> 7) == (lane & 63)
            both = jnp.where(lane < 64, recv & 255, off & 255)
            rest = ((recv >> 8) << 2) | (off >> 8)
            first = small(jnp.where(here, both, 0))
            second = small(jnp.where(here & (lane < 64), rest, 0))
            left.append(jnp.concatenate([first, second], axis=1))
            right.append(
                jnp.where(small(position & 127) == lane_place, jnp.ones((), BF16), zero)
            )
        return moved + dot(jnp.concatenate(left, axis=0), jnp.concatenate(right, axis=0), TN)

    moved = lax.fori_loop(0, rows // group, place, jnp.zeros((2 * LANES, LANES), F32))
    moved = moved.astype(jnp.int32)
    rest = moved[LANES : LANES + rows]
    recv = moved[0:rows] + ((rest >> 2) << 8)
    send = recv + moved[64 : 64 + rows] + ((rest & 3) << 8)
    ordered[0] = recv
    ordered[1] = send
    lane = lax.broadcasted_iota(jnp.int32, (rows, LANES), 1)
    recv, send = recv.astype(F32), send.astype(F32)
    stats = jnp.where(
        lane < 2,
        jnp.where(
            lane == 0,
            jnp.min(recv, axis=1, keepdims=True),
            jnp.max(recv, axis=1, keepdims=True),
        ),
        jnp.where(
            lane == 2,
            jnp.min(send, axis=1, keepdims=True),
            jnp.max(send, axis=1, keepdims=True),
        ),
    )
    stats_vmem[...] = stats.astype(jnp.int32)


def tile_bases(stats, tile, fine_count):
    count = TILE // LANES
    rows = [tile * count + i for i in range(count)]

    def extreme(pick, at):
        value = stats[rows[0], at]
        for row in rows[1:]:
            value = pick(value, stats[row, at])
        return value

    recv_base = jnp.minimum((extreme(jnp.minimum, 0) >> 4) << 4, fine_count - SPAN)
    send_base = jnp.minimum(
        (extreme(jnp.minimum, 2) >> 4) << 4, fine_count + 2 * HB - SENDERS * SPAN
    )
    fits = (extreme(jnp.maximum, 1) - recv_base < SPAN) & (
        extreme(jnp.maximum, 3) - send_base < SENDERS * SPAN
    )
    return recv_base, send_base, fits


def either(fits, recv_base, send_base, fine_count, work):
    @pl.when(fits)
    def _():
        work(recv_base, 1, send_base, SENDERS)

    @pl.when(jnp.logical_not(fits))
    def _():
        work(0, fine_count // SPAN, 0, fine_count // SPAN + 2)


def block_rows(base, block):
    return pl.ds(pl.multiple_of(base + block * SPAN, 16), SPAN)


def gather_blocks(cols, table, base, blocks):
    local = cols - base
    hot = place_hot(local)
    block = local >> 8
    found = None
    for start in range(0, blocks, 2):
        some = range(start, min(start + 2, blocks))
        part = dot(hot, jnp.concatenate([table[block_rows(base, j), :] for j in some], axis=1))
        for i, j in enumerate(some):
            one = part[:, i * LANES : (i + 1) * LANES]
            found = one if found is None else jnp.where(block == j, one, found)
    return found


def slope_kernel(
    recv_hbm,
    off_hbm,
    fine_hbm,
    weight_hbm,
    low_hbm,
    high_hbm,
    slope_hbm,
    ordered,
    stats_vmem,
    recv_ref,
    off_ref,
    window,
    weight_ref,
    wide,
    counts,
    slope_ref,
    stats,
    arrivals,
    stats_done,
    leaving,
):
    fine_count = fine_hbm.shape[0]
    copies = fetch(
        (recv_hbm, off_hbm, fine_hbm, weight_hbm, low_hbm, high_hbm),
        (
            recv_ref,
            off_ref,
            window.at[pl.ds(HB, fine_count)],
            weight_ref,
            window.at[pl.ds(0, HB)],
            window.at[pl.ds(HB + fine_count, HB)],
        ),
        arrivals,
    )
    copies[0].wait()
    copies[1].wait()
    order_edges(recv_ref, off_ref, ordered, stats_vmem, wide, counts, fine_count)
    stats_copy = pltpu.make_async_copy(stats_vmem, stats, stats_done)
    stats_copy.start()
    for copy in copies[2:]:
        copy.wait()
    stats_copy.wait()
    count = TILE // LANES
    weight = weight_ref[...]

    def leave(tile):
        rows = pl.ds(pl.multiple_of(tile * TILE, TILE), TILE)
        return pltpu.make_async_copy(slope_ref.at[rows], slope_hbm.at[rows], leaving.at[tile])

    def step(tile, carry):
        recv_base, send_base, fits = tile_bases(stats, tile, fine_count)

        def work(recv_base, recv_blocks, send_base, send_blocks):
            recv = index_columns(ordered.at[0], tile * count, count)
            send = index_columns(ordered.at[1], tile * count, count)
            sender = gather_blocks(send, window, send_base, send_blocks)
            receiver = gather_blocks(recv + HB, window, recv_base + HB, recv_blocks)
            inputs = jnp.concatenate([sender.astype(BF16), receiver.astype(BF16)], axis=1)
            slope_ref[pl.ds(pl.multiple_of(tile * TILE, TILE), TILE), :] = silu_slope(
                dot(inputs, weight)
            )

        either(fits, recv_base, send_base, fine_count, work)
        leave(tile).start()
        return carry

    tiles = slope_ref.shape[0] // TILE
    lax.fori_loop(0, tiles, step, 0)
    for tile in range(tiles):
        leave(tile).wait()


def edge_kernel(
    stats,
    arrived_hbm,
    slots_hbm,
    slope_hbm,
    ordered_hbm,
    low_hbm,
    fine_hbm,
    high_hbm,
    weight_hbm,
    summed_ref,
    to_prev_ref,
    to_next_ref,
    term_ref,
    coarse_ref,
    gain_ref,
    slot_table,
    grad_table,
    grad_rows,
    send_sum,
    recv_sum,
    arrived_ref,
    slots_ref,
    slope_ref,
    ordered,
    window,
    weight_ref,
    arrivals,
):
    fine_count = fine_hbm.shape[0]
    copies = fetch(
        (
            arrived_hbm,
            slots_hbm,
            ordered_hbm,
            slope_hbm,
            fine_hbm,
            low_hbm,
            high_hbm,
            weight_hbm,
        ),
        (
            arrived_ref,
            slots_ref,
            ordered,
            slope_ref,
            window.at[pl.ds(HB, fine_count)],
            window.at[pl.ds(0, HB)],
            window.at[pl.ds(HB + fine_count, HB)],
            weight_ref,
        ),
        arrivals,
    )
    send_sum[...] = jnp.zeros(send_sum.shape, F32)
    recv_sum[...] = jnp.zeros(recv_sum.shape, F32)
    peers = arrived_ref.shape[0]
    share = max(EXTRA, SPAN // peers)
    capacity = arrived_ref.shape[1] - EXTRA - share
    per_block = SPAN // capacity
    copies[0].wait()
    copies[1].wait()
    coarse = jnp.zeros((share, LANES), F32)
    gain = jnp.zeros((1, LANES), F32)
    for peer in range(peers):
        block, part = divmod(peer, per_block)
        rows = slice(part * capacity, (part + 1) * capacity)
        slot_table[rows, block * SPAN : block * SPAN + LANES] = arrived_ref[peer, 0:capacity, :]
        extra = arrived_ref[peer, capacity : capacity + EXTRA, :].astype(F32)
        square = jnp.concatenate([extra, jnp.zeros((LANES - EXTRA, LANES), F32)], axis=0).T
        slot_table[rows, block * SPAN + LANES : (block + 1) * SPAN] = square[0:capacity].astype(
            BF16
        )
        gain += extra[2:3] + extra[3:4]
        coarse += arrived_ref[peer, capacity + EXTRA :, :].astype(F32)
    coarse_ref[...] = coarse.astype(BF16)
    gain_ref[...] = gain

    per_step = SPAN // LANES
    for first in range(0, slots_ref.shape[0], per_step):
        cols = index_columns(slots_ref, first, per_step)
        grad, weight = gather_rows(cols, slot_table, SPAN)
        for r in range(2):
            rows = (grad * weight[:, r : r + 1]).astype(BF16).astype(F32)
            grad_rows[pl.ds(2 * first * LANES + r, SPAN, stride=2), :] = rows
    grad_table[...] = grad_rows[...].astype(BF16)
    for copy in copies[2:]:
        copy.wait()

    count = TILE // LANES
    one, zero = jnp.ones((), BF16), jnp.zeros((), BF16)
    sub = small(lax.broadcasted_iota(jnp.int32, (SPAN, LANES), 0))

    def add_rows(total, base, blocks, at, cols, values):
        hot = []
        for i in range(count):
            row = ordered[at, pl.ds(cols[0] * count + i, 1), :] - base
            hot.append(jnp.where(sub == small(row & (SPAN - 1)), one, zero))
        hot = jnp.concatenate(hot, axis=1)
        if blocks == 1:
            total[block_rows(base, 0), :] += dot(hot, values)
            return
        block = small((cols[1] - base) >> 8)
        for start in range(0, blocks, 2):
            some = range(start, min(start + 2, blocks))
            spread = [jnp.where(block == jnp.full((), j, BF16), values, zero) for j in some]
            part = dot(hot, jnp.concatenate(spread, axis=1))
            for i, j in enumerate(some):
                total[block_rows(base, j), :] += part[:, i * LANES : (i + 1) * LANES]

    def step(tile, carry):
        recv_base, send_base, fits = tile_bases(stats, tile, fine_count)

        def work(recv_base, recv_blocks, send_base, send_blocks):
            recv = index_columns(ordered.at[0], tile * count, count)
            send = index_columns(ordered.at[1], tile * count, count)
            upstream = gather_blocks(recv, grad_table, recv_base, recv_blocks)
            slope = slope_ref[pl.ds(pl.multiple_of(tile * TILE, TILE), TILE), :]
            values = (upstream * slope).astype(BF16)
            add_rows(recv_sum, recv_base, recv_blocks, 0, (tile, recv), values)
            add_rows(send_sum, send_base, send_blocks, 1, (tile, send), values)

        either(fits, recv_base, send_base, fine_count, work)
        return carry

    lax.fori_loop(0, slope_ref.shape[0] // TILE, step, 0)

    weight_send = weight_ref[0:LANES, :]
    weight_recv = weight_ref[LANES:, :]
    to_prev_ref[...] = back(send_sum[0:HB, :], weight_send).astype(BF16)
    to_next_ref[...] = back(send_sum[HB + fine_count :, :], weight_send).astype(BF16)
    term_send = jnp.zeros((LANES, LANES), F32)
    term_recv = jnp.zeros((LANES, LANES), F32)
    for first in range(0, fine_count + 2 * HB, SPAN):
        at = slice(first, first + SPAN)
        term_send += outer(window[at, :], send_sum[at, :])
    for first in range(0, fine_count, SPAN):
        at = slice(first, first + SPAN)
        moved = slice(HB + first, HB + first + SPAN)
        term_recv += outer(window[moved, :], recv_sum[at, :])
        summed_ref[at, :] = (
            grad_rows[at, :]
            + back(send_sum[moved, :], weight_send)
            + back(recv_sum[at, :], weight_recv)
        )
    term_ref[0:LANES, :] = term_send
    term_ref[LANES:, :] = term_recv


def pair_exchange(upward, downward, even, peers):
    first = [(i, i ^ 1) for i in range(peers)]
    second = [(i, ((i + 1) ^ 1) - 1) for i in range(1, peers - 1)]
    one = lax.ppermute(jnp.where(even, upward, downward), "curve", first)
    two = lax.ppermute(jnp.where(even, downward, upward), "curve", second)
    return jnp.where(even, two, one), jnp.where(even, one, two)


def joined(later, own, there):
    return jnp.where(
        later, jnp.concatenate([there, own], axis=0), jnp.concatenate([own, there], axis=0)
    )


def reduced(term, coarse, device, peers):
    half = term.shape[0] // 2
    odd = (device & 1) == 1
    low, high = term[:half], term[half:]
    gift = jnp.where(odd, low, high).astype(BF16)
    own = jnp.where(odd, high, low) + lax.ppermute(
        gift, "curve", [(i, i ^ 1) for i in range(peers)]
    ).astype(F32)
    hops = peers // 2
    while hops > 1:
        rounded = own.astype(BF16)
        there = lax.ppermute(
            jnp.concatenate([rounded, coarse], axis=0),
            "curve",
            [(i, i ^ hops) for i in range(peers)],
        )
        own = rounded.astype(F32) + there[:half].astype(F32)
        coarse = joined((device & hops) != 0, coarse, there[half:])
        hops //= 2
    coarse = coarse.astype(F32)
    there = lax.ppermute(
        jnp.concatenate([own, coarse], axis=0), "curve", [(i, i ^ 1) for i in range(peers)]
    )
    return joined(odd, own, there[:half]), joined(odd, coarse, there[half:])


def per_device(
    fine_latent,
    coarse_latent,
    grad_coarse,
    restrict_weights,
    send_rows,
    pair_slots,
    edge_receivers,
    edge_offsets,
    edge_weight,
    node_weight_in,
    node_weight_out,
    node_gain,
):
    peers = lax.axis_size("curve")
    device = lax.axis_index("curve")
    even = (device & 1) == 0
    coarse_count = coarse_latent.shape[0]
    fine_count = fine_latent.shape[0]
    edge_count = edge_receivers.shape[0]
    capacity = send_rows.shape[0] // peers
    chunk = SPAN // peers
    share = max(EXTRA, chunk)
    payload = capacity + EXTRA + share
    edge_rows = edge_count // LANES
    window_count = fine_count + 2 * HB
    params = pltpu.CompilerParams(vmem_limit_bytes=64 * 1024 * 1024 - 256 * 1024)
    anywhere = pl.BlockSpec(memory_space=pl.ANY)

    low, high = pair_exchange(fine_latent[fine_count - HB :], fine_latent[:HB], even, peers)

    sent = pl.pallas_call(
        functools.partial(coarse_kernel, peers),
        out_shape=jax.ShapeDtypeStruct((peers, payload, LANES), BF16),
        in_specs=[anywhere] * 7,
        scratch_shapes=[
            pltpu.VMEM((SPAN, coarse_count), BF16),
            pltpu.VMEM((coarse_count, LANES), BF16),
            pltpu.VMEM((coarse_count, LANES), BF16),
            pltpu.VMEM((2, coarse_count), BF16),
            pltpu.VMEM((peers * capacity // LANES, LANES), jnp.int32),
            pltpu.VMEM((LANES, LANES), BF16),
            pltpu.VMEM((LANES, LANES), BF16),
            pltpu.VMEM((1, LANES), F32),
            pltpu.SemaphoreType.DMA((7,)),
        ],
        compiler_params=params,
        cost_estimate=pl.CostEstimate(
            flops=2_000_000_000, bytes_accessed=2_000_000, transcendentals=400_000
        ),
        name="coarse_block",
    )(
        coarse_latent,
        grad_coarse,
        restrict_weights,
        send_rows.reshape(-1, LANES),
        node_weight_in,
        node_weight_out,
        node_gain.reshape(1, LANES),
    )
    arrived = lax.all_to_all(sent, "curve", split_axis=0, concat_axis=0, tiled=True)

    slope, ordered, stats = pl.pallas_call(
        slope_kernel,
        out_shape=(
            jax.ShapeDtypeStruct((edge_count, LANES), F32),
            jax.ShapeDtypeStruct((2, edge_rows, LANES), jnp.int32),
            jax.ShapeDtypeStruct((edge_rows, LANES), jnp.int32),
        ),
        in_specs=[anywhere] * 6,
        out_specs=(
            anywhere,
            pl.BlockSpec(memory_space=pltpu.VMEM),
            pl.BlockSpec(memory_space=pltpu.VMEM),
        ),
        scratch_shapes=[
            pltpu.VMEM((edge_rows, LANES), jnp.int32),
            pltpu.VMEM((edge_rows, LANES), jnp.int32),
            pltpu.VMEM((window_count, LANES), BF16),
            pltpu.VMEM((2 * LANES, LANES), BF16),
            pltpu.VMEM((edge_count, LANES), jnp.int32),
            pltpu.VMEM((LANES, LANES), F32),
            pltpu.VMEM((edge_count, LANES), F32),
            pltpu.SMEM((edge_rows, LANES), jnp.int32),
            pltpu.SemaphoreType.DMA((6,)),
            pltpu.SemaphoreType.DMA,
            pltpu.SemaphoreType.DMA((edge_count // TILE,)),
        ],
        compiler_params=params,
        cost_estimate=pl.CostEstimate(
            flops=16_000_000_000, bytes_accessed=5_000_000, transcendentals=800_000
        ),
        name="edge_slope",
    )(
        edge_receivers.reshape(-1, LANES),
        edge_offsets.reshape(-1, LANES),
        fine_latent,
        edge_weight,
        low,
        high,
    )

    summed, to_prev, to_next, term_edge, coarse_share, term_gain = pl.pallas_call(
        edge_kernel,
        out_shape=(
            jax.ShapeDtypeStruct((fine_count, LANES), F32),
            jax.ShapeDtypeStruct((HB, LANES), BF16),
            jax.ShapeDtypeStruct((HB, LANES), BF16),
            jax.ShapeDtypeStruct((2 * LANES, LANES), F32),
            jax.ShapeDtypeStruct((share, LANES), BF16),
            jax.ShapeDtypeStruct((1, LANES), F32),
        ),
        in_specs=[pl.BlockSpec(memory_space=pltpu.SMEM)] + [anywhere] * 8,
        scratch_shapes=[
            pltpu.VMEM((SPAN, peers * capacity), BF16),
            pltpu.VMEM((fine_count, LANES), BF16),
            pltpu.VMEM((fine_count, LANES), F32),
            pltpu.VMEM((window_count, LANES), F32),
            pltpu.VMEM((fine_count, LANES), F32),
            pltpu.VMEM((peers, payload, LANES), BF16),
            pltpu.VMEM((fine_count // 2 // LANES, LANES), jnp.int32),
            pltpu.VMEM((edge_count, LANES), F32),
            pltpu.VMEM((2, edge_rows, LANES), jnp.int32),
            pltpu.VMEM((window_count, LANES), BF16),
            pltpu.VMEM((2 * LANES, LANES), BF16),
            pltpu.SemaphoreType.DMA((8,)),
        ],
        compiler_params=params,
        cost_estimate=pl.CostEstimate(
            flops=24_000_000_000, bytes_accessed=8_000_000, transcendentals=0
        ),
        name="edge_back",
    )(
        stats,
        arrived,
        pair_slots.reshape(-1, LANES),
        slope,
        ordered,
        low,
        fine_latent,
        high,
        edge_weight,
    )
    edge_terms, coarse_terms = reduced(term_edge, coarse_share[:chunk], device, peers)
    from_prev, from_next = pair_exchange(to_next, to_prev, even, peers)
    coarse_scale = 1.0 / math.sqrt(coarse_count * peers)
    edge_scale = 1.0 / math.sqrt(edge_count * peers)
    grad_fine = jnp.concatenate(
        [
            summed[:HB] + from_prev.astype(F32),
            summed[HB : fine_count - HB],
            summed[fine_count - HB :] + from_next.astype(F32),
        ],
        axis=0,
    ).astype(BF16)
    return (
        grad_fine,
        edge_terms * edge_scale,
        coarse_terms[:LANES] * coarse_scale,
        coarse_terms[LANES:] * coarse_scale,
        term_gain.reshape(LANES) * coarse_scale,
    )


def solution(mesh):
    placed = (
        P(("groups", "curve"), None),
        P(("groups", "curve"), None),
        P(("groups", "curve"), None),
        P(None, ("groups", "curve")),
        P(("groups", "curve")),
        P(("groups", "curve")),
        P(("groups", "curve")),
        P(("groups", "curve")),
        P(),
        P(),
        P(),
        P(),
    )
    return jax.shard_map(
        per_device,
        mesh=mesh,
        in_specs=placed,
        out_specs=(
            P(("groups", "curve"), None),
            P("groups", None),
            P("groups", None),
            P("groups", None),
            P("groups"),
        ),
        check_vma=False,
    )
```

```python
import functools
import math

import jax
import jax.numpy as jnp
from jax import lax
from jax.experimental import pallas as pl
from jax.experimental.pallas import tpu as pltpu
from jax.sharding import PartitionSpec as P

HB = 256
LANES = 128
SPAN = 256
EXTRA = 16
TILE = 512
GROUP = 4
SENDERS = 3

F32 = jnp.float32
BF16 = jnp.bfloat16
NT = (((1,), (1,)), ((), ()))
TN = (((0,), (0,)), ((), ()))


def dot(left, right, dims=(((1,), (0,)), ((), ()))):
    return lax.dot_general(left, right, dims, preferred_element_type=F32)


def silu_slope(values):
    sigm = jax.nn.sigmoid(values)
    return sigm * (1.0 + values * (1.0 - sigm))


def columns(row):
    return jnp.broadcast_to(row, (LANES, LANES)).T


def index_columns(ref, first, count):
    return jnp.concatenate([columns(ref[pl.ds(first + i, 1), :]) for i in range(count)], axis=0)


def small(values):
    return values.astype(F32).astype(BF16)


def place_hot(cols):
    place = small(cols & (SPAN - 1))
    lane = lax.broadcasted_iota(jnp.int32, place.shape, 1)
    one, zero = jnp.ones((), BF16), jnp.zeros((), BF16)
    return jnp.concatenate(
        [jnp.where(place == small(lane + start), one, zero) for start in range(0, SPAN, LANES)],
        axis=1,
    )


def gather_rows(cols, table, width):
    hot = place_hot(cols)
    block = cols // SPAN
    total = table.shape[1]
    step = max(width, 2 * LANES)
    found = [jnp.zeros(cols.shape, F32) for _ in range(width // LANES)]
    for start in range(0, total, step):
        part = dot(hot, table[:, start : start + step])
        for inner in range(0, step, width):
            here = block == (start + inner) // width
            for i in range(len(found)):
                at = inner + i * LANES
                found[i] = jnp.where(here, part[:, at : at + LANES], found[i])
    return found


def two_parts(values):
    high = values.astype(BF16)
    return high, (values - high.astype(F32)).astype(BF16)


def back(values, weight):
    high, low = two_parts(values)
    return dot(high, weight, NT) + dot(low, weight, NT)


def outer(rows, values):
    high, low = two_parts(values)
    both = dot(rows, jnp.concatenate([high, low], axis=1), TN)
    return both[:, 0:LANES] + both[:, LANES:]


def reversed_bits(number, limit):
    result = 0
    while limit > 1:
        result = 2 * result + number % 2
        number //= 2
        limit //= 2
    return result


def fetch(sources, targets, arrivals):
    copies = [
        pltpu.make_async_copy(source, target, arrivals.at[i])
        for i, (source, target) in enumerate(zip(sources, targets))
    ]
    for copy in copies:
        copy.start()
    return copies


def coarse_kernel(
    peers,
    latent_ref,
    grad_ref,
    weights_ref,
    rows_ref,
    w_in_ref,
    w_out_ref,
    gain_ref,
    sent_ref,
    table_ref,
    *held,
):
    *held, arrivals = held
    sources = (latent_ref, grad_ref, weights_ref, rows_ref, w_in_ref, w_out_ref, gain_ref)
    copies = fetch(sources, held, arrivals)
    for copy in copies:
        copy.wait()
    latent_ref, grad_ref, weights_ref, rows_ref, w_in_ref, w_out_ref, gain_ref = held
    count = latent_ref.shape[0]
    chunk = SPAN // peers
    capacity = sent_ref.shape[1] - EXTRA - max(EXTRA, chunk)
    w_in, w_out, gain = w_in_ref[...], w_out_ref[...], gain_ref[...]
    term_in = jnp.zeros((LANES, LANES), F32)
    term_out = jnp.zeros((LANES, LANES), F32)
    term_gain = jnp.zeros((1, LANES), F32)
    for block in range(count // SPAN):
        rows = pl.ds(block * SPAN, SPAN)
        latent = latent_ref[rows, :]
        pre = dot(latent, w_in)
        sigm = jax.nn.sigmoid(pre)
        hidden = (pre * sigm).astype(BF16)
        slope = sigm * (1.0 + pre * (1.0 - sigm))
        mapped = dot(hidden, w_out)
        centred = mapped - jnp.mean(mapped, axis=1, keepdims=True)
        inverse = lax.rsqrt(jnp.mean(centred * centred, axis=1, keepdims=True) + 1e-05)
        normed = centred * inverse
        upstream = grad_ref[rows, :].astype(F32)
        scaled = upstream * gain
        grad_mapped = (
            inverse
            * (
                scaled
                - jnp.mean(scaled, axis=1, keepdims=True)
                - normed * jnp.mean(scaled * normed, axis=1, keepdims=True)
            )
        ).astype(BF16)
        grad_pre = (dot(grad_mapped, w_out, NT) * slope).astype(BF16)
        grad_in = (upstream + dot(grad_pre, w_in, NT)).astype(BF16)
        term_gain += jnp.sum(upstream * normed, axis=0, keepdims=True)
        term_in += dot(latent, grad_pre, TN)
        term_out += dot(hidden, grad_mapped, TN)
        table_ref[:, block * SPAN : block * SPAN + LANES] = grad_in
        for half in range(SPAN // LANES):
            at = block * SPAN + half * LANES
            pair = weights_ref[:, at : at + LANES].astype(F32)
            square = jnp.concatenate([pair, jnp.zeros((LANES - 2, LANES), F32)], axis=0)
            table_ref[
                half * LANES : (half + 1) * LANES, block * SPAN + LANES : (block + 1) * SPAN
            ] = square.T.astype(BF16)
    gain_high, gain_low = two_parts(term_gain)
    gain_rows = jnp.concatenate([gain_high.astype(F32), gain_low.astype(F32)], axis=0)
    terms = jnp.concatenate([term_in, term_out], axis=0)
    per_step = 256 // LANES
    for first in range(0, rows_ref.shape[0], per_step):
        cols = index_columns(rows_ref, first, per_step)
        sent, weight = gather_rows(cols, table_ref[...], SPAN)
        for part in range(per_step * LANES // capacity):
            peer = first * LANES // capacity + part
            rows = slice(part * capacity, (part + 1) * capacity)
            sent_ref[peer, 0:capacity, :] = sent[rows].astype(BF16)
            square = weight[rows]
            if capacity < LANES:
                square = jnp.concatenate(
                    [square, jnp.zeros((LANES - capacity, LANES), F32)], axis=0
                )
            extra = jnp.concatenate(
                [square.T[0:2], gain_rows, jnp.zeros((EXTRA - 4, LANES), F32)], axis=0
            )
            sent_ref[peer, capacity : capacity + EXTRA, :] = extra.astype(BF16)
            first_row = reversed_bits(peer, peers) * chunk
            share = terms[first_row : first_row + chunk]
            if chunk < EXTRA:
                share = jnp.concatenate([share, jnp.zeros((EXTRA - chunk, LANES), F32)], axis=0)
            sent_ref[peer, capacity + EXTRA :, :] = share.astype(BF16)


def order_edges(recv_ref, off_ref, ordered, stats_vmem, positions, fine_count):
    rows = recv_ref.shape[0]
    shift = (fine_count // LANES).bit_length() - 1
    lane = lax.broadcasted_iota(jnp.int32, (LANES, LANES), 1)
    sub = lax.broadcasted_iota(jnp.int32, (LANES, LANES), 0)
    level = small(sub)
    one, zero = jnp.ones((), BF16), jnp.zeros((), BF16)

    def hot(row):
        return jnp.where(level == small(row), one, zero)

    number = jnp.zeros((LANES, LANES), BF16)
    for row in range(rows):
        number += hot(recv_ref[row : row + 1, :] >> shift)
    ones = jnp.ones((LANES, LANES), BF16)
    total = dot(number, ones)
    high = jnp.floor(total * (1.0 / 64.0))
    low = total - 64.0 * high
    before = jnp.where(lane < sub, 1.0, 0.0).astype(BF16)
    start = 64.0 * dot(before, high.astype(BF16)) + dot(before, low.astype(BF16))
    after = jnp.where(sub < lane, 1.0, 0.0).astype(BF16)
    prefix = jnp.concatenate([after, ones], axis=1)
    group = 16

    def place(step, filled):
        for i in range(group):
            row = step * group + i
            bucket = recv_ref[pl.ds(row, 1), :] >> shift
            found = dot(hot(bucket), prefix)
            mine = jnp.where(sub == bucket, found[:, 0:LANES] + filled, 0.0)
            positions[pl.ds(row, 1), :] = jnp.sum(mine, axis=0, keepdims=True).astype(jnp.int32)
            filled = filled + found[:, LANES:]
        return filled

    lax.fori_loop(0, rows // group, place, start)

    def move(step, moved):
        for part in range(0, group, 4):
            left, right = [], []
            for i in range(part, part + 4):
                row = step * group + i
                position = positions[pl.ds(row, 1), :]
                recv = recv_ref[pl.ds(row, 1), :]
                off = off_ref[pl.ds(row, 1), :] + HB
                rest = ((recv >> 8) << 2) | (off >> 8)
                here = level[0:64] == small(position >> 7)
                left.append(
                    jnp.concatenate(
                        [
                            jnp.where(here, small(value), zero)
                            for value in (recv & 255, off & 255, rest)
                        ],
                        axis=0,
                    )
                )
                right.append(hot(position & 127))
            moved = moved + dot(
                jnp.concatenate(left, axis=1), jnp.concatenate(right, axis=1), NT
            )
        return moved

    moved = lax.fori_loop(0, rows // group, move, jnp.zeros((192, LANES), F32))
    moved = moved.astype(jnp.int32)
    rest = moved[LANES : LANES + rows]
    recv = moved[0:rows] + ((rest >> 2) << 8)
    send = recv + moved[64 : 64 + rows] + ((rest & 3) << 8)
    ordered[0] = recv
    ordered[1] = send
    lane = lax.broadcasted_iota(jnp.int32, (rows, LANES), 1)
    recv, send = recv.astype(F32), send.astype(F32)
    stats = jnp.where(
        lane < 2,
        jnp.where(
            lane == 0,
            jnp.min(recv, axis=1, keepdims=True),
            jnp.max(recv, axis=1, keepdims=True),
        ),
        jnp.where(
            lane == 2,
            jnp.min(send, axis=1, keepdims=True),
            jnp.max(send, axis=1, keepdims=True),
        ),
    )
    stats_vmem[...] = stats.astype(jnp.int32)


def tile_bases(stats, tile, fine_count):
    count = TILE // LANES
    rows = [tile * count + i for i in range(count)]

    def extreme(pick, at):
        value = stats[rows[0], at]
        for row in rows[1:]:
            value = pick(value, stats[row, at])
        return value

    recv_base = jnp.minimum((extreme(jnp.minimum, 0) >> 4) << 4, fine_count - SPAN)
    send_base = jnp.minimum(
        (extreme(jnp.minimum, 2) >> 4) << 4, fine_count + 2 * HB - SENDERS * SPAN
    )
    fits = (extreme(jnp.maximum, 1) - recv_base < SPAN) & (
        extreme(jnp.maximum, 3) - send_base < SENDERS * SPAN
    )
    return recv_base, send_base, fits


def each_group(step, stats, fine_count, near, far):
    tiles = [step * GROUP + i for i in range(GROUP)]
    places = [tile_bases(stats, tile, fine_count) for tile in tiles]
    fits = functools.reduce(jnp.logical_and, [place[2] for place in places])

    @pl.when(fits)
    def _():
        near(tiles, [place[:2] for place in places])

    @pl.when(jnp.logical_not(fits))
    def _():
        def one(i, carry):
            far(step * GROUP + i)
            return carry

        lax.fori_loop(0, GROUP, one, 0)


def block_rows(base, block):
    return pl.ds(pl.multiple_of(base + block * SPAN, 16), SPAN)


def gather_blocks(cols, table, base, blocks):
    local = cols - base
    hot = place_hot(local)
    block = local >> 8
    found = None
    for start in range(0, blocks, 2):
        some = range(start, min(start + 2, blocks))
        part = dot(hot, jnp.concatenate([table[block_rows(base, j), :] for j in some], axis=1))
        for i, j in enumerate(some):
            one = part[:, i * LANES : (i + 1) * LANES]
            found = one if found is None else jnp.where(block == j, one, found)
    return found


def slope_kernel(
    odd_ref,
    recv_hbm,
    off_hbm,
    fine_hbm,
    weight_hbm,
    first_hbm,
    second_hbm,
    slope_hbm,
    window_out,
    ordered,
    stats_vmem,
    recv_ref,
    off_ref,
    window,
    weight_ref,
    halos,
    positions,
    slope_ref,
    stats,
    arrivals,
    stats_done,
    leaving,
):
    fine_count = fine_hbm.shape[0]
    copies = fetch(
        (recv_hbm, off_hbm, fine_hbm, weight_hbm, first_hbm, second_hbm),
        (
            recv_ref,
            off_ref,
            window.at[pl.ds(HB, fine_count)],
            weight_ref,
            halos.at[0],
            halos.at[1],
        ),
        arrivals,
    )
    copies[0].wait()
    copies[1].wait()
    order_edges(recv_ref, off_ref, ordered, stats_vmem, positions, fine_count)
    stats_copy = pltpu.make_async_copy(stats_vmem, stats, stats_done)
    stats_copy.start()
    for copy in copies[2:]:
        copy.wait()
    odd = odd_ref[0]
    window[0:HB, :] = halos[1 - odd]
    window[HB + fine_count :, :] = halos[odd]
    window_copy = pltpu.make_async_copy(window, window_out, leaving.at[leaving.shape[0] - 1])
    window_copy.start()
    stats_copy.wait()
    count = TILE // LANES
    weight = weight_ref[...]

    def tile_rows(tile):
        return pl.ds(pl.multiple_of(tile * TILE, TILE), TILE)

    def leave(tile):
        rows = tile_rows(tile)
        return pltpu.make_async_copy(slope_ref.at[rows], slope_hbm.at[rows], leaving.at[tile])

    def near(tiles, places):
        work = []
        for tile, (recv_base, send_base) in zip(tiles, places):
            recv = index_columns(ordered.at[0], tile * count, count)
            send = index_columns(ordered.at[1], tile * count, count)
            sender = gather_blocks(send, window, send_base, SENDERS)
            receiver = gather_blocks(recv + HB, window, recv_base + HB, 1)
            work.append((sender, receiver))
        for tile, (sender, receiver) in zip(tiles, work):
            inputs = jnp.concatenate([sender.astype(BF16), receiver.astype(BF16)], axis=1)
            slope_ref[tile_rows(tile), :] = silu_slope(dot(inputs, weight))

    def far(tile):
        recv = index_columns(ordered.at[0], tile * count, count)
        send = index_columns(ordered.at[1], tile * count, count)
        sender = gather_blocks(send, window, 0, fine_count // SPAN + 2)
        receiver = gather_blocks(recv + HB, window, HB, fine_count // SPAN)
        inputs = jnp.concatenate([sender.astype(BF16), receiver.astype(BF16)], axis=1)
        slope_ref[tile_rows(tile), :] = silu_slope(dot(inputs, weight))

    def step(index, carry):
        each_group(index, stats, fine_count, near, far)
        for i in range(GROUP):
            leave(index * GROUP + i).start()
        return carry

    tiles = slope_ref.shape[0] // TILE
    lax.fori_loop(0, tiles // GROUP, step, 0)
    window_copy.wait()
    for tile in range(tiles):
        leave(tile).wait()


def edge_kernel(
    odd_ref,
    stats,
    arrived_hbm,
    slots_hbm,
    slope_hbm,
    ordered_hbm,
    window_hbm,
    weight_hbm,
    summed_ref,
    first_ref,
    second_ref,
    keep_ref,
    gift_ref,
    coarse_ref,
    gain_ref,
    slot_table,
    grad_table,
    grad_rows,
    send_sum,
    recv_sum,
    arrived_ref,
    slots_ref,
    slope_ref,
    ordered,
    window,
    weight_ref,
    arrivals,
):
    fine_count = summed_ref.shape[0]
    copies = fetch(
        (arrived_hbm, slots_hbm, ordered_hbm, slope_hbm, window_hbm, weight_hbm),
        (arrived_ref, slots_ref, ordered, slope_ref, window, weight_ref),
        arrivals,
    )
    send_sum[...] = jnp.zeros(send_sum.shape, F32)
    recv_sum[...] = jnp.zeros(recv_sum.shape, F32)
    peers = arrived_ref.shape[0]
    share = max(EXTRA, SPAN // peers)
    capacity = arrived_ref.shape[1] - EXTRA - share
    per_block = SPAN // capacity
    copies[0].wait()
    copies[1].wait()
    coarse = jnp.zeros((share, LANES), F32)
    gain = jnp.zeros((1, LANES), F32)
    for peer in range(peers):
        block, part = divmod(peer, per_block)
        rows = slice(part * capacity, (part + 1) * capacity)
        slot_table[rows, block * SPAN : block * SPAN + LANES] = arrived_ref[peer, 0:capacity, :]
        extra = arrived_ref[peer, capacity : capacity + EXTRA, :].astype(F32)
        square = jnp.concatenate([extra, jnp.zeros((LANES - EXTRA, LANES), F32)], axis=0).T
        slot_table[rows, block * SPAN + LANES : (block + 1) * SPAN] = square[0:capacity].astype(
            BF16
        )
        gain += extra[2:3] + extra[3:4]
        coarse += arrived_ref[peer, capacity + EXTRA :, :].astype(F32)
    coarse_ref[...] = coarse.astype(BF16)
    gain_ref[...] = gain

    per_step = SPAN // LANES
    for first in range(0, slots_ref.shape[0], per_step):
        cols = index_columns(slots_ref, first, per_step)
        grad, weight = gather_rows(cols, slot_table, SPAN)
        for r in range(2):
            rows = (grad * weight[:, r : r + 1]).astype(BF16).astype(F32)
            grad_rows[pl.ds(2 * first * LANES + r, SPAN, stride=2), :] = rows
    grad_table[...] = grad_rows[...].astype(BF16)
    for copy in copies[2:]:
        copy.wait()

    count = TILE // LANES
    one, zero = jnp.ones((), BF16), jnp.zeros((), BF16)
    sub = small(lax.broadcasted_iota(jnp.int32, (SPAN, LANES), 0))

    def spread_rows(base, blocks, at, tile, cols, values):
        hot = []
        for i in range(count):
            row = ordered[at, pl.ds(tile * count + i, 1), :] - base
            hot.append(jnp.where(sub == small(row & (SPAN - 1)), one, zero))
        hot = jnp.concatenate(hot, axis=1)
        if blocks == 1:
            return [dot(hot, values)]
        block = small((cols - base) >> 8)
        parts = []
        for start in range(0, blocks, 2):
            some = range(start, min(start + 2, blocks))
            spread = [jnp.where(block == jnp.full((), j, BF16), values, zero) for j in some]
            part = dot(hot, jnp.concatenate(spread, axis=1))
            parts += [part[:, i * LANES : (i + 1) * LANES] for i in range(len(some))]
        return parts

    def add_parts(total, base, parts):
        for j, part in enumerate(parts):
            total[block_rows(base, j), :] += part

    def edge_values(tile, recv, base, blocks):
        upstream = gather_blocks(recv, grad_table, base, blocks)
        slope = slope_ref[pl.ds(pl.multiple_of(tile * TILE, TILE), TILE), :]
        return (upstream * slope).astype(BF16)

    def near(tiles, places):
        work = []
        for tile, (recv_base, send_base) in zip(tiles, places):
            recv = index_columns(ordered.at[0], tile * count, count)
            values = edge_values(tile, recv, recv_base, 1)
            work.append((spread_rows(recv_base, 1, 0, tile, recv, values), values))
        for (recv_base, _), (parts, _) in zip(places, work):
            add_parts(recv_sum, recv_base, parts)
        sums = []
        for tile, (_, send_base), (_, values) in zip(tiles, places, work):
            send = index_columns(ordered.at[1], tile * count, count)
            sums.append(spread_rows(send_base, SENDERS, 1, tile, send, values))
        for (_, send_base), parts in zip(places, sums):
            add_parts(send_sum, send_base, parts)

    def far(tile):
        recv = index_columns(ordered.at[0], tile * count, count)
        send = index_columns(ordered.at[1], tile * count, count)
        blocks = fine_count // SPAN
        values = edge_values(tile, recv, 0, blocks)
        add_parts(recv_sum, 0, spread_rows(0, blocks, 0, tile, recv, values))
        add_parts(send_sum, 0, spread_rows(0, blocks + 2, 1, tile, send, values))

    def step(index, carry):
        each_group(index, stats, fine_count, near, far)
        return carry

    lax.fori_loop(0, slope_ref.shape[0] // TILE // GROUP, step, 0)

    weight_send = weight_ref[0:LANES, :]
    weight_recv = weight_ref[LANES:, :]
    odd = odd_ref[0]
    to_prev = back(send_sum[0:HB, :], weight_send)
    to_next = back(send_sum[HB + fine_count :, :], weight_send)
    first_ref[...] = jnp.where(odd == 0, to_next, to_prev).astype(BF16)
    second_ref[...] = jnp.where(odd == 0, to_prev, to_next).astype(BF16)
    term_send = jnp.zeros((LANES, LANES), F32)
    term_recv = jnp.zeros((LANES, LANES), F32)
    for first in range(0, fine_count + 2 * HB, SPAN):
        at = slice(first, first + SPAN)
        term_send += outer(window[at, :], send_sum[at, :])
    for first in range(0, fine_count, SPAN):
        at = slice(first, first + SPAN)
        moved = slice(HB + first, HB + first + SPAN)
        term_recv += outer(window[moved, :], recv_sum[at, :])
        summed_ref[at, :] = (
            grad_rows[at, :]
            + back(send_sum[moved, :], weight_send)
            + back(recv_sum[at, :], weight_recv)
        )
    keep_ref[...] = jnp.where(odd == 0, term_send, term_recv)
    gift_ref[...] = jnp.where(odd == 0, term_recv, term_send).astype(BF16)


def pair_exchange(first, second, peers):
    pairs = [(i, i ^ 1) for i in range(peers)]
    between = [(i, ((i + 1) ^ 1) - 1) for i in range(1, peers - 1)]
    return lax.ppermute(first, "curve", pairs), lax.ppermute(second, "curve", between)


def joined(later, own, there):
    return jnp.where(
        later, jnp.concatenate([there, own], axis=0), jnp.concatenate([own, there], axis=0)
    )


def reduced(keep, gift, coarse, device, peers):
    half = keep.shape[0]
    odd = (device & 1) == 1
    own = keep + lax.ppermute(gift, "curve", [(i, i ^ 1) for i in range(peers)]).astype(F32)
    hops = peers // 2
    while hops > 1:
        rounded = own.astype(BF16)
        there = lax.ppermute(
            jnp.concatenate([rounded, coarse], axis=0),
            "curve",
            [(i, i ^ hops) for i in range(peers)],
        )
        own = rounded.astype(F32) + there[:half].astype(F32)
        coarse = joined((device & hops) != 0, coarse, there[half:])
        hops //= 2
    coarse = coarse.astype(F32)
    there = lax.ppermute(
        jnp.concatenate([own, coarse], axis=0), "curve", [(i, i ^ 1) for i in range(peers)]
    )
    return joined(odd, own, there[:half]), joined(odd, coarse, there[half:])


def per_device(
    fine_latent,
    coarse_latent,
    grad_coarse,
    restrict_weights,
    send_rows,
    pair_slots,
    edge_receivers,
    edge_offsets,
    edge_weight,
    node_weight_in,
    node_weight_out,
    node_gain,
):
    peers = lax.axis_size("curve")
    device = lax.axis_index("curve")
    odd = (device & 1).astype(jnp.int32)
    even = odd == 0
    coarse_count = coarse_latent.shape[0]
    fine_count = fine_latent.shape[0]
    edge_count = edge_receivers.shape[0]
    capacity = send_rows.shape[0] // peers
    chunk = SPAN // peers
    share = max(EXTRA, chunk)
    payload = capacity + EXTRA + share
    edge_rows = edge_count // LANES
    window_count = fine_count + 2 * HB
    params = pltpu.CompilerParams(vmem_limit_bytes=64 * 1024 * 1024 - 256 * 1024)
    anywhere = pl.BlockSpec(memory_space=pl.ANY)

    head, end = fine_latent[:HB], fine_latent[fine_count - HB :]
    halos = pair_exchange(jnp.where(even, end, head), jnp.where(even, head, end), peers)
    parity = odd.reshape(1)
    scalar = pl.BlockSpec(memory_space=pltpu.SMEM)

    sent = pl.pallas_call(
        functools.partial(coarse_kernel, peers),
        out_shape=jax.ShapeDtypeStruct((peers, payload, LANES), BF16),
        in_specs=[anywhere] * 7,
        scratch_shapes=[
            pltpu.VMEM((SPAN, coarse_count), BF16),
            pltpu.VMEM((coarse_count, LANES), BF16),
            pltpu.VMEM((coarse_count, LANES), BF16),
            pltpu.VMEM((2, coarse_count), BF16),
            pltpu.VMEM((peers * capacity // LANES, LANES), jnp.int32),
            pltpu.VMEM((LANES, LANES), BF16),
            pltpu.VMEM((LANES, LANES), BF16),
            pltpu.VMEM((1, LANES), F32),
            pltpu.SemaphoreType.DMA((7,)),
        ],
        compiler_params=params,
        cost_estimate=pl.CostEstimate(
            flops=2_000_000_000, bytes_accessed=2_000_000, transcendentals=400_000
        ),
        name="coarse_block",
    )(
        coarse_latent,
        grad_coarse,
        restrict_weights,
        send_rows.reshape(-1, LANES),
        node_weight_in,
        node_weight_out,
        node_gain.reshape(1, LANES),
    )
    arrived = lax.all_to_all(sent, "curve", split_axis=0, concat_axis=0, tiled=True)

    slope, window, ordered, stats = pl.pallas_call(
        slope_kernel,
        out_shape=(
            jax.ShapeDtypeStruct((edge_count, LANES), F32),
            jax.ShapeDtypeStruct((window_count, LANES), BF16),
            jax.ShapeDtypeStruct((2, edge_rows, LANES), jnp.int32),
            jax.ShapeDtypeStruct((edge_rows, LANES), jnp.int32),
        ),
        in_specs=[scalar] + [anywhere] * 6,
        out_specs=(
            anywhere,
            anywhere,
            pl.BlockSpec(memory_space=pltpu.VMEM),
            pl.BlockSpec(memory_space=pltpu.VMEM),
        ),
        scratch_shapes=[
            pltpu.VMEM((edge_rows, LANES), jnp.int32),
            pltpu.VMEM((edge_rows, LANES), jnp.int32),
            pltpu.VMEM((window_count, LANES), BF16),
            pltpu.VMEM((2 * LANES, LANES), BF16),
            pltpu.VMEM((2, HB, LANES), BF16),
            pltpu.VMEM((edge_rows, LANES), jnp.int32),
            pltpu.VMEM((edge_count, LANES), F32),
            pltpu.SMEM((edge_rows, LANES), jnp.int32),
            pltpu.SemaphoreType.DMA((6,)),
            pltpu.SemaphoreType.DMA,
            pltpu.SemaphoreType.DMA((edge_count // TILE + 1,)),
        ],
        compiler_params=params,
        cost_estimate=pl.CostEstimate(
            flops=16_000_000_000, bytes_accessed=5_000_000, transcendentals=800_000
        ),
        name="edge_slope",
    )(
        parity,
        edge_receivers.reshape(-1, LANES),
        edge_offsets.reshape(-1, LANES),
        fine_latent,
        edge_weight,
        *halos,
    )

    summed, first, second, keep, gift, coarse_share, term_gain = pl.pallas_call(
        edge_kernel,
        out_shape=(
            jax.ShapeDtypeStruct((fine_count, LANES), F32),
            jax.ShapeDtypeStruct((HB, LANES), BF16),
            jax.ShapeDtypeStruct((HB, LANES), BF16),
            jax.ShapeDtypeStruct((LANES, LANES), F32),
            jax.ShapeDtypeStruct((LANES, LANES), BF16),
            jax.ShapeDtypeStruct((share, LANES), BF16),
            jax.ShapeDtypeStruct((1, LANES), F32),
        ),
        in_specs=[scalar] * 2 + [anywhere] * 6,
        scratch_shapes=[
            pltpu.VMEM((SPAN, peers * capacity), BF16),
            pltpu.VMEM((fine_count, LANES), BF16),
            pltpu.VMEM((fine_count, LANES), F32),
            pltpu.VMEM((window_count, LANES), F32),
            pltpu.VMEM((fine_count, LANES), F32),
            pltpu.VMEM((peers, payload, LANES), BF16),
            pltpu.VMEM((fine_count // 2 // LANES, LANES), jnp.int32),
            pltpu.VMEM((edge_count, LANES), F32),
            pltpu.VMEM((2, edge_rows, LANES), jnp.int32),
            pltpu.VMEM((window_count, LANES), BF16),
            pltpu.VMEM((2 * LANES, LANES), BF16),
            pltpu.SemaphoreType.DMA((6,)),
        ],
        compiler_params=params,
        cost_estimate=pl.CostEstimate(
            flops=24_000_000_000, bytes_accessed=8_000_000, transcendentals=0
        ),
        name="edge_back",
    )(
        parity,
        stats,
        arrived,
        pair_slots.reshape(-1, LANES),
        slope,
        ordered,
        window,
        edge_weight,
    )
    edge_terms, coarse_terms = reduced(keep, gift, coarse_share[:chunk], device, peers)
    one, two = pair_exchange(first, second, peers)
    from_next, from_prev = jnp.where(even, one, two), jnp.where(even, two, one)
    coarse_scale = 1.0 / math.sqrt(coarse_count * peers)
    edge_scale = 1.0 / math.sqrt(edge_count * peers)
    grad_fine = jnp.concatenate(
        [
            summed[:HB] + from_prev.astype(F32),
            summed[HB : fine_count - HB],
            summed[fine_count - HB :] + from_next.astype(F32),
        ],
        axis=0,
    ).astype(BF16)
    return (
        grad_fine,
        edge_terms * edge_scale,
        coarse_terms[:LANES] * coarse_scale,
        coarse_terms[LANES:] * coarse_scale,
        term_gain.reshape(LANES) * coarse_scale,
    )


def solution(mesh):
    placed = (
        P(("groups", "curve"), None),
        P(("groups", "curve"), None),
        P(("groups", "curve"), None),
        P(None, ("groups", "curve")),
        P(("groups", "curve")),
        P(("groups", "curve")),
        P(("groups", "curve")),
        P(("groups", "curve")),
        P(),
        P(),
        P(),
        P(),
    )
    return jax.shard_map(
        per_device,
        mesh=mesh,
        in_specs=placed,
        out_specs=(
            P(("groups", "curve"), None),
            P("groups", None),
            P("groups", None),
            P("groups", None),
            P("groups"),
        ),
        check_vma=False,
    )
```

```python
import functools
import math

import jax
import jax.numpy as jnp
from jax import lax
from jax.experimental import pallas as pl
from jax.experimental.pallas import tpu as pltpu
from jax.sharding import PartitionSpec as P

HB = 256
LANES = 128
SPAN = 256
EXTRA = 16
TILE = 512
GROUP = 4
SENDERS = 3

F32 = jnp.float32
BF16 = jnp.bfloat16
NT = (((1,), (1,)), ((), ()))
TN = (((0,), (0,)), ((), ()))


def dot(left, right, dims=(((1,), (0,)), ((), ()))):
    return lax.dot_general(left, right, dims, preferred_element_type=F32)


def silu_slope(values):
    sigm = jax.nn.sigmoid(values)
    return sigm * (1.0 + values * (1.0 - sigm))


def columns(row):
    return jnp.broadcast_to(row, (LANES, LANES)).T


def index_columns(ref, first, count):
    return jnp.concatenate([columns(ref[pl.ds(first + i, 1), :]) for i in range(count)], axis=0)


def small(values):
    return values.astype(F32).astype(BF16)


def place_hot(cols):
    place = small(cols & (SPAN - 1))
    lane = lax.broadcasted_iota(jnp.int32, place.shape, 1)
    one, zero = jnp.ones((), BF16), jnp.zeros((), BF16)
    return jnp.concatenate(
        [jnp.where(place == small(lane + start), one, zero) for start in range(0, SPAN, LANES)],
        axis=1,
    )


def gather_rows(hot, block, table, width):
    total = table.shape[1]
    step = max(width, 2 * LANES)
    found = [jnp.zeros(block.shape, F32) for _ in range(width // LANES)]
    for start in range(0, total, step):
        part = dot(hot, table[:, start : start + step])
        for inner in range(0, step, width):
            here = block == (start + inner) // width
            for i in range(len(found)):
                at = inner + i * LANES
                found[i] = jnp.where(here, part[:, at : at + LANES], found[i])
    return found


def spread_rows(hot, block, blocks, values):
    if blocks == 1:
        return [dot(hot, values)]
    parts = []
    zero = jnp.zeros((), BF16)
    for start in range(0, blocks, 2):
        some = range(start, min(start + 2, blocks))
        spread = [jnp.where(block == jnp.full((), j, BF16), values, zero) for j in some]
        part = dot(hot, jnp.concatenate(spread, axis=1))
        parts += [part[:, i * LANES : (i + 1) * LANES] for i in range(len(some))]
    return parts


def add_parts(total, base, parts):
    for j, part in enumerate(parts):
        total[block_rows(base, j), :] += part


def place_hot_rows(ordered, at, tile, base, level):
    one, zero = jnp.ones((), BF16), jnp.zeros((), BF16)
    hot = []
    for i in range(TILE // LANES):
        row = ordered[at, pl.ds(tile * (TILE // LANES) + i, 1), :] - base
        hot.append(jnp.where(level == small(row & (SPAN - 1)), one, zero))
    return jnp.concatenate(hot, axis=1)


def levels():
    return small(lax.broadcasted_iota(jnp.int32, (SPAN, LANES), 0))


def two_parts(values):
    high = values.astype(BF16)
    return high, (values - high.astype(F32)).astype(BF16)


def back(values, weight):
    high, low = two_parts(values)
    return dot(high, weight, NT) + dot(low, weight, NT)


def outer(rows, values):
    high, low = two_parts(values)
    both = dot(rows, jnp.concatenate([high, low], axis=1), TN)
    return both[:, 0:LANES] + both[:, LANES:]


def reversed_bits(number, limit):
    result = 0
    while limit > 1:
        result = 2 * result + number % 2
        number //= 2
        limit //= 2
    return result


def fetch(sources, targets, arrivals):
    copies = [
        pltpu.make_async_copy(source, target, arrivals.at[i])
        for i, (source, target) in enumerate(zip(sources, targets))
    ]
    for copy in copies:
        copy.start()
    return copies


def coarse_kernel(
    peers,
    latent_ref,
    grad_ref,
    weights_ref,
    rows_ref,
    w_in_ref,
    w_out_ref,
    gain_ref,
    sent_ref,
    table_ref,
    *held,
):
    *held, arrivals = held
    sources = (latent_ref, grad_ref, weights_ref, rows_ref, w_in_ref, w_out_ref, gain_ref)
    copies = fetch(sources, held, arrivals)
    for copy in copies:
        copy.wait()
    latent_ref, grad_ref, weights_ref, rows_ref, w_in_ref, w_out_ref, gain_ref = held
    count = latent_ref.shape[0]
    chunk = SPAN // peers
    capacity = sent_ref.shape[1] - EXTRA - max(EXTRA, chunk)
    w_in, w_out, gain = w_in_ref[...], w_out_ref[...], gain_ref[...]
    latent = latent_ref[...]
    pre = dot(latent, w_in)
    sigm = jax.nn.sigmoid(pre)
    hidden = (pre * sigm).astype(BF16)
    slope = sigm * (1.0 + pre * (1.0 - sigm))
    mapped = dot(hidden, w_out)
    centred = mapped - jnp.mean(mapped, axis=1, keepdims=True)
    inverse = lax.rsqrt(jnp.mean(centred * centred, axis=1, keepdims=True) + 1e-05)
    normed = centred * inverse
    upstream = grad_ref[...].astype(F32)
    scaled = upstream * gain
    grad_mapped = (
        inverse
        * (
            scaled
            - jnp.mean(scaled, axis=1, keepdims=True)
            - normed * jnp.mean(scaled * normed, axis=1, keepdims=True)
        )
    ).astype(BF16)
    grad_pre = (dot(grad_mapped, w_out, NT) * slope).astype(BF16)
    grad_in = (upstream + dot(grad_pre, w_in, NT)).astype(BF16)
    term_gain = jnp.sum(upstream * normed, axis=0, keepdims=True)
    term_in = dot(latent, grad_pre, TN)
    term_out = dot(hidden, grad_mapped, TN)
    for block in range(count // SPAN):
        at = block * SPAN
        table_ref[:, at : at + LANES] = grad_in[at : at + SPAN]
        for half in range(SPAN // LANES):
            at = block * SPAN + half * LANES
            pair = weights_ref[:, at : at + LANES].astype(F32)
            square = jnp.concatenate([pair, jnp.zeros((LANES - 2, LANES), F32)], axis=0)
            table_ref[
                half * LANES : (half + 1) * LANES, block * SPAN + LANES : (block + 1) * SPAN
            ] = square.T.astype(BF16)
    gain_high, gain_low = two_parts(term_gain)
    gain_rows = jnp.concatenate([gain_high.astype(F32), gain_low.astype(F32)], axis=0)
    terms = jnp.concatenate([term_in, term_out], axis=0)
    per_step = 256 // LANES
    for first in range(0, rows_ref.shape[0], per_step):
        cols = index_columns(rows_ref, first, per_step)
        sent, weight = gather_rows(place_hot(cols), cols // SPAN, table_ref, SPAN)
        for part in range(per_step * LANES // capacity):
            peer = first * LANES // capacity + part
            rows = slice(part * capacity, (part + 1) * capacity)
            sent_ref[peer, 0:capacity, :] = sent[rows].astype(BF16)
            square = weight[rows]
            if capacity < LANES:
                square = jnp.concatenate(
                    [square, jnp.zeros((LANES - capacity, LANES), F32)], axis=0
                )
            extra = jnp.concatenate(
                [square.T[0:2], gain_rows, jnp.zeros((EXTRA - 4, LANES), F32)], axis=0
            )
            sent_ref[peer, capacity : capacity + EXTRA, :] = extra.astype(BF16)
            first_row = reversed_bits(peer, peers) * chunk
            share = terms[first_row : first_row + chunk]
            if chunk < EXTRA:
                share = jnp.concatenate([share, jnp.zeros((EXTRA - chunk, LANES), F32)], axis=0)
            sent_ref[peer, capacity + EXTRA :, :] = share.astype(BF16)


def order_edges(recv_ref, off_ref, ordered, stats_vmem, positions, fine_count):
    rows = recv_ref.shape[0]
    shift = (fine_count // LANES).bit_length() - 1
    lane = lax.broadcasted_iota(jnp.int32, (LANES, LANES), 1)
    sub = lax.broadcasted_iota(jnp.int32, (LANES, LANES), 0)
    level = small(sub)
    one, zero = jnp.ones((), BF16), jnp.zeros((), BF16)

    def hot(row):
        return jnp.where(level == small(row), one, zero)

    number = jnp.zeros((LANES, LANES), BF16)
    for row in range(rows):
        number += hot(recv_ref[row : row + 1, :] >> shift)
    ones = jnp.ones((LANES, LANES), BF16)
    total = dot(number, ones)
    high = jnp.floor(total * (1.0 / 64.0))
    low = total - 64.0 * high
    before = jnp.where(lane < sub, 1.0, 0.0).astype(BF16)
    start = 64.0 * dot(before, high.astype(BF16)) + dot(before, low.astype(BF16))
    after = jnp.where(sub < lane, 1.0, 0.0).astype(BF16)
    prefix = jnp.concatenate([after, ones], axis=1)
    group = 16

    def place(step, filled):
        for i in range(group):
            row = step * group + i
            bucket = recv_ref[pl.ds(row, 1), :] >> shift
            found = dot(hot(bucket), prefix)
            mine = jnp.where(sub == bucket, found[:, 0:LANES] + filled, 0.0)
            positions[pl.ds(row, 1), :] = jnp.sum(mine, axis=0, keepdims=True).astype(jnp.int32)
            filled = filled + found[:, LANES:]
        return filled

    lax.fori_loop(0, rows // group, place, start)

    def move(step, moved):
        for part in range(0, group, 4):
            left, right = [], []
            for i in range(part, part + 4):
                row = step * group + i
                position = positions[pl.ds(row, 1), :]
                recv = recv_ref[pl.ds(row, 1), :]
                off = off_ref[pl.ds(row, 1), :] + HB
                rest = ((recv >> 8) << 2) | (off >> 8)
                here = level[0:64] == small(position >> 7)
                left.append(
                    jnp.concatenate(
                        [
                            jnp.where(here, small(value), zero)
                            for value in (recv & 255, off & 255, rest)
                        ],
                        axis=0,
                    )
                )
                right.append(hot(position & 127))
            moved = moved + dot(
                jnp.concatenate(left, axis=1), jnp.concatenate(right, axis=1), NT
            )
        return moved

    moved = lax.fori_loop(0, rows // group, move, jnp.zeros((192, LANES), F32))
    moved = moved.astype(jnp.int32)
    rest = moved[LANES : LANES + rows]
    recv = moved[0:rows] + ((rest >> 2) << 8)
    send = recv + moved[64 : 64 + rows] + ((rest & 3) << 8)
    ordered[0] = recv
    ordered[1] = send
    lane = lax.broadcasted_iota(jnp.int32, (rows, LANES), 1)
    recv, send = recv.astype(F32), send.astype(F32)
    stats = jnp.where(
        lane < 2,
        jnp.where(
            lane == 0,
            jnp.min(recv, axis=1, keepdims=True),
            jnp.max(recv, axis=1, keepdims=True),
        ),
        jnp.where(
            lane == 2,
            jnp.min(send, axis=1, keepdims=True),
            jnp.max(send, axis=1, keepdims=True),
        ),
    )
    stats_vmem[...] = stats.astype(jnp.int32)


def tile_bases(stats, tile, fine_count):
    count = TILE // LANES
    rows = [tile * count + i for i in range(count)]

    def extreme(pick, at):
        value = stats[rows[0], at]
        for row in rows[1:]:
            value = pick(value, stats[row, at])
        return value

    recv_base = jnp.minimum((extreme(jnp.minimum, 0) >> 4) << 4, fine_count - SPAN)
    send_base = jnp.minimum(
        (extreme(jnp.minimum, 2) >> 4) << 4, fine_count + 2 * HB - SENDERS * SPAN
    )
    fits = (extreme(jnp.maximum, 1) - recv_base < SPAN) & (
        extreme(jnp.maximum, 3) - send_base < SENDERS * SPAN
    )
    return recv_base, send_base, fits


def each_group(step, stats, fine_count, near, far):
    tiles = [step * GROUP + i for i in range(GROUP)]
    places = [tile_bases(stats, tile, fine_count) for tile in tiles]
    fits = functools.reduce(jnp.logical_and, [place[2] for place in places])

    @pl.when(fits)
    def _():
        near(tiles, [place[:2] for place in places])

    @pl.when(jnp.logical_not(fits))
    def _():
        def one(i, carry):
            far(step * GROUP + i)
            return carry

        lax.fori_loop(0, GROUP, one, 0)


def block_rows(base, block):
    return pl.ds(pl.multiple_of(base + block * SPAN, 16), SPAN)


def gather_blocks(hot, block, table, base, blocks):
    found = None
    for start in range(0, blocks, 2):
        some = range(start, min(start + 2, blocks))
        part = dot(hot, jnp.concatenate([table[block_rows(base, j), :] for j in some], axis=1))
        for i, j in enumerate(some):
            one = part[:, i * LANES : (i + 1) * LANES]
            found = one if found is None else jnp.where(block == j, one, found)
    return found


def tile_rows(tile):
    return pl.ds(pl.multiple_of(tile * TILE, TILE), TILE)


def slope_kernel(
    recv_hbm,
    off_hbm,
    slots_hbm,
    fine_hbm,
    weight_hbm,
    first_hbm,
    second_hbm,
    slope_hbm,
    hot_hbm,
    block_hbm,
    window_hbm,
    slope_sum,
    ordered,
    stats_vmem,
    slot_hot,
    slot_block,
    recv_ref,
    off_ref,
    slots_ref,
    window,
    weight_ref,
    halos,
    positions,
    slope_ref,
    hot_ref,
    block_ref,
    stats,
    arrivals,
    stats_done,
    leaving,
    window_left,
):
    fine_count = fine_hbm.shape[0]
    copies = fetch(
        (recv_hbm, off_hbm, slots_hbm, fine_hbm, weight_hbm, first_hbm, second_hbm),
        (
            recv_ref,
            off_ref,
            slots_ref,
            window.at[pl.ds(HB, fine_count)],
            weight_ref,
            halos.at[0],
            halos.at[1],
        ),
        arrivals,
    )
    copies[0].wait()
    copies[1].wait()
    order_edges(recv_ref, off_ref, ordered, stats_vmem, positions, fine_count)
    stats_copy = pltpu.make_async_copy(stats_vmem, stats, stats_done)
    stats_copy.start()
    for copy in copies[2:]:
        copy.wait()
    slope_sum[...] = jnp.zeros(slope_sum.shape, F32)
    slots = index_columns(slots_ref, 0, slots_ref.shape[0])
    slot_hot[...] = place_hot(slots)
    slot_block[...] = slots // SPAN
    odd = lax.axis_index("curve") & 1
    window[0:HB, :] = halos[1 - odd]
    window[HB + fine_count :, :] = halos[odd]
    window_copy = pltpu.make_async_copy(window, window_hbm, window_left)
    window_copy.start()
    stats_copy.wait()
    count = TILE // LANES
    weight = weight_ref[...]
    level = levels()

    def leave(tile):
        rows = tile_rows(tile)
        pairs = ((slope_ref, slope_hbm), (hot_ref, hot_hbm), (block_ref, block_hbm))
        return [
            pltpu.make_async_copy(source.at[rows], target.at[rows], leaving.at[i, tile])
            for i, (source, target) in enumerate(pairs)
        ]

    def near(tiles, places):
        work = []
        for tile, (recv_base, send_base) in zip(tiles, places):
            recv = index_columns(ordered.at[0], tile * count, count) - recv_base
            send = index_columns(ordered.at[1], tile * count, count) - send_base
            block = send >> 8
            hot = place_hot(recv)
            hot_ref[tile_rows(tile), :] = hot
            block_ref[tile_rows(tile), :] = small(block)
            sender = gather_blocks(place_hot(send), block, window, send_base, SENDERS)
            receiver = gather_blocks(hot, None, window, recv_base + HB, 1)
            work.append((sender, receiver))
        slopes = []
        for tile, (sender, receiver) in zip(tiles, work):
            inputs = jnp.concatenate([sender.astype(BF16), receiver.astype(BF16)], axis=1)
            slope = silu_slope(dot(inputs, weight))
            slope_ref[tile_rows(tile), :] = slope
            slopes.append(jnp.concatenate(two_parts(slope), axis=1))
        sums = []
        for tile, (recv_base, _), slope in zip(tiles, places, slopes):
            hot = place_hot_rows(ordered, 0, tile, recv_base, level)
            both = dot(hot, slope)
            sums.append(both[:, 0:LANES] + both[:, LANES:])
        for (recv_base, _), part in zip(places, sums):
            add_parts(slope_sum, recv_base, [part])

    def far(tile):
        recv = index_columns(ordered.at[0], tile * count, count)
        send = index_columns(ordered.at[1], tile * count, count)
        blocks = fine_count // SPAN
        sender = gather_blocks(place_hot(send), send >> 8, window, 0, blocks + 2)
        receiver = gather_blocks(place_hot(recv), recv >> 8, window, HB, blocks)
        inputs = jnp.concatenate([sender.astype(BF16), receiver.astype(BF16)], axis=1)
        slope = silu_slope(dot(inputs, weight))
        slope_ref[tile_rows(tile), :] = slope
        hot = place_hot_rows(ordered, 0, tile, 0, level)
        for part in two_parts(slope):
            add_parts(slope_sum, 0, spread_rows(hot, small(recv >> 8), blocks, part))
        hot_ref[tile_rows(tile), :] = jnp.zeros((TILE, SPAN), BF16)
        block_ref[tile_rows(tile), :] = jnp.zeros((TILE, LANES), BF16)

    def step(index, carry):
        each_group(index, stats, fine_count, near, far)
        for i in range(GROUP):
            for copy in leave(index * GROUP + i):
                copy.start()
        return carry

    tiles = slope_ref.shape[0] // TILE
    lax.fori_loop(0, tiles // GROUP, step, 0)
    window_copy.wait()
    for tile in range(tiles):
        for copy in leave(tile):
            copy.wait()


def edge_kernel(
    coarse_scale,
    stats,
    arrived_hbm,
    slot_hot_hbm,
    slot_block_hbm,
    hot_hbm,
    slope_hbm,
    block_hbm,
    ordered_hbm,
    window_hbm,
    slope_sum_hbm,
    weight_hbm,
    fine_ref,
    ends_ref,
    first_ref,
    second_ref,
    keep_ref,
    gift_ref,
    gain_ref,
    slot_table,
    grad_table,
    grad_rows,
    send_sum,
    arrived_ref,
    slot_hot,
    slot_block,
    hot_ref,
    slope_ref,
    block_ref,
    ordered,
    window,
    slope_sum,
    weight_ref,
    arrivals,
):
    fine_count = fine_ref.shape[0]
    copies = fetch(
        (
            arrived_hbm,
            slot_hot_hbm,
            slot_block_hbm,
            hot_hbm,
            slope_hbm,
            block_hbm,
            ordered_hbm,
            window_hbm,
            slope_sum_hbm,
            weight_hbm,
        ),
        (
            arrived_ref,
            slot_hot,
            slot_block,
            hot_ref,
            slope_ref,
            block_ref,
            ordered,
            window,
            slope_sum,
            weight_ref,
        ),
        arrivals,
    )
    send_sum[...] = jnp.zeros(send_sum.shape, F32)
    peers = arrived_ref.shape[0]
    share = max(EXTRA, SPAN // peers)
    capacity = arrived_ref.shape[1] - EXTRA - share
    per_block = SPAN // capacity
    for copy in copies[:3]:
        copy.wait()
    coarse = jnp.zeros((share, LANES), F32)
    gain = jnp.zeros((1, LANES), F32)
    for peer in range(peers):
        block, part = divmod(peer, per_block)
        rows = slice(part * capacity, (part + 1) * capacity)
        slot_table[rows, block * SPAN : block * SPAN + LANES] = arrived_ref[peer, 0:capacity, :]
        extra = arrived_ref[peer, capacity : capacity + EXTRA, :].astype(F32)
        square = jnp.concatenate([extra, jnp.zeros((LANES - EXTRA, LANES), F32)], axis=0).T
        slot_table[rows, block * SPAN + LANES : (block + 1) * SPAN] = square[0:capacity].astype(
            BF16
        )
        gain += extra[2:3] + extra[3:4]
        coarse += arrived_ref[peer, capacity + EXTRA :, :].astype(F32)
    keep_ref[LANES:, :] = coarse
    gain_ref[...] = gain * coarse_scale

    for first in range(0, slot_hot.shape[0], SPAN):
        at = slice(first, first + SPAN)
        grad, weight = gather_rows(slot_hot[at, :], slot_block[at, :], slot_table, SPAN)
        for r in range(2):
            rows = (grad * weight[:, r : r + 1]).astype(BF16).astype(F32)
            grad_rows[pl.ds(2 * first + r, SPAN, stride=2), :] = rows
    grad_table[...] = grad_rows[...].astype(BF16)
    for copy in copies[3:]:
        copy.wait()

    count = TILE // LANES
    level = levels()

    def near(tiles, places):
        work = []
        for tile, (recv_base, _) in zip(tiles, places):
            rows = tile_rows(tile)
            upstream = gather_blocks(hot_ref[rows, :], None, grad_table, recv_base, 1)
            work.append((upstream * slope_ref[rows, :]).astype(BF16))
        sums = []
        for tile, (_, send_base), values in zip(tiles, places, work):
            hot = place_hot_rows(ordered, 1, tile, send_base, level)
            sums.append(spread_rows(hot, block_ref[tile_rows(tile), :], SENDERS, values))
        for (_, send_base), parts in zip(places, sums):
            add_parts(send_sum, send_base, parts)

    def far(tile):
        rows = tile_rows(tile)
        recv = index_columns(ordered.at[0], tile * count, count)
        send = index_columns(ordered.at[1], tile * count, count)
        blocks = fine_count // SPAN
        upstream = gather_blocks(place_hot(recv), recv >> 8, grad_table, 0, blocks)
        values = (upstream * slope_ref[rows, :]).astype(BF16)
        hot = place_hot_rows(ordered, 1, tile, 0, level)
        add_parts(send_sum, 0, spread_rows(hot, small(send >> 8), blocks + 2, values))

    def step(index, carry):
        each_group(index, stats, fine_count, near, far)
        return carry

    lax.fori_loop(0, slope_ref.shape[0] // TILE // GROUP, step, 0)

    weight_send = weight_ref[0:LANES, :]
    weight_recv = weight_ref[LANES:, :]
    odd = lax.axis_index("curve") & 1
    to_prev = back(send_sum[0:HB, :], weight_send)
    to_next = back(send_sum[HB + fine_count :, :], weight_send)
    first_ref[...] = jnp.where(odd == 0, to_next, to_prev).astype(BF16)
    second_ref[...] = jnp.where(odd == 0, to_prev, to_next).astype(BF16)
    term_send = jnp.zeros((LANES, LANES), F32)
    term_recv = jnp.zeros((LANES, LANES), F32)
    for first in range(0, fine_count + 2 * HB, SPAN):
        at = slice(first, first + SPAN)
        term_send += outer(window[at, :], send_sum[at, :])
    for first in range(0, fine_count, SPAN):
        at = slice(first, first + SPAN)
        moved = slice(HB + first, HB + first + SPAN)
        received = grad_rows[at, :] * slope_sum[at, :]
        term_recv += outer(window[moved, :], received)
        summed = (
            grad_rows[at, :] + back(send_sum[moved, :], weight_send) + back(received, weight_recv)
        )
        fine_ref[at, :] = summed.astype(BF16)
        if first == 0:
            ends_ref[0] = summed
        if first == fine_count - SPAN:
            ends_ref[1] = summed
    keep_ref[0:LANES, :] = jnp.where(odd == 0, term_send, term_recv)
    gift_ref[...] = jnp.where(odd == 0, term_recv, term_send).astype(BF16)


def pair_exchange(first, second, peers):
    pairs = [(i, i ^ 1) for i in range(peers)]
    between = [(i, ((i + 1) ^ 1) - 1) for i in range(1, peers - 1)]
    return lax.ppermute(first, "curve", pairs), lax.ppermute(second, "curve", between)


def joined(later, own, there):
    return jnp.where(
        later, jnp.concatenate([there, own], axis=0), jnp.concatenate([own, there], axis=0)
    )


def reduced(keep, gift, device, peers):
    half = gift.shape[0]
    odd = (device & 1) == 1
    there = lax.ppermute(gift, "curve", [(i, i ^ 1) for i in range(peers)]).astype(F32)
    sent = (keep + jnp.pad(there, ((0, keep.shape[0] - half), (0, 0)))).astype(BF16)
    own, coarse = sent[:half].astype(F32), sent[half:]
    hops = peers // 2
    while hops > 1:
        there = lax.ppermute(sent, "curve", [(i, i ^ hops) for i in range(peers)])
        own = own.astype(BF16).astype(F32) + there[:half].astype(F32)
        coarse = joined((device & hops) != 0, coarse, there[half:])
        sent = jnp.concatenate([own.astype(BF16), coarse], axis=0)
        hops //= 2
    coarse = coarse.astype(F32)
    there = lax.ppermute(
        jnp.concatenate([own, coarse], axis=0), "curve", [(i, i ^ 1) for i in range(peers)]
    )
    other, other_coarse = there[:half], there[half:]
    return (
        joined(odd, own, other),
        jnp.where(odd, other_coarse, coarse),
        jnp.where(odd, coarse, other_coarse),
    )


def per_device(
    fine_latent,
    coarse_latent,
    grad_coarse,
    restrict_weights,
    send_rows,
    pair_slots,
    edge_receivers,
    edge_offsets,
    edge_weight,
    node_weight_in,
    node_weight_out,
    node_gain,
):
    peers = lax.axis_size("curve")
    device = lax.axis_index("curve")
    even = (device & 1) == 0
    coarse_count = coarse_latent.shape[0]
    fine_count = fine_latent.shape[0]
    edge_count = edge_receivers.shape[0]
    capacity = send_rows.shape[0] // peers
    chunk = SPAN // peers
    share = max(EXTRA, chunk)
    payload = capacity + EXTRA + share
    edge_rows = edge_count // LANES
    window_count = fine_count + 2 * HB
    params = pltpu.CompilerParams(vmem_limit_bytes=64 * 1024 * 1024 - 256 * 1024)
    anywhere = pl.BlockSpec(memory_space=pl.ANY)

    head, end = fine_latent[:HB], fine_latent[fine_count - HB :]
    halos = pair_exchange(jnp.where(even, end, head), jnp.where(even, head, end), peers)
    scalar = pl.BlockSpec(memory_space=pltpu.SMEM)

    sent = pl.pallas_call(
        functools.partial(coarse_kernel, peers),
        out_shape=jax.ShapeDtypeStruct((peers, payload, LANES), BF16),
        in_specs=[anywhere] * 7,
        scratch_shapes=[
            pltpu.VMEM((SPAN, coarse_count), BF16),
            pltpu.VMEM((coarse_count, LANES), BF16),
            pltpu.VMEM((coarse_count, LANES), BF16),
            pltpu.VMEM((2, coarse_count), BF16),
            pltpu.VMEM((peers * capacity // LANES, LANES), jnp.int32),
            pltpu.VMEM((LANES, LANES), BF16),
            pltpu.VMEM((LANES, LANES), BF16),
            pltpu.VMEM((1, LANES), F32),
            pltpu.SemaphoreType.DMA((7,)),
        ],
        compiler_params=params,
        cost_estimate=pl.CostEstimate(
            flops=2_000_000_000, bytes_accessed=2_000_000, transcendentals=400_000
        ),
        name="coarse_block",
    )(
        coarse_latent,
        grad_coarse,
        restrict_weights,
        send_rows.reshape(-1, LANES),
        node_weight_in,
        node_weight_out,
        node_gain.reshape(1, LANES),
    )
    arrived = lax.all_to_all(sent, "curve", split_axis=0, concat_axis=0, tiled=True)

    pair_count = fine_count // 2
    in_vmem = pl.BlockSpec(memory_space=pltpu.VMEM)
    slope, hot, block, window, slope_sum, ordered, stats, slot_hot, slot_block = pl.pallas_call(
        slope_kernel,
        out_shape=(
            jax.ShapeDtypeStruct((edge_count, LANES), F32),
            jax.ShapeDtypeStruct((edge_count, SPAN), BF16),
            jax.ShapeDtypeStruct((edge_count, LANES), BF16),
            jax.ShapeDtypeStruct((window_count, LANES), BF16),
            jax.ShapeDtypeStruct((fine_count, LANES), F32),
            jax.ShapeDtypeStruct((2, edge_rows, LANES), jnp.int32),
            jax.ShapeDtypeStruct((edge_rows, LANES), jnp.int32),
            jax.ShapeDtypeStruct((pair_count, SPAN), BF16),
            jax.ShapeDtypeStruct((pair_count, LANES), jnp.int32),
        ),
        in_specs=[anywhere] * 7,
        out_specs=[anywhere] * 4 + [in_vmem] * 5,
        scratch_shapes=[
            pltpu.VMEM((edge_rows, LANES), jnp.int32),
            pltpu.VMEM((edge_rows, LANES), jnp.int32),
            pltpu.VMEM((pair_count // LANES, LANES), jnp.int32),
            pltpu.VMEM((window_count, LANES), BF16),
            pltpu.VMEM((2 * LANES, LANES), BF16),
            pltpu.VMEM((2, HB, LANES), BF16),
            pltpu.VMEM((edge_rows, LANES), jnp.int32),
            pltpu.VMEM((edge_count, LANES), F32),
            pltpu.VMEM((edge_count, SPAN), BF16),
            pltpu.VMEM((edge_count, LANES), BF16),
            pltpu.SMEM((edge_rows, LANES), jnp.int32),
            pltpu.SemaphoreType.DMA((7,)),
            pltpu.SemaphoreType.DMA,
            pltpu.SemaphoreType.DMA((3, edge_count // TILE)),
            pltpu.SemaphoreType.DMA,
        ],
        compiler_params=params,
        cost_estimate=pl.CostEstimate(
            flops=16_000_000_000, bytes_accessed=5_000_000, transcendentals=800_000
        ),
        name="edge_slope",
    )(
        edge_receivers.reshape(-1, LANES),
        edge_offsets.reshape(-1, LANES),
        pair_slots.reshape(-1, LANES),
        fine_latent,
        edge_weight,
        *halos,
    )

    coarse_scale = 1.0 / math.sqrt(coarse_count * peers)
    edge_scale = 1.0 / math.sqrt(edge_count * peers)
    fine_rows, ends, first, second, keep, gift, term_gain = pl.pallas_call(
        functools.partial(edge_kernel, coarse_scale),
        out_shape=(
            jax.ShapeDtypeStruct((fine_count, LANES), BF16),
            jax.ShapeDtypeStruct((2, HB, LANES), F32),
            jax.ShapeDtypeStruct((HB, LANES), BF16),
            jax.ShapeDtypeStruct((HB, LANES), BF16),
            jax.ShapeDtypeStruct((LANES + share, LANES), F32),
            jax.ShapeDtypeStruct((LANES, LANES), BF16),
            jax.ShapeDtypeStruct((1, LANES), F32),
        ),
        in_specs=[scalar] + [anywhere] * 10,
        scratch_shapes=[
            pltpu.VMEM((SPAN, peers * capacity), BF16),
            pltpu.VMEM((fine_count, LANES), BF16),
            pltpu.VMEM((fine_count, LANES), F32),
            pltpu.VMEM((window_count, LANES), F32),
            pltpu.VMEM((peers, payload, LANES), BF16),
            pltpu.VMEM((pair_count, SPAN), BF16),
            pltpu.VMEM((pair_count, LANES), jnp.int32),
            pltpu.VMEM((edge_count, SPAN), BF16),
            pltpu.VMEM((edge_count, LANES), F32),
            pltpu.VMEM((edge_count, LANES), BF16),
            pltpu.VMEM((2, edge_rows, LANES), jnp.int32),
            pltpu.VMEM((window_count, LANES), BF16),
            pltpu.VMEM((fine_count, LANES), F32),
            pltpu.VMEM((2 * LANES, LANES), BF16),
            pltpu.SemaphoreType.DMA((10,)),
        ],
        compiler_params=params,
        cost_estimate=pl.CostEstimate(
            flops=24_000_000_000, bytes_accessed=8_000_000, transcendentals=0
        ),
        name="edge_back",
    )(
        stats,
        arrived,
        slot_hot,
        slot_block,
        hot,
        slope,
        block,
        ordered,
        window,
        slope_sum,
        edge_weight,
    )
    edge_terms, term_in, term_out = reduced(keep[: LANES + chunk], gift, device, peers)
    one, two = pair_exchange(first, second, peers)
    from_next, from_prev = jnp.where(even, one, two), jnp.where(even, two, one)
    grad_fine = fine_rows.at[:HB].set((ends[0] + from_prev.astype(F32)).astype(BF16))
    grad_fine = grad_fine.at[fine_count - HB :].set((ends[1] + from_next.astype(F32)).astype(BF16))
    return (
        grad_fine,
        edge_terms * edge_scale,
        term_in * coarse_scale,
        term_out * coarse_scale,
        term_gain.reshape(LANES),
    )


def solution(mesh):
    placed = (
        P(("groups", "curve"), None),
        P(("groups", "curve"), None),
        P(("groups", "curve"), None),
        P(None, ("groups", "curve")),
        P(("groups", "curve")),
        P(("groups", "curve")),
        P(("groups", "curve")),
        P(("groups", "curve")),
        P(),
        P(),
        P(),
        P(),
    )
    return jax.shard_map(
        per_device,
        mesh=mesh,
        in_specs=placed,
        out_specs=(
            P(("groups", "curve"), None),
            P("groups", None),
            P("groups", None),
            P("groups", None),
            P("groups"),
        ),
        check_vma=False,
    )
```

```python
import functools
import math

import jax
import jax.numpy as jnp
from jax import lax
from jax.experimental import pallas as pl
from jax.experimental.pallas import tpu as pltpu
from jax.sharding import PartitionSpec as P

HB = 256
LANES = 128
SPAN = 256
EXTRA = 16
TILE = 512
GROUP = 4
SENDERS = 3

F32 = jnp.float32
BF16 = jnp.bfloat16
NT = (((1,), (1,)), ((), ()))
TN = (((0,), (0,)), ((), ()))


def dot(left, right, dims=(((1,), (0,)), ((), ()))):
    return lax.dot_general(left, right, dims, preferred_element_type=F32)


def silu_slope(values):
    sigm = jax.nn.sigmoid(values)
    return sigm * (1.0 + values * (1.0 - sigm))


def columns(row):
    return jnp.broadcast_to(row, (LANES, LANES)).T


def index_columns(ref, first, count):
    return jnp.concatenate([columns(ref[pl.ds(first + i, 1), :]) for i in range(count)], axis=0)


def small(values):
    return values.astype(F32).astype(BF16)


def place_hot(cols):
    place = small(cols & (SPAN - 1))
    lane = lax.broadcasted_iota(jnp.int32, place.shape, 1)
    one, zero = jnp.ones((), BF16), jnp.zeros((), BF16)
    return jnp.concatenate(
        [jnp.where(place == small(lane + start), one, zero) for start in range(0, SPAN, LANES)],
        axis=1,
    )


def gather_rows(hot, block, table, width):
    total = table.shape[1]
    step = max(width, 2 * LANES)
    found = [jnp.zeros(block.shape, F32) for _ in range(width // LANES)]
    for start in range(0, total, step):
        part = dot(hot, table[:, start : start + step])
        for inner in range(0, step, width):
            here = block == (start + inner) // width
            for i in range(len(found)):
                at = inner + i * LANES
                found[i] = jnp.where(here, part[:, at : at + LANES], found[i])
    return found


def spread_rows(hot, block, blocks, values):
    if blocks == 1:
        return [dot(hot, values)]
    parts = []
    zero = jnp.zeros((), BF16)
    for start in range(0, blocks, 2):
        some = range(start, min(start + 2, blocks))
        spread = [jnp.where(block == jnp.full((), j, BF16), values, zero) for j in some]
        part = dot(hot, jnp.concatenate(spread, axis=1))
        parts += [part[:, i * LANES : (i + 1) * LANES] for i in range(len(some))]
    return parts


def add_parts(total, base, parts):
    for j, part in enumerate(parts):
        total[block_rows(base, j), :] += part


def place_hot_rows(ordered, at, tile, base, level):
    one, zero = jnp.ones((), BF16), jnp.zeros((), BF16)
    hot = []
    for i in range(TILE // LANES):
        row = ordered[at, pl.ds(tile * (TILE // LANES) + i, 1), :] - base
        hot.append(jnp.where(level == small(row & (SPAN - 1)), one, zero))
    return jnp.concatenate(hot, axis=1)


def levels():
    return small(lax.broadcasted_iota(jnp.int32, (SPAN, LANES), 0))


def two_parts(values):
    high = values.astype(BF16)
    return high, (values - high.astype(F32)).astype(BF16)


def back(values, weight):
    high, low = two_parts(values)
    return dot(high, weight, NT) + dot(low, weight, NT)


def outer(rows, values):
    high, low = two_parts(values)
    both = dot(rows, jnp.concatenate([high, low], axis=1), TN)
    return both[:, 0:LANES] + both[:, LANES:]


def reversed_bits(number, limit):
    result = 0
    while limit > 1:
        result = 2 * result + number % 2
        number //= 2
        limit //= 2
    return result


def fetch(sources, targets, arrivals):
    copies = [
        pltpu.make_async_copy(source, target, arrivals.at[i])
        for i, (source, target) in enumerate(zip(sources, targets))
    ]
    for copy in copies:
        copy.start()
    return copies


def coarse_kernel(
    peers,
    latent_ref,
    grad_ref,
    weights_ref,
    rows_ref,
    w_in_ref,
    w_out_ref,
    gain_ref,
    sent_ref,
    table_ref,
    *held,
):
    *held, arrivals = held
    sources = (latent_ref, grad_ref, weights_ref, rows_ref, w_in_ref, w_out_ref, gain_ref)
    copies = fetch(sources, held, arrivals)
    for copy in copies:
        copy.wait()
    latent_ref, grad_ref, weights_ref, rows_ref, w_in_ref, w_out_ref, gain_ref = held
    count = latent_ref.shape[0]
    chunk = SPAN // peers
    capacity = sent_ref.shape[1] - EXTRA - max(EXTRA, chunk)
    w_in, w_out, gain = w_in_ref[...], w_out_ref[...], gain_ref[...]
    latent = latent_ref[...]
    pre = dot(latent, w_in)
    sigm = jax.nn.sigmoid(pre)
    hidden = (pre * sigm).astype(BF16)
    slope = sigm * (1.0 + pre * (1.0 - sigm))
    mapped = dot(hidden, w_out)
    centred = mapped - jnp.mean(mapped, axis=1, keepdims=True)
    inverse = lax.rsqrt(jnp.mean(centred * centred, axis=1, keepdims=True) + 1e-05)
    normed = centred * inverse
    upstream = grad_ref[...].astype(F32)
    scaled = upstream * gain
    grad_mapped = (
        inverse
        * (
            scaled
            - jnp.mean(scaled, axis=1, keepdims=True)
            - normed * jnp.mean(scaled * normed, axis=1, keepdims=True)
        )
    ).astype(BF16)
    grad_pre = (dot(grad_mapped, w_out, NT) * slope).astype(BF16)
    grad_in = (upstream + dot(grad_pre, w_in, NT)).astype(BF16)
    term_gain = jnp.sum(upstream * normed, axis=0, keepdims=True)
    term_in = dot(latent, grad_pre, TN)
    term_out = dot(hidden, grad_mapped, TN)
    for block in range(count // SPAN):
        at = block * SPAN
        table_ref[:, at : at + LANES] = grad_in[at : at + SPAN]
        for half in range(SPAN // LANES):
            at = block * SPAN + half * LANES
            pair = weights_ref[:, at : at + LANES].astype(F32)
            square = jnp.concatenate([pair, jnp.zeros((LANES - 2, LANES), F32)], axis=0)
            table_ref[
                half * LANES : (half + 1) * LANES, block * SPAN + LANES : (block + 1) * SPAN
            ] = square.T.astype(BF16)
    gain_high, gain_low = two_parts(term_gain)
    gain_rows = jnp.concatenate([gain_high.astype(F32), gain_low.astype(F32)], axis=0)
    terms = jnp.concatenate([term_in, term_out], axis=0)
    per_step = 256 // LANES
    for first in range(0, rows_ref.shape[0], per_step):
        cols = index_columns(rows_ref, first, per_step)
        sent, weight = gather_rows(place_hot(cols), cols // SPAN, table_ref, SPAN)
        for part in range(per_step * LANES // capacity):
            peer = first * LANES // capacity + part
            rows = slice(part * capacity, (part + 1) * capacity)
            sent_ref[peer, 0:capacity, :] = sent[rows].astype(BF16)
            square = weight[rows]
            if capacity < LANES:
                square = jnp.concatenate(
                    [square, jnp.zeros((LANES - capacity, LANES), F32)], axis=0
                )
            extra = jnp.concatenate(
                [square.T[0:2], gain_rows, jnp.zeros((EXTRA - 4, LANES), F32)], axis=0
            )
            sent_ref[peer, capacity : capacity + EXTRA, :] = extra.astype(BF16)
            first_row = reversed_bits(peer, peers) * chunk
            share = terms[first_row : first_row + chunk]
            if chunk < EXTRA:
                share = jnp.concatenate([share, jnp.zeros((EXTRA - chunk, LANES), F32)], axis=0)
            sent_ref[peer, capacity + EXTRA :, :] = share.astype(BF16)


def order_edges(recv_ref, off_ref, ordered, stats_vmem, positions, fine_count):
    rows = recv_ref.shape[0]
    shift = (fine_count // LANES).bit_length() - 1
    lane = lax.broadcasted_iota(jnp.int32, (LANES, LANES), 1)
    sub = lax.broadcasted_iota(jnp.int32, (LANES, LANES), 0)
    level = small(sub)
    one, zero = jnp.ones((), BF16), jnp.zeros((), BF16)

    def hot(row):
        return jnp.where(level == small(row), one, zero)

    number = jnp.zeros((LANES, LANES), BF16)
    for row in range(rows):
        number += hot(recv_ref[row : row + 1, :] >> shift)
    ones = jnp.ones((LANES, LANES), BF16)
    total = dot(number, ones)
    high = jnp.floor(total * (1.0 / 64.0))
    low = total - 64.0 * high
    before = jnp.where(lane < sub, 1.0, 0.0).astype(BF16)
    start = 64.0 * dot(before, high.astype(BF16)) + dot(before, low.astype(BF16))
    after = jnp.where(sub < lane, 1.0, 0.0).astype(BF16)
    prefix = jnp.concatenate([after, ones], axis=1)
    group = 16

    def place(step, filled):
        for i in range(group):
            row = step * group + i
            bucket = recv_ref[pl.ds(row, 1), :] >> shift
            found = dot(hot(bucket), prefix)
            mine = jnp.where(sub == bucket, found[:, 0:LANES] + filled, 0.0)
            positions[pl.ds(row, 1), :] = jnp.sum(mine, axis=0, keepdims=True).astype(jnp.int32)
            filled = filled + found[:, LANES:]
        return filled

    lax.fori_loop(0, rows // group, place, start)

    def move(step, moved):
        for part in range(0, group, 4):
            left, right = [], []
            for i in range(part, part + 4):
                row = step * group + i
                position = positions[pl.ds(row, 1), :]
                recv = recv_ref[pl.ds(row, 1), :]
                off = off_ref[pl.ds(row, 1), :] + HB
                rest = ((recv >> 8) << 2) | (off >> 8)
                here = level[0:64] == small(position >> 7)
                left.append(
                    jnp.concatenate(
                        [
                            jnp.where(here, small(value), zero)
                            for value in (recv & 255, off & 255, rest)
                        ],
                        axis=0,
                    )
                )
                right.append(hot(position & 127))
            moved = moved + dot(
                jnp.concatenate(left, axis=1), jnp.concatenate(right, axis=1), NT
            )
        return moved

    moved = lax.fori_loop(0, rows // group, move, jnp.zeros((192, LANES), F32))
    moved = moved.astype(jnp.int32)
    rest = moved[LANES : LANES + rows]
    recv = moved[0:rows] + ((rest >> 2) << 8)
    send = recv + moved[64 : 64 + rows] + ((rest & 3) << 8)
    ordered[0] = recv
    ordered[1] = send
    lane = lax.broadcasted_iota(jnp.int32, (rows, LANES), 1)
    recv, send = recv.astype(F32), send.astype(F32)
    stats = jnp.where(
        lane < 2,
        jnp.where(
            lane == 0,
            jnp.min(recv, axis=1, keepdims=True),
            jnp.max(recv, axis=1, keepdims=True),
        ),
        jnp.where(
            lane == 2,
            jnp.min(send, axis=1, keepdims=True),
            jnp.max(send, axis=1, keepdims=True),
        ),
    )
    stats_vmem[...] = stats.astype(jnp.int32)


def tile_bases(stats, tile, fine_count):
    count = TILE // LANES
    rows = [tile * count + i for i in range(count)]

    def extreme(pick, at):
        value = stats[rows[0], at]
        for row in rows[1:]:
            value = pick(value, stats[row, at])
        return value

    recv_base = jnp.minimum((extreme(jnp.minimum, 0) >> 4) << 4, fine_count - SPAN)
    send_base = jnp.minimum(
        (extreme(jnp.minimum, 2) >> 4) << 4, fine_count + 2 * HB - SENDERS * SPAN
    )
    fits = (extreme(jnp.maximum, 1) - recv_base < SPAN) & (
        extreme(jnp.maximum, 3) - send_base < SENDERS * SPAN
    )
    return recv_base, send_base, fits


def each_group(step, stats, fine_count, near, far):
    tiles = [step * GROUP + i for i in range(GROUP)]
    places = [tile_bases(stats, tile, fine_count) for tile in tiles]
    fits = functools.reduce(jnp.logical_and, [place[2] for place in places])

    @pl.when(fits)
    def _():
        near(tiles, [place[:2] for place in places])

    @pl.when(jnp.logical_not(fits))
    def _():
        def one(i, carry):
            far(step * GROUP + i)
            return carry

        lax.fori_loop(0, GROUP, one, 0)


def block_rows(base, block):
    return pl.ds(pl.multiple_of(base + block * SPAN, 16), SPAN)


def gather_blocks(hot, block, table, base, blocks):
    found = None
    for start in range(0, blocks, 2):
        some = range(start, min(start + 2, blocks))
        part = dot(hot, jnp.concatenate([table[block_rows(base, j), :] for j in some], axis=1))
        for i, j in enumerate(some):
            one = part[:, i * LANES : (i + 1) * LANES]
            found = one if found is None else jnp.where(block == j, one, found)
    return found


def tile_rows(tile):
    return pl.ds(pl.multiple_of(tile * TILE, TILE), TILE)


def slope_kernel(
    recv_hbm,
    off_hbm,
    slots_hbm,
    fine_hbm,
    weight_hbm,
    first_hbm,
    second_hbm,
    slope_hbm,
    hot_hbm,
    block_hbm,
    window_hbm,
    slope_sum,
    ordered,
    stats_vmem,
    slot_hot,
    slot_block,
    recv_ref,
    off_ref,
    slots_ref,
    window,
    weight_ref,
    halos,
    positions,
    slope_ref,
    hot_ref,
    block_ref,
    stats,
    arrivals,
    stats_done,
    leaving,
    window_left,
):
    fine_count = fine_hbm.shape[0]
    copies = fetch(
        (recv_hbm, off_hbm, slots_hbm, fine_hbm, weight_hbm, first_hbm, second_hbm),
        (
            recv_ref,
            off_ref,
            slots_ref,
            window.at[pl.ds(HB, fine_count)],
            weight_ref,
            halos.at[0],
            halos.at[1],
        ),
        arrivals,
    )
    copies[0].wait()
    copies[1].wait()
    order_edges(recv_ref, off_ref, ordered, stats_vmem, positions, fine_count)
    stats_copy = pltpu.make_async_copy(stats_vmem, stats, stats_done)
    stats_copy.start()
    for copy in copies[2:]:
        copy.wait()
    slope_sum[...] = jnp.zeros(slope_sum.shape, F32)
    slots = index_columns(slots_ref, 0, slots_ref.shape[0])
    slot_hot[...] = place_hot(slots)
    slot_block[...] = slots // SPAN
    odd = lax.axis_index("curve") & 1
    window[0:HB, :] = halos[1 - odd]
    window[HB + fine_count :, :] = halos[odd]
    window_copy = pltpu.make_async_copy(window, window_hbm, window_left)
    window_copy.start()
    stats_copy.wait()
    count = TILE // LANES
    weight = weight_ref[...]
    level = levels()

    def leave(tile):
        rows = tile_rows(tile)
        pairs = ((slope_ref, slope_hbm), (hot_ref, hot_hbm), (block_ref, block_hbm))
        return [
            pltpu.make_async_copy(source.at[rows], target.at[rows], leaving.at[i, tile])
            for i, (source, target) in enumerate(pairs)
        ]

    def near(tiles, places):
        work = []
        for tile, (recv_base, send_base) in zip(tiles, places):
            recv = index_columns(ordered.at[0], tile * count, count) - recv_base
            send = index_columns(ordered.at[1], tile * count, count) - send_base
            block = send >> 8
            hot = place_hot(recv)
            hot_ref[tile_rows(tile), :] = hot
            block_ref[tile_rows(tile), :] = small(block)
            sender = gather_blocks(place_hot(send), block, window, send_base, SENDERS)
            receiver = gather_blocks(hot, None, window, recv_base + HB, 1)
            work.append((sender, receiver))
        slopes = []
        for tile, (sender, receiver) in zip(tiles, work):
            inputs = jnp.concatenate([sender.astype(BF16), receiver.astype(BF16)], axis=1)
            slope = silu_slope(dot(inputs, weight))
            slope_ref[tile_rows(tile), :] = slope
            slopes.append(jnp.concatenate(two_parts(slope), axis=1))
        sums = []
        for tile, (recv_base, _), slope in zip(tiles, places, slopes):
            hot = place_hot_rows(ordered, 0, tile, recv_base, level)
            both = dot(hot, slope)
            sums.append(both[:, 0:LANES] + both[:, LANES:])
        for (recv_base, _), part in zip(places, sums):
            add_parts(slope_sum, recv_base, [part])

    def far(tile):
        recv = index_columns(ordered.at[0], tile * count, count)
        send = index_columns(ordered.at[1], tile * count, count)
        blocks = fine_count // SPAN
        sender = gather_blocks(place_hot(send), send >> 8, window, 0, blocks + 2)
        receiver = gather_blocks(place_hot(recv), recv >> 8, window, HB, blocks)
        inputs = jnp.concatenate([sender.astype(BF16), receiver.astype(BF16)], axis=1)
        slope = silu_slope(dot(inputs, weight))
        slope_ref[tile_rows(tile), :] = slope
        hot = place_hot_rows(ordered, 0, tile, 0, level)
        for part in two_parts(slope):
            add_parts(slope_sum, 0, spread_rows(hot, small(recv >> 8), blocks, part))
        hot_ref[tile_rows(tile), :] = jnp.zeros((TILE, SPAN), BF16)
        block_ref[tile_rows(tile), :] = jnp.zeros((TILE, LANES), BF16)

    def step(index, carry):
        each_group(index, stats, fine_count, near, far)
        for i in range(GROUP):
            for copy in leave(index * GROUP + i):
                copy.start()
        return carry

    tiles = slope_ref.shape[0] // TILE
    lax.fori_loop(0, tiles // GROUP, step, 0)
    window_copy.wait()
    for tile in range(tiles):
        for copy in leave(tile):
            copy.wait()


def edge_kernel(
    coarse_scale,
    stats,
    arrived_hbm,
    slot_hot_hbm,
    slot_block_hbm,
    hot_hbm,
    slope_hbm,
    block_hbm,
    ordered_hbm,
    window_hbm,
    slope_sum_hbm,
    weight_hbm,
    grad_table,
    send_sum,
    first_ref,
    second_ref,
    keep_ref,
    gain_ref,
    slot_table,
    grad_rows,
    arrived_ref,
    slot_hot,
    slot_block,
    hot_ref,
    slope_ref,
    block_ref,
    ordered,
    window,
    slope_sum,
    weight_ref,
    arrivals,
):
    fine_count = grad_table.shape[0]
    copies = fetch(
        (
            arrived_hbm,
            slot_hot_hbm,
            slot_block_hbm,
            hot_hbm,
            slope_hbm,
            block_hbm,
            ordered_hbm,
            window_hbm,
            slope_sum_hbm,
            weight_hbm,
        ),
        (
            arrived_ref,
            slot_hot,
            slot_block,
            hot_ref,
            slope_ref,
            block_ref,
            ordered,
            window,
            slope_sum,
            weight_ref,
        ),
        arrivals,
    )
    send_sum[...] = jnp.zeros(send_sum.shape, F32)
    peers = arrived_ref.shape[0]
    share = max(EXTRA, SPAN // peers)
    capacity = arrived_ref.shape[1] - EXTRA - share
    per_block = SPAN // capacity
    for copy in copies[:3]:
        copy.wait()
    coarse = jnp.zeros((share, LANES), F32)
    gain = jnp.zeros((1, LANES), F32)
    for peer in range(peers):
        block, part = divmod(peer, per_block)
        rows = slice(part * capacity, (part + 1) * capacity)
        slot_table[rows, block * SPAN : block * SPAN + LANES] = arrived_ref[peer, 0:capacity, :]
        extra = arrived_ref[peer, capacity : capacity + EXTRA, :].astype(F32)
        square = jnp.concatenate([extra, jnp.zeros((LANES - EXTRA, LANES), F32)], axis=0).T
        slot_table[rows, block * SPAN + LANES : (block + 1) * SPAN] = square[0:capacity].astype(
            BF16
        )
        gain += extra[2:3] + extra[3:4]
        coarse += arrived_ref[peer, capacity + EXTRA :, :].astype(F32)
    keep_ref[LANES:, :] = coarse
    gain_ref[...] = gain * coarse_scale

    found = []
    for first in range(0, slot_hot.shape[0], SPAN):
        at = slice(first, first + SPAN)
        found.append(gather_rows(slot_hot[at, :], slot_block[at, :], slot_table, SPAN))
    for i, (grad, weight) in enumerate(found):
        first = i * SPAN
        for r in range(2):
            rows = (grad * weight[:, r : r + 1]).astype(BF16).astype(F32)
            grad_rows[pl.ds(2 * first + r, SPAN, stride=2), :] = rows
    grad_table[...] = grad_rows[...].astype(BF16)
    for copy in copies[3:]:
        copy.wait()

    count = TILE // LANES
    level = levels()

    def near(tiles, places):
        work = []
        for tile, (recv_base, _) in zip(tiles, places):
            rows = tile_rows(tile)
            upstream = gather_blocks(hot_ref[rows, :], None, grad_table, recv_base, 1)
            work.append((upstream * slope_ref[rows, :]).astype(BF16))
        sums = []
        for tile, (_, send_base), values in zip(tiles, places, work):
            hot = place_hot_rows(ordered, 1, tile, send_base, level)
            sums.append(spread_rows(hot, block_ref[tile_rows(tile), :], SENDERS, values))
        for (_, send_base), parts in zip(places, sums):
            add_parts(send_sum, send_base, parts)

    def far(tile):
        rows = tile_rows(tile)
        recv = index_columns(ordered.at[0], tile * count, count)
        send = index_columns(ordered.at[1], tile * count, count)
        blocks = fine_count // SPAN
        upstream = gather_blocks(place_hot(recv), recv >> 8, grad_table, 0, blocks)
        values = (upstream * slope_ref[rows, :]).astype(BF16)
        hot = place_hot_rows(ordered, 1, tile, 0, level)
        add_parts(send_sum, 0, spread_rows(hot, small(send >> 8), blocks + 2, values))

    def step(index, carry):
        each_group(index, stats, fine_count, near, far)
        return carry

    lax.fori_loop(0, slope_ref.shape[0] // TILE // GROUP, step, 0)

    weight_send = weight_ref[0:LANES, :]
    odd = lax.axis_index("curve") & 1
    to_prev = back(send_sum[0:HB, :], weight_send)
    to_next = back(send_sum[HB + fine_count :, :], weight_send)
    first_ref[LANES:, :] = jnp.where(odd == 0, to_next, to_prev).astype(BF16)
    second_ref[...] = jnp.where(odd == 0, to_prev, to_next).astype(BF16)
    term_send = jnp.zeros((LANES, LANES), F32)
    term_recv = jnp.zeros((LANES, LANES), F32)
    for first in range(0, fine_count + 2 * HB, SPAN):
        at = slice(first, first + SPAN)
        term_send += outer(window[at, :], send_sum[at, :])
    for first in range(0, fine_count, SPAN):
        at = slice(first, first + SPAN)
        moved = slice(HB + first, HB + first + SPAN)
        term_recv += outer(window[moved, :], grad_rows[at, :] * slope_sum[at, :])
    keep_ref[0:LANES, :] = jnp.where(odd == 0, term_send, term_recv)
    first_ref[0:LANES, :] = jnp.where(odd == 0, term_recv, term_send).astype(BF16)


def fine_kernel(
    grad_hbm,
    send_sum_hbm,
    slope_sum_hbm,
    weight_hbm,
    first_hbm,
    second_hbm,
    fine_ref,
    grad_table,
    send_sum,
    slope_sum,
    weight_ref,
    first_ref,
    second_ref,
    arrivals,
):
    fine_count = fine_ref.shape[0]
    for copy in fetch(
        (grad_hbm, send_sum_hbm, slope_sum_hbm, weight_hbm, first_hbm, second_hbm),
        (grad_table, send_sum, slope_sum, weight_ref, first_ref, second_ref),
        arrivals,
    ):
        copy.wait()
    odd = lax.axis_index("curve") & 1
    one, two = first_ref[LANES:, :].astype(F32), second_ref[...].astype(F32)
    from_next, from_prev = jnp.where(odd == 0, one, two), jnp.where(odd == 0, two, one)
    for first in range(0, fine_count, SPAN):
        at = slice(first, first + SPAN)
        moved = slice(HB + first, HB + first + SPAN)
        grad = grad_table[at, :].astype(F32)
        summed = (
            grad
            + back(send_sum[moved, :], weight_ref[0:LANES, :])
            + back(grad * slope_sum[at, :], weight_ref[LANES:, :])
        )
        if first == 0:
            summed += from_prev
        if first == fine_count - SPAN:
            summed += from_next
        fine_ref[at, :] = summed.astype(BF16)


def last_kernel(
    edge_scale, coarse_scale, own_ref, coarse_ref, there_ref, edge_ref, in_ref, out_ref
):
    odd = lax.axis_index("curve") & 1
    own, coarse = own_ref[...], coarse_ref[...].astype(F32)
    other, other_coarse = there_ref[0:LANES, :], there_ref[LANES:, :]
    edge_ref[0:LANES, :] = jnp.where(odd == 0, own, other) * edge_scale
    edge_ref[LANES:, :] = jnp.where(odd == 0, other, own) * edge_scale
    in_ref[...] = jnp.where(odd == 0, coarse, other_coarse) * coarse_scale
    out_ref[...] = jnp.where(odd == 0, other_coarse, coarse) * coarse_scale


def pair_exchange(first, second, peers):
    pairs = [(i, i ^ 1) for i in range(peers)]
    between = [(i, ((i + 1) ^ 1) - 1) for i in range(1, peers - 1)]
    return lax.ppermute(first, "curve", pairs), lax.ppermute(second, "curve", between)


def joined(later, own, there):
    return jnp.where(
        later, jnp.concatenate([there, own], axis=0), jnp.concatenate([own, there], axis=0)
    )


def reduced(sent, half, device, peers):
    own, coarse = sent[:half].astype(F32), sent[half:]
    hops = peers // 2
    while hops > 1:
        there = lax.ppermute(sent, "curve", [(i, i ^ hops) for i in range(peers)])
        own = own.astype(BF16).astype(F32) + there[:half].astype(F32)
        coarse = joined((device & hops) != 0, coarse, there[half:])
        sent = jnp.concatenate([own.astype(BF16), coarse], axis=0)
        hops //= 2
    return own, coarse


def per_device(
    fine_latent,
    coarse_latent,
    grad_coarse,
    restrict_weights,
    send_rows,
    pair_slots,
    edge_receivers,
    edge_offsets,
    edge_weight,
    node_weight_in,
    node_weight_out,
    node_gain,
):
    peers = lax.axis_size("curve")
    device = lax.axis_index("curve")
    even = (device & 1) == 0
    coarse_count = coarse_latent.shape[0]
    fine_count = fine_latent.shape[0]
    edge_count = edge_receivers.shape[0]
    capacity = send_rows.shape[0] // peers
    chunk = SPAN // peers
    share = max(EXTRA, chunk)
    payload = capacity + EXTRA + share
    edge_rows = edge_count // LANES
    window_count = fine_count + 2 * HB
    params = pltpu.CompilerParams(vmem_limit_bytes=64 * 1024 * 1024 - 256 * 1024)
    roomy = pltpu.CompilerParams(vmem_limit_bytes=62 * 1024 * 1024)
    anywhere = pl.BlockSpec(memory_space=pl.ANY)

    head, end = fine_latent[:HB], fine_latent[fine_count - HB :]
    halos = pair_exchange(jnp.where(even, end, head), jnp.where(even, head, end), peers)
    scalar = pl.BlockSpec(memory_space=pltpu.SMEM)

    sent = pl.pallas_call(
        functools.partial(coarse_kernel, peers),
        out_shape=jax.ShapeDtypeStruct((peers, payload, LANES), BF16),
        in_specs=[anywhere] * 7,
        scratch_shapes=[
            pltpu.VMEM((SPAN, coarse_count), BF16),
            pltpu.VMEM((coarse_count, LANES), BF16),
            pltpu.VMEM((coarse_count, LANES), BF16),
            pltpu.VMEM((2, coarse_count), BF16),
            pltpu.VMEM((peers * capacity // LANES, LANES), jnp.int32),
            pltpu.VMEM((LANES, LANES), BF16),
            pltpu.VMEM((LANES, LANES), BF16),
            pltpu.VMEM((1, LANES), F32),
            pltpu.SemaphoreType.DMA((7,)),
        ],
        compiler_params=params,
        cost_estimate=pl.CostEstimate(
            flops=2_000_000_000, bytes_accessed=2_000_000, transcendentals=400_000
        ),
        name="coarse_block",
    )(
        coarse_latent,
        grad_coarse,
        restrict_weights,
        send_rows.reshape(-1, LANES),
        node_weight_in,
        node_weight_out,
        node_gain.reshape(1, LANES),
    )
    arrived = lax.all_to_all(sent, "curve", split_axis=0, concat_axis=0, tiled=True)

    pair_count = fine_count // 2
    in_vmem = pl.BlockSpec(memory_space=pltpu.VMEM)
    slope, hot, block, window, slope_sum, ordered, stats, slot_hot, slot_block = pl.pallas_call(
        slope_kernel,
        out_shape=(
            jax.ShapeDtypeStruct((edge_count, LANES), F32),
            jax.ShapeDtypeStruct((edge_count, SPAN), BF16),
            jax.ShapeDtypeStruct((edge_count, LANES), BF16),
            jax.ShapeDtypeStruct((window_count, LANES), BF16),
            jax.ShapeDtypeStruct((fine_count, LANES), F32),
            jax.ShapeDtypeStruct((2, edge_rows, LANES), jnp.int32),
            jax.ShapeDtypeStruct((edge_rows, LANES), jnp.int32),
            jax.ShapeDtypeStruct((pair_count, SPAN), BF16),
            jax.ShapeDtypeStruct((pair_count, LANES), jnp.int32),
        ),
        in_specs=[anywhere] * 7,
        out_specs=[anywhere] * 4 + [in_vmem] * 5,
        scratch_shapes=[
            pltpu.VMEM((edge_rows, LANES), jnp.int32),
            pltpu.VMEM((edge_rows, LANES), jnp.int32),
            pltpu.VMEM((pair_count // LANES, LANES), jnp.int32),
            pltpu.VMEM((window_count, LANES), BF16),
            pltpu.VMEM((2 * LANES, LANES), BF16),
            pltpu.VMEM((2, HB, LANES), BF16),
            pltpu.VMEM((edge_rows, LANES), jnp.int32),
            pltpu.VMEM((edge_count, LANES), F32),
            pltpu.VMEM((edge_count, SPAN), BF16),
            pltpu.VMEM((edge_count, LANES), BF16),
            pltpu.SMEM((edge_rows, LANES), jnp.int32),
            pltpu.SemaphoreType.DMA((7,)),
            pltpu.SemaphoreType.DMA,
            pltpu.SemaphoreType.DMA((3, edge_count // TILE)),
            pltpu.SemaphoreType.DMA,
        ],
        compiler_params=params,
        cost_estimate=pl.CostEstimate(
            flops=16_000_000_000, bytes_accessed=5_000_000, transcendentals=800_000
        ),
        name="edge_slope",
    )(
        edge_receivers.reshape(-1, LANES),
        edge_offsets.reshape(-1, LANES),
        pair_slots.reshape(-1, LANES),
        fine_latent,
        edge_weight,
        *halos,
    )

    coarse_scale = 1.0 / math.sqrt(coarse_count * peers)
    edge_scale = 1.0 / math.sqrt(edge_count * peers)
    grad_rows, send_sum, first, second, keep, term_gain = pl.pallas_call(
        functools.partial(edge_kernel, coarse_scale),
        out_shape=(
            jax.ShapeDtypeStruct((fine_count, LANES), BF16),
            jax.ShapeDtypeStruct((window_count, LANES), F32),
            pltpu.VMEM((LANES + HB, LANES), BF16),
            pltpu.VMEM((HB, LANES), BF16),
            pltpu.VMEM((LANES + share, LANES), F32),
            jax.ShapeDtypeStruct((1, LANES), F32),
        ),
        in_specs=[scalar] + [anywhere] * 10,
        scratch_shapes=[
            pltpu.VMEM((SPAN, peers * capacity), BF16),
            pltpu.VMEM((fine_count, LANES), F32),
            pltpu.VMEM((peers, payload, LANES), BF16),
            pltpu.VMEM((pair_count, SPAN), BF16),
            pltpu.VMEM((pair_count, LANES), jnp.int32),
            pltpu.VMEM((edge_count, SPAN), BF16),
            pltpu.VMEM((edge_count, LANES), F32),
            pltpu.VMEM((edge_count, LANES), BF16),
            pltpu.VMEM((2, edge_rows, LANES), jnp.int32),
            pltpu.VMEM((window_count, LANES), BF16),
            pltpu.VMEM((fine_count, LANES), F32),
            pltpu.VMEM((2 * LANES, LANES), BF16),
            pltpu.SemaphoreType.DMA((10,)),
        ],
        compiler_params=roomy,
        cost_estimate=pl.CostEstimate(
            flops=24_000_000_000, bytes_accessed=8_000_000, transcendentals=0
        ),
        name="edge_back",
    )(
        stats,
        arrived,
        slot_hot,
        slot_block,
        hot,
        slope,
        block,
        ordered,
        window,
        slope_sum,
        edge_weight,
    )
    one, two = pair_exchange(first, second, peers)
    sent = keep[: LANES + chunk] + jnp.pad(one[:LANES].astype(F32), ((0, chunk), (0, 0)))
    sent, two = lax.optimization_barrier((sent.astype(BF16), two))
    grad_fine = pl.pallas_call(
        fine_kernel,
        out_shape=jax.ShapeDtypeStruct((fine_count, LANES), BF16),
        in_specs=[anywhere] * 6,
        scratch_shapes=[
            pltpu.VMEM((fine_count, LANES), BF16),
            pltpu.VMEM((window_count, LANES), F32),
            pltpu.VMEM((fine_count, LANES), F32),
            pltpu.VMEM((2 * LANES, LANES), BF16),
            pltpu.VMEM((LANES + HB, LANES), BF16),
            pltpu.VMEM((HB, LANES), BF16),
            pltpu.SemaphoreType.DMA((6,)),
        ],
        compiler_params=pltpu.CompilerParams(vmem_limit_bytes=64 * 1024 * 1024 - 640 * 1024),
        cost_estimate=pl.CostEstimate(
            flops=1_000_000_000, bytes_accessed=4_000_000, transcendentals=0
        ),
        name="fine_sums",
    )(grad_rows, send_sum, slope_sum, edge_weight, one, two)
    own, coarse = reduced(sent, LANES, device, peers)
    there = lax.ppermute(
        jnp.concatenate([own, coarse.astype(F32)], axis=0),
        "curve",
        [(i, i ^ 1) for i in range(peers)],
    )
    edge_terms, term_in, term_out = pl.pallas_call(
        functools.partial(last_kernel, edge_scale, coarse_scale),
        out_shape=(
            jax.ShapeDtypeStruct((2 * LANES, LANES), F32),
            jax.ShapeDtypeStruct((LANES, LANES), F32),
            jax.ShapeDtypeStruct((LANES, LANES), F32),
        ),
        compiler_params=pltpu.CompilerParams(vmem_limit_bytes=4 * 1024 * 1024),
        name="last_terms",
    )(own, coarse, there)
    return grad_fine, edge_terms, term_in, term_out, term_gain.reshape(LANES)


def solution(mesh):
    placed = (
        P(("groups", "curve"), None),
        P(("groups", "curve"), None),
        P(("groups", "curve"), None),
        P(None, ("groups", "curve")),
        P(("groups", "curve")),
        P(("groups", "curve")),
        P(("groups", "curve")),
        P(("groups", "curve")),
        P(),
        P(),
        P(),
        P(),
    )
    return jax.shard_map(
        per_device,
        mesh=mesh,
        in_specs=placed,
        out_specs=(
            P(("groups", "curve"), None),
            P("groups", None),
            P("groups", None),
            P("groups", None),
            P("groups"),
        ),
        check_vma=False,
    )
```

```python
import functools
import math

import jax
import jax.numpy as jnp
from jax import lax
from jax.experimental import pallas as pl
from jax.experimental.pallas import tpu as pltpu
from jax.sharding import PartitionSpec as P

HB = 256
LANES = 128
SPAN = 256
EXTRA = 16
TILE = 512
GROUP = 4
SENDERS = 3

F32 = jnp.float32
BF16 = jnp.bfloat16
NT = (((1,), (1,)), ((), ()))
TN = (((0,), (0,)), ((), ()))


def dot(left, right, dims=(((1,), (0,)), ((), ()))):
    return lax.dot_general(left, right, dims, preferred_element_type=F32)


def silu_slope(values):
    sigm = jax.nn.sigmoid(values)
    return sigm * (1.0 + values * (1.0 - sigm))


def columns(row):
    return jnp.broadcast_to(row, (LANES, LANES)).T


def index_columns(ref, first, count):
    return jnp.concatenate([columns(ref[pl.ds(first + i, 1), :]) for i in range(count)], axis=0)


def small(values):
    return values.astype(F32).astype(BF16)


def place_hot(cols):
    place = small(cols & (SPAN - 1))
    lane = lax.broadcasted_iota(jnp.int32, place.shape, 1)
    one, zero = jnp.ones((), BF16), jnp.zeros((), BF16)
    return jnp.concatenate(
        [jnp.where(place == small(lane + start), one, zero) for start in range(0, SPAN, LANES)],
        axis=1,
    )


def gather_rows(hot, block, table, width):
    total = table.shape[1]
    step = max(width, 2 * LANES)
    found = [jnp.zeros(block.shape, F32) for _ in range(width // LANES)]
    for start in range(0, total, step):
        part = dot(hot, table[:, start : start + step])
        for inner in range(0, step, width):
            here = block == (start + inner) // width
            for i in range(len(found)):
                at = inner + i * LANES
                found[i] = jnp.where(here, part[:, at : at + LANES], found[i])
    return found


def spread_rows(hot, block, blocks, values):
    if blocks == 1:
        return [dot(hot, values)]
    parts = []
    zero = jnp.zeros((), BF16)
    for start in range(0, blocks, 2):
        some = range(start, min(start + 2, blocks))
        spread = [jnp.where(block == jnp.full((), j, BF16), values, zero) for j in some]
        part = dot(hot, jnp.concatenate(spread, axis=1))
        parts += [part[:, i * LANES : (i + 1) * LANES] for i in range(len(some))]
    return parts


def add_parts(total, base, parts):
    for j, part in enumerate(parts):
        total[block_rows(base, j), :] += part


def place_hot_rows(ordered, at, tile, base, level):
    one, zero = jnp.ones((), BF16), jnp.zeros((), BF16)
    hot = []
    for i in range(TILE // LANES):
        row = ordered[at, pl.ds(tile * (TILE // LANES) + i, 1), :] - base
        hot.append(jnp.where(level == small(row & (SPAN - 1)), one, zero))
    return jnp.concatenate(hot, axis=1)


def levels():
    return small(lax.broadcasted_iota(jnp.int32, (SPAN, LANES), 0))


def two_parts(values):
    high = values.astype(BF16)
    return high, (values - high.astype(F32)).astype(BF16)


def back(values, weight):
    high, low = two_parts(values)
    return dot(high, weight, NT) + dot(low, weight, NT)


def outer(rows, values):
    high, low = two_parts(values)
    both = dot(rows, jnp.concatenate([high, low], axis=1), TN)
    return both[:, 0:LANES] + both[:, LANES:]


def fetch(sources, targets, arrivals):
    copies = [
        pltpu.make_async_copy(source, target, arrivals.at[i])
        for i, (source, target) in enumerate(zip(sources, targets))
    ]
    for copy in copies:
        copy.start()
    return copies


def coarse_kernel(
    peers,
    latent_ref,
    grad_ref,
    weights_ref,
    rows_ref,
    w_in_ref,
    w_out_ref,
    gain_ref,
    sent_ref,
    table_ref,
    *held,
):
    *held, arrivals = held
    sources = (latent_ref, grad_ref, weights_ref, rows_ref, w_in_ref, w_out_ref, gain_ref)
    copies = fetch(sources, held, arrivals)
    for copy in copies:
        copy.wait()
    latent_ref, grad_ref, weights_ref, rows_ref, w_in_ref, w_out_ref, gain_ref = held
    count = latent_ref.shape[0]
    chunk = SPAN // peers
    capacity = sent_ref.shape[1] - EXTRA - max(EXTRA, chunk)
    w_in, w_out, gain = w_in_ref[...], w_out_ref[...], gain_ref[...]
    latent = latent_ref[...]
    pre = dot(latent, w_in)
    sigm = jax.nn.sigmoid(pre)
    hidden = (pre * sigm).astype(BF16)
    slope = sigm * (1.0 + pre * (1.0 - sigm))
    mapped = dot(hidden, w_out)
    centred = mapped - jnp.mean(mapped, axis=1, keepdims=True)
    inverse = lax.rsqrt(jnp.mean(centred * centred, axis=1, keepdims=True) + 1e-05)
    normed = centred * inverse
    upstream = grad_ref[...].astype(F32)
    scaled = upstream * gain
    grad_mapped = (
        inverse
        * (
            scaled
            - jnp.mean(scaled, axis=1, keepdims=True)
            - normed * jnp.mean(scaled * normed, axis=1, keepdims=True)
        )
    ).astype(BF16)
    grad_pre = (dot(grad_mapped, w_out, NT) * slope).astype(BF16)
    grad_in = (upstream + dot(grad_pre, w_in, NT)).astype(BF16)
    term_gain = jnp.sum(upstream * normed, axis=0, keepdims=True)
    term_in = dot(latent, grad_pre, TN)
    term_out = dot(hidden, grad_mapped, TN)
    for block in range(count // SPAN):
        at = block * SPAN
        table_ref[:, at : at + LANES] = grad_in[at : at + SPAN]
        for half in range(SPAN // LANES):
            at = block * SPAN + half * LANES
            pair = weights_ref[:, at : at + LANES].astype(F32)
            square = jnp.concatenate([pair, jnp.zeros((LANES - 2, LANES), F32)], axis=0)
            table_ref[
                half * LANES : (half + 1) * LANES, block * SPAN + LANES : (block + 1) * SPAN
            ] = square.T.astype(BF16)
    gain_high, gain_low = two_parts(term_gain)
    gain_rows = jnp.concatenate([gain_high.astype(F32), gain_low.astype(F32)], axis=0)
    terms = jnp.concatenate([term_in, term_out], axis=0)
    per_step = 256 // LANES
    for first in range(0, rows_ref.shape[0], per_step):
        cols = index_columns(rows_ref, first, per_step)
        sent, weight = gather_rows(place_hot(cols), cols // SPAN, table_ref, SPAN)
        for part in range(per_step * LANES // capacity):
            peer = first * LANES // capacity + part
            rows = slice(part * capacity, (part + 1) * capacity)
            sent_ref[peer, 0:capacity, :] = sent[rows].astype(BF16)
            square = weight[rows]
            if capacity < LANES:
                square = jnp.concatenate(
                    [square, jnp.zeros((LANES - capacity, LANES), F32)], axis=0
                )
            extra = jnp.concatenate(
                [square.T[0:2], gain_rows, jnp.zeros((EXTRA - 4, LANES), F32)], axis=0
            )
            sent_ref[peer, capacity : capacity + EXTRA, :] = extra.astype(BF16)
            first_row = (peer % 2 * (peers // 2) + peer // 2) * chunk
            share = terms[first_row : first_row + chunk]
            if chunk < EXTRA:
                share = jnp.concatenate([share, jnp.zeros((EXTRA - chunk, LANES), F32)], axis=0)
            sent_ref[peer, capacity + EXTRA :, :] = share.astype(BF16)


def order_edges(recv_ref, off_ref, ordered, stats_vmem, positions, fine_count):
    rows = recv_ref.shape[0]
    shift = (fine_count // LANES).bit_length() - 1
    lane = lax.broadcasted_iota(jnp.int32, (LANES, LANES), 1)
    sub = lax.broadcasted_iota(jnp.int32, (LANES, LANES), 0)
    level = small(sub)
    one, zero = jnp.ones((), BF16), jnp.zeros((), BF16)

    def hot(row):
        return jnp.where(level == small(row), one, zero)

    number = jnp.zeros((LANES, LANES), BF16)
    for row in range(rows):
        number += hot(recv_ref[row : row + 1, :] >> shift)
    ones = jnp.ones((LANES, LANES), BF16)
    total = dot(number, ones)
    high = jnp.floor(total * (1.0 / 64.0))
    low = total - 64.0 * high
    before = jnp.where(lane < sub, 1.0, 0.0).astype(BF16)
    start = 64.0 * dot(before, high.astype(BF16)) + dot(before, low.astype(BF16))
    after = jnp.where(sub < lane, 1.0, 0.0).astype(BF16)
    prefix = jnp.concatenate([after, ones], axis=1)
    group = 16

    def place(step, filled):
        for i in range(group):
            row = step * group + i
            bucket = recv_ref[pl.ds(row, 1), :] >> shift
            found = dot(hot(bucket), prefix)
            mine = jnp.where(sub == bucket, found[:, 0:LANES] + filled, 0.0)
            positions[pl.ds(row, 1), :] = jnp.sum(mine, axis=0, keepdims=True).astype(jnp.int32)
            filled = filled + found[:, LANES:]
        return filled

    lax.fori_loop(0, rows // group, place, start)

    def move(step, moved):
        for part in range(0, group, 4):
            left, right = [], []
            for i in range(part, part + 4):
                row = step * group + i
                position = positions[pl.ds(row, 1), :]
                recv = recv_ref[pl.ds(row, 1), :]
                off = off_ref[pl.ds(row, 1), :] + HB
                rest = ((recv >> 8) << 2) | (off >> 8)
                here = level[0:64] == small(position >> 7)
                left.append(
                    jnp.concatenate(
                        [
                            jnp.where(here, small(value), zero)
                            for value in (recv & 255, off & 255, rest)
                        ],
                        axis=0,
                    )
                )
                right.append(hot(position & 127))
            moved = moved + dot(
                jnp.concatenate(left, axis=1), jnp.concatenate(right, axis=1), NT
            )
        return moved

    moved = lax.fori_loop(0, rows // group, move, jnp.zeros((192, LANES), F32))
    moved = moved.astype(jnp.int32)
    rest = moved[LANES : LANES + rows]
    recv = moved[0:rows] + ((rest >> 2) << 8)
    send = recv + moved[64 : 64 + rows] + ((rest & 3) << 8)
    ordered[0] = recv
    ordered[1] = send
    lane = lax.broadcasted_iota(jnp.int32, (rows, LANES), 1)
    recv, send = recv.astype(F32), send.astype(F32)
    stats = jnp.where(
        lane < 2,
        jnp.where(
            lane == 0,
            jnp.min(recv, axis=1, keepdims=True),
            jnp.max(recv, axis=1, keepdims=True),
        ),
        jnp.where(
            lane == 2,
            jnp.min(send, axis=1, keepdims=True),
            jnp.max(send, axis=1, keepdims=True),
        ),
    )
    stats_vmem[...] = stats.astype(jnp.int32)


def tile_bases(stats, tile, fine_count):
    count = TILE // LANES
    rows = [tile * count + i for i in range(count)]

    def extreme(pick, at):
        value = stats[rows[0], at]
        for row in rows[1:]:
            value = pick(value, stats[row, at])
        return value

    recv_base = jnp.minimum((extreme(jnp.minimum, 0) >> 4) << 4, fine_count - SPAN)
    send_base = jnp.minimum(
        (extreme(jnp.minimum, 2) >> 4) << 4, fine_count + 2 * HB - SENDERS * SPAN
    )
    fits = (extreme(jnp.maximum, 1) - recv_base < SPAN) & (
        extreme(jnp.maximum, 3) - send_base < SENDERS * SPAN
    )
    return recv_base, send_base, fits


def each_group(step, stats, fine_count, near, far):
    tiles = [step * GROUP + i for i in range(GROUP)]
    places = [tile_bases(stats, tile, fine_count) for tile in tiles]
    fits = functools.reduce(jnp.logical_and, [place[2] for place in places])

    @pl.when(fits)
    def _():
        near(tiles, [place[:2] for place in places])

    @pl.when(jnp.logical_not(fits))
    def _():
        def one(i, carry):
            far(step * GROUP + i)
            return carry

        lax.fori_loop(0, GROUP, one, 0)


def block_rows(base, block):
    return pl.ds(pl.multiple_of(base + block * SPAN, 16), SPAN)


def gather_blocks(hot, block, table, base, blocks):
    found = None
    for start in range(0, blocks, 2):
        some = range(start, min(start + 2, blocks))
        part = dot(hot, jnp.concatenate([table[block_rows(base, j), :] for j in some], axis=1))
        for i, j in enumerate(some):
            one = part[:, i * LANES : (i + 1) * LANES]
            found = one if found is None else jnp.where(block == j, one, found)
    return found


def tile_rows(tile):
    return pl.ds(pl.multiple_of(tile * TILE, TILE), TILE)


def order_kernel(
    recv_hbm,
    off_hbm,
    slots_hbm,
    ordered,
    stats_ref,
    slot_hot,
    slot_block,
    recv_ref,
    off_ref,
    slots_ref,
    positions,
    arrivals,
    fine_count,
):
    for copy in fetch(
        (recv_hbm, off_hbm, slots_hbm), (recv_ref, off_ref, slots_ref), arrivals
    ):
        copy.wait()
    order_edges(recv_ref, off_ref, ordered, stats_ref, positions, fine_count)
    slots = index_columns(slots_ref, 0, slots_ref.shape[0])
    slot_hot[...] = place_hot(slots)
    slot_block[...] = slots // SPAN


def slope_kernel(
    stats,
    ordered_hbm,
    fine_hbm,
    weight_hbm,
    first_hbm,
    second_hbm,
    slope_hbm,
    hot_hbm,
    block_hbm,
    window_hbm,
    slope_sum,
    ordered,
    window,
    weight_ref,
    halos,
    slope_ref,
    hot_ref,
    block_ref,
    arrivals,
    leaving,
    window_left,
):
    fine_count = fine_hbm.shape[0]
    copies = fetch(
        (ordered_hbm, fine_hbm, weight_hbm, first_hbm, second_hbm),
        (ordered, window.at[pl.ds(HB, fine_count)], weight_ref, halos.at[0], halos.at[1]),
        arrivals,
    )
    slope_sum[...] = jnp.zeros(slope_sum.shape, F32)
    for copy in copies:
        copy.wait()
    odd = lax.axis_index("curve") & 1
    window[0:HB, :] = halos[1 - odd]
    window[HB + fine_count :, :] = halos[odd]
    window_copy = pltpu.make_async_copy(window, window_hbm, window_left)
    window_copy.start()
    count = TILE // LANES
    weight = weight_ref[...]
    level = levels()

    def leave(tile):
        rows = tile_rows(tile)
        pairs = ((slope_ref, slope_hbm), (hot_ref, hot_hbm), (block_ref, block_hbm))
        return [
            pltpu.make_async_copy(source.at[rows], target.at[rows], leaving.at[i, tile])
            for i, (source, target) in enumerate(pairs)
        ]

    def near(tiles, places):
        work = []
        for tile, (recv_base, send_base) in zip(tiles, places):
            recv = index_columns(ordered.at[0], tile * count, count) - recv_base
            send = index_columns(ordered.at[1], tile * count, count) - send_base
            block = send >> 8
            hot = place_hot(recv)
            hot_ref[tile_rows(tile), :] = hot
            block_ref[tile_rows(tile), :] = small(block)
            sender = gather_blocks(place_hot(send), block, window, send_base, SENDERS)
            receiver = gather_blocks(hot, None, window, recv_base + HB, 1)
            work.append((sender, receiver))
        slopes = []
        for tile, (sender, receiver) in zip(tiles, work):
            inputs = jnp.concatenate([sender.astype(BF16), receiver.astype(BF16)], axis=1)
            slope = silu_slope(dot(inputs, weight))
            slope_ref[tile_rows(tile), :] = slope
            slopes.append(jnp.concatenate(two_parts(slope), axis=1))
        sums = []
        for tile, (recv_base, _), slope in zip(tiles, places, slopes):
            hot = place_hot_rows(ordered, 0, tile, recv_base, level)
            both = dot(hot, slope)
            sums.append(both[:, 0:LANES] + both[:, LANES:])
        for (recv_base, _), part in zip(places, sums):
            add_parts(slope_sum, recv_base, [part])

    def far(tile):
        recv = index_columns(ordered.at[0], tile * count, count)
        send = index_columns(ordered.at[1], tile * count, count)
        blocks = fine_count // SPAN
        sender = gather_blocks(place_hot(send), send >> 8, window, 0, blocks + 2)
        receiver = gather_blocks(place_hot(recv), recv >> 8, window, HB, blocks)
        inputs = jnp.concatenate([sender.astype(BF16), receiver.astype(BF16)], axis=1)
        slope = silu_slope(dot(inputs, weight))
        slope_ref[tile_rows(tile), :] = slope
        hot = place_hot_rows(ordered, 0, tile, 0, level)
        for part in two_parts(slope):
            add_parts(slope_sum, 0, spread_rows(hot, small(recv >> 8), blocks, part))
        hot_ref[tile_rows(tile), :] = jnp.zeros((TILE, SPAN), BF16)
        block_ref[tile_rows(tile), :] = jnp.zeros((TILE, LANES), BF16)

    def step(index, carry):
        each_group(index, stats, fine_count, near, far)
        for i in range(GROUP):
            for copy in leave(index * GROUP + i):
                copy.start()
        return carry

    tiles = slope_ref.shape[0] // TILE
    lax.fori_loop(0, tiles // GROUP, step, 0)
    window_copy.wait()
    for tile in range(tiles):
        for copy in leave(tile):
            copy.wait()


def edge_kernel(
    coarse_scale,
    stats,
    arrived_hbm,
    slot_hot_hbm,
    slot_block_hbm,
    hot_hbm,
    slope_hbm,
    block_hbm,
    ordered_hbm,
    window_hbm,
    slope_sum_hbm,
    weight_hbm,
    grad_table,
    send_sum,
    first_ref,
    second_ref,
    keep_ref,
    gain_ref,
    slot_table,
    grad_rows,
    arrived_ref,
    slot_hot,
    slot_block,
    hot_ref,
    slope_ref,
    block_ref,
    ordered,
    window,
    slope_sum,
    weight_ref,
    arrivals,
):
    fine_count = grad_table.shape[0]
    copies = fetch(
        (
            arrived_hbm,
            slot_hot_hbm,
            slot_block_hbm,
            hot_hbm,
            slope_hbm,
            block_hbm,
            ordered_hbm,
            window_hbm,
            slope_sum_hbm,
            weight_hbm,
        ),
        (
            arrived_ref,
            slot_hot,
            slot_block,
            hot_ref,
            slope_ref,
            block_ref,
            ordered,
            window,
            slope_sum,
            weight_ref,
        ),
        arrivals,
    )
    send_sum[...] = jnp.zeros(send_sum.shape, F32)
    peers = arrived_ref.shape[0]
    share = max(EXTRA, SPAN // peers)
    capacity = arrived_ref.shape[1] - EXTRA - share
    per_block = SPAN // capacity
    for copy in copies[:3]:
        copy.wait()
    coarse = jnp.zeros((share, LANES), F32)
    gain = jnp.zeros((1, LANES), F32)
    for peer in range(peers):
        block, part = divmod(peer, per_block)
        rows = slice(part * capacity, (part + 1) * capacity)
        slot_table[rows, block * SPAN : block * SPAN + LANES] = arrived_ref[peer, 0:capacity, :]
        extra = arrived_ref[peer, capacity : capacity + EXTRA, :].astype(F32)
        square = jnp.concatenate([extra, jnp.zeros((LANES - EXTRA, LANES), F32)], axis=0).T
        slot_table[rows, block * SPAN + LANES : (block + 1) * SPAN] = square[0:capacity].astype(
            BF16
        )
        gain += extra[2:3] + extra[3:4]
        coarse += arrived_ref[peer, capacity + EXTRA :, :].astype(F32)
    keep_ref[LANES:, :] = coarse
    gain_ref[...] = gain * coarse_scale

    found = []
    for first in range(0, slot_hot.shape[0], SPAN):
        at = slice(first, first + SPAN)
        found.append(gather_rows(slot_hot[at, :], slot_block[at, :], slot_table, SPAN))
    for i, (grad, weight) in enumerate(found):
        first = i * SPAN
        for r in range(2):
            rows = (grad * weight[:, r : r + 1]).astype(BF16).astype(F32)
            grad_rows[pl.ds(2 * first + r, SPAN, stride=2), :] = rows
    grad_table[...] = grad_rows[...].astype(BF16)
    for copy in copies[3:]:
        copy.wait()

    count = TILE // LANES
    level = levels()

    def near(tiles, places):
        work = []
        for tile, (recv_base, _) in zip(tiles, places):
            rows = tile_rows(tile)
            upstream = gather_blocks(hot_ref[rows, :], None, grad_table, recv_base, 1)
            work.append((upstream * slope_ref[rows, :]).astype(BF16))
        sums = []
        for tile, (_, send_base), values in zip(tiles, places, work):
            hot = place_hot_rows(ordered, 1, tile, send_base, level)
            sums.append(spread_rows(hot, block_ref[tile_rows(tile), :], SENDERS, values))
        for (_, send_base), parts in zip(places, sums):
            add_parts(send_sum, send_base, parts)

    def far(tile):
        rows = tile_rows(tile)
        recv = index_columns(ordered.at[0], tile * count, count)
        send = index_columns(ordered.at[1], tile * count, count)
        blocks = fine_count // SPAN
        upstream = gather_blocks(place_hot(recv), recv >> 8, grad_table, 0, blocks)
        values = (upstream * slope_ref[rows, :]).astype(BF16)
        hot = place_hot_rows(ordered, 1, tile, 0, level)
        add_parts(send_sum, 0, spread_rows(hot, small(send >> 8), blocks + 2, values))

    def step(index, carry):
        each_group(index, stats, fine_count, near, far)
        return carry

    lax.fori_loop(0, slope_ref.shape[0] // TILE // GROUP, step, 0)

    weight_send = weight_ref[0:LANES, :]
    odd = lax.axis_index("curve") & 1
    to_prev = back(send_sum[0:HB, :], weight_send)
    to_next = back(send_sum[HB + fine_count :, :], weight_send)
    first_ref[LANES:, :] = jnp.where(odd == 0, to_next, to_prev).astype(BF16)
    second_ref[...] = jnp.where(odd == 0, to_prev, to_next).astype(BF16)
    term_send = jnp.zeros((LANES, LANES), F32)
    term_recv = jnp.zeros((LANES, LANES), F32)
    for first in range(0, fine_count + 2 * HB, SPAN):
        at = slice(first, first + SPAN)
        term_send += outer(window[at, :], send_sum[at, :])
    for first in range(0, fine_count, SPAN):
        at = slice(first, first + SPAN)
        moved = slice(HB + first, HB + first + SPAN)
        term_recv += outer(window[moved, :], grad_rows[at, :] * slope_sum[at, :])
    keep_ref[0:LANES, :] = jnp.where(odd == 0, term_send, term_recv)
    first_ref[0:LANES, :] = jnp.where(odd == 0, term_recv, term_send).astype(BF16)


def fine_kernel(
    grad_hbm,
    send_sum_hbm,
    slope_sum_hbm,
    weight_hbm,
    first_hbm,
    second_hbm,
    fine_ref,
    grad_table,
    send_sum,
    slope_sum,
    weight_ref,
    first_ref,
    second_ref,
    arrivals,
):
    fine_count = fine_ref.shape[0]
    for copy in fetch(
        (grad_hbm, send_sum_hbm, slope_sum_hbm, weight_hbm, first_hbm, second_hbm),
        (grad_table, send_sum, slope_sum, weight_ref, first_ref, second_ref),
        arrivals,
    ):
        copy.wait()
    odd = lax.axis_index("curve") & 1
    one, two = first_ref[LANES:, :].astype(F32), second_ref[...].astype(F32)
    from_next, from_prev = jnp.where(odd == 0, one, two), jnp.where(odd == 0, two, one)
    for first in range(0, fine_count, SPAN):
        at = slice(first, first + SPAN)
        moved = slice(HB + first, HB + first + SPAN)
        grad = grad_table[at, :].astype(F32)
        summed = (
            grad
            + back(send_sum[moved, :], weight_ref[0:LANES, :])
            + back(grad * slope_sum[at, :], weight_ref[LANES:, :])
        )
        if first == 0:
            summed += from_prev
        if first == fine_count - SPAN:
            summed += from_next
        fine_ref[at, :] = summed.astype(BF16)


def last_kernel(
    edge_scale, coarse_scale, own_ref, coarse_ref, there_ref, edge_ref, in_ref, out_ref
):
    odd = lax.axis_index("curve") & 1
    own, coarse = own_ref[...], coarse_ref[...].astype(F32)
    other, other_coarse = there_ref[0:LANES, :], there_ref[LANES:, :]
    edge_ref[0:LANES, :] = jnp.where(odd == 0, own, other) * edge_scale
    edge_ref[LANES:, :] = jnp.where(odd == 0, other, own) * edge_scale
    in_ref[...] = jnp.where(odd == 0, coarse, other_coarse) * coarse_scale
    out_ref[...] = jnp.where(odd == 0, other_coarse, coarse) * coarse_scale


def pair_exchange(first, second, peers):
    pairs = [(i, i ^ 1) for i in range(peers)]
    between = [(i, ((i + 1) ^ 1) - 1) for i in range(1, peers - 1)]
    return lax.ppermute(first, "curve", pairs), lax.ppermute(second, "curve", between)


def joined(later, own, there):
    return jnp.where(
        later, jnp.concatenate([there, own], axis=0), jnp.concatenate([own, there], axis=0)
    )


def swapped(values, hops, peers):
    return lax.ppermute(values, "curve", [(i, i ^ hops) for i in range(peers)])


def reduced(sent, half, device, peers, beside):
    hops = 2
    while hops < peers // 4:
        there = swapped(sent, hops, peers)
        own = sent[:half].astype(F32) + there[:half].astype(F32)
        coarse = joined((device & hops) != 0, sent[half:], there[half:])
        sent = jnp.concatenate([own.astype(BF16), coarse], axis=0)
        hops *= 2
    near, far = peers // 4, peers // 2
    parts = [sent] + [swapped(sent, hops, peers) for hops in (near, far, near + far)]
    *parts, beside = lax.optimization_barrier((*parts, beside))
    sums = [part[:half].astype(F32) for part in parts]
    rows = [part[half:] for part in parts]
    own = (sums[0] + sums[1]) + (sums[2] + sums[3])
    later = (device & near) != 0
    coarse = joined(
        (device & far) != 0, joined(later, rows[0], rows[1]), joined(later, rows[2], rows[3])
    )
    return own, coarse, beside


def per_device(
    fine_latent,
    coarse_latent,
    grad_coarse,
    restrict_weights,
    send_rows,
    pair_slots,
    edge_receivers,
    edge_offsets,
    edge_weight,
    node_weight_in,
    node_weight_out,
    node_gain,
):
    peers = lax.axis_size("curve")
    device = lax.axis_index("curve")
    even = (device & 1) == 0
    coarse_count = coarse_latent.shape[0]
    fine_count = fine_latent.shape[0]
    edge_count = edge_receivers.shape[0]
    capacity = send_rows.shape[0] // peers
    chunk = SPAN // peers
    share = max(EXTRA, chunk)
    payload = capacity + EXTRA + share
    edge_rows = edge_count // LANES
    window_count = fine_count + 2 * HB
    params = pltpu.CompilerParams(vmem_limit_bytes=64 * 1024 * 1024 - 256 * 1024)
    roomy = pltpu.CompilerParams(vmem_limit_bytes=62 * 1024 * 1024)
    anywhere = pl.BlockSpec(memory_space=pl.ANY)

    scalar = pl.BlockSpec(memory_space=pltpu.SMEM)

    sent = pl.pallas_call(
        functools.partial(coarse_kernel, peers),
        out_shape=jax.ShapeDtypeStruct((peers, payload, LANES), BF16),
        in_specs=[anywhere] * 7,
        scratch_shapes=[
            pltpu.VMEM((SPAN, coarse_count), BF16),
            pltpu.VMEM((coarse_count, LANES), BF16),
            pltpu.VMEM((coarse_count, LANES), BF16),
            pltpu.VMEM((2, coarse_count), BF16),
            pltpu.VMEM((peers * capacity // LANES, LANES), jnp.int32),
            pltpu.VMEM((LANES, LANES), BF16),
            pltpu.VMEM((LANES, LANES), BF16),
            pltpu.VMEM((1, LANES), F32),
            pltpu.SemaphoreType.DMA((7,)),
        ],
        compiler_params=params,
        cost_estimate=pl.CostEstimate(
            flops=2_000_000_000, bytes_accessed=2_000_000, transcendentals=400_000
        ),
        name="coarse_block",
    )(
        coarse_latent,
        grad_coarse,
        restrict_weights,
        send_rows.reshape(-1, LANES),
        node_weight_in,
        node_weight_out,
        node_gain.reshape(1, LANES),
    )
    sent, fine_rows, receivers, offsets, slots = lax.optimization_barrier(
        (sent, fine_latent, edge_receivers, edge_offsets, pair_slots)
    )
    arrived = lax.all_to_all(sent, "curve", split_axis=0, concat_axis=0, tiled=True)
    head, end = fine_rows[:HB], fine_rows[fine_count - HB :]
    halos = pair_exchange(jnp.where(even, end, head), jnp.where(even, head, end), peers)

    pair_count = fine_count // 2
    in_vmem = pl.BlockSpec(memory_space=pltpu.VMEM)
    ordered, stats, slot_hot, slot_block = pl.pallas_call(
        functools.partial(order_kernel, fine_count=fine_count),
        out_shape=(
            jax.ShapeDtypeStruct((2, edge_rows, LANES), jnp.int32),
            jax.ShapeDtypeStruct((edge_rows, LANES), jnp.int32),
            jax.ShapeDtypeStruct((pair_count, SPAN), BF16),
            jax.ShapeDtypeStruct((pair_count, LANES), jnp.int32),
        ),
        in_specs=[anywhere] * 3,
        scratch_shapes=[
            pltpu.VMEM((edge_rows, LANES), jnp.int32),
            pltpu.VMEM((edge_rows, LANES), jnp.int32),
            pltpu.VMEM((pair_count // LANES, LANES), jnp.int32),
            pltpu.VMEM((edge_rows, LANES), jnp.int32),
            pltpu.SemaphoreType.DMA((3,)),
        ],
        compiler_params=params,
        cost_estimate=pl.CostEstimate(
            flops=3_000_000_000, bytes_accessed=2_000_000, transcendentals=0
        ),
        name="edge_order",
    )(
        receivers.reshape(-1, LANES),
        offsets.reshape(-1, LANES),
        slots.reshape(-1, LANES),
    )
    slope, hot, block, window, slope_sum = pl.pallas_call(
        slope_kernel,
        out_shape=(
            jax.ShapeDtypeStruct((edge_count, LANES), F32),
            jax.ShapeDtypeStruct((edge_count, SPAN), BF16),
            jax.ShapeDtypeStruct((edge_count, LANES), BF16),
            jax.ShapeDtypeStruct((window_count, LANES), BF16),
            jax.ShapeDtypeStruct((fine_count, LANES), F32),
        ),
        in_specs=[scalar] + [anywhere] * 5,
        out_specs=[anywhere] * 4 + [in_vmem],
        scratch_shapes=[
            pltpu.VMEM((2, edge_rows, LANES), jnp.int32),
            pltpu.VMEM((window_count, LANES), BF16),
            pltpu.VMEM((2 * LANES, LANES), BF16),
            pltpu.VMEM((2, HB, LANES), BF16),
            pltpu.VMEM((edge_count, LANES), F32),
            pltpu.VMEM((edge_count, SPAN), BF16),
            pltpu.VMEM((edge_count, LANES), BF16),
            pltpu.SemaphoreType.DMA((5,)),
            pltpu.SemaphoreType.DMA((3, edge_count // TILE)),
            pltpu.SemaphoreType.DMA,
        ],
        compiler_params=params,
        cost_estimate=pl.CostEstimate(
            flops=13_000_000_000, bytes_accessed=9_000_000, transcendentals=800_000
        ),
        name="edge_slope",
    )(stats, ordered, fine_latent, edge_weight, *halos)

    coarse_scale = 1.0 / math.sqrt(coarse_count * peers)
    edge_scale = 1.0 / math.sqrt(edge_count * peers)
    grad_rows, send_sum, first, second, keep, term_gain = pl.pallas_call(
        functools.partial(edge_kernel, coarse_scale),
        out_shape=(
            jax.ShapeDtypeStruct((fine_count, LANES), BF16),
            jax.ShapeDtypeStruct((window_count, LANES), F32),
            pltpu.VMEM((LANES + HB, LANES), BF16),
            pltpu.VMEM((HB, LANES), BF16),
            pltpu.VMEM((LANES + share, LANES), F32),
            jax.ShapeDtypeStruct((1, LANES), F32),
        ),
        in_specs=[scalar] + [anywhere] * 10,
        scratch_shapes=[
            pltpu.VMEM((SPAN, peers * capacity), BF16),
            pltpu.VMEM((fine_count, LANES), F32),
            pltpu.VMEM((peers, payload, LANES), BF16),
            pltpu.VMEM((pair_count, SPAN), BF16),
            pltpu.VMEM((pair_count, LANES), jnp.int32),
            pltpu.VMEM((edge_count, SPAN), BF16),
            pltpu.VMEM((edge_count, LANES), F32),
            pltpu.VMEM((edge_count, LANES), BF16),
            pltpu.VMEM((2, edge_rows, LANES), jnp.int32),
            pltpu.VMEM((window_count, LANES), BF16),
            pltpu.VMEM((fine_count, LANES), F32),
            pltpu.VMEM((2 * LANES, LANES), BF16),
            pltpu.SemaphoreType.DMA((10,)),
        ],
        compiler_params=roomy,
        cost_estimate=pl.CostEstimate(
            flops=24_000_000_000, bytes_accessed=8_000_000, transcendentals=0
        ),
        name="edge_back",
    )(
        stats,
        arrived,
        slot_hot,
        slot_block,
        hot,
        slope,
        block,
        ordered,
        window,
        slope_sum,
        edge_weight,
    )
    one, two = pair_exchange(first, second, peers)
    sent = keep[: LANES + chunk] + jnp.pad(one[:LANES].astype(F32), ((0, chunk), (0, 0)))
    sent = sent.astype(BF16)
    grad_fine = pl.pallas_call(
        fine_kernel,
        out_shape=jax.ShapeDtypeStruct((fine_count, LANES), BF16),
        in_specs=[anywhere] * 6,
        scratch_shapes=[
            pltpu.VMEM((fine_count, LANES), BF16),
            pltpu.VMEM((window_count, LANES), F32),
            pltpu.VMEM((fine_count, LANES), F32),
            pltpu.VMEM((2 * LANES, LANES), BF16),
            pltpu.VMEM((LANES + HB, LANES), BF16),
            pltpu.VMEM((HB, LANES), BF16),
            pltpu.SemaphoreType.DMA((6,)),
        ],
        compiler_params=pltpu.CompilerParams(vmem_limit_bytes=64 * 1024 * 1024 - 640 * 1024),
        cost_estimate=pl.CostEstimate(
            flops=1_000_000_000, bytes_accessed=4_000_000, transcendentals=0
        ),
        name="fine_sums",
    )(grad_rows, send_sum, slope_sum, edge_weight, one, two)
    own, coarse, grad_fine = reduced(sent, LANES, device, peers, grad_fine)
    there = swapped(jnp.concatenate([own, coarse.astype(F32)], axis=0), 1, peers)
    edge_terms, term_in, term_out = pl.pallas_call(
        functools.partial(last_kernel, edge_scale, coarse_scale),
        out_shape=(
            jax.ShapeDtypeStruct((2 * LANES, LANES), F32),
            jax.ShapeDtypeStruct((LANES, LANES), F32),
            jax.ShapeDtypeStruct((LANES, LANES), F32),
        ),
        compiler_params=pltpu.CompilerParams(vmem_limit_bytes=4 * 1024 * 1024),
        name="last_terms",
    )(own, coarse, there)
    return grad_fine, edge_terms, term_in, term_out, term_gain.reshape(LANES)


def solution(mesh):
    placed = (
        P(("groups", "curve"), None),
        P(("groups", "curve"), None),
        P(("groups", "curve"), None),
        P(None, ("groups", "curve")),
        P(("groups", "curve")),
        P(("groups", "curve")),
        P(("groups", "curve")),
        P(("groups", "curve")),
        P(),
        P(),
        P(),
        P(),
    )
    return jax.shard_map(
        per_device,
        mesh=mesh,
        in_specs=placed,
        out_specs=(
            P(("groups", "curve"), None),
            P("groups", None),
            P("groups", None),
            P("groups", None),
            P("groups"),
        ),
        check_vma=False,
    )
```

```python
import functools
import math

import jax
import jax.numpy as jnp
from jax import lax
from jax.experimental import pallas as pl
from jax.experimental.pallas import tpu as pltpu
from jax.sharding import PartitionSpec as P

HB = 256
LANES = 128
SPAN = 256
EXTRA = 16
TILE = 512
GROUP = 4
SENDERS = 3

F32 = jnp.float32
BF16 = jnp.bfloat16
NT = (((1,), (1,)), ((), ()))
TN = (((0,), (0,)), ((), ()))


def dot(left, right, dims=(((1,), (0,)), ((), ()))):
    return lax.dot_general(left, right, dims, preferred_element_type=F32)


def silu_slope(values):
    sigm = jax.nn.sigmoid(values)
    return sigm * (1.0 + values * (1.0 - sigm))


def columns(row):
    return jnp.broadcast_to(row, (LANES, LANES)).T


def index_columns(ref, first, count):
    return jnp.concatenate([columns(ref[pl.ds(first + i, 1), :]) for i in range(count)], axis=0)


def small(values):
    return values.astype(F32).astype(BF16)


def place_hot(cols):
    place = small(cols & (SPAN - 1))
    lane = lax.broadcasted_iota(jnp.int32, place.shape, 1)
    one, zero = jnp.ones((), BF16), jnp.zeros((), BF16)
    return jnp.concatenate(
        [jnp.where(place == small(lane + start), one, zero) for start in range(0, SPAN, LANES)],
        axis=1,
    )


def gather_rows(hot, block, table, width):
    total = table.shape[1]
    step = max(width, 2 * LANES)
    found = [jnp.zeros(block.shape, F32) for _ in range(width // LANES)]
    for start in range(0, total, step):
        part = dot(hot, table[:, start : start + step])
        for inner in range(0, step, width):
            here = block == (start + inner) // width
            for i in range(len(found)):
                at = inner + i * LANES
                found[i] = jnp.where(here, part[:, at : at + LANES], found[i])
    return found


def spread_rows(hot, block, blocks, values):
    if blocks == 1:
        return [dot(hot, values)]
    parts = []
    zero = jnp.zeros((), BF16)
    for start in range(0, blocks, 2):
        some = range(start, min(start + 2, blocks))
        spread = [jnp.where(block == jnp.full((), j, BF16), values, zero) for j in some]
        part = dot(hot, jnp.concatenate(spread, axis=1))
        parts += [part[:, i * LANES : (i + 1) * LANES] for i in range(len(some))]
    return parts


def add_parts(total, base, parts):
    for j, part in enumerate(parts):
        total[block_rows(base, j), :] += part


def place_hot_rows(ordered, at, tile, base, level):
    one, zero = jnp.ones((), BF16), jnp.zeros((), BF16)
    hot = []
    for i in range(TILE // LANES):
        row = ordered[at, pl.ds(tile * (TILE // LANES) + i, 1), :] - base
        hot.append(jnp.where(level == small(row & (SPAN - 1)), one, zero))
    return jnp.concatenate(hot, axis=1)


def levels():
    return small(lax.broadcasted_iota(jnp.int32, (SPAN, LANES), 0))


def two_parts(values):
    high = values.astype(BF16)
    return high, (values - high.astype(F32)).astype(BF16)


def back(values, weight):
    high, low = two_parts(values)
    return dot(high, weight, NT) + dot(low, weight, NT)


def outer(rows, values):
    high, low = two_parts(values)
    both = dot(rows, jnp.concatenate([high, low], axis=1), TN)
    return both[:, 0:LANES] + both[:, LANES:]


def fetch(sources, targets, arrivals):
    copies = [
        pltpu.make_async_copy(source, target, arrivals.at[i])
        for i, (source, target) in enumerate(zip(sources, targets))
    ]
    for copy in copies:
        copy.start()
    return copies


def coarse_kernel(
    peers,
    latent_ref,
    grad_ref,
    weights_ref,
    rows_ref,
    w_in_ref,
    w_out_ref,
    gain_ref,
    sent_ref,
    table_ref,
    *held,
):
    *held, arrivals = held
    sources = (latent_ref, grad_ref, weights_ref, rows_ref, w_in_ref, w_out_ref, gain_ref)
    copies = fetch(sources, held, arrivals)
    for copy in copies:
        copy.wait()
    latent_ref, grad_ref, weights_ref, rows_ref, w_in_ref, w_out_ref, gain_ref = held
    count = latent_ref.shape[0]
    chunk = SPAN // peers
    capacity = sent_ref.shape[1] - EXTRA - max(EXTRA, chunk)
    w_in, w_out, gain = w_in_ref[...], w_out_ref[...], gain_ref[...]
    latent = latent_ref[...]
    pre = dot(latent, w_in)
    sigm = jax.nn.sigmoid(pre)
    hidden = (pre * sigm).astype(BF16)
    slope = sigm * (1.0 + pre * (1.0 - sigm))
    mapped = dot(hidden, w_out)
    centred = mapped - jnp.mean(mapped, axis=1, keepdims=True)
    inverse = lax.rsqrt(jnp.mean(centred * centred, axis=1, keepdims=True) + 1e-05)
    normed = centred * inverse
    upstream = grad_ref[...].astype(F32)
    scaled = upstream * gain
    grad_mapped = (
        inverse
        * (
            scaled
            - jnp.mean(scaled, axis=1, keepdims=True)
            - normed * jnp.mean(scaled * normed, axis=1, keepdims=True)
        )
    ).astype(BF16)
    grad_pre = (dot(grad_mapped, w_out, NT) * slope).astype(BF16)
    grad_in = (upstream + dot(grad_pre, w_in, NT)).astype(BF16)
    term_gain = jnp.sum(upstream * normed, axis=0, keepdims=True)
    term_in = dot(latent, grad_pre, TN)
    term_out = dot(hidden, grad_mapped, TN)
    for block in range(count // SPAN):
        at = block * SPAN
        table_ref[:, at : at + LANES] = grad_in[at : at + SPAN]
        for half in range(SPAN // LANES):
            at = block * SPAN + half * LANES
            pair = weights_ref[:, at : at + LANES].astype(F32)
            square = jnp.concatenate([pair, jnp.zeros((LANES - 2, LANES), F32)], axis=0)
            table_ref[
                half * LANES : (half + 1) * LANES, block * SPAN + LANES : (block + 1) * SPAN
            ] = square.T.astype(BF16)
    gain_high, gain_low = two_parts(term_gain)
    gain_rows = jnp.concatenate([gain_high.astype(F32), gain_low.astype(F32)], axis=0)
    terms = jnp.concatenate([term_in, term_out], axis=0)
    per_step = 256 // LANES
    for first in range(0, rows_ref.shape[0], per_step):
        cols = index_columns(rows_ref, first, per_step)
        sent, weight = gather_rows(place_hot(cols), cols // SPAN, table_ref, SPAN)
        for part in range(per_step * LANES // capacity):
            peer = first * LANES // capacity + part
            rows = slice(part * capacity, (part + 1) * capacity)
            sent_ref[peer, 0:capacity, :] = sent[rows].astype(BF16)
            square = weight[rows]
            if capacity < LANES:
                square = jnp.concatenate(
                    [square, jnp.zeros((LANES - capacity, LANES), F32)], axis=0
                )
            extra = jnp.concatenate(
                [square.T[0:2], gain_rows, jnp.zeros((EXTRA - 4, LANES), F32)], axis=0
            )
            sent_ref[peer, capacity : capacity + EXTRA, :] = extra.astype(BF16)
            first_row = (peer % 2 * (peers // 2) + peer // 2) * chunk
            share = terms[first_row : first_row + chunk]
            if chunk < EXTRA:
                share = jnp.concatenate([share, jnp.zeros((EXTRA - chunk, LANES), F32)], axis=0)
            sent_ref[peer, capacity + EXTRA :, :] = share.astype(BF16)


def order_edges(recv_ref, off_ref, ordered, stats_vmem, fine_count):
    rows = recv_ref.shape[0]
    shift = (fine_count // LANES).bit_length() - 1
    lane = lax.broadcasted_iota(jnp.int32, (LANES, LANES), 1)
    sub = lax.broadcasted_iota(jnp.int32, (LANES, LANES), 0)
    level = small(sub)
    one, zero = jnp.ones((), BF16), jnp.zeros((), BF16)

    def hot(row):
        return jnp.where(level == small(row), one, zero)

    number = jnp.zeros((LANES, LANES), BF16)
    for row in range(rows):
        number += hot(recv_ref[row : row + 1, :] >> shift)
    ones = jnp.ones((LANES, LANES), BF16)
    total = dot(number, ones)
    high = jnp.floor(total * (1.0 / 64.0))
    low = total - 64.0 * high
    before = jnp.where(lane < sub, 1.0, 0.0).astype(BF16)
    start = 64.0 * dot(before, high.astype(BF16)) + dot(before, low.astype(BF16))
    after = jnp.where(sub < lane, 1.0, 0.0).astype(BF16)
    prefix = jnp.concatenate([after, ones], axis=1)
    positions = []
    filled = start
    for row in range(rows):
        bucket = recv_ref[row : row + 1, :] >> shift
        found = dot(hot(bucket), prefix)
        mine = jnp.where(sub == bucket, found[:, 0:LANES] + filled, 0.0)
        positions.append(jnp.sum(mine, axis=0, keepdims=True).astype(jnp.int32))
        filled = filled + found[:, LANES:]
    moved = jnp.zeros((192, LANES), F32)
    for part in range(0, rows, 4):
        left, right = [], []
        for row in range(part, part + 4):
            position = positions[row]
            recv = recv_ref[row : row + 1, :]
            off = off_ref[row : row + 1, :] + HB
            rest = ((recv >> 8) << 2) | (off >> 8)
            here = level[0:64] == small(position >> 7)
            values = [small(value) for value in (recv & 255, off & 255, rest)]
            left.append(jnp.concatenate([jnp.where(here, v, zero) for v in values], axis=0))
            right.append(hot(position & 127))
        moved += dot(jnp.concatenate(left, axis=1), jnp.concatenate(right, axis=1), NT)
    moved = moved.astype(jnp.int32)
    rest = moved[LANES : LANES + rows]
    recv = moved[0:rows] + ((rest >> 2) << 8)
    send = recv + moved[64 : 64 + rows] + ((rest & 3) << 8)
    ordered[0] = recv
    ordered[1] = send
    lane = lax.broadcasted_iota(jnp.int32, (rows, LANES), 1)
    recv, send = recv.astype(F32), send.astype(F32)
    stats = jnp.where(
        lane < 2,
        jnp.where(
            lane == 0,
            jnp.min(recv, axis=1, keepdims=True),
            jnp.max(recv, axis=1, keepdims=True),
        ),
        jnp.where(
            lane == 2,
            jnp.min(send, axis=1, keepdims=True),
            jnp.max(send, axis=1, keepdims=True),
        ),
    )
    stats_vmem[...] = stats.astype(jnp.int32)


def tile_bases(stats, tile, fine_count):
    count = TILE // LANES
    rows = [tile * count + i for i in range(count)]

    def extreme(pick, at):
        value = stats[rows[0], at]
        for row in rows[1:]:
            value = pick(value, stats[row, at])
        return value

    recv_base = jnp.minimum((extreme(jnp.minimum, 0) >> 4) << 4, fine_count - SPAN)
    send_base = jnp.minimum(
        (extreme(jnp.minimum, 2) >> 4) << 4, fine_count + 2 * HB - SENDERS * SPAN
    )
    fits = (extreme(jnp.maximum, 1) - recv_base < SPAN) & (
        extreme(jnp.maximum, 3) - send_base < SENDERS * SPAN
    )
    return recv_base, send_base, fits


def each_group(step, stats, fine_count, near, far):
    tiles = [step * GROUP + i for i in range(GROUP)]
    places = [tile_bases(stats, tile, fine_count) for tile in tiles]
    fits = functools.reduce(jnp.logical_and, [place[2] for place in places])

    @pl.when(fits)
    def _():
        near(tiles, [place[:2] for place in places])

    @pl.when(jnp.logical_not(fits))
    def _():
        def one(i, carry):
            far(step * GROUP + i)
            return carry

        lax.fori_loop(0, GROUP, one, 0)


def block_rows(base, block):
    return pl.ds(pl.multiple_of(base + block * SPAN, 16), SPAN)


def gather_blocks(hot, block, table, base, blocks):
    found = None
    for start in range(0, blocks, 2):
        some = range(start, min(start + 2, blocks))
        part = dot(hot, jnp.concatenate([table[block_rows(base, j), :] for j in some], axis=1))
        for i, j in enumerate(some):
            one = part[:, i * LANES : (i + 1) * LANES]
            found = one if found is None else jnp.where(block == j, one, found)
    return found


def tile_rows(tile):
    return pl.ds(pl.multiple_of(tile * TILE, TILE), TILE)


def order_kernel(
    recv_hbm,
    off_hbm,
    slots_hbm,
    ordered,
    stats_ref,
    slot_hot,
    slot_block,
    recv_ref,
    off_ref,
    slots_ref,
    arrivals,
    fine_count,
):
    for copy in fetch(
        (recv_hbm, off_hbm, slots_hbm), (recv_ref, off_ref, slots_ref), arrivals
    ):
        copy.wait()
    order_edges(recv_ref, off_ref, ordered, stats_ref, fine_count)
    slots = index_columns(slots_ref, 0, slots_ref.shape[0])
    slot_hot[...] = place_hot(slots)
    slot_block[...] = slots // SPAN


def slope_kernel(
    stats,
    ordered_hbm,
    fine_hbm,
    weight_hbm,
    first_hbm,
    second_hbm,
    slope_hbm,
    hot_hbm,
    block_hbm,
    window_hbm,
    slope_sum,
    ordered,
    window,
    weight_ref,
    halos,
    slope_ref,
    hot_ref,
    block_ref,
    arrivals,
    leaving,
    window_left,
):
    fine_count = fine_hbm.shape[0]
    copies = fetch(
        (ordered_hbm, fine_hbm, weight_hbm, first_hbm, second_hbm),
        (ordered, window.at[pl.ds(HB, fine_count)], weight_ref, halos.at[0], halos.at[1]),
        arrivals,
    )
    slope_sum[...] = jnp.zeros(slope_sum.shape, F32)
    for copy in copies:
        copy.wait()
    odd = lax.axis_index("curve") & 1
    window[0:HB, :] = halos[1 - odd]
    window[HB + fine_count :, :] = halos[odd]
    window_copy = pltpu.make_async_copy(window, window_hbm, window_left)
    window_copy.start()
    count = TILE // LANES
    weight = weight_ref[...]
    level = levels()

    def leave(tile):
        rows = tile_rows(tile)
        pairs = ((slope_ref, slope_hbm), (hot_ref, hot_hbm), (block_ref, block_hbm))
        return [
            pltpu.make_async_copy(source.at[rows], target.at[rows], leaving.at[i, tile])
            for i, (source, target) in enumerate(pairs)
        ]

    def near(tiles, places):
        work = []
        for tile, (recv_base, send_base) in zip(tiles, places):
            recv = index_columns(ordered.at[0], tile * count, count) - recv_base
            send = index_columns(ordered.at[1], tile * count, count) - send_base
            block = send >> 8
            hot = place_hot(recv)
            hot_ref[tile_rows(tile), :] = hot
            block_ref[tile_rows(tile), :] = small(block)
            sender = gather_blocks(place_hot(send), block, window, send_base, SENDERS)
            receiver = gather_blocks(hot, None, window, recv_base + HB, 1)
            work.append((sender, receiver))
        slopes = []
        for tile, (sender, receiver) in zip(tiles, work):
            inputs = jnp.concatenate([sender.astype(BF16), receiver.astype(BF16)], axis=1)
            slope = silu_slope(dot(inputs, weight))
            slope_ref[tile_rows(tile), :] = slope
            slopes.append(jnp.concatenate(two_parts(slope), axis=1))
        sums = []
        for tile, (recv_base, _), slope in zip(tiles, places, slopes):
            hot = place_hot_rows(ordered, 0, tile, recv_base, level)
            both = dot(hot, slope)
            sums.append(both[:, 0:LANES] + both[:, LANES:])
        for (recv_base, _), part in zip(places, sums):
            add_parts(slope_sum, recv_base, [part])

    def far(tile):
        recv = index_columns(ordered.at[0], tile * count, count)
        send = index_columns(ordered.at[1], tile * count, count)
        blocks = fine_count // SPAN
        sender = gather_blocks(place_hot(send), send >> 8, window, 0, blocks + 2)
        receiver = gather_blocks(place_hot(recv), recv >> 8, window, HB, blocks)
        inputs = jnp.concatenate([sender.astype(BF16), receiver.astype(BF16)], axis=1)
        slope = silu_slope(dot(inputs, weight))
        slope_ref[tile_rows(tile), :] = slope
        hot = place_hot_rows(ordered, 0, tile, 0, level)
        for part in two_parts(slope):
            add_parts(slope_sum, 0, spread_rows(hot, small(recv >> 8), blocks, part))
        hot_ref[tile_rows(tile), :] = jnp.zeros((TILE, SPAN), BF16)
        block_ref[tile_rows(tile), :] = jnp.zeros((TILE, LANES), BF16)

    def step(index, carry):
        each_group(index, stats, fine_count, near, far)
        for i in range(GROUP):
            for copy in leave(index * GROUP + i):
                copy.start()
        return carry

    tiles = slope_ref.shape[0] // TILE
    lax.fori_loop(0, tiles // GROUP, step, 0)
    window_copy.wait()
    for tile in range(tiles):
        for copy in leave(tile):
            copy.wait()


def edge_kernel(
    coarse_scale,
    stats,
    arrived_hbm,
    slot_hot_hbm,
    slot_block_hbm,
    hot_hbm,
    slope_hbm,
    block_hbm,
    ordered_hbm,
    window_hbm,
    slope_sum_hbm,
    weight_hbm,
    grad_table,
    send_sum,
    first_ref,
    second_ref,
    keep_ref,
    gain_ref,
    slot_table,
    grad_rows,
    arrived_ref,
    slot_hot,
    slot_block,
    hot_ref,
    slope_ref,
    block_ref,
    ordered,
    window,
    slope_sum,
    weight_ref,
    arrivals,
):
    fine_count = grad_table.shape[0]
    copies = fetch(
        (
            arrived_hbm,
            slot_hot_hbm,
            slot_block_hbm,
            hot_hbm,
            slope_hbm,
            block_hbm,
            ordered_hbm,
            window_hbm,
            slope_sum_hbm,
            weight_hbm,
        ),
        (
            arrived_ref,
            slot_hot,
            slot_block,
            hot_ref,
            slope_ref,
            block_ref,
            ordered,
            window,
            slope_sum,
            weight_ref,
        ),
        arrivals,
    )
    send_sum[...] = jnp.zeros(send_sum.shape, F32)
    peers = arrived_ref.shape[0]
    share = max(EXTRA, SPAN // peers)
    capacity = arrived_ref.shape[1] - EXTRA - share
    per_block = SPAN // capacity
    for copy in copies[:3]:
        copy.wait()
    coarse = jnp.zeros((share, LANES), F32)
    gain = jnp.zeros((1, LANES), F32)
    for peer in range(peers):
        block, part = divmod(peer, per_block)
        rows = slice(part * capacity, (part + 1) * capacity)
        slot_table[rows, block * SPAN : block * SPAN + LANES] = arrived_ref[peer, 0:capacity, :]
        extra = arrived_ref[peer, capacity : capacity + EXTRA, :].astype(F32)
        square = jnp.concatenate([extra, jnp.zeros((LANES - EXTRA, LANES), F32)], axis=0).T
        slot_table[rows, block * SPAN + LANES : (block + 1) * SPAN] = square[0:capacity].astype(
            BF16
        )
        gain += extra[2:3] + extra[3:4]
        coarse += arrived_ref[peer, capacity + EXTRA :, :].astype(F32)
    keep_ref[LANES:, :] = coarse
    gain_ref[...] = gain * coarse_scale

    found = []
    for first in range(0, slot_hot.shape[0], SPAN):
        at = slice(first, first + SPAN)
        found.append(gather_rows(slot_hot[at, :], slot_block[at, :], slot_table, SPAN))
    for i, (grad, weight) in enumerate(found):
        first = i * SPAN
        for r in range(2):
            rows = (grad * weight[:, r : r + 1]).astype(BF16).astype(F32)
            grad_rows[pl.ds(2 * first + r, SPAN, stride=2), :] = rows
    grad_table[...] = grad_rows[...].astype(BF16)
    for copy in copies[3:]:
        copy.wait()

    count = TILE // LANES
    level = levels()

    def near(tiles, places):
        work = []
        for tile, (recv_base, _) in zip(tiles, places):
            rows = tile_rows(tile)
            upstream = gather_blocks(hot_ref[rows, :], None, grad_table, recv_base, 1)
            work.append((upstream * slope_ref[rows, :]).astype(BF16))
        sums = []
        for tile, (_, send_base), values in zip(tiles, places, work):
            hot = place_hot_rows(ordered, 1, tile, send_base, level)
            sums.append(spread_rows(hot, block_ref[tile_rows(tile), :], SENDERS, values))
        for (_, send_base), parts in zip(places, sums):
            add_parts(send_sum, send_base, parts)

    def far(tile):
        rows = tile_rows(tile)
        recv = index_columns(ordered.at[0], tile * count, count)
        send = index_columns(ordered.at[1], tile * count, count)
        blocks = fine_count // SPAN
        upstream = gather_blocks(place_hot(recv), recv >> 8, grad_table, 0, blocks)
        values = (upstream * slope_ref[rows, :]).astype(BF16)
        hot = place_hot_rows(ordered, 1, tile, 0, level)
        add_parts(send_sum, 0, spread_rows(hot, small(send >> 8), blocks + 2, values))

    def step(index, carry):
        each_group(index, stats, fine_count, near, far)
        return carry

    lax.fori_loop(0, slope_ref.shape[0] // TILE // GROUP, step, 0)

    weight_send = weight_ref[0:LANES, :]
    odd = lax.axis_index("curve") & 1
    to_prev = back(send_sum[0:HB, :], weight_send)
    to_next = back(send_sum[HB + fine_count :, :], weight_send)
    first_ref[LANES:, :] = jnp.where(odd == 0, to_next, to_prev).astype(BF16)
    second_ref[...] = jnp.where(odd == 0, to_prev, to_next).astype(BF16)
    term_send = jnp.zeros((LANES, LANES), F32)
    term_recv = jnp.zeros((LANES, LANES), F32)
    for first in range(0, fine_count + 2 * HB, SPAN):
        at = slice(first, first + SPAN)
        term_send += outer(window[at, :], send_sum[at, :])
    for first in range(0, fine_count, SPAN):
        at = slice(first, first + SPAN)
        moved = slice(HB + first, HB + first + SPAN)
        term_recv += outer(window[moved, :], grad_rows[at, :] * slope_sum[at, :])
    keep_ref[0:LANES, :] = jnp.where(odd == 0, term_send, term_recv)
    first_ref[0:LANES, :] = jnp.where(odd == 0, term_recv, term_send).astype(BF16)


def fine_kernel(
    grad_hbm,
    send_sum_hbm,
    slope_sum_hbm,
    weight_hbm,
    first_hbm,
    second_hbm,
    fine_ref,
    grad_table,
    send_sum,
    slope_sum,
    weight_ref,
    first_ref,
    second_ref,
    arrivals,
):
    fine_count = fine_ref.shape[0]
    for copy in fetch(
        (grad_hbm, send_sum_hbm, slope_sum_hbm, weight_hbm, first_hbm, second_hbm),
        (grad_table, send_sum, slope_sum, weight_ref, first_ref, second_ref),
        arrivals,
    ):
        copy.wait()
    odd = lax.axis_index("curve") & 1
    one, two = first_ref[LANES:, :].astype(F32), second_ref[...].astype(F32)
    from_next, from_prev = jnp.where(odd == 0, one, two), jnp.where(odd == 0, two, one)
    for first in range(0, fine_count, SPAN):
        at = slice(first, first + SPAN)
        moved = slice(HB + first, HB + first + SPAN)
        grad = grad_table[at, :].astype(F32)
        summed = (
            grad
            + back(send_sum[moved, :], weight_ref[0:LANES, :])
            + back(grad * slope_sum[at, :], weight_ref[LANES:, :])
        )
        if first == 0:
            summed += from_prev
        if first == fine_count - SPAN:
            summed += from_next
        fine_ref[at, :] = summed.astype(BF16)


def last_kernel(
    edge_scale, coarse_scale, own_ref, coarse_ref, there_ref, edge_ref, in_ref, out_ref
):
    odd = lax.axis_index("curve") & 1
    own, coarse = own_ref[...], coarse_ref[...].astype(F32)
    other, other_coarse = there_ref[0:LANES, :], there_ref[LANES:, :]
    edge_ref[0:LANES, :] = jnp.where(odd == 0, own, other) * edge_scale
    edge_ref[LANES:, :] = jnp.where(odd == 0, other, own) * edge_scale
    in_ref[...] = jnp.where(odd == 0, coarse, other_coarse) * coarse_scale
    out_ref[...] = jnp.where(odd == 0, other_coarse, coarse) * coarse_scale


def pair_exchange(first, second, peers):
    pairs = [(i, i ^ 1) for i in range(peers)]
    between = [(i, ((i + 1) ^ 1) - 1) for i in range(1, peers - 1)]
    return lax.ppermute(first, "curve", pairs), lax.ppermute(second, "curve", between)


def swapped(values, hops, peers):
    return lax.ppermute(values, "curve", [(i, i ^ hops) for i in range(peers)])


def from_same_core(sent, peers):
    count = peers // 2
    return lax.all_to_all(
        jnp.broadcast_to(sent[None], (count,) + sent.shape),
        "curve",
        split_axis=0,
        concat_axis=0,
        axis_index_groups=[list(range(core, peers, 2)) for core in range(2)],
        tiled=True,
    )


def per_device(
    fine_latent,
    coarse_latent,
    grad_coarse,
    restrict_weights,
    send_rows,
    pair_slots,
    edge_receivers,
    edge_offsets,
    edge_weight,
    node_weight_in,
    node_weight_out,
    node_gain,
):
    peers = lax.axis_size("curve")
    device = lax.axis_index("curve")
    even = (device & 1) == 0
    coarse_count = coarse_latent.shape[0]
    fine_count = fine_latent.shape[0]
    edge_count = edge_receivers.shape[0]
    capacity = send_rows.shape[0] // peers
    chunk = SPAN // peers
    share = max(EXTRA, chunk)
    payload = capacity + EXTRA + share
    edge_rows = edge_count // LANES
    window_count = fine_count + 2 * HB
    params = pltpu.CompilerParams(vmem_limit_bytes=64 * 1024 * 1024 - 256 * 1024)
    roomy = pltpu.CompilerParams(vmem_limit_bytes=64 * 1024 * 1024 - 1536 * 1024)
    anywhere = pl.BlockSpec(memory_space=pl.ANY)

    scalar = pl.BlockSpec(memory_space=pltpu.SMEM)

    sent = pl.pallas_call(
        functools.partial(coarse_kernel, peers),
        out_shape=jax.ShapeDtypeStruct((peers, payload, LANES), BF16),
        in_specs=[anywhere] * 7,
        scratch_shapes=[
            pltpu.VMEM((SPAN, coarse_count), BF16),
            pltpu.VMEM((coarse_count, LANES), BF16),
            pltpu.VMEM((coarse_count, LANES), BF16),
            pltpu.VMEM((2, coarse_count), BF16),
            pltpu.VMEM((peers * capacity // LANES, LANES), jnp.int32),
            pltpu.VMEM((LANES, LANES), BF16),
            pltpu.VMEM((LANES, LANES), BF16),
            pltpu.VMEM((1, LANES), F32),
            pltpu.SemaphoreType.DMA((7,)),
        ],
        compiler_params=params,
        cost_estimate=pl.CostEstimate(
            flops=2_000_000_000, bytes_accessed=2_000_000, transcendentals=400_000
        ),
        name="coarse_block",
    )(
        coarse_latent,
        grad_coarse,
        restrict_weights,
        send_rows.reshape(-1, LANES),
        node_weight_in,
        node_weight_out,
        node_gain.reshape(1, LANES),
    )
    sent, fine_rows, receivers, offsets, slots = lax.optimization_barrier(
        (sent, fine_latent, edge_receivers, edge_offsets, pair_slots)
    )
    arrived = lax.all_to_all(sent, "curve", split_axis=0, concat_axis=0, tiled=True)
    head, end = fine_rows[:HB], fine_rows[fine_count - HB :]
    halos = pair_exchange(jnp.where(even, end, head), jnp.where(even, head, end), peers)

    pair_count = fine_count // 2
    in_vmem = pl.BlockSpec(memory_space=pltpu.VMEM)
    ordered, stats, slot_hot, slot_block = pl.pallas_call(
        functools.partial(order_kernel, fine_count=fine_count),
        out_shape=(
            jax.ShapeDtypeStruct((2, edge_rows, LANES), jnp.int32),
            jax.ShapeDtypeStruct((edge_rows, LANES), jnp.int32),
            jax.ShapeDtypeStruct((pair_count, SPAN), BF16),
            jax.ShapeDtypeStruct((pair_count, LANES), jnp.int32),
        ),
        in_specs=[anywhere] * 3,
        scratch_shapes=[
            pltpu.VMEM((edge_rows, LANES), jnp.int32),
            pltpu.VMEM((edge_rows, LANES), jnp.int32),
            pltpu.VMEM((pair_count // LANES, LANES), jnp.int32),
            pltpu.SemaphoreType.DMA((3,)),
        ],
        compiler_params=roomy,
        cost_estimate=pl.CostEstimate(
            flops=3_000_000_000, bytes_accessed=2_000_000, transcendentals=0
        ),
        name="edge_order",
    )(
        receivers.reshape(-1, LANES),
        offsets.reshape(-1, LANES),
        slots.reshape(-1, LANES),
    )
    slope, hot, block, window, slope_sum = pl.pallas_call(
        slope_kernel,
        out_shape=(
            jax.ShapeDtypeStruct((edge_count, LANES), F32),
            jax.ShapeDtypeStruct((edge_count, SPAN), BF16),
            jax.ShapeDtypeStruct((edge_count, LANES), BF16),
            jax.ShapeDtypeStruct((window_count, LANES), BF16),
            jax.ShapeDtypeStruct((fine_count, LANES), F32),
        ),
        in_specs=[scalar] + [anywhere] * 5,
        out_specs=[anywhere] * 4 + [in_vmem],
        scratch_shapes=[
            pltpu.VMEM((2, edge_rows, LANES), jnp.int32),
            pltpu.VMEM((window_count, LANES), BF16),
            pltpu.VMEM((2 * LANES, LANES), BF16),
            pltpu.VMEM((2, HB, LANES), BF16),
            pltpu.VMEM((edge_count, LANES), F32),
            pltpu.VMEM((edge_count, SPAN), BF16),
            pltpu.VMEM((edge_count, LANES), BF16),
            pltpu.SemaphoreType.DMA((5,)),
            pltpu.SemaphoreType.DMA((3, edge_count // TILE)),
            pltpu.SemaphoreType.DMA,
        ],
        compiler_params=roomy,
        cost_estimate=pl.CostEstimate(
            flops=13_000_000_000, bytes_accessed=9_000_000, transcendentals=800_000
        ),
        name="edge_slope",
    )(stats, ordered, fine_latent, edge_weight, *halos)

    coarse_scale = 1.0 / math.sqrt(coarse_count * peers)
    edge_scale = 1.0 / math.sqrt(edge_count * peers)
    grad_rows, send_sum, first, second, keep, term_gain = pl.pallas_call(
        functools.partial(edge_kernel, coarse_scale),
        out_shape=(
            jax.ShapeDtypeStruct((fine_count, LANES), BF16),
            jax.ShapeDtypeStruct((window_count, LANES), F32),
            pltpu.VMEM((LANES + HB, LANES), BF16),
            pltpu.VMEM((HB, LANES), BF16),
            pltpu.VMEM((LANES + share, LANES), F32),
            jax.ShapeDtypeStruct((1, LANES), F32),
        ),
        in_specs=[scalar] + [anywhere] * 10,
        scratch_shapes=[
            pltpu.VMEM((SPAN, peers * capacity), BF16),
            pltpu.VMEM((fine_count, LANES), F32),
            pltpu.VMEM((peers, payload, LANES), BF16),
            pltpu.VMEM((pair_count, SPAN), BF16),
            pltpu.VMEM((pair_count, LANES), jnp.int32),
            pltpu.VMEM((edge_count, SPAN), BF16),
            pltpu.VMEM((edge_count, LANES), F32),
            pltpu.VMEM((edge_count, LANES), BF16),
            pltpu.VMEM((2, edge_rows, LANES), jnp.int32),
            pltpu.VMEM((window_count, LANES), BF16),
            pltpu.VMEM((fine_count, LANES), F32),
            pltpu.VMEM((2 * LANES, LANES), BF16),
            pltpu.SemaphoreType.DMA((10,)),
        ],
        compiler_params=roomy,
        cost_estimate=pl.CostEstimate(
            flops=24_000_000_000, bytes_accessed=8_000_000, transcendentals=0
        ),
        name="edge_back",
    )(
        stats,
        arrived,
        slot_hot,
        slot_block,
        hot,
        slope,
        block,
        ordered,
        window,
        slope_sum,
        edge_weight,
    )
    one, two = pair_exchange(first, second, peers)
    sent = keep[: LANES + chunk] + jnp.pad(one[:LANES].astype(F32), ((0, chunk), (0, 0)))
    sent = sent.astype(BF16)
    grad_fine = pl.pallas_call(
        fine_kernel,
        out_shape=jax.ShapeDtypeStruct((fine_count, LANES), BF16),
        in_specs=[anywhere] * 6,
        scratch_shapes=[
            pltpu.VMEM((fine_count, LANES), BF16),
            pltpu.VMEM((window_count, LANES), F32),
            pltpu.VMEM((fine_count, LANES), F32),
            pltpu.VMEM((2 * LANES, LANES), BF16),
            pltpu.VMEM((LANES + HB, LANES), BF16),
            pltpu.VMEM((HB, LANES), BF16),
            pltpu.SemaphoreType.DMA((6,)),
        ],
        compiler_params=roomy,
        cost_estimate=pl.CostEstimate(
            flops=1_000_000_000, bytes_accessed=4_000_000, transcendentals=0
        ),
        name="fine_sums",
    )(grad_rows, send_sum, slope_sum, edge_weight, one, two)
    parts, grad_fine = lax.optimization_barrier((from_same_core(sent, peers), grad_fine))
    own = jnp.sum(parts[:, :LANES].astype(F32), axis=0)
    coarse = parts[:, LANES:].reshape(LANES, LANES)
    there = swapped(jnp.concatenate([own, coarse.astype(F32)], axis=0), 1, peers)
    edge_terms, term_in, term_out = pl.pallas_call(
        functools.partial(last_kernel, edge_scale, coarse_scale),
        out_shape=(
            jax.ShapeDtypeStruct((2 * LANES, LANES), F32),
            jax.ShapeDtypeStruct((LANES, LANES), F32),
            jax.ShapeDtypeStruct((LANES, LANES), F32),
        ),
        compiler_params=pltpu.CompilerParams(vmem_limit_bytes=4 * 1024 * 1024),
        name="last_terms",
    )(own, coarse, there)
    return grad_fine, edge_terms, term_in, term_out, term_gain.reshape(LANES)


def solution(mesh):
    placed = (
        P(("groups", "curve"), None),
        P(("groups", "curve"), None),
        P(("groups", "curve"), None),
        P(None, ("groups", "curve")),
        P(("groups", "curve")),
        P(("groups", "curve")),
        P(("groups", "curve")),
        P(("groups", "curve")),
        P(),
        P(),
        P(),
        P(),
    )
    return jax.shard_map(
        per_device,
        mesh=mesh,
        in_specs=placed,
        out_specs=(
            P(("groups", "curve"), None),
            P("groups", None),
            P("groups", None),
            P("groups", None),
            P("groups"),
        ),
        check_vma=False,
    )
```

```python
import functools
import math

import jax
import jax.numpy as jnp
from jax import lax
from jax.experimental import pallas as pl
from jax.experimental.pallas import tpu as pltpu
from jax.sharding import PartitionSpec as P

HB = 256
LANES = 128
SPAN = 256
EXTRA = 16
TILE = 512
GROUP = 4
SENDERS = 3

F32 = jnp.float32
BF16 = jnp.bfloat16
NT = (((1,), (1,)), ((), ()))
TN = (((0,), (0,)), ((), ()))


def dot(left, right, dims=(((1,), (0,)), ((), ()))):
    return lax.dot_general(left, right, dims, preferred_element_type=F32)


def silu_slope(values):
    sigm = jax.nn.sigmoid(values)
    return sigm * (1.0 + values * (1.0 - sigm))


def columns(row):
    return jnp.broadcast_to(row, (LANES, LANES)).T


def index_columns(ref, first, count):
    return jnp.concatenate([columns(ref[pl.ds(first + i, 1), :]) for i in range(count)], axis=0)


def small(values):
    return values.astype(F32).astype(BF16)


def place_hot(cols):
    place = small(cols & (SPAN - 1))
    lane = lax.broadcasted_iota(jnp.int32, place.shape, 1)
    one, zero = jnp.ones((), BF16), jnp.zeros((), BF16)
    return jnp.concatenate(
        [jnp.where(place == small(lane + start), one, zero) for start in range(0, SPAN, LANES)],
        axis=1,
    )


def gather_rows(hot, block, table, width):
    total = table.shape[1]
    step = max(width, 2 * LANES)
    found = [jnp.zeros(block.shape, F32) for _ in range(width // LANES)]
    for start in range(0, total, step):
        part = dot(hot, table[:, start : start + step])
        for inner in range(0, step, width):
            here = block == (start + inner) // width
            for i in range(len(found)):
                at = inner + i * LANES
                found[i] = jnp.where(here, part[:, at : at + LANES], found[i])
    return found


def spread_rows(hot, block, blocks, values):
    if blocks == 1:
        return [dot(hot, values)]
    parts = []
    zero = jnp.zeros((), BF16)
    for start in range(0, blocks, 2):
        some = range(start, min(start + 2, blocks))
        spread = [jnp.where(block == jnp.full((), j, BF16), values, zero) for j in some]
        part = dot(hot, jnp.concatenate(spread, axis=1))
        parts += [part[:, i * LANES : (i + 1) * LANES] for i in range(len(some))]
    return parts


def add_parts(total, base, parts):
    for j, part in enumerate(parts):
        total[block_rows(base, j), :] += part


def place_hot_rows(ordered, at, tile, base, level):
    one, zero = jnp.ones((), BF16), jnp.zeros((), BF16)
    hot = []
    for i in range(TILE // LANES):
        row = ordered[at, pl.ds(tile * (TILE // LANES) + i, 1), :] - base
        hot.append(jnp.where(level == small(row & (SPAN - 1)), one, zero))
    return jnp.concatenate(hot, axis=1)


def levels():
    return small(lax.broadcasted_iota(jnp.int32, (SPAN, LANES), 0))


def two_parts(values):
    high = values.astype(BF16)
    return high, (values - high.astype(F32)).astype(BF16)


def back(values, weight):
    high, low = two_parts(values)
    return dot(high, weight, NT) + dot(low, weight, NT)


def outer(rows, values):
    high, low = two_parts(values)
    both = dot(rows, jnp.concatenate([high, low], axis=1), TN)
    return both[:, 0:LANES] + both[:, LANES:]


def fetch(sources, targets, arrivals):
    copies = [
        pltpu.make_async_copy(source, target, arrivals.at[i])
        for i, (source, target) in enumerate(zip(sources, targets))
    ]
    for copy in copies:
        copy.start()
    return copies


def coarse_kernel(
    peers,
    latent_ref,
    grad_ref,
    weights_ref,
    rows_ref,
    w_in_ref,
    w_out_ref,
    gain_ref,
    sent_ref,
    table_ref,
    *held,
):
    *held, arrivals = held
    sources = (latent_ref, grad_ref, weights_ref, rows_ref, w_in_ref, w_out_ref, gain_ref)
    copies = fetch(sources, held, arrivals)
    for copy in copies:
        copy.wait()
    latent_ref, grad_ref, weights_ref, rows_ref, w_in_ref, w_out_ref, gain_ref = held
    count = latent_ref.shape[0]
    chunk = SPAN // peers
    capacity = sent_ref.shape[1] - EXTRA - max(EXTRA, chunk)
    w_in, w_out, gain = w_in_ref[...], w_out_ref[...], gain_ref[...]
    latent = latent_ref[...]
    pre = dot(latent, w_in)
    sigm = jax.nn.sigmoid(pre)
    hidden = (pre * sigm).astype(BF16)
    slope = sigm * (1.0 + pre * (1.0 - sigm))
    mapped = dot(hidden, w_out)
    centred = mapped - jnp.mean(mapped, axis=1, keepdims=True)
    inverse = lax.rsqrt(jnp.mean(centred * centred, axis=1, keepdims=True) + 1e-05)
    normed = centred * inverse
    upstream = grad_ref[...].astype(F32)
    scaled = upstream * gain
    grad_mapped = (
        inverse
        * (
            scaled
            - jnp.mean(scaled, axis=1, keepdims=True)
            - normed * jnp.mean(scaled * normed, axis=1, keepdims=True)
        )
    ).astype(BF16)
    grad_pre = (dot(grad_mapped, w_out, NT) * slope).astype(BF16)
    grad_in = (upstream + dot(grad_pre, w_in, NT)).astype(BF16)
    term_gain = jnp.sum(upstream * normed, axis=0, keepdims=True)
    term_in = dot(latent, grad_pre, TN)
    term_out = dot(hidden, grad_mapped, TN)
    for block in range(count // SPAN):
        at = block * SPAN
        table_ref[:, at : at + LANES] = grad_in[at : at + SPAN]
        for half in range(SPAN // LANES):
            at = block * SPAN + half * LANES
            pair = weights_ref[:, at : at + LANES].astype(F32)
            square = jnp.concatenate([pair, jnp.zeros((LANES - 2, LANES), F32)], axis=0)
            table_ref[
                half * LANES : (half + 1) * LANES, block * SPAN + LANES : (block + 1) * SPAN
            ] = square.T.astype(BF16)
    gain_high, gain_low = two_parts(term_gain)
    gain_rows = jnp.concatenate([gain_high.astype(F32), gain_low.astype(F32)], axis=0)
    terms = jnp.concatenate([term_in, term_out], axis=0)
    per_step = 256 // LANES
    for first in range(0, rows_ref.shape[0], per_step):
        cols = index_columns(rows_ref, first, per_step)
        sent, weight = gather_rows(place_hot(cols), cols // SPAN, table_ref, SPAN)
        for part in range(per_step * LANES // capacity):
            peer = first * LANES // capacity + part
            rows = slice(part * capacity, (part + 1) * capacity)
            sent_ref[peer, 0:capacity, :] = sent[rows].astype(BF16)
            square = weight[rows]
            if capacity < LANES:
                square = jnp.concatenate(
                    [square, jnp.zeros((LANES - capacity, LANES), F32)], axis=0
                )
            extra = jnp.concatenate(
                [square.T[0:2], gain_rows, jnp.zeros((EXTRA - 4, LANES), F32)], axis=0
            )
            sent_ref[peer, capacity : capacity + EXTRA, :] = extra.astype(BF16)
            first_row = (peer % 2 * (peers // 2) + peer // 2) * chunk
            share = terms[first_row : first_row + chunk]
            if chunk < EXTRA:
                share = jnp.concatenate([share, jnp.zeros((EXTRA - chunk, LANES), F32)], axis=0)
            sent_ref[peer, capacity + EXTRA :, :] = share.astype(BF16)


def order_edges(recv_ref, off_ref, ordered, stats_vmem, fine_count):
    rows = recv_ref.shape[0]
    shift = (fine_count // LANES).bit_length() - 1
    lane = lax.broadcasted_iota(jnp.int32, (LANES, LANES), 1)
    sub = lax.broadcasted_iota(jnp.int32, (LANES, LANES), 0)
    level = small(sub)
    one, zero = jnp.ones((), BF16), jnp.zeros((), BF16)

    def hot(row):
        return jnp.where(level == small(row), one, zero)

    number = jnp.zeros((LANES, LANES), BF16)
    for row in range(rows):
        number += hot(recv_ref[row : row + 1, :] >> shift)
    ones = jnp.ones((LANES, LANES), BF16)
    total = dot(number, ones)
    high = jnp.floor(total * (1.0 / 64.0))
    low = total - 64.0 * high
    before = jnp.where(lane < sub, 1.0, 0.0).astype(BF16)
    start = 64.0 * dot(before, high.astype(BF16)) + dot(before, low.astype(BF16))
    after = jnp.where(sub < lane, 1.0, 0.0).astype(BF16)
    prefix = jnp.concatenate([after, ones], axis=1)
    positions = []
    filled = start
    for row in range(rows):
        bucket = recv_ref[row : row + 1, :] >> shift
        found = dot(hot(bucket), prefix)
        mine = jnp.where(sub == bucket, found[:, 0:LANES] + filled, 0.0)
        positions.append(jnp.sum(mine, axis=0, keepdims=True).astype(jnp.int32))
        filled = filled + found[:, LANES:]
    moved = jnp.zeros((192, LANES), F32)
    for part in range(0, rows, 4):
        left, right = [], []
        for row in range(part, part + 4):
            position = positions[row]
            recv = recv_ref[row : row + 1, :]
            off = off_ref[row : row + 1, :] + HB
            rest = ((recv >> 8) << 2) | (off >> 8)
            here = level[0:64] == small(position >> 7)
            values = [small(value) for value in (recv & 255, off & 255, rest)]
            left.append(jnp.concatenate([jnp.where(here, v, zero) for v in values], axis=0))
            right.append(hot(position & 127))
        moved += dot(jnp.concatenate(left, axis=1), jnp.concatenate(right, axis=1), NT)
    moved = moved.astype(jnp.int32)
    rest = moved[LANES : LANES + rows]
    recv = moved[0:rows] + ((rest >> 2) << 8)
    send = recv + moved[64 : 64 + rows] + ((rest & 3) << 8)
    ordered[0] = recv
    ordered[1] = send
    lane = lax.broadcasted_iota(jnp.int32, (rows, LANES), 1)
    recv, send = recv.astype(F32), send.astype(F32)
    stats = jnp.where(
        lane < 2,
        jnp.where(
            lane == 0,
            jnp.min(recv, axis=1, keepdims=True),
            jnp.max(recv, axis=1, keepdims=True),
        ),
        jnp.where(
            lane == 2,
            jnp.min(send, axis=1, keepdims=True),
            jnp.max(send, axis=1, keepdims=True),
        ),
    )
    stats_vmem[...] = stats.astype(jnp.int32)


def tile_bases(stats, tile, fine_count):
    count = TILE // LANES
    rows = [tile * count + i for i in range(count)]

    def extreme(pick, at):
        value = stats[rows[0], at]
        for row in rows[1:]:
            value = pick(value, stats[row, at])
        return value

    recv_base = jnp.minimum((extreme(jnp.minimum, 0) >> 4) << 4, fine_count - SPAN)
    send_base = jnp.minimum(
        (extreme(jnp.minimum, 2) >> 4) << 4, fine_count + 2 * HB - SENDERS * SPAN
    )
    fits = (extreme(jnp.maximum, 1) - recv_base < SPAN) & (
        extreme(jnp.maximum, 3) - send_base < SENDERS * SPAN
    )
    return recv_base, send_base, fits


def each_group(step, stats, fine_count, near, far):
    tiles = [step * GROUP + i for i in range(GROUP)]
    places = [tile_bases(stats, tile, fine_count) for tile in tiles]
    fits = functools.reduce(jnp.logical_and, [place[2] for place in places])

    @pl.when(fits)
    def _():
        near(tiles, [place[:2] for place in places])

    @pl.when(jnp.logical_not(fits))
    def _():
        def one(i, carry):
            far(step * GROUP + i)
            return carry

        lax.fori_loop(0, GROUP, one, 0)


def block_rows(base, block):
    return pl.ds(pl.multiple_of(base + block * SPAN, 16), SPAN)


def gather_blocks(hot, block, table, base, blocks):
    found = None
    for start in range(0, blocks, 2):
        some = range(start, min(start + 2, blocks))
        part = dot(hot, jnp.concatenate([table[block_rows(base, j), :] for j in some], axis=1))
        for i, j in enumerate(some):
            one = part[:, i * LANES : (i + 1) * LANES]
            found = one if found is None else jnp.where(block == j, one, found)
    return found


def tile_rows(tile):
    return pl.ds(pl.multiple_of(tile * TILE, TILE), TILE)


def order_kernel(
    recv_hbm,
    off_hbm,
    slots_hbm,
    ordered,
    stats_ref,
    slot_hot,
    slot_block,
    recv_ref,
    off_ref,
    slots_ref,
    arrivals,
    fine_count,
):
    for copy in fetch(
        (recv_hbm, off_hbm, slots_hbm), (recv_ref, off_ref, slots_ref), arrivals
    ):
        copy.wait()
    order_edges(recv_ref, off_ref, ordered, stats_ref, fine_count)
    slots = index_columns(slots_ref, 0, slots_ref.shape[0])
    slot_hot[...] = place_hot(slots)
    slot_block[...] = slots // SPAN


def slope_kernel(
    stats,
    ordered_hbm,
    fine_hbm,
    weight_hbm,
    first_hbm,
    second_hbm,
    slope_hbm,
    hot_hbm,
    block_hbm,
    window_hbm,
    slope_sum,
    ordered,
    window,
    weight_ref,
    halos,
    slope_ref,
    hot_ref,
    block_ref,
    arrivals,
    leaving,
    window_left,
):
    fine_count = fine_hbm.shape[0]
    copies = fetch(
        (ordered_hbm, fine_hbm, weight_hbm, first_hbm, second_hbm),
        (ordered, window.at[pl.ds(HB, fine_count)], weight_ref, halos.at[0], halos.at[1]),
        arrivals,
    )
    slope_sum[...] = jnp.zeros(slope_sum.shape, F32)
    for copy in copies:
        copy.wait()
    odd = lax.axis_index("curve") & 1
    window[0:HB, :] = halos[1 - odd]
    window[HB + fine_count :, :] = halos[odd]
    window_copy = pltpu.make_async_copy(window, window_hbm, window_left)
    window_copy.start()
    count = TILE // LANES
    weight = weight_ref[...]
    level = levels()

    def leave(tile):
        rows = tile_rows(tile)
        pairs = ((slope_ref, slope_hbm), (hot_ref, hot_hbm), (block_ref, block_hbm))
        return [
            pltpu.make_async_copy(source.at[rows], target.at[rows], leaving.at[i, tile])
            for i, (source, target) in enumerate(pairs)
        ]

    def near(tiles, places):
        work = []
        for tile, (recv_base, send_base) in zip(tiles, places):
            recv = index_columns(ordered.at[0], tile * count, count) - recv_base
            send = index_columns(ordered.at[1], tile * count, count) - send_base
            block = send >> 8
            hot = place_hot(recv)
            hot_ref[tile_rows(tile), :] = hot
            block_ref[tile_rows(tile), :] = small(block)
            sender = gather_blocks(place_hot(send), block, window, send_base, SENDERS)
            receiver = gather_blocks(hot, None, window, recv_base + HB, 1)
            work.append((sender, receiver))
        slopes = []
        for tile, (sender, receiver) in zip(tiles, work):
            inputs = jnp.concatenate([sender.astype(BF16), receiver.astype(BF16)], axis=1)
            slope = silu_slope(dot(inputs, weight))
            slope_ref[tile_rows(tile), :] = slope
            slopes.append(jnp.concatenate(two_parts(slope), axis=1))
        sums = []
        for tile, (recv_base, _), slope in zip(tiles, places, slopes):
            hot = place_hot_rows(ordered, 0, tile, recv_base, level)
            both = dot(hot, slope)
            sums.append(both[:, 0:LANES] + both[:, LANES:])
        for (recv_base, _), part in zip(places, sums):
            add_parts(slope_sum, recv_base, [part])

    def far(tile):
        recv = index_columns(ordered.at[0], tile * count, count)
        send = index_columns(ordered.at[1], tile * count, count)
        blocks = fine_count // SPAN
        sender = gather_blocks(place_hot(send), send >> 8, window, 0, blocks + 2)
        receiver = gather_blocks(place_hot(recv), recv >> 8, window, HB, blocks)
        inputs = jnp.concatenate([sender.astype(BF16), receiver.astype(BF16)], axis=1)
        slope = silu_slope(dot(inputs, weight))
        slope_ref[tile_rows(tile), :] = slope
        hot = place_hot_rows(ordered, 0, tile, 0, level)
        for part in two_parts(slope):
            add_parts(slope_sum, 0, spread_rows(hot, small(recv >> 8), blocks, part))
        hot_ref[tile_rows(tile), :] = jnp.zeros((TILE, SPAN), BF16)
        block_ref[tile_rows(tile), :] = jnp.zeros((TILE, LANES), BF16)

    def step(index, carry):
        each_group(index, stats, fine_count, near, far)
        for i in range(GROUP):
            for copy in leave(index * GROUP + i):
                copy.start()
        return carry

    tiles = slope_ref.shape[0] // TILE
    lax.fori_loop(0, tiles // GROUP, step, 0)
    window_copy.wait()
    for tile in range(tiles):
        for copy in leave(tile):
            copy.wait()


def edge_kernel(
    coarse_scale,
    stats,
    arrived_hbm,
    slot_hot_hbm,
    slot_block_hbm,
    hot_hbm,
    slope_hbm,
    block_hbm,
    ordered_hbm,
    window_hbm,
    slope_sum_hbm,
    weight_hbm,
    grad_table,
    send_sum,
    first_ref,
    second_ref,
    keep_ref,
    gain_ref,
    slot_table,
    grad_rows,
    arrived_ref,
    slot_hot,
    slot_block,
    hot_ref,
    slope_ref,
    block_ref,
    ordered,
    window,
    slope_sum,
    weight_ref,
    arrivals,
):
    fine_count = grad_table.shape[0]
    copies = fetch(
        (
            arrived_hbm,
            slot_hot_hbm,
            slot_block_hbm,
            hot_hbm,
            slope_hbm,
            block_hbm,
            ordered_hbm,
            window_hbm,
            slope_sum_hbm,
            weight_hbm,
        ),
        (
            arrived_ref,
            slot_hot,
            slot_block,
            hot_ref,
            slope_ref,
            block_ref,
            ordered,
            window,
            slope_sum,
            weight_ref,
        ),
        arrivals,
    )
    send_sum[...] = jnp.zeros(send_sum.shape, F32)
    peers = arrived_ref.shape[0]
    share = max(EXTRA, SPAN // peers)
    capacity = arrived_ref.shape[1] - EXTRA - share
    per_block = SPAN // capacity
    for copy in copies[:3]:
        copy.wait()
    coarse = jnp.zeros((share, LANES), F32)
    gain = jnp.zeros((1, LANES), F32)
    for peer in range(peers):
        block, part = divmod(peer, per_block)
        rows = slice(part * capacity, (part + 1) * capacity)
        slot_table[rows, block * SPAN : block * SPAN + LANES] = arrived_ref[peer, 0:capacity, :]
        extra = arrived_ref[peer, capacity : capacity + EXTRA, :].astype(F32)
        square = jnp.concatenate([extra, jnp.zeros((LANES - EXTRA, LANES), F32)], axis=0).T
        slot_table[rows, block * SPAN + LANES : (block + 1) * SPAN] = square[0:capacity].astype(
            BF16
        )
        gain += extra[2:3] + extra[3:4]
        coarse += arrived_ref[peer, capacity + EXTRA :, :].astype(F32)
    keep_ref[LANES:, :] = coarse
    gain_ref[...] = gain * coarse_scale

    found = []
    for first in range(0, slot_hot.shape[0], SPAN):
        at = slice(first, first + SPAN)
        found.append(gather_rows(slot_hot[at, :], slot_block[at, :], slot_table, SPAN))
    for i, (grad, weight) in enumerate(found):
        first = i * SPAN
        for r in range(2):
            rows = (grad * weight[:, r : r + 1]).astype(BF16).astype(F32)
            grad_rows[pl.ds(2 * first + r, SPAN, stride=2), :] = rows
    grad_table[...] = grad_rows[...].astype(BF16)
    for copy in copies[3:]:
        copy.wait()

    count = TILE // LANES
    level = levels()

    def near(tiles, places):
        work = []
        for tile, (recv_base, _) in zip(tiles, places):
            rows = tile_rows(tile)
            upstream = gather_blocks(hot_ref[rows, :], None, grad_table, recv_base, 1)
            work.append((upstream * slope_ref[rows, :]).astype(BF16))
        sums = []
        for tile, (_, send_base), values in zip(tiles, places, work):
            hot = place_hot_rows(ordered, 1, tile, send_base, level)
            sums.append(spread_rows(hot, block_ref[tile_rows(tile), :], SENDERS, values))
        for (_, send_base), parts in zip(places, sums):
            add_parts(send_sum, send_base, parts)

    def far(tile):
        rows = tile_rows(tile)
        recv = index_columns(ordered.at[0], tile * count, count)
        send = index_columns(ordered.at[1], tile * count, count)
        blocks = fine_count // SPAN
        upstream = gather_blocks(place_hot(recv), recv >> 8, grad_table, 0, blocks)
        values = (upstream * slope_ref[rows, :]).astype(BF16)
        hot = place_hot_rows(ordered, 1, tile, 0, level)
        add_parts(send_sum, 0, spread_rows(hot, small(send >> 8), blocks + 2, values))

    def step(index, carry):
        each_group(index, stats, fine_count, near, far)
        return carry

    lax.fori_loop(0, slope_ref.shape[0] // TILE // GROUP, step, 0)

    weight_send = weight_ref[0:LANES, :]
    odd = lax.axis_index("curve") & 1
    to_prev = back(send_sum[0:HB, :], weight_send)
    to_next = back(send_sum[HB + fine_count :, :], weight_send)
    first_ref[LANES:, :] = jnp.where(odd == 0, to_next, to_prev).astype(BF16)
    second_ref[...] = jnp.where(odd == 0, to_prev, to_next).astype(BF16)
    term_send = jnp.zeros((LANES, LANES), F32)
    term_recv = jnp.zeros((LANES, LANES), F32)
    for first in range(0, fine_count + 2 * HB, SPAN):
        at = slice(first, first + SPAN)
        term_send += outer(window[at, :], send_sum[at, :])
    for first in range(0, fine_count, SPAN):
        at = slice(first, first + SPAN)
        moved = slice(HB + first, HB + first + SPAN)
        term_recv += outer(window[moved, :], grad_rows[at, :] * slope_sum[at, :])
    keep_ref[0:LANES, :] = jnp.where(odd == 0, term_send, term_recv)
    first_ref[0:LANES, :] = jnp.where(odd == 0, term_recv, term_send).astype(BF16)


def fine_kernel(
    grad_hbm,
    send_sum_hbm,
    slope_sum_hbm,
    weight_hbm,
    first_hbm,
    second_hbm,
    fine_ref,
    grad_table,
    send_sum,
    slope_sum,
    weight_ref,
    first_ref,
    second_ref,
    arrivals,
):
    fine_count = fine_ref.shape[0]
    for copy in fetch(
        (grad_hbm, send_sum_hbm, slope_sum_hbm, weight_hbm, first_hbm, second_hbm),
        (grad_table, send_sum, slope_sum, weight_ref, first_ref, second_ref),
        arrivals,
    ):
        copy.wait()
    odd = lax.axis_index("curve") & 1
    one, two = first_ref[LANES:, :].astype(F32), second_ref[...].astype(F32)
    from_next, from_prev = jnp.where(odd == 0, one, two), jnp.where(odd == 0, two, one)
    for first in range(0, fine_count, SPAN):
        at = slice(first, first + SPAN)
        moved = slice(HB + first, HB + first + SPAN)
        grad = grad_table[at, :].astype(F32)
        summed = (
            grad
            + back(send_sum[moved, :], weight_ref[0:LANES, :])
            + back(grad * slope_sum[at, :], weight_ref[LANES:, :])
        )
        if first == 0:
            summed += from_prev
        if first == fine_count - SPAN:
            summed += from_next
        fine_ref[at, :] = summed.astype(BF16)


def last_kernel(
    edge_scale, coarse_scale, own_ref, coarse_ref, there_ref, edge_ref, in_ref, out_ref
):
    odd = lax.axis_index("curve") & 1
    own, coarse = own_ref[...], coarse_ref[...].astype(F32)
    other, other_coarse = there_ref[0:LANES, :], there_ref[LANES:, :]
    edge_ref[0:LANES, :] = jnp.where(odd == 0, own, other) * edge_scale
    edge_ref[LANES:, :] = jnp.where(odd == 0, other, own) * edge_scale
    in_ref[...] = jnp.where(odd == 0, coarse, other_coarse) * coarse_scale
    out_ref[...] = jnp.where(odd == 0, other_coarse, coarse) * coarse_scale


def pair_exchange(first, second, peers):
    pairs = [(i, i ^ 1) for i in range(peers)]
    between = [(i, ((i + 1) ^ 1) - 1) for i in range(1, peers - 1)]
    return lax.ppermute(first, "curve", pairs), lax.ppermute(second, "curve", between)


def swapped(values, hops, peers):
    return lax.ppermute(values, "curve", [(i, i ^ hops) for i in range(peers)])


def from_same_core(sent, peers):
    count = peers // 2
    return lax.all_to_all(
        jnp.broadcast_to(sent[None], (count,) + sent.shape),
        "curve",
        split_axis=0,
        concat_axis=0,
        axis_index_groups=[list(range(core, peers, 2)) for core in range(2)],
        tiled=True,
    )


def per_device(
    fine_latent,
    coarse_latent,
    grad_coarse,
    restrict_weights,
    send_rows,
    pair_slots,
    edge_receivers,
    edge_offsets,
    edge_weight,
    node_weight_in,
    node_weight_out,
    node_gain,
):
    peers = lax.axis_size("curve")
    device = lax.axis_index("curve")
    even = (device & 1) == 0
    coarse_count = coarse_latent.shape[0]
    fine_count = fine_latent.shape[0]
    edge_count = edge_receivers.shape[0]
    capacity = send_rows.shape[0] // peers
    chunk = SPAN // peers
    share = max(EXTRA, chunk)
    payload = capacity + EXTRA + share
    edge_rows = edge_count // LANES
    window_count = fine_count + 2 * HB
    params = pltpu.CompilerParams(vmem_limit_bytes=64 * 1024 * 1024 - 256 * 1024)
    roomy = pltpu.CompilerParams(vmem_limit_bytes=64 * 1024 * 1024 - 1536 * 1024)
    anywhere = pl.BlockSpec(memory_space=pl.ANY)

    scalar = pl.BlockSpec(memory_space=pltpu.SMEM)

    head, end = fine_latent[:HB], fine_latent[fine_count - HB :]
    halos = pair_exchange(jnp.where(even, end, head), jnp.where(even, head, end), peers)

    sent = pl.pallas_call(
        functools.partial(coarse_kernel, peers),
        out_shape=jax.ShapeDtypeStruct((peers, payload, LANES), BF16),
        in_specs=[anywhere] * 7,
        scratch_shapes=[
            pltpu.VMEM((SPAN, coarse_count), BF16),
            pltpu.VMEM((coarse_count, LANES), BF16),
            pltpu.VMEM((coarse_count, LANES), BF16),
            pltpu.VMEM((2, coarse_count), BF16),
            pltpu.VMEM((peers * capacity // LANES, LANES), jnp.int32),
            pltpu.VMEM((LANES, LANES), BF16),
            pltpu.VMEM((LANES, LANES), BF16),
            pltpu.VMEM((1, LANES), F32),
            pltpu.SemaphoreType.DMA((7,)),
        ],
        compiler_params=params,
        cost_estimate=pl.CostEstimate(
            flops=2_000_000_000, bytes_accessed=2_000_000, transcendentals=400_000
        ),
        name="coarse_block",
    )(
        coarse_latent,
        grad_coarse,
        restrict_weights,
        send_rows.reshape(-1, LANES),
        node_weight_in,
        node_weight_out,
        node_gain.reshape(1, LANES),
    )
    sent, receivers, offsets, slots = lax.optimization_barrier(
        (sent, edge_receivers, edge_offsets, pair_slots)
    )
    arrived = lax.all_to_all(sent, "curve", split_axis=0, concat_axis=0, tiled=True)

    pair_count = fine_count // 2
    in_vmem = pl.BlockSpec(memory_space=pltpu.VMEM)
    ordered, stats, slot_hot, slot_block = pl.pallas_call(
        functools.partial(order_kernel, fine_count=fine_count),
        out_shape=(
            jax.ShapeDtypeStruct((2, edge_rows, LANES), jnp.int32),
            jax.ShapeDtypeStruct((edge_rows, LANES), jnp.int32),
            jax.ShapeDtypeStruct((pair_count, SPAN), BF16),
            jax.ShapeDtypeStruct((pair_count, LANES), jnp.int32),
        ),
        in_specs=[anywhere] * 3,
        scratch_shapes=[
            pltpu.VMEM((edge_rows, LANES), jnp.int32),
            pltpu.VMEM((edge_rows, LANES), jnp.int32),
            pltpu.VMEM((pair_count // LANES, LANES), jnp.int32),
            pltpu.SemaphoreType.DMA((3,)),
        ],
        compiler_params=roomy,
        cost_estimate=pl.CostEstimate(
            flops=3_000_000_000, bytes_accessed=2_000_000, transcendentals=0
        ),
        name="edge_order",
    )(
        receivers.reshape(-1, LANES),
        offsets.reshape(-1, LANES),
        slots.reshape(-1, LANES),
    )
    slope, hot, block, window, slope_sum = pl.pallas_call(
        slope_kernel,
        out_shape=(
            jax.ShapeDtypeStruct((edge_count, LANES), F32),
            jax.ShapeDtypeStruct((edge_count, SPAN), BF16),
            jax.ShapeDtypeStruct((edge_count, LANES), BF16),
            jax.ShapeDtypeStruct((window_count, LANES), BF16),
            jax.ShapeDtypeStruct((fine_count, LANES), F32),
        ),
        in_specs=[scalar] + [anywhere] * 5,
        out_specs=[anywhere] * 4 + [in_vmem],
        scratch_shapes=[
            pltpu.VMEM((2, edge_rows, LANES), jnp.int32),
            pltpu.VMEM((window_count, LANES), BF16),
            pltpu.VMEM((2 * LANES, LANES), BF16),
            pltpu.VMEM((2, HB, LANES), BF16),
            pltpu.VMEM((edge_count, LANES), F32),
            pltpu.VMEM((edge_count, SPAN), BF16),
            pltpu.VMEM((edge_count, LANES), BF16),
            pltpu.SemaphoreType.DMA((5,)),
            pltpu.SemaphoreType.DMA((3, edge_count // TILE)),
            pltpu.SemaphoreType.DMA,
        ],
        compiler_params=roomy,
        cost_estimate=pl.CostEstimate(
            flops=13_000_000_000, bytes_accessed=9_000_000, transcendentals=800_000
        ),
        name="edge_slope",
    )(stats, ordered, fine_latent, edge_weight, *halos)

    coarse_scale = 1.0 / math.sqrt(coarse_count * peers)
    edge_scale = 1.0 / math.sqrt(edge_count * peers)
    grad_rows, send_sum, first, second, keep, term_gain = pl.pallas_call(
        functools.partial(edge_kernel, coarse_scale),
        out_shape=(
            jax.ShapeDtypeStruct((fine_count, LANES), BF16),
            jax.ShapeDtypeStruct((window_count, LANES), F32),
            pltpu.VMEM((LANES + HB, LANES), BF16),
            pltpu.VMEM((HB, LANES), BF16),
            pltpu.VMEM((LANES + share, LANES), F32),
            jax.ShapeDtypeStruct((1, LANES), F32),
        ),
        in_specs=[scalar] + [anywhere] * 10,
        scratch_shapes=[
            pltpu.VMEM((SPAN, peers * capacity), BF16),
            pltpu.VMEM((fine_count, LANES), F32),
            pltpu.VMEM((peers, payload, LANES), BF16),
            pltpu.VMEM((pair_count, SPAN), BF16),
            pltpu.VMEM((pair_count, LANES), jnp.int32),
            pltpu.VMEM((edge_count, SPAN), BF16),
            pltpu.VMEM((edge_count, LANES), F32),
            pltpu.VMEM((edge_count, LANES), BF16),
            pltpu.VMEM((2, edge_rows, LANES), jnp.int32),
            pltpu.VMEM((window_count, LANES), BF16),
            pltpu.VMEM((fine_count, LANES), F32),
            pltpu.VMEM((2 * LANES, LANES), BF16),
            pltpu.SemaphoreType.DMA((10,)),
        ],
        compiler_params=roomy,
        cost_estimate=pl.CostEstimate(
            flops=24_000_000_000, bytes_accessed=8_000_000, transcendentals=0
        ),
        name="edge_back",
    )(
        stats,
        arrived,
        slot_hot,
        slot_block,
        hot,
        slope,
        block,
        ordered,
        window,
        slope_sum,
        edge_weight,
    )
    one, two = pair_exchange(first, second, peers)
    sent = keep[: LANES + chunk] + jnp.pad(one[:LANES].astype(F32), ((0, chunk), (0, 0)))
    sent = sent.astype(BF16)
    grad_fine = pl.pallas_call(
        fine_kernel,
        out_shape=jax.ShapeDtypeStruct((fine_count, LANES), BF16),
        in_specs=[anywhere] * 6,
        scratch_shapes=[
            pltpu.VMEM((fine_count, LANES), BF16),
            pltpu.VMEM((window_count, LANES), F32),
            pltpu.VMEM((fine_count, LANES), F32),
            pltpu.VMEM((2 * LANES, LANES), BF16),
            pltpu.VMEM((LANES + HB, LANES), BF16),
            pltpu.VMEM((HB, LANES), BF16),
            pltpu.SemaphoreType.DMA((6,)),
        ],
        compiler_params=roomy,
        cost_estimate=pl.CostEstimate(
            flops=1_000_000_000, bytes_accessed=4_000_000, transcendentals=0
        ),
        name="fine_sums",
    )(grad_rows, send_sum, slope_sum, edge_weight, one, two)
    parts, grad_fine = lax.optimization_barrier((from_same_core(sent, peers), grad_fine))
    own = jnp.sum(parts[:, :LANES].astype(F32), axis=0)
    coarse = parts[:, LANES:].reshape(LANES, LANES)
    there = swapped(jnp.concatenate([own, coarse.astype(F32)], axis=0), 1, peers)
    edge_terms, term_in, term_out = pl.pallas_call(
        functools.partial(last_kernel, edge_scale, coarse_scale),
        out_shape=(
            jax.ShapeDtypeStruct((2 * LANES, LANES), F32),
            jax.ShapeDtypeStruct((LANES, LANES), F32),
            jax.ShapeDtypeStruct((LANES, LANES), F32),
        ),
        compiler_params=pltpu.CompilerParams(vmem_limit_bytes=4 * 1024 * 1024),
        name="last_terms",
    )(own, coarse, there)
    return grad_fine, edge_terms, term_in, term_out, term_gain.reshape(LANES)


def solution(mesh):
    placed = (
        P(("groups", "curve"), None),
        P(("groups", "curve"), None),
        P(("groups", "curve"), None),
        P(None, ("groups", "curve")),
        P(("groups", "curve")),
        P(("groups", "curve")),
        P(("groups", "curve")),
        P(("groups", "curve")),
        P(),
        P(),
        P(),
        P(),
    )
    return jax.shard_map(
        per_device,
        mesh=mesh,
        in_specs=placed,
        out_specs=(
            P(("groups", "curve"), None),
            P("groups", None),
            P("groups", None),
            P("groups", None),
            P("groups"),
        ),
        check_vma=False,
    )
```

```python
import functools
import math

import jax
import jax.numpy as jnp
from jax import lax
from jax.experimental import pallas as pl
from jax.experimental.pallas import tpu as pltpu
from jax.sharding import PartitionSpec as P

HB = 256
LANES = 128
SPAN = 256
EXTRA = 16
TILE = 512
GROUP = 4
SENDERS = 3

F32 = jnp.float32
BF16 = jnp.bfloat16
NT = (((1,), (1,)), ((), ()))
TN = (((0,), (0,)), ((), ()))


def dot(left, right, dims=(((1,), (0,)), ((), ()))):
    return lax.dot_general(left, right, dims, preferred_element_type=F32)


def silu_slope(values):
    sigm = jax.nn.sigmoid(values)
    return sigm * (1.0 + values * (1.0 - sigm))


def columns(row):
    return jnp.broadcast_to(row, (LANES, LANES)).T


def index_columns(ref, first, count):
    return jnp.concatenate([columns(ref[pl.ds(first + i, 1), :]) for i in range(count)], axis=0)


def small(values):
    return values.astype(F32).astype(BF16)


def place_hot(cols):
    place = small(cols & (SPAN - 1))
    lane = lax.broadcasted_iota(jnp.int32, place.shape, 1)
    one, zero = jnp.ones((), BF16), jnp.zeros((), BF16)
    return jnp.concatenate(
        [jnp.where(place == small(lane + start), one, zero) for start in range(0, SPAN, LANES)],
        axis=1,
    )


def gather_rows(hot, block, table, width):
    total = table.shape[1]
    step = max(width, 2 * LANES)
    found = [jnp.zeros(block.shape, F32) for _ in range(width // LANES)]
    for start in range(0, total, step):
        part = dot(hot, table[:, start : start + step])
        for inner in range(0, step, width):
            here = block == (start + inner) // width
            for i in range(len(found)):
                at = inner + i * LANES
                found[i] = jnp.where(here, part[:, at : at + LANES], found[i])
    return found


def spread_rows(hot, block, blocks, values):
    if blocks == 1:
        return [dot(hot, values)]
    parts = []
    zero = jnp.zeros((), BF16)
    for start in range(0, blocks, 2):
        some = range(start, min(start + 2, blocks))
        spread = [jnp.where(block == jnp.full((), j, BF16), values, zero) for j in some]
        part = dot(hot, jnp.concatenate(spread, axis=1))
        parts += [part[:, i * LANES : (i + 1) * LANES] for i in range(len(some))]
    return parts


def add_parts(total, base, parts):
    for j, part in enumerate(parts):
        total[block_rows(base, j), :] += part


def place_hot_rows(ordered, at, tile, base, level):
    one, zero = jnp.ones((), BF16), jnp.zeros((), BF16)
    hot = []
    for i in range(TILE // LANES):
        row = ordered[at, pl.ds(tile * (TILE // LANES) + i, 1), :] - base
        hot.append(jnp.where(level == small(row & (SPAN - 1)), one, zero))
    return jnp.concatenate(hot, axis=1)


def levels():
    return small(lax.broadcasted_iota(jnp.int32, (SPAN, LANES), 0))


def two_parts(values):
    high = values.astype(BF16)
    return high, (values - high.astype(F32)).astype(BF16)


def back(values, weight):
    high, low = two_parts(values)
    return dot(high, weight, NT) + dot(low, weight, NT)


def outer(rows, values):
    high, low = two_parts(values)
    both = dot(rows, jnp.concatenate([high, low], axis=1), TN)
    return both[:, 0:LANES] + both[:, LANES:]


def fetch(sources, targets, arrivals):
    copies = [
        pltpu.make_async_copy(source, target, arrivals.at[i])
        for i, (source, target) in enumerate(zip(sources, targets))
    ]
    for copy in copies:
        copy.start()
    return copies


def coarse_kernel(
    peers,
    latent_ref,
    grad_ref,
    weights_ref,
    rows_ref,
    w_in_ref,
    w_out_ref,
    gain_ref,
    sent_ref,
    table_ref,
    *held,
):
    *held, arrivals = held
    sources = (latent_ref, grad_ref, weights_ref, rows_ref, w_in_ref, w_out_ref, gain_ref)
    copies = fetch(sources, held, arrivals)
    for copy in copies:
        copy.wait()
    latent_ref, grad_ref, weights_ref, rows_ref, w_in_ref, w_out_ref, gain_ref = held
    count = latent_ref.shape[0]
    chunk = SPAN // peers
    capacity = sent_ref.shape[1] - EXTRA - max(EXTRA, chunk)
    w_in, w_out, gain = w_in_ref[...], w_out_ref[...], gain_ref[...]
    latent = latent_ref[...]
    pre = dot(latent, w_in)
    sigm = jax.nn.sigmoid(pre)
    hidden = (pre * sigm).astype(BF16)
    slope = sigm * (1.0 + pre * (1.0 - sigm))
    mapped = dot(hidden, w_out)
    centred = mapped - jnp.mean(mapped, axis=1, keepdims=True)
    inverse = lax.rsqrt(jnp.mean(centred * centred, axis=1, keepdims=True) + 1e-05)
    normed = centred * inverse
    upstream = grad_ref[...].astype(F32)
    scaled = upstream * gain
    grad_mapped = (
        inverse
        * (
            scaled
            - jnp.mean(scaled, axis=1, keepdims=True)
            - normed * jnp.mean(scaled * normed, axis=1, keepdims=True)
        )
    ).astype(BF16)
    grad_pre = (dot(grad_mapped, w_out, NT) * slope).astype(BF16)
    grad_in = (upstream + dot(grad_pre, w_in, NT)).astype(BF16)
    term_gain = jnp.sum(upstream * normed, axis=0, keepdims=True)
    term_in = dot(latent, grad_pre, TN)
    term_out = dot(hidden, grad_mapped, TN)
    for block in range(count // SPAN):
        at = block * SPAN
        table_ref[:, at : at + LANES] = grad_in[at : at + SPAN]
        for half in range(SPAN // LANES):
            at = block * SPAN + half * LANES
            pair = weights_ref[:, at : at + LANES].astype(F32)
            square = jnp.concatenate([pair, jnp.zeros((LANES - 2, LANES), F32)], axis=0)
            table_ref[
                half * LANES : (half + 1) * LANES, block * SPAN + LANES : (block + 1) * SPAN
            ] = square.T.astype(BF16)
    gain_high, gain_low = two_parts(term_gain)
    gain_rows = jnp.concatenate([gain_high.astype(F32), gain_low.astype(F32)], axis=0)
    terms = jnp.concatenate([term_in, term_out], axis=0)
    per_step = 256 // LANES
    for first in range(0, rows_ref.shape[0], per_step):
        cols = index_columns(rows_ref, first, per_step)
        sent, weight = gather_rows(place_hot(cols), cols // SPAN, table_ref, SPAN)
        for part in range(per_step * LANES // capacity):
            peer = first * LANES // capacity + part
            rows = slice(part * capacity, (part + 1) * capacity)
            sent_ref[peer, 0:capacity, :] = sent[rows].astype(BF16)
            square = weight[rows]
            if capacity < LANES:
                square = jnp.concatenate(
                    [square, jnp.zeros((LANES - capacity, LANES), F32)], axis=0
                )
            extra = jnp.concatenate(
                [square.T[0:2], gain_rows, jnp.zeros((EXTRA - 4, LANES), F32)], axis=0
            )
            sent_ref[peer, capacity : capacity + EXTRA, :] = extra.astype(BF16)
            first_row = (peer % 2 * (peers // 2) + peer // 2) * chunk
            share = terms[first_row : first_row + chunk]
            if chunk < EXTRA:
                share = jnp.concatenate([share, jnp.zeros((EXTRA - chunk, LANES), F32)], axis=0)
            sent_ref[peer, capacity + EXTRA :, :] = share.astype(BF16)


def order_edges(recv_ref, off_ref, ordered, stats_vmem, fine_count):
    rows = recv_ref.shape[0]
    shift = (fine_count // LANES).bit_length() - 1
    lane = lax.broadcasted_iota(jnp.int32, (LANES, LANES), 1)
    sub = lax.broadcasted_iota(jnp.int32, (LANES, LANES), 0)
    level = small(sub)
    one, zero = jnp.ones((), BF16), jnp.zeros((), BF16)

    def hot(row):
        return jnp.where(level == small(row), one, zero)

    number = jnp.zeros((LANES, LANES), BF16)
    for row in range(rows):
        number += hot(recv_ref[row : row + 1, :] >> shift)
    ones = jnp.ones((LANES, LANES), BF16)
    total = dot(number, ones)
    high = jnp.floor(total * (1.0 / 64.0))
    low = total - 64.0 * high
    before = jnp.where(lane < sub, 1.0, 0.0).astype(BF16)
    start = 64.0 * dot(before, high.astype(BF16)) + dot(before, low.astype(BF16))
    after = jnp.where(sub < lane, 1.0, 0.0).astype(BF16)
    prefix = jnp.concatenate([after, ones], axis=1)
    positions = []
    filled = start
    for row in range(rows):
        bucket = recv_ref[row : row + 1, :] >> shift
        found = dot(hot(bucket), prefix)
        mine = jnp.where(sub == bucket, found[:, 0:LANES] + filled, 0.0)
        positions.append(jnp.sum(mine, axis=0, keepdims=True).astype(jnp.int32))
        filled = filled + found[:, LANES:]
    moved = jnp.zeros((192, LANES), F32)
    for part in range(0, rows, 4):
        left, right = [], []
        for row in range(part, part + 4):
            position = positions[row]
            recv = recv_ref[row : row + 1, :]
            off = off_ref[row : row + 1, :] + HB
            rest = ((recv >> 8) << 2) | (off >> 8)
            here = level[0:64] == small(position >> 7)
            values = [small(value) for value in (recv & 255, off & 255, rest)]
            left.append(jnp.concatenate([jnp.where(here, v, zero) for v in values], axis=0))
            right.append(hot(position & 127))
        moved += dot(jnp.concatenate(left, axis=1), jnp.concatenate(right, axis=1), NT)
    moved = moved.astype(jnp.int32)
    rest = moved[LANES : LANES + rows]
    recv = moved[0:rows] + ((rest >> 2) << 8)
    send = recv + moved[64 : 64 + rows] + ((rest & 3) << 8)
    ordered[0] = recv
    ordered[1] = send
    lane = lax.broadcasted_iota(jnp.int32, (rows, LANES), 1)
    recv, send = recv.astype(F32), send.astype(F32)
    stats = jnp.where(
        lane < 2,
        jnp.where(
            lane == 0,
            jnp.min(recv, axis=1, keepdims=True),
            jnp.max(recv, axis=1, keepdims=True),
        ),
        jnp.where(
            lane == 2,
            jnp.min(send, axis=1, keepdims=True),
            jnp.max(send, axis=1, keepdims=True),
        ),
    )
    stats_vmem[...] = stats.astype(jnp.int32)


def tile_bases(stats, tile, fine_count):
    count = TILE // LANES
    rows = [tile * count + i for i in range(count)]

    def extreme(pick, at):
        value = stats[rows[0], at]
        for row in rows[1:]:
            value = pick(value, stats[row, at])
        return value

    recv_base = jnp.minimum((extreme(jnp.minimum, 0) >> 4) << 4, fine_count - SPAN)
    send_base = jnp.minimum(
        (extreme(jnp.minimum, 2) >> 4) << 4, fine_count + 2 * HB - SENDERS * SPAN
    )
    fits = (extreme(jnp.maximum, 1) - recv_base < SPAN) & (
        extreme(jnp.maximum, 3) - send_base < SENDERS * SPAN
    )
    return recv_base, send_base, fits


def each_group(step, stats, fine_count, near, far):
    tiles = [step * GROUP + i for i in range(GROUP)]
    places = [tile_bases(stats, tile, fine_count) for tile in tiles]
    fits = functools.reduce(jnp.logical_and, [place[2] for place in places])

    @pl.when(fits)
    def _():
        near(tiles, [place[:2] for place in places])

    @pl.when(jnp.logical_not(fits))
    def _():
        def one(i, carry):
            far(step * GROUP + i)
            return carry

        lax.fori_loop(0, GROUP, one, 0)


def block_rows(base, block):
    return pl.ds(pl.multiple_of(base + block * SPAN, 16), SPAN)


def gather_blocks(hot, block, table, base, blocks):
    found = None
    for start in range(0, blocks, 2):
        some = range(start, min(start + 2, blocks))
        part = dot(hot, jnp.concatenate([table[block_rows(base, j), :] for j in some], axis=1))
        for i, j in enumerate(some):
            one = part[:, i * LANES : (i + 1) * LANES]
            found = one if found is None else jnp.where(block == j, one, found)
    return found


def tile_rows(tile):
    return pl.ds(pl.multiple_of(tile * TILE, TILE), TILE)


def slope_kernel(
    recv_hbm,
    off_hbm,
    slots_hbm,
    fine_hbm,
    weight_hbm,
    first_hbm,
    second_hbm,
    slope_hbm,
    hot_hbm,
    block_hbm,
    window_hbm,
    slope_sum,
    ordered,
    stats_vmem,
    slot_hot,
    slot_block,
    recv_ref,
    off_ref,
    slots_ref,
    window,
    weight_ref,
    halos,
    slope_ref,
    hot_ref,
    block_ref,
    stats,
    arrivals,
    stats_done,
    leaving,
    window_left,
):
    fine_count = fine_hbm.shape[0]
    copies = fetch(
        (recv_hbm, off_hbm, slots_hbm, fine_hbm, weight_hbm, first_hbm, second_hbm),
        (
            recv_ref,
            off_ref,
            slots_ref,
            window.at[pl.ds(HB, fine_count)],
            weight_ref,
            halos.at[0],
            halos.at[1],
        ),
        arrivals,
    )
    copies[0].wait()
    copies[1].wait()
    order_edges(recv_ref, off_ref, ordered, stats_vmem, fine_count)
    stats_copy = pltpu.make_async_copy(stats_vmem, stats, stats_done)
    stats_copy.start()
    for copy in copies[2:]:
        copy.wait()
    slope_sum[...] = jnp.zeros(slope_sum.shape, F32)
    slots = index_columns(slots_ref, 0, slots_ref.shape[0])
    slot_hot[...] = place_hot(slots)
    slot_block[...] = slots // SPAN
    odd = lax.axis_index("curve") & 1
    window[0:HB, :] = halos[1 - odd]
    window[HB + fine_count :, :] = halos[odd]
    window_copy = pltpu.make_async_copy(window, window_hbm, window_left)
    window_copy.start()
    stats_copy.wait()
    count = TILE // LANES
    weight = weight_ref[...]
    level = levels()

    def leave(tile):
        rows = tile_rows(tile)
        pairs = ((slope_ref, slope_hbm), (hot_ref, hot_hbm), (block_ref, block_hbm))
        return [
            pltpu.make_async_copy(source.at[rows], target.at[rows], leaving.at[i, tile])
            for i, (source, target) in enumerate(pairs)
        ]

    def near(tiles, places):
        work = []
        for tile, (recv_base, send_base) in zip(tiles, places):
            recv = index_columns(ordered.at[0], tile * count, count) - recv_base
            send = index_columns(ordered.at[1], tile * count, count) - send_base
            block = send >> 8
            hot = place_hot(recv)
            hot_ref[tile_rows(tile), :] = hot
            block_ref[tile_rows(tile), :] = small(block)
            sender = gather_blocks(place_hot(send), block, window, send_base, SENDERS)
            receiver = gather_blocks(hot, None, window, recv_base + HB, 1)
            work.append((sender, receiver))
        slopes = []
        for tile in tiles:
            for copy in leave(tile)[1:]:
                copy.start()
        for tile, (sender, receiver) in zip(tiles, work):
            inputs = jnp.concatenate([sender.astype(BF16), receiver.astype(BF16)], axis=1)
            slope = silu_slope(dot(inputs, weight))
            slope_ref[tile_rows(tile), :] = slope
            leave(tile)[0].start()
            slopes.append(jnp.concatenate(two_parts(slope), axis=1))
        sums = []
        for tile, (recv_base, _), slope in zip(tiles, places, slopes):
            hot = place_hot_rows(ordered, 0, tile, recv_base, level)
            both = dot(hot, slope)
            sums.append(both[:, 0:LANES] + both[:, LANES:])
        for (recv_base, _), part in zip(places, sums):
            add_parts(slope_sum, recv_base, [part])

    def far(tile):
        recv = index_columns(ordered.at[0], tile * count, count)
        send = index_columns(ordered.at[1], tile * count, count)
        blocks = fine_count // SPAN
        sender = gather_blocks(place_hot(send), send >> 8, window, 0, blocks + 2)
        receiver = gather_blocks(place_hot(recv), recv >> 8, window, HB, blocks)
        inputs = jnp.concatenate([sender.astype(BF16), receiver.astype(BF16)], axis=1)
        slope = silu_slope(dot(inputs, weight))
        slope_ref[tile_rows(tile), :] = slope
        hot = place_hot_rows(ordered, 0, tile, 0, level)
        for part in two_parts(slope):
            add_parts(slope_sum, 0, spread_rows(hot, small(recv >> 8), blocks, part))
        hot_ref[tile_rows(tile), :] = jnp.zeros((TILE, SPAN), BF16)
        block_ref[tile_rows(tile), :] = jnp.zeros((TILE, LANES), BF16)
        for copy in leave(tile):
            copy.start()

    def step(index, carry):
        each_group(index, stats, fine_count, near, far)
        return carry

    tiles = slope_ref.shape[0] // TILE
    lax.fori_loop(0, tiles // GROUP, step, 0)
    window_copy.wait()
    for tile in range(tiles):
        for copy in leave(tile):
            copy.wait()


def edge_kernel(
    coarse_scale,
    stats,
    arrived_hbm,
    slot_hot_hbm,
    slot_block_hbm,
    hot_hbm,
    slope_hbm,
    block_hbm,
    ordered_hbm,
    window_hbm,
    slope_sum_hbm,
    weight_hbm,
    grad_table,
    send_sum,
    first_ref,
    second_ref,
    keep_ref,
    gain_ref,
    slot_table,
    grad_rows,
    arrived_ref,
    slot_hot,
    slot_block,
    hot_ref,
    slope_ref,
    block_ref,
    ordered,
    window,
    slope_sum,
    weight_ref,
    arrivals,
):
    fine_count = grad_table.shape[0]
    copies = fetch(
        (
            arrived_hbm,
            slot_hot_hbm,
            slot_block_hbm,
            hot_hbm,
            slope_hbm,
            block_hbm,
            ordered_hbm,
            window_hbm,
            slope_sum_hbm,
            weight_hbm,
        ),
        (
            arrived_ref,
            slot_hot,
            slot_block,
            hot_ref,
            slope_ref,
            block_ref,
            ordered,
            window,
            slope_sum,
            weight_ref,
        ),
        arrivals,
    )
    send_sum[...] = jnp.zeros(send_sum.shape, F32)
    peers = arrived_ref.shape[0]
    share = max(EXTRA, SPAN // peers)
    capacity = arrived_ref.shape[1] - EXTRA - share
    per_block = SPAN // capacity
    for copy in copies[:3]:
        copy.wait()
    coarse = jnp.zeros((share, LANES), F32)
    gain = jnp.zeros((1, LANES), F32)
    for peer in range(peers):
        block, part = divmod(peer, per_block)
        rows = slice(part * capacity, (part + 1) * capacity)
        slot_table[rows, block * SPAN : block * SPAN + LANES] = arrived_ref[peer, 0:capacity, :]
        extra = arrived_ref[peer, capacity : capacity + EXTRA, :].astype(F32)
        square = jnp.concatenate([extra, jnp.zeros((LANES - EXTRA, LANES), F32)], axis=0).T
        slot_table[rows, block * SPAN + LANES : (block + 1) * SPAN] = square[0:capacity].astype(
            BF16
        )
        gain += extra[2:3] + extra[3:4]
        coarse += arrived_ref[peer, capacity + EXTRA :, :].astype(F32)
    keep_ref[LANES:, :] = coarse
    gain_ref[...] = gain * coarse_scale

    found = []
    for first in range(0, slot_hot.shape[0], SPAN):
        at = slice(first, first + SPAN)
        found.append(gather_rows(slot_hot[at, :], slot_block[at, :], slot_table, SPAN))
    for i, (grad, weight) in enumerate(found):
        first = i * SPAN
        for r in range(2):
            rows = (grad * weight[:, r : r + 1]).astype(BF16).astype(F32)
            grad_rows[pl.ds(2 * first + r, SPAN, stride=2), :] = rows
    grad_table[...] = grad_rows[...].astype(BF16)
    for copy in copies[3:]:
        copy.wait()

    count = TILE // LANES
    level = levels()

    def near(tiles, places):
        work = []
        for tile, (recv_base, _) in zip(tiles, places):
            rows = tile_rows(tile)
            upstream = gather_blocks(hot_ref[rows, :], None, grad_table, recv_base, 1)
            work.append((upstream * slope_ref[rows, :]).astype(BF16))
        sums = []
        for tile, (_, send_base), values in zip(tiles, places, work):
            hot = place_hot_rows(ordered, 1, tile, send_base, level)
            sums.append(spread_rows(hot, block_ref[tile_rows(tile), :], SENDERS, values))
        for (_, send_base), parts in zip(places, sums):
            add_parts(send_sum, send_base, parts)

    def far(tile):
        rows = tile_rows(tile)
        recv = index_columns(ordered.at[0], tile * count, count)
        send = index_columns(ordered.at[1], tile * count, count)
        blocks = fine_count // SPAN
        upstream = gather_blocks(place_hot(recv), recv >> 8, grad_table, 0, blocks)
        values = (upstream * slope_ref[rows, :]).astype(BF16)
        hot = place_hot_rows(ordered, 1, tile, 0, level)
        add_parts(send_sum, 0, spread_rows(hot, small(send >> 8), blocks + 2, values))

    def step(index, carry):
        each_group(index, stats, fine_count, near, far)
        return carry

    lax.fori_loop(0, slope_ref.shape[0] // TILE // GROUP, step, 0)

    weight_send = weight_ref[0:LANES, :]
    odd = lax.axis_index("curve") & 1
    to_prev = back(send_sum[0:HB, :], weight_send)
    to_next = back(send_sum[HB + fine_count :, :], weight_send)
    first_ref[LANES:, :] = jnp.where(odd == 0, to_next, to_prev).astype(BF16)
    second_ref[...] = jnp.where(odd == 0, to_prev, to_next).astype(BF16)
    term_send = jnp.zeros((LANES, LANES), F32)
    term_recv = jnp.zeros((LANES, LANES), F32)
    for first in range(0, fine_count + 2 * HB, SPAN):
        at = slice(first, first + SPAN)
        term_send += outer(window[at, :], send_sum[at, :])
    for first in range(0, fine_count, SPAN):
        at = slice(first, first + SPAN)
        moved = slice(HB + first, HB + first + SPAN)
        term_recv += outer(window[moved, :], grad_rows[at, :] * slope_sum[at, :])
    keep_ref[0:LANES, :] = jnp.where(odd == 0, term_send, term_recv)
    first_ref[0:LANES, :] = jnp.where(odd == 0, term_recv, term_send).astype(BF16)


def fine_kernel(
    grad_hbm,
    send_sum_hbm,
    slope_sum_hbm,
    weight_hbm,
    first_hbm,
    second_hbm,
    fine_ref,
    grad_table,
    send_sum,
    slope_sum,
    weight_ref,
    first_ref,
    second_ref,
    arrivals,
):
    fine_count = fine_ref.shape[0]
    for copy in fetch(
        (grad_hbm, send_sum_hbm, slope_sum_hbm, weight_hbm, first_hbm, second_hbm),
        (grad_table, send_sum, slope_sum, weight_ref, first_ref, second_ref),
        arrivals,
    ):
        copy.wait()
    odd = lax.axis_index("curve") & 1
    one, two = first_ref[LANES:, :].astype(F32), second_ref[...].astype(F32)
    from_next, from_prev = jnp.where(odd == 0, one, two), jnp.where(odd == 0, two, one)
    for first in range(0, fine_count, SPAN):
        at = slice(first, first + SPAN)
        moved = slice(HB + first, HB + first + SPAN)
        grad = grad_table[at, :].astype(F32)
        summed = (
            grad
            + back(send_sum[moved, :], weight_ref[0:LANES, :])
            + back(grad * slope_sum[at, :], weight_ref[LANES:, :])
        )
        if first == 0:
            summed += from_prev
        if first == fine_count - SPAN:
            summed += from_next
        fine_ref[at, :] = summed.astype(BF16)


def last_kernel(
    edge_scale, coarse_scale, own_ref, coarse_ref, there_ref, edge_ref, in_ref, out_ref
):
    odd = lax.axis_index("curve") & 1
    own, coarse = own_ref[...], coarse_ref[...].astype(F32)
    other, other_coarse = there_ref[0:LANES, :], there_ref[LANES:, :]
    edge_ref[0:LANES, :] = jnp.where(odd == 0, own, other) * edge_scale
    edge_ref[LANES:, :] = jnp.where(odd == 0, other, own) * edge_scale
    in_ref[...] = jnp.where(odd == 0, coarse, other_coarse) * coarse_scale
    out_ref[...] = jnp.where(odd == 0, other_coarse, coarse) * coarse_scale


def pair_exchange(first, second, peers):
    pairs = [(i, i ^ 1) for i in range(peers)]
    between = [(i, ((i + 1) ^ 1) - 1) for i in range(1, peers - 1)]
    return lax.ppermute(first, "curve", pairs), lax.ppermute(second, "curve", between)


def joined(later, own, there):
    return jnp.where(
        later, jnp.concatenate([there, own], axis=0), jnp.concatenate([own, there], axis=0)
    )


def swapped(values, hops, peers):
    return lax.ppermute(values, "curve", [(i, i ^ hops) for i in range(peers)])


def reduced(sent, half, device, peers, beside):
    hops = 2
    while hops < peers // 4:
        there = swapped(sent, hops, peers)
        own = sent[:half].astype(F32) + there[:half].astype(F32)
        coarse = joined((device & hops) != 0, sent[half:], there[half:])
        sent = jnp.concatenate([own.astype(BF16), coarse], axis=0)
        hops *= 2
    near, far = peers // 4, peers // 2
    parts = [sent] + [swapped(sent, hops, peers) for hops in (near, far, near + far)]
    *parts, beside = lax.optimization_barrier((*parts, beside))
    sums = [part[:half].astype(F32) for part in parts]
    rows = [part[half:] for part in parts]
    own = (sums[0] + sums[1]) + (sums[2] + sums[3])
    later = (device & near) != 0
    coarse = joined(
        (device & far) != 0, joined(later, rows[0], rows[1]), joined(later, rows[2], rows[3])
    )
    return own, coarse, beside


def per_device(
    fine_latent,
    coarse_latent,
    grad_coarse,
    restrict_weights,
    send_rows,
    pair_slots,
    edge_receivers,
    edge_offsets,
    edge_weight,
    node_weight_in,
    node_weight_out,
    node_gain,
):
    peers = lax.axis_size("curve")
    device = lax.axis_index("curve")
    even = (device & 1) == 0
    coarse_count = coarse_latent.shape[0]
    fine_count = fine_latent.shape[0]
    edge_count = edge_receivers.shape[0]
    capacity = send_rows.shape[0] // peers
    chunk = SPAN // peers
    share = max(EXTRA, chunk)
    payload = capacity + EXTRA + share
    edge_rows = edge_count // LANES
    window_count = fine_count + 2 * HB
    params = pltpu.CompilerParams(vmem_limit_bytes=64 * 1024 * 1024 - 256 * 1024)
    roomy = pltpu.CompilerParams(vmem_limit_bytes=62 * 1024 * 1024)
    anywhere = pl.BlockSpec(memory_space=pl.ANY)

    scalar = pl.BlockSpec(memory_space=pltpu.SMEM)

    head, end = fine_latent[:HB], fine_latent[fine_count - HB :]
    halos = pair_exchange(jnp.where(even, end, head), jnp.where(even, head, end), peers)

    sent = pl.pallas_call(
        functools.partial(coarse_kernel, peers),
        out_shape=jax.ShapeDtypeStruct((peers, payload, LANES), BF16),
        in_specs=[anywhere] * 7,
        scratch_shapes=[
            pltpu.VMEM((SPAN, coarse_count), BF16),
            pltpu.VMEM((coarse_count, LANES), BF16),
            pltpu.VMEM((coarse_count, LANES), BF16),
            pltpu.VMEM((2, coarse_count), BF16),
            pltpu.VMEM((peers * capacity // LANES, LANES), jnp.int32),
            pltpu.VMEM((LANES, LANES), BF16),
            pltpu.VMEM((LANES, LANES), BF16),
            pltpu.VMEM((1, LANES), F32),
            pltpu.SemaphoreType.DMA((7,)),
        ],
        compiler_params=params,
        cost_estimate=pl.CostEstimate(
            flops=2_000_000_000, bytes_accessed=2_000_000, transcendentals=400_000
        ),
        name="coarse_block",
    )(
        coarse_latent,
        grad_coarse,
        restrict_weights,
        send_rows.reshape(-1, LANES),
        node_weight_in,
        node_weight_out,
        node_gain.reshape(1, LANES),
    )
    arrived = lax.all_to_all(sent, "curve", split_axis=0, concat_axis=0, tiled=True)

    pair_count = fine_count // 2
    in_vmem = pl.BlockSpec(memory_space=pltpu.VMEM)
    slope, hot, block, window, slope_sum, ordered, stats, slot_hot, slot_block = pl.pallas_call(
        slope_kernel,
        out_shape=(
            jax.ShapeDtypeStruct((edge_count, LANES), F32),
            jax.ShapeDtypeStruct((edge_count, SPAN), BF16),
            jax.ShapeDtypeStruct((edge_count, LANES), BF16),
            jax.ShapeDtypeStruct((window_count, LANES), BF16),
            jax.ShapeDtypeStruct((fine_count, LANES), F32),
            jax.ShapeDtypeStruct((2, edge_rows, LANES), jnp.int32),
            jax.ShapeDtypeStruct((edge_rows, LANES), jnp.int32),
            jax.ShapeDtypeStruct((pair_count, SPAN), BF16),
            jax.ShapeDtypeStruct((pair_count, LANES), jnp.int32),
        ),
        in_specs=[anywhere] * 7,
        out_specs=[anywhere] * 4 + [in_vmem] * 5,
        scratch_shapes=[
            pltpu.VMEM((edge_rows, LANES), jnp.int32),
            pltpu.VMEM((edge_rows, LANES), jnp.int32),
            pltpu.VMEM((pair_count // LANES, LANES), jnp.int32),
            pltpu.VMEM((window_count, LANES), BF16),
            pltpu.VMEM((2 * LANES, LANES), BF16),
            pltpu.VMEM((2, HB, LANES), BF16),
            pltpu.VMEM((edge_count, LANES), F32),
            pltpu.VMEM((edge_count, SPAN), BF16),
            pltpu.VMEM((edge_count, LANES), BF16),
            pltpu.SMEM((edge_rows, LANES), jnp.int32),
            pltpu.SemaphoreType.DMA((7,)),
            pltpu.SemaphoreType.DMA,
            pltpu.SemaphoreType.DMA((3, edge_count // TILE)),
            pltpu.SemaphoreType.DMA,
        ],
        compiler_params=params,
        cost_estimate=pl.CostEstimate(
            flops=16_000_000_000, bytes_accessed=5_000_000, transcendentals=800_000
        ),
        name="edge_slope",
    )(
        edge_receivers.reshape(-1, LANES),
        edge_offsets.reshape(-1, LANES),
        pair_slots.reshape(-1, LANES),
        fine_latent,
        edge_weight,
        *halos,
    )

    coarse_scale = 1.0 / math.sqrt(coarse_count * peers)
    edge_scale = 1.0 / math.sqrt(edge_count * peers)
    grad_rows, send_sum, first, second, keep, term_gain = pl.pallas_call(
        functools.partial(edge_kernel, coarse_scale),
        out_shape=(
            jax.ShapeDtypeStruct((fine_count, LANES), BF16),
            jax.ShapeDtypeStruct((window_count, LANES), F32),
            pltpu.VMEM((LANES + HB, LANES), BF16),
            pltpu.VMEM((HB, LANES), BF16),
            pltpu.VMEM((LANES + share, LANES), F32),
            jax.ShapeDtypeStruct((1, LANES), F32),
        ),
        in_specs=[scalar] + [anywhere] * 10,
        scratch_shapes=[
            pltpu.VMEM((SPAN, peers * capacity), BF16),
            pltpu.VMEM((fine_count, LANES), F32),
            pltpu.VMEM((peers, payload, LANES), BF16),
            pltpu.VMEM((pair_count, SPAN), BF16),
            pltpu.VMEM((pair_count, LANES), jnp.int32),
            pltpu.VMEM((edge_count, SPAN), BF16),
            pltpu.VMEM((edge_count, LANES), F32),
            pltpu.VMEM((edge_count, LANES), BF16),
            pltpu.VMEM((2, edge_rows, LANES), jnp.int32),
            pltpu.VMEM((window_count, LANES), BF16),
            pltpu.VMEM((fine_count, LANES), F32),
            pltpu.VMEM((2 * LANES, LANES), BF16),
            pltpu.SemaphoreType.DMA((10,)),
        ],
        compiler_params=roomy,
        cost_estimate=pl.CostEstimate(
            flops=24_000_000_000, bytes_accessed=8_000_000, transcendentals=0
        ),
        name="edge_back",
    )(
        stats,
        arrived,
        slot_hot,
        slot_block,
        hot,
        slope,
        block,
        ordered,
        window,
        slope_sum,
        edge_weight,
    )
    one, two = pair_exchange(first, second, peers)
    sent = keep[: LANES + chunk] + jnp.pad(one[:LANES].astype(F32), ((0, chunk), (0, 0)))
    sent = sent.astype(BF16)
    grad_fine = pl.pallas_call(
        fine_kernel,
        out_shape=jax.ShapeDtypeStruct((fine_count, LANES), BF16),
        in_specs=[anywhere] * 6,
        scratch_shapes=[
            pltpu.VMEM((fine_count, LANES), BF16),
            pltpu.VMEM((window_count, LANES), F32),
            pltpu.VMEM((fine_count, LANES), F32),
            pltpu.VMEM((2 * LANES, LANES), BF16),
            pltpu.VMEM((LANES + HB, LANES), BF16),
            pltpu.VMEM((HB, LANES), BF16),
            pltpu.SemaphoreType.DMA((6,)),
        ],
        compiler_params=pltpu.CompilerParams(vmem_limit_bytes=64 * 1024 * 1024 - 640 * 1024),
        cost_estimate=pl.CostEstimate(
            flops=1_000_000_000, bytes_accessed=4_000_000, transcendentals=0
        ),
        name="fine_sums",
    )(grad_rows, send_sum, slope_sum, edge_weight, one, two)
    own, coarse, grad_fine = reduced(sent, LANES, device, peers, grad_fine)
    there = swapped(jnp.concatenate([own, coarse.astype(F32)], axis=0), 1, peers)
    edge_terms, term_in, term_out = pl.pallas_call(
        functools.partial(last_kernel, edge_scale, coarse_scale),
        out_shape=(
            jax.ShapeDtypeStruct((2 * LANES, LANES), F32),
            jax.ShapeDtypeStruct((LANES, LANES), F32),
            jax.ShapeDtypeStruct((LANES, LANES), F32),
        ),
        compiler_params=pltpu.CompilerParams(vmem_limit_bytes=4 * 1024 * 1024),
        name="last_terms",
    )(own, coarse, there)
    return grad_fine, edge_terms, term_in, term_out, term_gain.reshape(LANES)


def solution(mesh):
    placed = (
        P(("groups", "curve"), None),
        P(("groups", "curve"), None),
        P(("groups", "curve"), None),
        P(None, ("groups", "curve")),
        P(("groups", "curve")),
        P(("groups", "curve")),
        P(("groups", "curve")),
        P(("groups", "curve")),
        P(),
        P(),
        P(),
        P(),
    )
    return jax.shard_map(
        per_device,
        mesh=mesh,
        in_specs=placed,
        out_specs=(
            P(("groups", "curve"), None),
            P("groups", None),
            P("groups", None),
            P("groups", None),
            P("groups"),
        ),
        check_vma=False,
    )
```

```python
import functools
import math

import jax
import jax.numpy as jnp
from jax import lax
from jax.experimental import pallas as pl
from jax.experimental.pallas import tpu as pltpu
from jax.sharding import PartitionSpec as P

HB = 256
LANES = 128
SPAN = 256
EXTRA = 16
WEIGHTS = EXTRA - 2
TILE = 512
GROUP = 4
SENDERS = 3

F32 = jnp.float32
BF16 = jnp.bfloat16
NT = (((1,), (1,)), ((), ()))
TN = (((0,), (0,)), ((), ()))


def dot(left, right, dims=(((1,), (0,)), ((), ()))):
    return lax.dot_general(left, right, dims, preferred_element_type=F32)


def silu_slope(values):
    sigm = jax.nn.sigmoid(values)
    return sigm * (1.0 + values * (1.0 - sigm))


def columns(row):
    return jnp.broadcast_to(row, (LANES, LANES)).T


def index_columns(ref, first, count):
    return jnp.concatenate([columns(ref[pl.ds(first + i, 1), :]) for i in range(count)], axis=0)


def small(values):
    return values.astype(F32).astype(BF16)


def place_hot(cols):
    place = small(cols & (SPAN - 1))
    lane = lax.broadcasted_iota(jnp.int32, place.shape, 1)
    one, zero = jnp.ones((), BF16), jnp.zeros((), BF16)
    return jnp.concatenate(
        [jnp.where(place == small(lane + start), one, zero) for start in range(0, SPAN, LANES)],
        axis=1,
    )


def gather_rows(hot, block, table, width):
    total = table.shape[1]
    step = max(width, 2 * LANES)
    found = [jnp.zeros(block.shape, F32) for _ in range(width // LANES)]
    for start in range(0, total, step):
        part = dot(hot, table[:, start : start + step])
        for inner in range(0, step, width):
            here = block == (start + inner) // width
            for i in range(len(found)):
                at = inner + i * LANES
                found[i] = jnp.where(here, part[:, at : at + LANES], found[i])
    return found


def spread_rows(hot, block, blocks, values):
    if blocks == 1:
        return [dot(hot, values)]
    parts = []
    zero = jnp.zeros((), BF16)
    for start in range(0, blocks, 2):
        some = range(start, min(start + 2, blocks))
        spread = [jnp.where(block == jnp.full((), j, BF16), values, zero) for j in some]
        part = dot(hot, jnp.concatenate(spread, axis=1))
        parts += [part[:, i * LANES : (i + 1) * LANES] for i in range(len(some))]
    return parts


def add_parts(total, base, parts):
    for j, part in enumerate(parts):
        total[block_rows(base, j), :] += part


def place_hot_rows(ordered, at, tile, base, level):
    one, zero = jnp.ones((), BF16), jnp.zeros((), BF16)
    hot = []
    for i in range(TILE // LANES):
        row = ordered[at, pl.ds(tile * (TILE // LANES) + i, 1), :] - base
        hot.append(jnp.where(level == small(row & (SPAN - 1)), one, zero))
    return jnp.concatenate(hot, axis=1)


def levels():
    return small(lax.broadcasted_iota(jnp.int32, (SPAN, LANES), 0))


def two_parts(values):
    high = values.astype(BF16)
    return high, (values - high.astype(F32)).astype(BF16)


def back(values, weight):
    high, low = two_parts(values)
    return dot(high, weight, NT) + dot(low, weight, NT)


def outer(rows, values):
    high, low = two_parts(values)
    both = dot(rows, jnp.concatenate([high, low], axis=1), TN)
    return both[:, 0:LANES] + both[:, LANES:]


def term_sizes(peers):
    chunk = min(WEIGHTS, SPAN // peers)
    half = (SPAN - chunk * peers) // 2
    return chunk, half, -(-(half + 1) // EXTRA) * EXTRA


def fetch(sources, targets, arrivals):
    copies = [
        pltpu.make_async_copy(source, target, arrivals.at[i])
        for i, (source, target) in enumerate(zip(sources, targets))
    ]
    for copy in copies:
        copy.start()
    return copies


def coarse_kernel(
    peers,
    latent_ref,
    grad_ref,
    weights_ref,
    rows_ref,
    w_in_ref,
    w_out_ref,
    gain_ref,
    sent_ref,
    rest_ref,
    table_ref,
    terms,
    *held,
):
    *held, arrivals = held
    sources = (latent_ref, grad_ref, weights_ref, rows_ref, w_in_ref, w_out_ref, gain_ref)
    copies = fetch(sources, held, arrivals)
    for copy in copies:
        copy.wait()
    latent_ref, grad_ref, weights_ref, rows_ref, w_in_ref, w_out_ref, gain_ref = held
    count = latent_ref.shape[0]
    chunk, half_rest, rest_rows = term_sizes(peers)
    capacity = sent_ref.shape[1] - EXTRA
    per_step = 256 // LANES
    steps = range(0, rows_ref.shape[0], per_step)
    slots = []
    for first in steps:
        cols = index_columns(rows_ref, first, per_step)
        slots.append((place_hot(cols), cols // SPAN))
    w_in, w_out, gain = w_in_ref[...], w_out_ref[...], gain_ref[...]
    latent = latent_ref[...]
    pre = dot(latent, w_in)
    sigm = jax.nn.sigmoid(pre)
    hidden = (pre * sigm).astype(BF16)
    slope = sigm * (1.0 + pre * (1.0 - sigm))
    mapped = dot(hidden, w_out)
    centred = mapped - jnp.mean(mapped, axis=1, keepdims=True)
    inverse = lax.rsqrt(jnp.mean(centred * centred, axis=1, keepdims=True) + 1e-05)
    normed = centred * inverse
    upstream = grad_ref[...].astype(F32)
    scaled = upstream * gain
    grad_mapped = (
        inverse
        * (
            scaled
            - jnp.mean(scaled, axis=1, keepdims=True)
            - normed * jnp.mean(scaled * normed, axis=1, keepdims=True)
        )
    ).astype(BF16)
    grad_pre = (dot(grad_mapped, w_out, NT) * slope).astype(BF16)
    grad_in = (upstream + dot(grad_pre, w_in, NT)).astype(BF16)
    term_gain = jnp.sum(upstream * normed, axis=0, keepdims=True)
    term_in = dot(latent, grad_pre, TN)
    term_out = dot(hidden, grad_mapped, TN)
    for block in range(count // SPAN):
        at = block * SPAN
        table_ref[:, at : at + LANES] = grad_in[at : at + SPAN]
        for half in range(SPAN // LANES):
            at = block * SPAN + half * LANES
            pair = weights_ref[:, at : at + LANES].astype(F32)
            square = jnp.concatenate([pair, jnp.zeros((LANES - 2, LANES), F32)], axis=0)
            table_ref[
                half * LANES : (half + 1) * LANES, block * SPAN + LANES : (block + 1) * SPAN
            ] = square.T.astype(BF16)
    terms[0:LANES, :] = term_in
    terms[LANES:, :] = term_out
    rest_ref[...] = jnp.zeros(rest_ref.shape, F32)
    shared = chunk * peers
    if half_rest:
        rest_ref[0:half_rest, :] = terms[shared : shared + half_rest, :]
        rest_ref[rest_rows : rest_rows + half_rest, :] = terms[shared + half_rest :, :]
    rest_ref[half_rest : half_rest + 1, :] = term_gain
    found = [gather_rows(hot, block, table_ref, SPAN) for hot, block in slots]
    for first, (sent, weight) in zip(steps, found):
        for part in range(per_step * LANES // capacity):
            peer = first * LANES // capacity + part
            rows = slice(part * capacity, (part + 1) * capacity)
            sent_ref[peer, 0:capacity, :] = sent[rows].astype(BF16)
            square = weight[rows]
            if capacity < LANES:
                square = jnp.concatenate(
                    [square, jnp.zeros((LANES - capacity, LANES), F32)], axis=0
                )
            first_row = (peer % 2 * (peers // 2) + peer // 2) * chunk
            extra = [terms[first_row : first_row + chunk, :]]
            if chunk < WEIGHTS:
                extra.append(jnp.zeros((WEIGHTS - chunk, LANES), F32))
            extra.append(square.T[0:2])
            sent_ref[peer, capacity:, :] = jnp.concatenate(extra, axis=0).astype(BF16)


def order_edges(recv_ref, off_ref, ordered, stats_vmem, fine_count):
    rows = recv_ref.shape[0]
    shift = (fine_count // LANES).bit_length() - 1
    lane = lax.broadcasted_iota(jnp.int32, (LANES, LANES), 1)
    sub = lax.broadcasted_iota(jnp.int32, (LANES, LANES), 0)
    level = small(sub)
    one, zero = jnp.ones((), BF16), jnp.zeros((), BF16)

    def hot(row):
        return jnp.where(level == small(row), one, zero)

    number = jnp.zeros((LANES, LANES), BF16)
    for row in range(rows):
        number += hot(recv_ref[row : row + 1, :] >> shift)
    ones = jnp.ones((LANES, LANES), BF16)
    total = dot(number, ones)
    high = jnp.floor(total * (1.0 / 64.0))
    low = total - 64.0 * high
    before = jnp.where(lane < sub, 1.0, 0.0).astype(BF16)
    start = 64.0 * dot(before, high.astype(BF16)) + dot(before, low.astype(BF16))
    after = jnp.where(sub < lane, 1.0, 0.0).astype(BF16)
    prefix = jnp.concatenate([after, ones], axis=1)
    positions = []
    filled = start
    for row in range(rows):
        bucket = recv_ref[row : row + 1, :] >> shift
        found = dot(hot(bucket), prefix)
        mine = jnp.where(sub == bucket, found[:, 0:LANES] + filled, 0.0)
        positions.append(jnp.sum(mine, axis=0, keepdims=True).astype(jnp.int32))
        filled = filled + found[:, LANES:]
    moved = jnp.zeros((192, LANES), F32)
    for part in range(0, rows, 4):
        left, right = [], []
        for row in range(part, part + 4):
            position = positions[row]
            recv = recv_ref[row : row + 1, :]
            off = off_ref[row : row + 1, :] + HB
            rest = ((recv >> 8) << 2) | (off >> 8)
            here = level[0:64] == small(position >> 7)
            values = [small(value) for value in (recv & 255, off & 255, rest)]
            left.append(jnp.concatenate([jnp.where(here, v, zero) for v in values], axis=0))
            right.append(hot(position & 127))
        moved += dot(jnp.concatenate(left, axis=1), jnp.concatenate(right, axis=1), NT)
    moved = moved.astype(jnp.int32)
    rest = moved[LANES : LANES + rows]
    recv = moved[0:rows] + ((rest >> 2) << 8)
    send = recv + moved[64 : 64 + rows] + ((rest & 3) << 8)
    ordered[0] = recv
    ordered[1] = send
    lane = lax.broadcasted_iota(jnp.int32, (rows, LANES), 1)
    recv, send = recv.astype(F32), send.astype(F32)
    stats = jnp.where(
        lane < 2,
        jnp.where(
            lane == 0,
            jnp.min(recv, axis=1, keepdims=True),
            jnp.max(recv, axis=1, keepdims=True),
        ),
        jnp.where(
            lane == 2,
            jnp.min(send, axis=1, keepdims=True),
            jnp.max(send, axis=1, keepdims=True),
        ),
    )
    stats_vmem[...] = stats.astype(jnp.int32)


def tile_bases(stats, tile, fine_count):
    count = TILE // LANES
    rows = [tile * count + i for i in range(count)]

    def extreme(pick, at):
        value = stats[rows[0], at]
        for row in rows[1:]:
            value = pick(value, stats[row, at])
        return value

    recv_base = jnp.minimum((extreme(jnp.minimum, 0) >> 4) << 4, fine_count - SPAN)
    send_base = jnp.minimum(
        (extreme(jnp.minimum, 2) >> 4) << 4, fine_count + 2 * HB - SENDERS * SPAN
    )
    fits = (extreme(jnp.maximum, 1) - recv_base < SPAN) & (
        extreme(jnp.maximum, 3) - send_base < SENDERS * SPAN
    )
    return recv_base, send_base, fits


def each_group(step, stats, fine_count, near, far):
    tiles = [step * GROUP + i for i in range(GROUP)]
    places = [tile_bases(stats, tile, fine_count) for tile in tiles]
    fits = functools.reduce(jnp.logical_and, [place[2] for place in places])

    @pl.when(fits)
    def _():
        near(tiles, [place[:2] for place in places])

    @pl.when(jnp.logical_not(fits))
    def _():
        def one(i, carry):
            far(step * GROUP + i)
            return carry

        lax.fori_loop(0, GROUP, one, 0)


def block_rows(base, block):
    return pl.ds(pl.multiple_of(base + block * SPAN, 16), SPAN)


def gather_blocks(hot, block, table, base, blocks):
    found = None
    for start in range(0, blocks, 2):
        some = range(start, min(start + 2, blocks))
        part = dot(hot, jnp.concatenate([table[block_rows(base, j), :] for j in some], axis=1))
        for i, j in enumerate(some):
            one = part[:, i * LANES : (i + 1) * LANES]
            found = one if found is None else jnp.where(block == j, one, found)
    return found


def tile_rows(tile):
    return pl.ds(pl.multiple_of(tile * TILE, TILE), TILE)


def slope_kernel(
    recv_hbm,
    off_hbm,
    slots_hbm,
    fine_hbm,
    weight_hbm,
    first_hbm,
    second_hbm,
    slope_hbm,
    hot_hbm,
    block_hbm,
    window_hbm,
    slope_sum,
    ordered,
    stats_vmem,
    slot_hot,
    slot_block,
    recv_ref,
    off_ref,
    slots_ref,
    window,
    weight_ref,
    halos,
    slope_ref,
    hot_ref,
    block_ref,
    stats,
    arrivals,
    stats_done,
    leaving,
    window_left,
):
    fine_count = fine_hbm.shape[0]
    copies = fetch(
        (recv_hbm, off_hbm, slots_hbm, fine_hbm, weight_hbm, first_hbm, second_hbm),
        (
            recv_ref,
            off_ref,
            slots_ref,
            window.at[pl.ds(HB, fine_count)],
            weight_ref,
            halos.at[0],
            halos.at[1],
        ),
        arrivals,
    )
    copies[0].wait()
    copies[1].wait()
    order_edges(recv_ref, off_ref, ordered, stats_vmem, fine_count)
    stats_copy = pltpu.make_async_copy(stats_vmem, stats, stats_done)
    stats_copy.start()
    for copy in copies[2:]:
        copy.wait()
    slope_sum[...] = jnp.zeros(slope_sum.shape, F32)
    slots = index_columns(slots_ref, 0, slots_ref.shape[0])
    slot_hot[...] = place_hot(slots)
    slot_block[...] = slots // SPAN
    odd = lax.axis_index("curve") & 1
    window[0:HB, :] = halos[1 - odd]
    window[HB + fine_count :, :] = halos[odd]
    window_copy = pltpu.make_async_copy(window, window_hbm, window_left)
    window_copy.start()
    stats_copy.wait()
    count = TILE // LANES
    weight = weight_ref[...]
    level = levels()

    def leave(tile):
        rows = tile_rows(tile)
        pairs = ((slope_ref, slope_hbm), (hot_ref, hot_hbm), (block_ref, block_hbm))
        return [
            pltpu.make_async_copy(source.at[rows], target.at[rows], leaving.at[i, tile])
            for i, (source, target) in enumerate(pairs)
        ]

    def near(tiles, places):
        work = []
        for tile, (recv_base, send_base) in zip(tiles, places):
            recv = index_columns(ordered.at[0], tile * count, count) - recv_base
            send = index_columns(ordered.at[1], tile * count, count) - send_base
            block = send >> 8
            hot = place_hot(recv)
            hot_ref[tile_rows(tile), :] = hot
            block_ref[tile_rows(tile), :] = small(block)
            sender = gather_blocks(place_hot(send), block, window, send_base, SENDERS)
            receiver = gather_blocks(hot, None, window, recv_base + HB, 1)
            work.append((sender, receiver))
        slopes = []
        for tile in tiles:
            for copy in leave(tile)[1:]:
                copy.start()
        for tile, (sender, receiver) in zip(tiles, work):
            inputs = jnp.concatenate([sender.astype(BF16), receiver.astype(BF16)], axis=1)
            slope = silu_slope(dot(inputs, weight))
            slope_ref[tile_rows(tile), :] = slope
            leave(tile)[0].start()
            slopes.append(jnp.concatenate(two_parts(slope), axis=1))
        sums = []
        for tile, (recv_base, _), slope in zip(tiles, places, slopes):
            hot = place_hot_rows(ordered, 0, tile, recv_base, level)
            both = dot(hot, slope)
            sums.append(both[:, 0:LANES] + both[:, LANES:])
        for (recv_base, _), part in zip(places, sums):
            add_parts(slope_sum, recv_base, [part])

    def far(tile):
        recv = index_columns(ordered.at[0], tile * count, count)
        send = index_columns(ordered.at[1], tile * count, count)
        blocks = fine_count // SPAN
        sender = gather_blocks(place_hot(send), send >> 8, window, 0, blocks + 2)
        receiver = gather_blocks(place_hot(recv), recv >> 8, window, HB, blocks)
        inputs = jnp.concatenate([sender.astype(BF16), receiver.astype(BF16)], axis=1)
        slope = silu_slope(dot(inputs, weight))
        slope_ref[tile_rows(tile), :] = slope
        hot = place_hot_rows(ordered, 0, tile, 0, level)
        for part in two_parts(slope):
            add_parts(slope_sum, 0, spread_rows(hot, small(recv >> 8), blocks, part))
        hot_ref[tile_rows(tile), :] = jnp.zeros((TILE, SPAN), BF16)
        block_ref[tile_rows(tile), :] = jnp.zeros((TILE, LANES), BF16)
        for copy in leave(tile):
            copy.start()

    def step(index, carry):
        each_group(index, stats, fine_count, near, far)
        return carry

    tiles = slope_ref.shape[0] // TILE
    lax.fori_loop(0, tiles // GROUP, step, 0)
    window_copy.wait()
    for tile in range(tiles):
        for copy in leave(tile):
            copy.wait()


def edge_kernel(
    stats,
    arrived_hbm,
    slot_hot_hbm,
    slot_block_hbm,
    hot_hbm,
    slope_hbm,
    block_hbm,
    ordered_hbm,
    window_hbm,
    slope_sum_hbm,
    weight_hbm,
    rest_hbm,
    grad_table,
    send_sum,
    first_ref,
    second_ref,
    keep_ref,
    slot_table,
    grad_rows,
    arrived_ref,
    slot_hot,
    slot_block,
    hot_ref,
    slope_ref,
    block_ref,
    ordered,
    window,
    slope_sum,
    weight_ref,
    rest_ref,
    arrivals,
):
    fine_count = grad_table.shape[0]
    copies = fetch(
        (
            arrived_hbm,
            slot_hot_hbm,
            slot_block_hbm,
            hot_hbm,
            slope_hbm,
            block_hbm,
            ordered_hbm,
            window_hbm,
            slope_sum_hbm,
            weight_hbm,
            rest_hbm,
        ),
        (
            arrived_ref,
            slot_hot,
            slot_block,
            hot_ref,
            slope_ref,
            block_ref,
            ordered,
            window,
            slope_sum,
            weight_ref,
            rest_ref,
        ),
        arrivals,
    )
    send_sum[...] = jnp.zeros(send_sum.shape, F32)
    peers = arrived_ref.shape[0]
    half = LANES + rest_ref.shape[0] // 2
    capacity = arrived_ref.shape[1] - EXTRA
    per_block = SPAN // capacity
    for copy in copies[:3]:
        copy.wait()
    coarse = jnp.zeros((EXTRA, LANES), F32)
    for peer in range(peers):
        block, part = divmod(peer, per_block)
        rows = slice(part * capacity, (part + 1) * capacity)
        slot_table[rows, block * SPAN : block * SPAN + LANES] = arrived_ref[peer, 0:capacity, :]
        extra = arrived_ref[peer, capacity:, :].astype(F32)
        square = jnp.concatenate([extra, jnp.zeros((LANES - EXTRA, LANES), F32)], axis=0).T
        slot_table[rows, block * SPAN + LANES : (block + 1) * SPAN] = square[0:capacity].astype(
            BF16
        )
        coarse += extra
    keep_ref[half:, :] = coarse

    found = []
    for first in range(0, slot_hot.shape[0], SPAN):
        at = slice(first, first + SPAN)
        found.append(gather_rows(slot_hot[at, :], slot_block[at, :], slot_table, SPAN))
    for i, (grad, weight) in enumerate(found):
        first = i * SPAN
        for r in range(2):
            factor = weight[:, WEIGHTS + r : WEIGHTS + r + 1]
            rows = (grad * factor).astype(BF16).astype(F32)
            grad_rows[pl.ds(2 * first + r, SPAN, stride=2), :] = rows
    grad_table[...] = grad_rows[...].astype(BF16)
    for copy in copies[3:]:
        copy.wait()

    count = TILE // LANES
    level = levels()

    def near(tiles, places):
        work = []
        for tile, (recv_base, _) in zip(tiles, places):
            rows = tile_rows(tile)
            upstream = gather_blocks(hot_ref[rows, :], None, grad_table, recv_base, 1)
            work.append((upstream * slope_ref[rows, :]).astype(BF16))
        sums = []
        for tile, (_, send_base), values in zip(tiles, places, work):
            hot = place_hot_rows(ordered, 1, tile, send_base, level)
            sums.append(spread_rows(hot, block_ref[tile_rows(tile), :], SENDERS, values))
        for (_, send_base), parts in zip(places, sums):
            add_parts(send_sum, send_base, parts)

    def far(tile):
        rows = tile_rows(tile)
        recv = index_columns(ordered.at[0], tile * count, count)
        send = index_columns(ordered.at[1], tile * count, count)
        blocks = fine_count // SPAN
        upstream = gather_blocks(place_hot(recv), recv >> 8, grad_table, 0, blocks)
        values = (upstream * slope_ref[rows, :]).astype(BF16)
        hot = place_hot_rows(ordered, 1, tile, 0, level)
        add_parts(send_sum, 0, spread_rows(hot, small(send >> 8), blocks + 2, values))

    def step(index, carry):
        each_group(index, stats, fine_count, near, far)
        return carry

    lax.fori_loop(0, slope_ref.shape[0] // TILE // GROUP, step, 0)

    weight_send = weight_ref[0:LANES, :]
    odd = lax.axis_index("curve") & 1
    to_prev = back(send_sum[0:HB, :], weight_send)
    to_next = back(send_sum[HB + fine_count :, :], weight_send)
    first_ref[half:, :] = jnp.where(odd == 0, to_next, to_prev).astype(BF16)
    second_ref[...] = jnp.where(odd == 0, to_prev, to_next).astype(BF16)
    term_send = jnp.zeros((LANES, LANES), F32)
    term_recv = jnp.zeros((LANES, LANES), F32)
    for first in range(0, fine_count + 2 * HB, SPAN):
        at = slice(first, first + SPAN)
        term_send += outer(window[at, :], send_sum[at, :])
    for first in range(0, fine_count, SPAN):
        at = slice(first, first + SPAN)
        moved = slice(HB + first, HB + first + SPAN)
        term_recv += outer(window[moved, :], grad_rows[at, :] * slope_sum[at, :])
    keep_ref[0:LANES, :] = jnp.where(odd == 0, term_send, term_recv)
    first_ref[0:LANES, :] = jnp.where(odd == 0, term_recv, term_send).astype(BF16)
    rest_first, rest_second = rest_ref[0 : half - LANES, :], rest_ref[half - LANES :, :]
    keep_ref[LANES:half, :] = jnp.where(odd == 0, rest_first, rest_second)
    first_ref[LANES:half, :] = jnp.where(odd == 0, rest_second, rest_first).astype(BF16)


def fine_kernel(
    grad_hbm,
    send_sum_hbm,
    slope_sum_hbm,
    weight_hbm,
    first_hbm,
    second_hbm,
    fine_ref,
    grad_table,
    send_sum,
    slope_sum,
    weight_ref,
    first_ref,
    second_ref,
    arrivals,
):
    fine_count = fine_ref.shape[0]
    for copy in fetch(
        (grad_hbm, send_sum_hbm, slope_sum_hbm, weight_hbm, first_hbm, second_hbm),
        (grad_table, send_sum, slope_sum, weight_ref, first_ref, second_ref),
        arrivals,
    ):
        copy.wait()
    odd = lax.axis_index("curve") & 1
    half = first_ref.shape[0] - HB
    one, two = first_ref[half:, :].astype(F32), second_ref[...].astype(F32)
    from_next, from_prev = jnp.where(odd == 0, one, two), jnp.where(odd == 0, two, one)
    for first in range(0, fine_count, SPAN):
        at = slice(first, first + SPAN)
        moved = slice(HB + first, HB + first + SPAN)
        grad = grad_table[at, :].astype(F32)
        summed = (
            grad
            + back(send_sum[moved, :], weight_ref[0:LANES, :])
            + back(grad * slope_sum[at, :], weight_ref[LANES:, :])
        )
        if first == 0:
            summed += from_prev
        if first == fine_count - SPAN:
            summed += from_next
        fine_ref[at, :] = summed.astype(BF16)


def last_kernel(
    edge_scale,
    coarse_scale,
    peers,
    own_ref,
    coarse_ref,
    there_ref,
    edge_ref,
    in_ref,
    out_ref,
    gain_ref,
    terms,
):
    chunk, half_rest, _ = term_sizes(peers)
    half = own_ref.shape[0]
    odd = lax.axis_index("curve") & 1
    own, coarse = own_ref[...], coarse_ref[...].astype(F32)
    other, other_coarse = there_ref[0:half, :], there_ref[half:, :]
    halves = (jnp.where(odd == 0, own, other), jnp.where(odd == 0, other, own))
    shares = (
        jnp.where(odd == 0, coarse, other_coarse),
        jnp.where(odd == 0, other_coarse, coarse),
    )
    for core in range(2):
        edge_ref[core * LANES : (core + 1) * LANES, :] = halves[core][0:LANES] * edge_scale
        for i in range(peers // 2):
            at = (core * (peers // 2) + i) * chunk
            terms[at : at + chunk, :] = shares[core][i * EXTRA : i * EXTRA + chunk]
        if half_rest:
            at = chunk * peers + core * half_rest
            terms[at : at + half_rest, :] = halves[core][LANES : LANES + half_rest]
    in_ref[...] = terms[0:LANES, :] * coarse_scale
    out_ref[...] = terms[LANES:, :] * coarse_scale
    gain_ref[...] = halves[0][LANES + half_rest : LANES + half_rest + 1] * coarse_scale


def pair_exchange(first, second, peers):
    pairs = [(i, i ^ 1) for i in range(peers)]
    between = [(i, ((i + 1) ^ 1) - 1) for i in range(1, peers - 1)]
    return lax.ppermute(first, "curve", pairs), lax.ppermute(second, "curve", between)


def joined(later, own, there):
    return jnp.where(
        later, jnp.concatenate([there, own], axis=0), jnp.concatenate([own, there], axis=0)
    )


def swapped(values, hops, peers):
    return lax.ppermute(values, "curve", [(i, i ^ hops) for i in range(peers)])


def reduced(sent, half, device, peers, beside):
    hops = 2
    while hops < peers // 4:
        there = swapped(sent, hops, peers)
        own = sent[:half].astype(F32) + there[:half].astype(F32)
        coarse = joined((device & hops) != 0, sent[half:], there[half:])
        sent = jnp.concatenate([own.astype(BF16), coarse], axis=0)
        hops *= 2
    near, far = peers // 4, peers // 2
    parts = [sent] + [swapped(sent, hops, peers) for hops in (near, far, near + far)]
    *parts, beside = lax.optimization_barrier((*parts, beside))
    sums = [part[:half].astype(F32) for part in parts]
    rows = [part[half:] for part in parts]
    own = (sums[0] + sums[1]) + (sums[2] + sums[3])
    later = (device & near) != 0
    coarse = joined(
        (device & far) != 0, joined(later, rows[0], rows[1]), joined(later, rows[2], rows[3])
    )
    return own, coarse, beside


def per_device(
    fine_latent,
    coarse_latent,
    grad_coarse,
    restrict_weights,
    send_rows,
    pair_slots,
    edge_receivers,
    edge_offsets,
    edge_weight,
    node_weight_in,
    node_weight_out,
    node_gain,
):
    peers = lax.axis_size("curve")
    device = lax.axis_index("curve")
    even = (device & 1) == 0
    coarse_count = coarse_latent.shape[0]
    fine_count = fine_latent.shape[0]
    edge_count = edge_receivers.shape[0]
    capacity = send_rows.shape[0] // peers
    rest_rows = term_sizes(peers)[2]
    half = LANES + rest_rows
    payload = capacity + EXTRA
    edge_rows = edge_count // LANES
    window_count = fine_count + 2 * HB
    params = pltpu.CompilerParams(vmem_limit_bytes=64 * 1024 * 1024 - 256 * 1024)
    roomy = pltpu.CompilerParams(vmem_limit_bytes=62 * 1024 * 1024)
    anywhere = pl.BlockSpec(memory_space=pl.ANY)

    scalar = pl.BlockSpec(memory_space=pltpu.SMEM)

    head, end = fine_latent[:HB], fine_latent[fine_count - HB :]
    halos = pair_exchange(jnp.where(even, end, head), jnp.where(even, head, end), peers)

    sent, rest = pl.pallas_call(
        functools.partial(coarse_kernel, peers),
        out_shape=(
            jax.ShapeDtypeStruct((peers, payload, LANES), BF16),
            jax.ShapeDtypeStruct((2 * rest_rows, LANES), F32),
        ),
        in_specs=[anywhere] * 7,
        scratch_shapes=[
            pltpu.VMEM((SPAN, coarse_count), BF16),
            pltpu.VMEM((2 * LANES, LANES), F32),
            pltpu.VMEM((coarse_count, LANES), BF16),
            pltpu.VMEM((coarse_count, LANES), BF16),
            pltpu.VMEM((2, coarse_count), BF16),
            pltpu.VMEM((peers * capacity // LANES, LANES), jnp.int32),
            pltpu.VMEM((LANES, LANES), BF16),
            pltpu.VMEM((LANES, LANES), BF16),
            pltpu.VMEM((1, LANES), F32),
            pltpu.SemaphoreType.DMA((7,)),
        ],
        compiler_params=params,
        cost_estimate=pl.CostEstimate(
            flops=2_000_000_000, bytes_accessed=2_000_000, transcendentals=400_000
        ),
        name="coarse_block",
    )(
        coarse_latent,
        grad_coarse,
        restrict_weights,
        send_rows.reshape(-1, LANES),
        node_weight_in,
        node_weight_out,
        node_gain.reshape(1, LANES),
    )
    arrived = lax.all_to_all(sent, "curve", split_axis=0, concat_axis=0, tiled=True)

    pair_count = fine_count // 2
    in_vmem = pl.BlockSpec(memory_space=pltpu.VMEM)
    slope, hot, block, window, slope_sum, ordered, stats, slot_hot, slot_block = pl.pallas_call(
        slope_kernel,
        out_shape=(
            jax.ShapeDtypeStruct((edge_count, LANES), F32),
            jax.ShapeDtypeStruct((edge_count, SPAN), BF16),
            jax.ShapeDtypeStruct((edge_count, LANES), BF16),
            jax.ShapeDtypeStruct((window_count, LANES), BF16),
            jax.ShapeDtypeStruct((fine_count, LANES), F32),
            jax.ShapeDtypeStruct((2, edge_rows, LANES), jnp.int32),
            jax.ShapeDtypeStruct((edge_rows, LANES), jnp.int32),
            jax.ShapeDtypeStruct((pair_count, SPAN), BF16),
            jax.ShapeDtypeStruct((pair_count, LANES), jnp.int32),
        ),
        in_specs=[anywhere] * 7,
        out_specs=[anywhere] * 4 + [in_vmem] * 5,
        scratch_shapes=[
            pltpu.VMEM((edge_rows, LANES), jnp.int32),
            pltpu.VMEM((edge_rows, LANES), jnp.int32),
            pltpu.VMEM((pair_count // LANES, LANES), jnp.int32),
            pltpu.VMEM((window_count, LANES), BF16),
            pltpu.VMEM((2 * LANES, LANES), BF16),
            pltpu.VMEM((2, HB, LANES), BF16),
            pltpu.VMEM((edge_count, LANES), F32),
            pltpu.VMEM((edge_count, SPAN), BF16),
            pltpu.VMEM((edge_count, LANES), BF16),
            pltpu.SMEM((edge_rows, LANES), jnp.int32),
            pltpu.SemaphoreType.DMA((7,)),
            pltpu.SemaphoreType.DMA,
            pltpu.SemaphoreType.DMA((3, edge_count // TILE)),
            pltpu.SemaphoreType.DMA,
        ],
        compiler_params=params,
        cost_estimate=pl.CostEstimate(
            flops=16_000_000_000, bytes_accessed=5_000_000, transcendentals=800_000
        ),
        name="edge_slope",
    )(
        edge_receivers.reshape(-1, LANES),
        edge_offsets.reshape(-1, LANES),
        pair_slots.reshape(-1, LANES),
        fine_latent,
        edge_weight,
        *halos,
    )

    coarse_scale = 1.0 / math.sqrt(coarse_count * peers)
    edge_scale = 1.0 / math.sqrt(edge_count * peers)
    grad_rows, send_sum, first, second, keep = pl.pallas_call(
        edge_kernel,
        out_shape=(
            jax.ShapeDtypeStruct((fine_count, LANES), BF16),
            jax.ShapeDtypeStruct((window_count, LANES), F32),
            pltpu.VMEM((half + HB, LANES), BF16),
            pltpu.VMEM((HB, LANES), BF16),
            pltpu.VMEM((half + EXTRA, LANES), F32),
        ),
        in_specs=[scalar] + [anywhere] * 11,
        scratch_shapes=[
            pltpu.VMEM((SPAN, peers * capacity), BF16),
            pltpu.VMEM((fine_count, LANES), F32),
            pltpu.VMEM((peers, payload, LANES), BF16),
            pltpu.VMEM((pair_count, SPAN), BF16),
            pltpu.VMEM((pair_count, LANES), jnp.int32),
            pltpu.VMEM((edge_count, SPAN), BF16),
            pltpu.VMEM((edge_count, LANES), F32),
            pltpu.VMEM((edge_count, LANES), BF16),
            pltpu.VMEM((2, edge_rows, LANES), jnp.int32),
            pltpu.VMEM((window_count, LANES), BF16),
            pltpu.VMEM((fine_count, LANES), F32),
            pltpu.VMEM((2 * LANES, LANES), BF16),
            pltpu.VMEM((2 * rest_rows, LANES), F32),
            pltpu.SemaphoreType.DMA((11,)),
        ],
        compiler_params=roomy,
        cost_estimate=pl.CostEstimate(
            flops=24_000_000_000, bytes_accessed=8_000_000, transcendentals=0
        ),
        name="edge_back",
    )(
        stats,
        arrived,
        slot_hot,
        slot_block,
        hot,
        slope,
        block,
        ordered,
        window,
        slope_sum,
        edge_weight,
        rest,
    )
    one, two = pair_exchange(first, second, peers)
    sent = keep + jnp.pad(one[:half].astype(F32), ((0, EXTRA), (0, 0)))
    sent = sent.astype(BF16)
    grad_fine = pl.pallas_call(
        fine_kernel,
        out_shape=jax.ShapeDtypeStruct((fine_count, LANES), BF16),
        in_specs=[anywhere] * 6,
        scratch_shapes=[
            pltpu.VMEM((fine_count, LANES), BF16),
            pltpu.VMEM((window_count, LANES), F32),
            pltpu.VMEM((fine_count, LANES), F32),
            pltpu.VMEM((2 * LANES, LANES), BF16),
            pltpu.VMEM((half + HB, LANES), BF16),
            pltpu.VMEM((HB, LANES), BF16),
            pltpu.SemaphoreType.DMA((6,)),
        ],
        compiler_params=pltpu.CompilerParams(vmem_limit_bytes=64 * 1024 * 1024 - 640 * 1024),
        cost_estimate=pl.CostEstimate(
            flops=1_000_000_000, bytes_accessed=4_000_000, transcendentals=0
        ),
        name="fine_sums",
    )(grad_rows, send_sum, slope_sum, edge_weight, one, two)
    own, coarse, grad_fine = reduced(sent, half, device, peers, grad_fine)
    there = swapped(jnp.concatenate([own, coarse.astype(F32)], axis=0), 1, peers)
    edge_terms, term_in, term_out, term_gain = pl.pallas_call(
        functools.partial(last_kernel, edge_scale, coarse_scale, peers),
        out_shape=(
            jax.ShapeDtypeStruct((2 * LANES, LANES), F32),
            jax.ShapeDtypeStruct((LANES, LANES), F32),
            jax.ShapeDtypeStruct((LANES, LANES), F32),
            jax.ShapeDtypeStruct((1, LANES), F32),
        ),
        scratch_shapes=[pltpu.VMEM((2 * LANES, LANES), F32)],
        compiler_params=pltpu.CompilerParams(vmem_limit_bytes=4 * 1024 * 1024),
        name="last_terms",
    )(own, coarse, there)
    return grad_fine, edge_terms, term_in, term_out, term_gain.reshape(LANES)


def solution(mesh):
    placed = (
        P(("groups", "curve"), None),
        P(("groups", "curve"), None),
        P(("groups", "curve"), None),
        P(None, ("groups", "curve")),
        P(("groups", "curve")),
        P(("groups", "curve")),
        P(("groups", "curve")),
        P(("groups", "curve")),
        P(),
        P(),
        P(),
        P(),
    )
    return jax.shard_map(
        per_device,
        mesh=mesh,
        in_specs=placed,
        out_specs=(
            P(("groups", "curve"), None),
            P("groups", None),
            P("groups", None),
            P("groups", None),
            P("groups"),
        ),
        check_vma=False,
    )
```

```python
import functools
import math

import jax
import jax.numpy as jnp
from jax import lax
from jax.experimental import pallas as pl
from jax.experimental.pallas import tpu as pltpu
from jax.sharding import PartitionSpec as P

HB = 256
LANES = 128
SPAN = 256
EXTRA = 16
WEIGHTS = EXTRA - 2
TILE = 512
GROUP = 4
SENDERS = 3

F32 = jnp.float32
BF16 = jnp.bfloat16
NT = (((1,), (1,)), ((), ()))
TN = (((0,), (0,)), ((), ()))


def dot(left, right, dims=(((1,), (0,)), ((), ()))):
    return lax.dot_general(left, right, dims, preferred_element_type=F32)


def silu_slope(values):
    sigm = jax.nn.sigmoid(values)
    return sigm * (1.0 + values * (1.0 - sigm))


def columns(row):
    return jnp.broadcast_to(row, (LANES, LANES)).T


def index_columns(ref, first, count):
    return jnp.concatenate([columns(ref[pl.ds(first + i, 1), :]) for i in range(count)], axis=0)


def small(values):
    return values.astype(F32).astype(BF16)


def place_hot(cols):
    place = small(cols & (SPAN - 1))
    lane = lax.broadcasted_iota(jnp.int32, place.shape, 1)
    one, zero = jnp.ones((), BF16), jnp.zeros((), BF16)
    return jnp.concatenate(
        [jnp.where(place == small(lane + start), one, zero) for start in range(0, SPAN, LANES)],
        axis=1,
    )


def gather_rows(hot, block, table, width):
    total = table.shape[1]
    step = max(width, 2 * LANES)
    found = [jnp.zeros(block.shape, F32) for _ in range(width // LANES)]
    for start in range(0, total, step):
        part = dot(hot, table[:, start : start + step])
        for inner in range(0, step, width):
            here = block == (start + inner) // width
            for i in range(len(found)):
                at = inner + i * LANES
                found[i] = jnp.where(here, part[:, at : at + LANES], found[i])
    return found


def spread_rows(hot, block, blocks, values):
    if blocks == 1:
        return [dot(hot, values)]
    parts = []
    zero = jnp.zeros((), BF16)
    for start in range(0, blocks, 2):
        some = range(start, min(start + 2, blocks))
        spread = [jnp.where(block == jnp.full((), j, BF16), values, zero) for j in some]
        part = dot(hot, jnp.concatenate(spread, axis=1))
        parts += [part[:, i * LANES : (i + 1) * LANES] for i in range(len(some))]
    return parts


def add_parts(total, base, parts):
    for j, part in enumerate(parts):
        total[block_rows(base, j), :] += part


def place_hot_rows(ordered, at, tile, base, level):
    one, zero = jnp.ones((), BF16), jnp.zeros((), BF16)
    hot = []
    for i in range(TILE // LANES):
        row = ordered[at, pl.ds(tile * (TILE // LANES) + i, 1), :] - base
        hot.append(jnp.where(level == small(row & (SPAN - 1)), one, zero))
    return jnp.concatenate(hot, axis=1)


def levels():
    return small(lax.broadcasted_iota(jnp.int32, (SPAN, LANES), 0))


def two_parts(values):
    high = values.astype(BF16)
    return high, (values - high.astype(F32)).astype(BF16)


def back(values, weight):
    both = jnp.concatenate(two_parts(values), axis=1)
    return dot(both, jnp.concatenate([weight, weight], axis=1), NT)


def outer(rows, values):
    high, low = two_parts(values)
    both = dot(rows, jnp.concatenate([high, low], axis=1), TN)
    return both[:, 0:LANES] + both[:, LANES:]


def term_sizes(peers):
    chunk = min(WEIGHTS, SPAN // peers)
    half = (SPAN - chunk * peers) // 2
    return chunk, half, -(-(half + 1) // EXTRA) * EXTRA


def fetch(sources, targets, arrivals):
    copies = [
        pltpu.make_async_copy(source, target, arrivals.at[i])
        for i, (source, target) in enumerate(zip(sources, targets))
    ]
    for copy in copies:
        copy.start()
    return copies


def coarse_kernel(
    peers,
    latent_ref,
    grad_ref,
    weights_ref,
    rows_ref,
    w_in_ref,
    w_out_ref,
    gain_ref,
    sent_ref,
    rest_ref,
    table_ref,
    terms,
    *held,
):
    *held, arrivals = held
    sources = (latent_ref, grad_ref, weights_ref, rows_ref, w_in_ref, w_out_ref, gain_ref)
    copies = fetch(sources, held, arrivals)
    for copy in copies:
        copy.wait()
    latent_ref, grad_ref, weights_ref, rows_ref, w_in_ref, w_out_ref, gain_ref = held
    count = latent_ref.shape[0]
    chunk, half_rest, rest_rows = term_sizes(peers)
    capacity = sent_ref.shape[1] - EXTRA
    per_step = 256 // LANES
    steps = range(0, rows_ref.shape[0], per_step)
    slots = []
    for first in steps:
        cols = index_columns(rows_ref, first, per_step)
        slots.append((place_hot(cols), cols // SPAN))
    w_in, w_out, gain = w_in_ref[...], w_out_ref[...], gain_ref[...]
    latent = latent_ref[...]
    pre = dot(latent, w_in)
    sigm = jax.nn.sigmoid(pre)
    hidden = (pre * sigm).astype(BF16)
    slope = sigm * (1.0 + pre * (1.0 - sigm))
    mapped = dot(hidden, w_out)
    centred = mapped - jnp.mean(mapped, axis=1, keepdims=True)
    inverse = lax.rsqrt(jnp.mean(centred * centred, axis=1, keepdims=True) + 1e-05)
    normed = centred * inverse
    upstream = grad_ref[...].astype(F32)
    scaled = upstream * gain
    grad_mapped = (
        inverse
        * (
            scaled
            - jnp.mean(scaled, axis=1, keepdims=True)
            - normed * jnp.mean(scaled * normed, axis=1, keepdims=True)
        )
    ).astype(BF16)
    grad_pre = (dot(grad_mapped, w_out, NT) * slope).astype(BF16)
    grad_in = (upstream + dot(grad_pre, w_in, NT)).astype(BF16)
    term_gain = jnp.sum(upstream * normed, axis=0, keepdims=True)
    term_in = dot(latent, grad_pre, TN)
    term_out = dot(hidden, grad_mapped, TN)
    for block in range(count // SPAN):
        at = block * SPAN
        table_ref[:, at : at + LANES] = grad_in[at : at + SPAN]
        for half in range(SPAN // LANES):
            at = block * SPAN + half * LANES
            pair = weights_ref[:, at : at + LANES].astype(F32)
            square = jnp.concatenate([pair, jnp.zeros((LANES - 2, LANES), F32)], axis=0)
            table_ref[
                half * LANES : (half + 1) * LANES, block * SPAN + LANES : (block + 1) * SPAN
            ] = square.T.astype(BF16)
    terms[0:LANES, :] = term_in
    terms[LANES:, :] = term_out
    rest_ref[...] = jnp.zeros(rest_ref.shape, F32)
    shared = chunk * peers
    if half_rest:
        rest_ref[0:half_rest, :] = terms[shared : shared + half_rest, :]
        rest_ref[rest_rows : rest_rows + half_rest, :] = terms[shared + half_rest :, :]
    rest_ref[half_rest : half_rest + 1, :] = term_gain
    found = [gather_rows(hot, block, table_ref, SPAN) for hot, block in slots]
    for first, (sent, weight) in zip(steps, found):
        for part in range(per_step * LANES // capacity):
            peer = first * LANES // capacity + part
            rows = slice(part * capacity, (part + 1) * capacity)
            sent_ref[peer, 0:capacity, :] = sent[rows].astype(BF16)
            square = weight[rows]
            if capacity < LANES:
                square = jnp.concatenate(
                    [square, jnp.zeros((LANES - capacity, LANES), F32)], axis=0
                )
            first_row = (peer % 2 * (peers // 2) + peer // 2) * chunk
            extra = [terms[first_row : first_row + chunk, :]]
            if chunk < WEIGHTS:
                extra.append(jnp.zeros((WEIGHTS - chunk, LANES), F32))
            extra.append(square.T[0:2])
            sent_ref[peer, capacity:, :] = jnp.concatenate(extra, axis=0).astype(BF16)


def order_edges(recv_ref, off_ref, ordered, stats_vmem, fine_count):
    rows = recv_ref.shape[0]
    shift = (fine_count // LANES).bit_length() - 1
    lane = lax.broadcasted_iota(jnp.int32, (LANES, LANES), 1)
    sub = lax.broadcasted_iota(jnp.int32, (LANES, LANES), 0)
    level = small(sub)
    one, zero = jnp.ones((), BF16), jnp.zeros((), BF16)

    def hot(row):
        return jnp.where(level == small(row), one, zero)

    number = jnp.zeros((LANES, LANES), BF16)
    for row in range(rows):
        number += hot(recv_ref[row : row + 1, :] >> shift)
    ones = jnp.ones((LANES, LANES), BF16)
    total = dot(number, ones)
    high = jnp.floor(total * (1.0 / 64.0))
    low = total - 64.0 * high
    before = jnp.where(lane < sub, 1.0, 0.0).astype(BF16)
    start = 64.0 * dot(before, high.astype(BF16)) + dot(before, low.astype(BF16))
    after = jnp.where(sub < lane, 1.0, 0.0).astype(BF16)
    prefix = jnp.concatenate([after, ones], axis=1)
    positions = []
    filled = start
    for row in range(rows):
        bucket = recv_ref[row : row + 1, :] >> shift
        found = dot(hot(bucket), prefix)
        mine = jnp.where(sub == bucket, found[:, 0:LANES] + filled, 0.0)
        positions.append(jnp.sum(mine, axis=0, keepdims=True).astype(jnp.int32))
        filled = filled + found[:, LANES:]
    moved = jnp.zeros((192, LANES), F32)
    for part in range(0, rows, 4):
        left, right = [], []
        for row in range(part, part + 4):
            position = positions[row]
            recv = recv_ref[row : row + 1, :]
            off = off_ref[row : row + 1, :] + HB
            rest = ((recv >> 8) << 2) | (off >> 8)
            here = level[0:64] == small(position >> 7)
            values = [small(value) for value in (recv & 255, off & 255, rest)]
            left.append(jnp.concatenate([jnp.where(here, v, zero) for v in values], axis=0))
            right.append(hot(position & 127))
        moved += dot(jnp.concatenate(left, axis=1), jnp.concatenate(right, axis=1), NT)
    moved = moved.astype(jnp.int32)
    rest = moved[LANES : LANES + rows]
    recv = moved[0:rows] + ((rest >> 2) << 8)
    send = recv + moved[64 : 64 + rows] + ((rest & 3) << 8)
    ordered[0] = recv
    ordered[1] = send
    lane = lax.broadcasted_iota(jnp.int32, (rows, LANES), 1)
    recv, send = recv.astype(F32), send.astype(F32)
    stats = jnp.where(
        lane < 2,
        jnp.where(
            lane == 0,
            jnp.min(recv, axis=1, keepdims=True),
            jnp.max(recv, axis=1, keepdims=True),
        ),
        jnp.where(
            lane == 2,
            jnp.min(send, axis=1, keepdims=True),
            jnp.max(send, axis=1, keepdims=True),
        ),
    )
    stats_vmem[...] = stats.astype(jnp.int32)


def tile_bases(stats, tile, fine_count):
    count = TILE // LANES
    rows = [tile * count + i for i in range(count)]

    def extreme(pick, at):
        value = stats[rows[0], at]
        for row in rows[1:]:
            value = pick(value, stats[row, at])
        return value

    recv_base = jnp.minimum((extreme(jnp.minimum, 0) >> 4) << 4, fine_count - SPAN)
    send_base = jnp.minimum(
        (extreme(jnp.minimum, 2) >> 4) << 4, fine_count + 2 * HB - SENDERS * SPAN
    )
    fits = (extreme(jnp.maximum, 1) - recv_base < SPAN) & (
        extreme(jnp.maximum, 3) - send_base < SENDERS * SPAN
    )
    return recv_base, send_base, fits


def each_group(step, stats, fine_count, near, far):
    tiles = [step * GROUP + i for i in range(GROUP)]
    places = [tile_bases(stats, tile, fine_count) for tile in tiles]
    fits = functools.reduce(jnp.logical_and, [place[2] for place in places])

    @pl.when(fits)
    def _():
        near(tiles, [place[:2] for place in places])

    @pl.when(jnp.logical_not(fits))
    def _():
        def one(i, carry):
            far(step * GROUP + i)
            return carry

        lax.fori_loop(0, GROUP, one, 0)


def block_rows(base, block):
    return pl.ds(pl.multiple_of(base + block * SPAN, 16), SPAN)


def gather_blocks(hot, block, table, base, blocks):
    found = None
    for start in range(0, blocks, 2):
        some = range(start, min(start + 2, blocks))
        part = dot(hot, jnp.concatenate([table[block_rows(base, j), :] for j in some], axis=1))
        for i, j in enumerate(some):
            one = part[:, i * LANES : (i + 1) * LANES]
            found = one if found is None else jnp.where(block == j, one, found)
    return found


def tile_rows(tile):
    return pl.ds(pl.multiple_of(tile * TILE, TILE), TILE)


def slope_kernel(
    recv_hbm,
    off_hbm,
    slots_hbm,
    fine_hbm,
    weight_hbm,
    first_hbm,
    second_hbm,
    slope_hbm,
    hot_hbm,
    block_hbm,
    window_hbm,
    slope_sum,
    ordered,
    stats_vmem,
    slot_hot,
    slot_block,
    recv_ref,
    off_ref,
    slots_ref,
    window,
    weight_ref,
    halos,
    slope_ref,
    hot_ref,
    block_ref,
    stats,
    arrivals,
    stats_done,
    leaving,
    window_left,
):
    fine_count = fine_hbm.shape[0]
    copies = fetch(
        (recv_hbm, off_hbm, slots_hbm, fine_hbm, weight_hbm, first_hbm, second_hbm),
        (
            recv_ref,
            off_ref,
            slots_ref,
            window.at[pl.ds(HB, fine_count)],
            weight_ref,
            halos.at[0],
            halos.at[1],
        ),
        arrivals,
    )
    copies[0].wait()
    copies[1].wait()
    order_edges(recv_ref, off_ref, ordered, stats_vmem, fine_count)
    stats_copy = pltpu.make_async_copy(stats_vmem, stats, stats_done)
    stats_copy.start()
    for copy in copies[2:]:
        copy.wait()
    slope_sum[...] = jnp.zeros(slope_sum.shape, F32)
    slots = index_columns(slots_ref, 0, slots_ref.shape[0])
    slot_hot[...] = place_hot(slots)
    slot_block[...] = slots // SPAN
    odd = lax.axis_index("curve") & 1
    window[0:HB, :] = halos[1 - odd]
    window[HB + fine_count :, :] = halos[odd]
    window_copy = pltpu.make_async_copy(window, window_hbm, window_left)
    window_copy.start()
    stats_copy.wait()
    count = TILE // LANES
    weight = weight_ref[...]
    level = levels()

    def leave(tile):
        rows = tile_rows(tile)
        pairs = ((slope_ref, slope_hbm), (hot_ref, hot_hbm), (block_ref, block_hbm))
        return [
            pltpu.make_async_copy(source.at[rows], target.at[rows], leaving.at[i, tile])
            for i, (source, target) in enumerate(pairs)
        ]

    def near(tiles, places):
        work = []
        for tile, (recv_base, send_base) in zip(tiles, places):
            recv = index_columns(ordered.at[0], tile * count, count) - recv_base
            send = index_columns(ordered.at[1], tile * count, count) - send_base
            block = send >> 8
            hot = place_hot(recv)
            hot_ref[tile_rows(tile), :] = hot
            block_ref[tile_rows(tile), :] = small(block)
            sender = gather_blocks(place_hot(send), block, window, send_base, SENDERS)
            receiver = gather_blocks(hot, None, window, recv_base + HB, 1)
            work.append((sender, receiver))
        slopes = []
        for tile in tiles:
            for copy in leave(tile)[1:]:
                copy.start()
        for tile, (sender, receiver) in zip(tiles, work):
            inputs = jnp.concatenate([sender.astype(BF16), receiver.astype(BF16)], axis=1)
            slope = silu_slope(dot(inputs, weight))
            slope_ref[tile_rows(tile), :] = slope
            leave(tile)[0].start()
            slopes.append(jnp.concatenate(two_parts(slope), axis=1))
        sums = []
        for tile, (recv_base, _), slope in zip(tiles, places, slopes):
            hot = place_hot_rows(ordered, 0, tile, recv_base, level)
            both = dot(hot, slope)
            sums.append(both[:, 0:LANES] + both[:, LANES:])
        for (recv_base, _), part in zip(places, sums):
            add_parts(slope_sum, recv_base, [part])

    def far(tile):
        recv = index_columns(ordered.at[0], tile * count, count)
        send = index_columns(ordered.at[1], tile * count, count)
        blocks = fine_count // SPAN
        sender = gather_blocks(place_hot(send), send >> 8, window, 0, blocks + 2)
        receiver = gather_blocks(place_hot(recv), recv >> 8, window, HB, blocks)
        inputs = jnp.concatenate([sender.astype(BF16), receiver.astype(BF16)], axis=1)
        slope = silu_slope(dot(inputs, weight))
        slope_ref[tile_rows(tile), :] = slope
        hot = place_hot_rows(ordered, 0, tile, 0, level)
        for part in two_parts(slope):
            add_parts(slope_sum, 0, spread_rows(hot, small(recv >> 8), blocks, part))
        hot_ref[tile_rows(tile), :] = jnp.zeros((TILE, SPAN), BF16)
        block_ref[tile_rows(tile), :] = jnp.zeros((TILE, LANES), BF16)
        for copy in leave(tile):
            copy.start()

    def step(index, carry):
        each_group(index, stats, fine_count, near, far)
        return carry

    tiles = slope_ref.shape[0] // TILE
    lax.fori_loop(0, tiles // GROUP, step, 0)
    window_copy.wait()
    for tile in range(tiles):
        for copy in leave(tile):
            copy.wait()


def edge_kernel(
    stats,
    arrived_hbm,
    slot_hot_hbm,
    slot_block_hbm,
    hot_hbm,
    slope_hbm,
    block_hbm,
    ordered_hbm,
    window_hbm,
    slope_sum_hbm,
    weight_hbm,
    rest_hbm,
    grad_table,
    send_sum,
    first_ref,
    second_ref,
    keep_ref,
    slot_table,
    grad_rows,
    arrived_ref,
    slot_hot,
    slot_block,
    hot_ref,
    slope_ref,
    block_ref,
    ordered,
    window,
    slope_sum,
    weight_ref,
    rest_ref,
    arrivals,
):
    fine_count = grad_table.shape[0]
    copies = fetch(
        (
            arrived_hbm,
            slot_hot_hbm,
            slot_block_hbm,
            hot_hbm,
            slope_hbm,
            block_hbm,
            ordered_hbm,
            window_hbm,
            slope_sum_hbm,
            weight_hbm,
            rest_hbm,
        ),
        (
            arrived_ref,
            slot_hot,
            slot_block,
            hot_ref,
            slope_ref,
            block_ref,
            ordered,
            window,
            slope_sum,
            weight_ref,
            rest_ref,
        ),
        arrivals,
    )
    send_sum[...] = jnp.zeros(send_sum.shape, F32)
    peers = arrived_ref.shape[0]
    half = LANES + rest_ref.shape[0] // 2
    capacity = arrived_ref.shape[1] - EXTRA
    per_block = SPAN // capacity
    for copy in copies[:3]:
        copy.wait()
    coarse = jnp.zeros((EXTRA, LANES), F32)
    for peer in range(peers):
        block, part = divmod(peer, per_block)
        rows = slice(part * capacity, (part + 1) * capacity)
        slot_table[rows, block * SPAN : block * SPAN + LANES] = arrived_ref[peer, 0:capacity, :]
        extra = arrived_ref[peer, capacity:, :].astype(F32)
        square = jnp.concatenate([extra, jnp.zeros((LANES - EXTRA, LANES), F32)], axis=0).T
        slot_table[rows, block * SPAN + LANES : (block + 1) * SPAN] = square[0:capacity].astype(
            BF16
        )
        coarse += extra
    keep_ref[half:, :] = coarse

    found = []
    for first in range(0, slot_hot.shape[0], SPAN):
        at = slice(first, first + SPAN)
        found.append(gather_rows(slot_hot[at, :], slot_block[at, :], slot_table, SPAN))
    for i, (grad, weight) in enumerate(found):
        first = i * SPAN
        for r in range(2):
            factor = weight[:, WEIGHTS + r : WEIGHTS + r + 1]
            rows = (grad * factor).astype(BF16).astype(F32)
            grad_rows[pl.ds(2 * first + r, SPAN, stride=2), :] = rows
    grad_table[...] = grad_rows[...].astype(BF16)
    for copy in copies[3:]:
        copy.wait()

    count = TILE // LANES
    level = levels()

    def near(tiles, places):
        work = []
        for tile, (recv_base, _) in zip(tiles, places):
            rows = tile_rows(tile)
            upstream = gather_blocks(hot_ref[rows, :], None, grad_table, recv_base, 1)
            work.append((upstream * slope_ref[rows, :]).astype(BF16))
        sums = []
        for tile, (_, send_base), values in zip(tiles, places, work):
            hot = place_hot_rows(ordered, 1, tile, send_base, level)
            sums.append(spread_rows(hot, block_ref[tile_rows(tile), :], SENDERS, values))
        for (_, send_base), parts in zip(places, sums):
            add_parts(send_sum, send_base, parts)

    def far(tile):
        rows = tile_rows(tile)
        recv = index_columns(ordered.at[0], tile * count, count)
        send = index_columns(ordered.at[1], tile * count, count)
        blocks = fine_count // SPAN
        upstream = gather_blocks(place_hot(recv), recv >> 8, grad_table, 0, blocks)
        values = (upstream * slope_ref[rows, :]).astype(BF16)
        hot = place_hot_rows(ordered, 1, tile, 0, level)
        add_parts(send_sum, 0, spread_rows(hot, small(send >> 8), blocks + 2, values))

    def step(index, carry):
        each_group(index, stats, fine_count, near, far)
        return carry

    lax.fori_loop(0, slope_ref.shape[0] // TILE // GROUP, step, 0)

    weight_send = weight_ref[0:LANES, :]
    odd = lax.axis_index("curve") & 1
    to_prev = back(send_sum[0:HB, :], weight_send)
    to_next = back(send_sum[HB + fine_count :, :], weight_send)
    first_ref[half:, :] = jnp.where(odd == 0, to_next, to_prev).astype(BF16)
    second_ref[...] = jnp.where(odd == 0, to_prev, to_next).astype(BF16)
    term_send = jnp.zeros((LANES, LANES), F32)
    term_recv = jnp.zeros((LANES, LANES), F32)
    for first in range(0, fine_count + 2 * HB, SPAN):
        at = slice(first, first + SPAN)
        term_send += outer(window[at, :], send_sum[at, :])
    for first in range(0, fine_count, SPAN):
        at = slice(first, first + SPAN)
        moved = slice(HB + first, HB + first + SPAN)
        term_recv += outer(window[moved, :], grad_rows[at, :] * slope_sum[at, :])
    keep_ref[0:LANES, :] = jnp.where(odd == 0, term_send, term_recv)
    first_ref[0:LANES, :] = jnp.where(odd == 0, term_recv, term_send).astype(BF16)
    rest_first, rest_second = rest_ref[0 : half - LANES, :], rest_ref[half - LANES :, :]
    keep_ref[LANES:half, :] = jnp.where(odd == 0, rest_first, rest_second)
    first_ref[LANES:half, :] = jnp.where(odd == 0, rest_second, rest_first).astype(BF16)


def fine_kernel(
    grad_hbm,
    send_sum_hbm,
    slope_sum_hbm,
    weight_hbm,
    first_hbm,
    second_hbm,
    fine_ref,
    grad_table,
    send_sum,
    slope_sum,
    weight_ref,
    first_ref,
    second_ref,
    arrivals,
):
    fine_count = fine_ref.shape[0]
    for copy in fetch(
        (grad_hbm, send_sum_hbm, slope_sum_hbm, weight_hbm, first_hbm, second_hbm),
        (grad_table, send_sum, slope_sum, weight_ref, first_ref, second_ref),
        arrivals,
    ):
        copy.wait()
    odd = lax.axis_index("curve") & 1
    half = first_ref.shape[0] - HB
    one, two = first_ref[half:, :].astype(F32), second_ref[...].astype(F32)
    from_next, from_prev = jnp.where(odd == 0, one, two), jnp.where(odd == 0, two, one)
    for first in range(0, fine_count, SPAN):
        at = slice(first, first + SPAN)
        moved = slice(HB + first, HB + first + SPAN)
        grad = grad_table[at, :].astype(F32)
        summed = (
            grad
            + back(send_sum[moved, :], weight_ref[0:LANES, :])
            + back(grad * slope_sum[at, :], weight_ref[LANES:, :])
        )
        if first == 0:
            summed += from_prev
        if first == fine_count - SPAN:
            summed += from_next
        fine_ref[at, :] = summed.astype(BF16)


def last_kernel(
    edge_scale,
    coarse_scale,
    peers,
    own_ref,
    coarse_ref,
    there_ref,
    edge_ref,
    in_ref,
    out_ref,
    gain_ref,
    terms,
):
    chunk, half_rest, _ = term_sizes(peers)
    half = own_ref.shape[0]
    odd = lax.axis_index("curve") & 1
    own, coarse = own_ref[...], coarse_ref[...].astype(F32)
    other, other_coarse = there_ref[0:half, :], there_ref[half:, :]
    halves = (jnp.where(odd == 0, own, other), jnp.where(odd == 0, other, own))
    shares = (
        jnp.where(odd == 0, coarse, other_coarse),
        jnp.where(odd == 0, other_coarse, coarse),
    )
    for core in range(2):
        edge_ref[core * LANES : (core + 1) * LANES, :] = halves[core][0:LANES] * edge_scale
        for i in range(peers // 2):
            at = (core * (peers // 2) + i) * chunk
            terms[at : at + chunk, :] = shares[core][i * EXTRA : i * EXTRA + chunk]
        if half_rest:
            at = chunk * peers + core * half_rest
            terms[at : at + half_rest, :] = halves[core][LANES : LANES + half_rest]
    in_ref[...] = terms[0:LANES, :] * coarse_scale
    out_ref[...] = terms[LANES:, :] * coarse_scale
    gain_ref[...] = halves[0][LANES + half_rest : LANES + half_rest + 1] * coarse_scale


def pair_exchange(first, second, peers):
    pairs = [(i, i ^ 1) for i in range(peers)]
    between = [(i, ((i + 1) ^ 1) - 1) for i in range(1, peers - 1)]
    return lax.ppermute(first, "curve", pairs), lax.ppermute(second, "curve", between)


def joined(later, own, there):
    return jnp.where(
        later, jnp.concatenate([there, own], axis=0), jnp.concatenate([own, there], axis=0)
    )


def swapped(values, hops, peers):
    return lax.ppermute(values, "curve", [(i, i ^ hops) for i in range(peers)])


def reduced(sent, half, device, peers, beside):
    hops = 2
    while hops < peers // 4:
        there = swapped(sent, hops, peers)
        own = sent[:half].astype(F32) + there[:half].astype(F32)
        coarse = joined((device & hops) != 0, sent[half:], there[half:])
        sent = jnp.concatenate([own.astype(BF16), coarse], axis=0)
        hops *= 2
    near, far = peers // 4, peers // 2
    parts = [sent] + [swapped(sent, hops, peers) for hops in (near, far, near + far)]
    *parts, beside = lax.optimization_barrier((*parts, beside))
    sums = [part[:half].astype(F32) for part in parts]
    rows = [part[half:] for part in parts]
    own = (sums[0] + sums[1]) + (sums[2] + sums[3])
    later = (device & near) != 0
    coarse = joined(
        (device & far) != 0, joined(later, rows[0], rows[1]), joined(later, rows[2], rows[3])
    )
    return own, coarse, beside


def per_device(
    fine_latent,
    coarse_latent,
    grad_coarse,
    restrict_weights,
    send_rows,
    pair_slots,
    edge_receivers,
    edge_offsets,
    edge_weight,
    node_weight_in,
    node_weight_out,
    node_gain,
):
    peers = lax.axis_size("curve")
    device = lax.axis_index("curve")
    even = (device & 1) == 0
    coarse_count = coarse_latent.shape[0]
    fine_count = fine_latent.shape[0]
    edge_count = edge_receivers.shape[0]
    capacity = send_rows.shape[0] // peers
    rest_rows = term_sizes(peers)[2]
    half = LANES + rest_rows
    payload = capacity + EXTRA
    edge_rows = edge_count // LANES
    window_count = fine_count + 2 * HB
    params = pltpu.CompilerParams(vmem_limit_bytes=64 * 1024 * 1024 - 256 * 1024)
    roomy = pltpu.CompilerParams(vmem_limit_bytes=62 * 1024 * 1024)
    anywhere = pl.BlockSpec(memory_space=pl.ANY)

    scalar = pl.BlockSpec(memory_space=pltpu.SMEM)

    head, end = fine_latent[:HB], fine_latent[fine_count - HB :]
    halos = pair_exchange(jnp.where(even, end, head), jnp.where(even, head, end), peers)

    sent, rest = pl.pallas_call(
        functools.partial(coarse_kernel, peers),
        out_shape=(
            jax.ShapeDtypeStruct((peers, payload, LANES), BF16),
            jax.ShapeDtypeStruct((2 * rest_rows, LANES), F32),
        ),
        in_specs=[anywhere] * 7,
        scratch_shapes=[
            pltpu.VMEM((SPAN, coarse_count), BF16),
            pltpu.VMEM((2 * LANES, LANES), F32),
            pltpu.VMEM((coarse_count, LANES), BF16),
            pltpu.VMEM((coarse_count, LANES), BF16),
            pltpu.VMEM((2, coarse_count), BF16),
            pltpu.VMEM((peers * capacity // LANES, LANES), jnp.int32),
            pltpu.VMEM((LANES, LANES), BF16),
            pltpu.VMEM((LANES, LANES), BF16),
            pltpu.VMEM((1, LANES), F32),
            pltpu.SemaphoreType.DMA((7,)),
        ],
        compiler_params=params,
        cost_estimate=pl.CostEstimate(
            flops=2_000_000_000, bytes_accessed=2_000_000, transcendentals=400_000
        ),
        name="coarse_block",
    )(
        coarse_latent,
        grad_coarse,
        restrict_weights,
        send_rows.reshape(-1, LANES),
        node_weight_in,
        node_weight_out,
        node_gain.reshape(1, LANES),
    )
    arrived = lax.all_to_all(sent, "curve", split_axis=0, concat_axis=0, tiled=True)

    pair_count = fine_count // 2
    in_vmem = pl.BlockSpec(memory_space=pltpu.VMEM)
    slope, hot, block, window, slope_sum, ordered, stats, slot_hot, slot_block = pl.pallas_call(
        slope_kernel,
        out_shape=(
            jax.ShapeDtypeStruct((edge_count, LANES), F32),
            jax.ShapeDtypeStruct((edge_count, SPAN), BF16),
            jax.ShapeDtypeStruct((edge_count, LANES), BF16),
            jax.ShapeDtypeStruct((window_count, LANES), BF16),
            jax.ShapeDtypeStruct((fine_count, LANES), F32),
            jax.ShapeDtypeStruct((2, edge_rows, LANES), jnp.int32),
            jax.ShapeDtypeStruct((edge_rows, LANES), jnp.int32),
            jax.ShapeDtypeStruct((pair_count, SPAN), BF16),
            jax.ShapeDtypeStruct((pair_count, LANES), jnp.int32),
        ),
        in_specs=[anywhere] * 7,
        out_specs=[anywhere] * 4 + [in_vmem] * 5,
        scratch_shapes=[
            pltpu.VMEM((edge_rows, LANES), jnp.int32),
            pltpu.VMEM((edge_rows, LANES), jnp.int32),
            pltpu.VMEM((pair_count // LANES, LANES), jnp.int32),
            pltpu.VMEM((window_count, LANES), BF16),
            pltpu.VMEM((2 * LANES, LANES), BF16),
            pltpu.VMEM((2, HB, LANES), BF16),
            pltpu.VMEM((edge_count, LANES), F32),
            pltpu.VMEM((edge_count, SPAN), BF16),
            pltpu.VMEM((edge_count, LANES), BF16),
            pltpu.SMEM((edge_rows, LANES), jnp.int32),
            pltpu.SemaphoreType.DMA((7,)),
            pltpu.SemaphoreType.DMA,
            pltpu.SemaphoreType.DMA((3, edge_count // TILE)),
            pltpu.SemaphoreType.DMA,
        ],
        compiler_params=params,
        cost_estimate=pl.CostEstimate(
            flops=16_000_000_000, bytes_accessed=5_000_000, transcendentals=800_000
        ),
        name="edge_slope",
    )(
        edge_receivers.reshape(-1, LANES),
        edge_offsets.reshape(-1, LANES),
        pair_slots.reshape(-1, LANES),
        fine_latent,
        edge_weight,
        *halos,
    )

    coarse_scale = 1.0 / math.sqrt(coarse_count * peers)
    edge_scale = 1.0 / math.sqrt(edge_count * peers)
    grad_rows, send_sum, first, second, keep = pl.pallas_call(
        edge_kernel,
        out_shape=(
            jax.ShapeDtypeStruct((fine_count, LANES), BF16),
            jax.ShapeDtypeStruct((window_count, LANES), F32),
            pltpu.VMEM((half + HB, LANES), BF16),
            pltpu.VMEM((HB, LANES), BF16),
            pltpu.VMEM((half + EXTRA, LANES), F32),
        ),
        in_specs=[scalar] + [anywhere] * 11,
        scratch_shapes=[
            pltpu.VMEM((SPAN, peers * capacity), BF16),
            pltpu.VMEM((fine_count, LANES), F32),
            pltpu.VMEM((peers, payload, LANES), BF16),
            pltpu.VMEM((pair_count, SPAN), BF16),
            pltpu.VMEM((pair_count, LANES), jnp.int32),
            pltpu.VMEM((edge_count, SPAN), BF16),
            pltpu.VMEM((edge_count, LANES), F32),
            pltpu.VMEM((edge_count, LANES), BF16),
            pltpu.VMEM((2, edge_rows, LANES), jnp.int32),
            pltpu.VMEM((window_count, LANES), BF16),
            pltpu.VMEM((fine_count, LANES), F32),
            pltpu.VMEM((2 * LANES, LANES), BF16),
            pltpu.VMEM((2 * rest_rows, LANES), F32),
            pltpu.SemaphoreType.DMA((11,)),
        ],
        compiler_params=roomy,
        cost_estimate=pl.CostEstimate(
            flops=24_000_000_000, bytes_accessed=8_000_000, transcendentals=0
        ),
        name="edge_back",
    )(
        stats,
        arrived,
        slot_hot,
        slot_block,
        hot,
        slope,
        block,
        ordered,
        window,
        slope_sum,
        edge_weight,
        rest,
    )
    one, two = pair_exchange(first, second, peers)
    sent = keep + jnp.pad(one[:half].astype(F32), ((0, EXTRA), (0, 0)))
    sent = sent.astype(BF16)
    grad_fine = pl.pallas_call(
        fine_kernel,
        out_shape=jax.ShapeDtypeStruct((fine_count, LANES), BF16),
        in_specs=[anywhere] * 6,
        scratch_shapes=[
            pltpu.VMEM((fine_count, LANES), BF16),
            pltpu.VMEM((window_count, LANES), F32),
            pltpu.VMEM((fine_count, LANES), F32),
            pltpu.VMEM((2 * LANES, LANES), BF16),
            pltpu.VMEM((half + HB, LANES), BF16),
            pltpu.VMEM((HB, LANES), BF16),
            pltpu.SemaphoreType.DMA((6,)),
        ],
        compiler_params=pltpu.CompilerParams(vmem_limit_bytes=64 * 1024 * 1024 - 1536 * 1024),
        cost_estimate=pl.CostEstimate(
            flops=1_000_000_000, bytes_accessed=4_000_000, transcendentals=0
        ),
        name="fine_sums",
    )(grad_rows, send_sum, slope_sum, edge_weight, one, two)
    own, coarse, grad_fine = reduced(sent, half, device, peers, grad_fine)
    there = swapped(jnp.concatenate([own, coarse.astype(F32)], axis=0), 1, peers)
    edge_terms, term_in, term_out, term_gain = pl.pallas_call(
        functools.partial(last_kernel, edge_scale, coarse_scale, peers),
        out_shape=(
            jax.ShapeDtypeStruct((2 * LANES, LANES), F32),
            jax.ShapeDtypeStruct((LANES, LANES), F32),
            jax.ShapeDtypeStruct((LANES, LANES), F32),
            jax.ShapeDtypeStruct((1, LANES), F32),
        ),
        scratch_shapes=[pltpu.VMEM((2 * LANES, LANES), F32)],
        compiler_params=pltpu.CompilerParams(vmem_limit_bytes=4 * 1024 * 1024),
        name="last_terms",
    )(own, coarse, there)
    return grad_fine, edge_terms, term_in, term_out, term_gain.reshape(LANES)


def solution(mesh):
    placed = (
        P(("groups", "curve"), None),
        P(("groups", "curve"), None),
        P(("groups", "curve"), None),
        P(None, ("groups", "curve")),
        P(("groups", "curve")),
        P(("groups", "curve")),
        P(("groups", "curve")),
        P(("groups", "curve")),
        P(),
        P(),
        P(),
        P(),
    )
    return jax.shard_map(
        per_device,
        mesh=mesh,
        in_specs=placed,
        out_specs=(
            P(("groups", "curve"), None),
            P("groups", None),
            P("groups", None),
            P("groups", None),
            P("groups"),
        ),
        check_vma=False,
    )
```

```python
import functools
import math

import jax
import jax.numpy as jnp
from jax import lax
from jax.experimental import pallas as pl
from jax.experimental.pallas import tpu as pltpu
from jax.sharding import PartitionSpec as P

HB = 256
LANES = 128
SPAN = 256
EXTRA = 16
WEIGHTS = EXTRA - 2
TILE = 512
GROUP = 4
SENDERS = 3

F32 = jnp.float32
BF16 = jnp.bfloat16
NT = (((1,), (1,)), ((), ()))
TN = (((0,), (0,)), ((), ()))


def dot(left, right, dims=(((1,), (0,)), ((), ()))):
    return lax.dot_general(left, right, dims, preferred_element_type=F32)


def silu_slope(values):
    sigm = jax.nn.sigmoid(values)
    return sigm * (1.0 + values * (1.0 - sigm))


def columns(row):
    return jnp.broadcast_to(row, (LANES, LANES)).T


def index_columns(ref, first, count):
    return jnp.concatenate([columns(ref[pl.ds(first + i, 1), :]) for i in range(count)], axis=0)


def small(values):
    return values.astype(F32).astype(BF16)


def place_hot(cols):
    place = small(cols & (SPAN - 1))
    lane = lax.broadcasted_iota(jnp.int32, place.shape, 1)
    one, zero = jnp.ones((), BF16), jnp.zeros((), BF16)
    return jnp.concatenate(
        [jnp.where(place == small(lane + start), one, zero) for start in range(0, SPAN, LANES)],
        axis=1,
    )


def gather_rows(hot, block, table, width):
    total = table.shape[1]
    step = max(width, 2 * LANES)
    found = [jnp.zeros(block.shape, F32) for _ in range(width // LANES)]
    for start in range(0, total, step):
        part = dot(hot, table[:, start : start + step])
        for inner in range(0, step, width):
            here = block == (start + inner) // width
            for i in range(len(found)):
                at = inner + i * LANES
                found[i] = jnp.where(here, part[:, at : at + LANES], found[i])
    return found


def spread_rows(hot, block, blocks, values):
    if blocks == 1:
        return [dot(hot, values)]
    parts = []
    zero = jnp.zeros((), BF16)
    for start in range(0, blocks, 2):
        some = range(start, min(start + 2, blocks))
        spread = [jnp.where(block == jnp.full((), j, BF16), values, zero) for j in some]
        part = dot(hot, jnp.concatenate(spread, axis=1))
        parts += [part[:, i * LANES : (i + 1) * LANES] for i in range(len(some))]
    return parts


def add_parts(total, base, parts):
    for j, part in enumerate(parts):
        total[block_rows(base, j), :] += part


def place_hot_rows(ordered, at, tile, base, level):
    one, zero = jnp.ones((), BF16), jnp.zeros((), BF16)
    hot = []
    for i in range(TILE // LANES):
        row = ordered[at, pl.ds(tile * (TILE // LANES) + i, 1), :] - base
        hot.append(jnp.where(level == small(row & (SPAN - 1)), one, zero))
    return jnp.concatenate(hot, axis=1)


def levels():
    return small(lax.broadcasted_iota(jnp.int32, (SPAN, LANES), 0))


def two_parts(values):
    high = values.astype(BF16)
    return high, (values - high.astype(F32)).astype(BF16)


def back(values, weight):
    both = jnp.concatenate(two_parts(values), axis=1)
    return dot(both, jnp.concatenate([weight, weight], axis=1), NT)


def outer(rows, values):
    high, low = two_parts(values)
    both = dot(rows, jnp.concatenate([high, low], axis=1), TN)
    return both[:, 0:LANES] + both[:, LANES:]


def term_sizes(peers):
    chunk = min(WEIGHTS, SPAN // peers)
    half = (SPAN - chunk * peers) // 2
    return chunk, half, -(-(half + 1) // EXTRA) * EXTRA


def fetch(sources, targets, arrivals):
    copies = [
        pltpu.make_async_copy(source, target, arrivals.at[i])
        for i, (source, target) in enumerate(zip(sources, targets))
    ]
    for copy in copies:
        copy.start()
    return copies


def coarse_kernel(
    peers,
    latent_ref,
    grad_ref,
    weights_ref,
    rows_ref,
    w_in_ref,
    w_out_ref,
    gain_ref,
    sent_ref,
    rest_ref,
    table_ref,
    terms,
    *held,
):
    *held, arrivals = held
    sources = (latent_ref, grad_ref, weights_ref, rows_ref, w_in_ref, w_out_ref, gain_ref)
    copies = fetch(sources, held, arrivals)
    for copy in copies:
        copy.wait()
    latent_ref, grad_ref, weights_ref, rows_ref, w_in_ref, w_out_ref, gain_ref = held
    count = latent_ref.shape[0]
    chunk, half_rest, rest_rows = term_sizes(peers)
    capacity = sent_ref.shape[1] - EXTRA
    per_step = 256 // LANES
    steps = range(0, rows_ref.shape[0], per_step)
    slots = []
    for first in steps:
        cols = index_columns(rows_ref, first, per_step)
        slots.append((place_hot(cols), cols // SPAN))
    w_in, w_out, gain = w_in_ref[...], w_out_ref[...], gain_ref[...]
    latent = latent_ref[...]
    pre = dot(latent, w_in)
    sigm = jax.nn.sigmoid(pre)
    hidden = (pre * sigm).astype(BF16)
    slope = sigm * (1.0 + pre * (1.0 - sigm))
    mapped = dot(hidden, w_out)
    centred = mapped - jnp.mean(mapped, axis=1, keepdims=True)
    inverse = lax.rsqrt(jnp.mean(centred * centred, axis=1, keepdims=True) + 1e-05)
    normed = centred * inverse
    upstream = grad_ref[...].astype(F32)
    scaled = upstream * gain
    grad_mapped = (
        inverse
        * (
            scaled
            - jnp.mean(scaled, axis=1, keepdims=True)
            - normed * jnp.mean(scaled * normed, axis=1, keepdims=True)
        )
    ).astype(BF16)
    grad_pre = (dot(grad_mapped, w_out, NT) * slope).astype(BF16)
    grad_in = (upstream + dot(grad_pre, w_in, NT)).astype(BF16)
    term_gain = jnp.sum(upstream * normed, axis=0, keepdims=True)
    term_in = dot(latent, grad_pre, TN)
    term_out = dot(hidden, grad_mapped, TN)
    for block in range(count // SPAN):
        at = block * SPAN
        table_ref[:, at : at + LANES] = grad_in[at : at + SPAN]
        for half in range(SPAN // LANES):
            at = block * SPAN + half * LANES
            pair = weights_ref[:, at : at + LANES].astype(F32)
            square = jnp.concatenate([pair, jnp.zeros((LANES - 2, LANES), F32)], axis=0)
            table_ref[
                half * LANES : (half + 1) * LANES, block * SPAN + LANES : (block + 1) * SPAN
            ] = square.T.astype(BF16)
    terms[0:LANES, :] = term_in
    terms[LANES:, :] = term_out
    rest_ref[...] = jnp.zeros(rest_ref.shape, F32)
    shared = chunk * peers
    if half_rest:
        rest_ref[0:half_rest, :] = terms[shared : shared + half_rest, :]
        rest_ref[rest_rows : rest_rows + half_rest, :] = terms[shared + half_rest :, :]
    rest_ref[half_rest : half_rest + 1, :] = term_gain
    found = [gather_rows(hot, block, table_ref, SPAN) for hot, block in slots]
    for first, (sent, weight) in zip(steps, found):
        for part in range(per_step * LANES // capacity):
            peer = first * LANES // capacity + part
            rows = slice(part * capacity, (part + 1) * capacity)
            sent_ref[peer, 0:capacity, :] = sent[rows].astype(BF16)
            square = weight[rows]
            if capacity < LANES:
                square = jnp.concatenate(
                    [square, jnp.zeros((LANES - capacity, LANES), F32)], axis=0
                )
            first_row = (peer % 2 * (peers // 2) + peer // 2) * chunk
            extra = [terms[first_row : first_row + chunk, :]]
            if chunk < WEIGHTS:
                extra.append(jnp.zeros((WEIGHTS - chunk, LANES), F32))
            extra.append(square.T[0:2])
            sent_ref[peer, capacity:, :] = jnp.concatenate(extra, axis=0).astype(BF16)


def order_edges(recv_ref, off_ref, ordered, stats_vmem, fine_count):
    rows = recv_ref.shape[0]
    shift = (fine_count // LANES).bit_length() - 1
    lane = lax.broadcasted_iota(jnp.int32, (LANES, LANES), 1)
    sub = lax.broadcasted_iota(jnp.int32, (LANES, LANES), 0)
    level = small(sub)
    one, zero = jnp.ones((), BF16), jnp.zeros((), BF16)

    def hot(row):
        return jnp.where(level == small(row), one, zero)

    number = jnp.zeros((LANES, LANES), BF16)
    for row in range(rows):
        number += hot(recv_ref[row : row + 1, :] >> shift)
    ones = jnp.ones((LANES, LANES), BF16)
    total = dot(number, ones)
    high = jnp.floor(total * (1.0 / 64.0))
    low = total - 64.0 * high
    before = jnp.where(lane < sub, 1.0, 0.0).astype(BF16)
    start = 64.0 * dot(before, high.astype(BF16)) + dot(before, low.astype(BF16))
    after = jnp.where(sub < lane, 1.0, 0.0).astype(BF16)
    prefix = jnp.concatenate([after, ones], axis=1)
    positions = []
    filled = start
    for row in range(rows):
        bucket = recv_ref[row : row + 1, :] >> shift
        found = dot(hot(bucket), prefix)
        mine = jnp.where(sub == bucket, found[:, 0:LANES] + filled, 0.0)
        positions.append(jnp.sum(mine, axis=0, keepdims=True).astype(jnp.int32))
        filled = filled + found[:, LANES:]
    moved = jnp.zeros((192, LANES), F32)
    for part in range(0, rows, 4):
        left, right = [], []
        for row in range(part, part + 4):
            position = positions[row]
            recv = recv_ref[row : row + 1, :]
            off = off_ref[row : row + 1, :] + HB
            rest = ((recv >> 8) << 2) | (off >> 8)
            here = level[0:64] == small(position >> 7)
            values = [small(value) for value in (recv & 255, off & 255, rest)]
            left.append(jnp.concatenate([jnp.where(here, v, zero) for v in values], axis=0))
            right.append(hot(position & 127))
        moved += dot(jnp.concatenate(left, axis=1), jnp.concatenate(right, axis=1), NT)
    moved = moved.astype(jnp.int32)
    rest = moved[LANES : LANES + rows]
    recv = moved[0:rows] + ((rest >> 2) << 8)
    send = recv + moved[64 : 64 + rows] + ((rest & 3) << 8)
    ordered[0] = recv
    ordered[1] = send
    lane = lax.broadcasted_iota(jnp.int32, (rows, LANES), 1)
    recv, send = recv.astype(F32), send.astype(F32)
    stats = jnp.where(
        lane < 2,
        jnp.where(
            lane == 0,
            jnp.min(recv, axis=1, keepdims=True),
            jnp.max(recv, axis=1, keepdims=True),
        ),
        jnp.where(
            lane == 2,
            jnp.min(send, axis=1, keepdims=True),
            jnp.max(send, axis=1, keepdims=True),
        ),
    )
    stats_vmem[...] = stats.astype(jnp.int32)


def tile_bases(stats, tile, fine_count):
    count = TILE // LANES
    rows = [tile * count + i for i in range(count)]

    def extreme(pick, at):
        value = stats[rows[0], at]
        for row in rows[1:]:
            value = pick(value, stats[row, at])
        return value

    recv_base = jnp.minimum((extreme(jnp.minimum, 0) >> 4) << 4, fine_count - SPAN)
    send_base = jnp.minimum(
        (extreme(jnp.minimum, 2) >> 4) << 4, fine_count + 2 * HB - SENDERS * SPAN
    )
    fits = (extreme(jnp.maximum, 1) - recv_base < SPAN) & (
        extreme(jnp.maximum, 3) - send_base < SENDERS * SPAN
    )
    return recv_base, send_base, fits


def each_group(step, stats, fine_count, near, far):
    tiles = [step * GROUP + i for i in range(GROUP)]
    places = [tile_bases(stats, tile, fine_count) for tile in tiles]
    fits = functools.reduce(jnp.logical_and, [place[2] for place in places])

    @pl.when(fits)
    def _():
        near(tiles, [place[:2] for place in places])

    @pl.when(jnp.logical_not(fits))
    def _():
        def one(i, carry):
            far(step * GROUP + i)
            return carry

        lax.fori_loop(0, GROUP, one, 0)


def block_rows(base, block):
    return pl.ds(pl.multiple_of(base + block * SPAN, 16), SPAN)


def gather_blocks(hot, block, table, base, blocks):
    found = None
    for start in range(0, blocks, 2):
        some = range(start, min(start + 2, blocks))
        part = dot(hot, jnp.concatenate([table[block_rows(base, j), :] for j in some], axis=1))
        for i, j in enumerate(some):
            one = part[:, i * LANES : (i + 1) * LANES]
            found = one if found is None else jnp.where(block == j, one, found)
    return found


def tile_rows(tile):
    return pl.ds(pl.multiple_of(tile * TILE, TILE), TILE)


def slope_kernel(
    recv_hbm,
    off_hbm,
    slots_hbm,
    fine_hbm,
    weight_hbm,
    first_hbm,
    second_hbm,
    slope_hbm,
    hot_hbm,
    block_hbm,
    window_hbm,
    slope_sum,
    ordered,
    stats_vmem,
    slot_hot,
    slot_block,
    recv_ref,
    off_ref,
    slots_ref,
    window,
    weight_ref,
    halos,
    slope_ref,
    hot_ref,
    block_ref,
    stats,
    arrivals,
    stats_done,
    leaving,
    window_left,
):
    fine_count = fine_hbm.shape[0]
    copies = fetch(
        (recv_hbm, off_hbm, slots_hbm, fine_hbm, weight_hbm, first_hbm, second_hbm),
        (
            recv_ref,
            off_ref,
            slots_ref,
            window.at[pl.ds(HB, fine_count)],
            weight_ref,
            halos.at[0],
            halos.at[1],
        ),
        arrivals,
    )
    copies[0].wait()
    copies[1].wait()
    order_edges(recv_ref, off_ref, ordered, stats_vmem, fine_count)
    stats_copy = pltpu.make_async_copy(stats_vmem, stats, stats_done)
    stats_copy.start()
    for copy in copies[2:]:
        copy.wait()
    slope_sum[...] = jnp.zeros(slope_sum.shape, F32)
    slots = index_columns(slots_ref, 0, slots_ref.shape[0])
    slot_hot[...] = place_hot(slots)
    slot_block[...] = slots // SPAN
    odd = lax.axis_index("curve") & 1
    window[0:HB, :] = halos[1 - odd]
    window[HB + fine_count :, :] = halos[odd]
    window_copy = pltpu.make_async_copy(window, window_hbm, window_left)
    window_copy.start()
    stats_copy.wait()
    count = TILE // LANES
    weight = weight_ref[...]
    level = levels()

    def leave(tile):
        rows = tile_rows(tile)
        pairs = ((slope_ref, slope_hbm), (hot_ref, hot_hbm), (block_ref, block_hbm))
        return [
            pltpu.make_async_copy(source.at[rows], target.at[rows], leaving.at[i, tile])
            for i, (source, target) in enumerate(pairs)
        ]

    def near(tiles, places):
        work = []
        for tile, (recv_base, send_base) in zip(tiles, places):
            recv = index_columns(ordered.at[0], tile * count, count) - recv_base
            send = index_columns(ordered.at[1], tile * count, count) - send_base
            block = send >> 8
            hot = place_hot(recv)
            hot_ref[tile_rows(tile), :] = hot
            block_ref[tile_rows(tile), :] = small(block)
            sender = gather_blocks(place_hot(send), block, window, send_base, SENDERS)
            receiver = gather_blocks(hot, None, window, recv_base + HB, 1)
            work.append((sender, receiver))
        slopes = []
        for tile in tiles:
            for copy in leave(tile)[1:]:
                copy.start()
        for tile, (sender, receiver) in zip(tiles, work):
            inputs = jnp.concatenate([sender.astype(BF16), receiver.astype(BF16)], axis=1)
            slope = silu_slope(dot(inputs, weight))
            slope_ref[tile_rows(tile), :] = slope
            leave(tile)[0].start()
            slopes.append(jnp.concatenate(two_parts(slope), axis=1))
        sums = []
        for tile, (recv_base, _), slope in zip(tiles, places, slopes):
            hot = place_hot_rows(ordered, 0, tile, recv_base, level)
            both = dot(hot, slope)
            sums.append(both[:, 0:LANES] + both[:, LANES:])
        for (recv_base, _), part in zip(places, sums):
            add_parts(slope_sum, recv_base, [part])

    def far(tile):
        recv = index_columns(ordered.at[0], tile * count, count)
        send = index_columns(ordered.at[1], tile * count, count)
        blocks = fine_count // SPAN
        sender = gather_blocks(place_hot(send), send >> 8, window, 0, blocks + 2)
        receiver = gather_blocks(place_hot(recv), recv >> 8, window, HB, blocks)
        inputs = jnp.concatenate([sender.astype(BF16), receiver.astype(BF16)], axis=1)
        slope = silu_slope(dot(inputs, weight))
        slope_ref[tile_rows(tile), :] = slope
        hot = place_hot_rows(ordered, 0, tile, 0, level)
        for part in two_parts(slope):
            add_parts(slope_sum, 0, spread_rows(hot, small(recv >> 8), blocks, part))
        hot_ref[tile_rows(tile), :] = jnp.zeros((TILE, SPAN), BF16)
        block_ref[tile_rows(tile), :] = jnp.zeros((TILE, LANES), BF16)
        for copy in leave(tile):
            copy.start()

    def step(index, carry):
        each_group(index, stats, fine_count, near, far)
        return carry

    tiles = slope_ref.shape[0] // TILE
    lax.fori_loop(0, tiles // GROUP, step, 0)
    window_copy.wait()
    for tile in range(tiles):
        for copy in leave(tile):
            copy.wait()


def edge_kernel(
    stats,
    arrived_hbm,
    slot_hot_hbm,
    slot_block_hbm,
    hot_hbm,
    slope_hbm,
    block_hbm,
    ordered_hbm,
    window_hbm,
    slope_sum_hbm,
    weight_hbm,
    rest_hbm,
    grad_table,
    send_sum,
    first_ref,
    second_ref,
    keep_ref,
    slot_table,
    grad_rows,
    arrived_ref,
    slot_hot,
    slot_block,
    hot_ref,
    slope_ref,
    block_ref,
    ordered,
    window,
    slope_sum,
    weight_ref,
    rest_ref,
    arrivals,
):
    fine_count = grad_table.shape[0]
    copies = fetch(
        (
            arrived_hbm,
            slot_hot_hbm,
            slot_block_hbm,
            hot_hbm,
            slope_hbm,
            block_hbm,
            ordered_hbm,
            window_hbm,
            slope_sum_hbm,
            weight_hbm,
            rest_hbm,
        ),
        (
            arrived_ref,
            slot_hot,
            slot_block,
            hot_ref,
            slope_ref,
            block_ref,
            ordered,
            window,
            slope_sum,
            weight_ref,
            rest_ref,
        ),
        arrivals,
    )
    send_sum[...] = jnp.zeros(send_sum.shape, F32)
    peers = arrived_ref.shape[0]
    half = LANES + rest_ref.shape[0] // 2
    capacity = arrived_ref.shape[1] - EXTRA
    per_block = SPAN // capacity
    for copy in copies[:3]:
        copy.wait()
    coarse = jnp.zeros((EXTRA, LANES), F32)
    for peer in range(peers):
        block, part = divmod(peer, per_block)
        rows = slice(part * capacity, (part + 1) * capacity)
        slot_table[rows, block * SPAN : block * SPAN + LANES] = arrived_ref[peer, 0:capacity, :]
        extra = arrived_ref[peer, capacity:, :].astype(F32)
        square = jnp.concatenate([extra, jnp.zeros((LANES - EXTRA, LANES), F32)], axis=0).T
        slot_table[rows, block * SPAN + LANES : (block + 1) * SPAN] = square[0:capacity].astype(
            BF16
        )
        coarse += extra
    keep_ref[half:, :] = coarse

    found = []
    for first in range(0, slot_hot.shape[0], SPAN):
        at = slice(first, first + SPAN)
        found.append(gather_rows(slot_hot[at, :], slot_block[at, :], slot_table, SPAN))
    for i, (grad, weight) in enumerate(found):
        first = i * SPAN
        for r in range(2):
            factor = weight[:, WEIGHTS + r : WEIGHTS + r + 1]
            rows = (grad * factor).astype(BF16).astype(F32)
            grad_rows[pl.ds(2 * first + r, SPAN, stride=2), :] = rows
    grad_table[...] = grad_rows[...].astype(BF16)
    for copy in copies[3:]:
        copy.wait()

    count = TILE // LANES
    level = levels()

    def near(tiles, places):
        work = []
        for tile, (recv_base, _) in zip(tiles, places):
            rows = tile_rows(tile)
            upstream = gather_blocks(hot_ref[rows, :], None, grad_table, recv_base, 1)
            work.append((upstream * slope_ref[rows, :]).astype(BF16))
        sums = []
        for tile, (_, send_base), values in zip(tiles, places, work):
            hot = place_hot_rows(ordered, 1, tile, send_base, level)
            sums.append(spread_rows(hot, block_ref[tile_rows(tile), :], SENDERS, values))
        for (_, send_base), parts in zip(places, sums):
            add_parts(send_sum, send_base, parts)

    def far(tile):
        rows = tile_rows(tile)
        recv = index_columns(ordered.at[0], tile * count, count)
        send = index_columns(ordered.at[1], tile * count, count)
        blocks = fine_count // SPAN
        upstream = gather_blocks(place_hot(recv), recv >> 8, grad_table, 0, blocks)
        values = (upstream * slope_ref[rows, :]).astype(BF16)
        hot = place_hot_rows(ordered, 1, tile, 0, level)
        add_parts(send_sum, 0, spread_rows(hot, small(send >> 8), blocks + 2, values))

    def step(index, carry):
        each_group(index, stats, fine_count, near, far)
        return carry

    lax.fori_loop(0, slope_ref.shape[0] // TILE // GROUP, step, 0)

    weight_send = weight_ref[0:LANES, :]
    odd = lax.axis_index("curve") & 1
    to_prev = back(send_sum[0:HB, :], weight_send)
    to_next = back(send_sum[HB + fine_count :, :], weight_send)
    first_ref[half:, :] = jnp.where(odd == 0, to_next, to_prev).astype(BF16)
    second_ref[...] = jnp.where(odd == 0, to_prev, to_next).astype(BF16)
    term_send = jnp.zeros((LANES, LANES), F32)
    term_recv = jnp.zeros((LANES, LANES), F32)
    for first in range(0, fine_count + 2 * HB, SPAN):
        at = slice(first, first + SPAN)
        term_send += outer(window[at, :], send_sum[at, :])
    for first in range(0, fine_count, SPAN):
        at = slice(first, first + SPAN)
        moved = slice(HB + first, HB + first + SPAN)
        term_recv += outer(window[moved, :], grad_rows[at, :] * slope_sum[at, :])
    keep_ref[0:LANES, :] = jnp.where(odd == 0, term_send, term_recv)
    first_ref[0:LANES, :] = jnp.where(odd == 0, term_recv, term_send).astype(BF16)
    rest_first, rest_second = rest_ref[0 : half - LANES, :], rest_ref[half - LANES :, :]
    keep_ref[LANES:half, :] = jnp.where(odd == 0, rest_first, rest_second)
    first_ref[LANES:half, :] = jnp.where(odd == 0, rest_second, rest_first).astype(BF16)


def fine_kernel(
    grad_hbm,
    send_sum_hbm,
    slope_sum_hbm,
    weight_hbm,
    first_hbm,
    second_hbm,
    fine_hbm,
    grad_table,
    send_sum,
    slope_sum,
    weight_ref,
    first_ref,
    second_ref,
    fine_ref,
    arrivals,
    leaving,
):
    fine_count = fine_ref.shape[0]
    for copy in fetch(
        (grad_hbm, send_sum_hbm, slope_sum_hbm, weight_hbm, first_hbm, second_hbm),
        (grad_table, send_sum, slope_sum, weight_ref, first_ref, second_ref),
        arrivals,
    ):
        copy.wait()
    odd = lax.axis_index("curve") & 1
    half = first_ref.shape[0] - HB
    one, two = first_ref[half:, :].astype(F32), second_ref[...].astype(F32)
    from_next, from_prev = jnp.where(odd == 0, one, two), jnp.where(odd == 0, two, one)
    send_weight, recv_weight = weight_ref[0:LANES, :], weight_ref[LANES:, :]
    weights = jnp.concatenate([send_weight, send_weight, recv_weight, recv_weight], axis=1)
    copies = []
    for first in range(0, fine_count, SPAN):
        at = slice(first, first + SPAN)
        moved = slice(HB + first, HB + first + SPAN)
        grad = grad_table[at, :].astype(F32)
        parts = two_parts(send_sum[moved, :]) + two_parts(grad * slope_sum[at, :])
        summed = grad + dot(jnp.concatenate(parts, axis=1), weights, NT)
        if first == 0:
            summed += from_prev
        if first == fine_count - SPAN:
            summed += from_next
        fine_ref[at, :] = summed.astype(BF16)
        rows = pl.ds(first, SPAN)
        copies.append(
            pltpu.make_async_copy(
                fine_ref.at[rows], fine_hbm.at[rows], leaving.at[first // SPAN]
            )
        )
        copies[-1].start()
    for copy in copies:
        copy.wait()


def last_kernel(
    edge_scale,
    coarse_scale,
    peers,
    own_ref,
    coarse_ref,
    there_ref,
    edge_ref,
    in_ref,
    out_ref,
    gain_ref,
    terms,
):
    chunk, half_rest, _ = term_sizes(peers)
    half = own_ref.shape[0]
    odd = lax.axis_index("curve") & 1
    own, coarse = own_ref[...], coarse_ref[...].astype(F32)
    other, other_coarse = there_ref[0:half, :], there_ref[half:, :]
    halves = (jnp.where(odd == 0, own, other), jnp.where(odd == 0, other, own))
    shares = (
        jnp.where(odd == 0, coarse, other_coarse),
        jnp.where(odd == 0, other_coarse, coarse),
    )
    for core in range(2):
        edge_ref[core * LANES : (core + 1) * LANES, :] = halves[core][0:LANES] * edge_scale
        for i in range(peers // 2):
            at = (core * (peers // 2) + i) * chunk
            terms[at : at + chunk, :] = shares[core][i * EXTRA : i * EXTRA + chunk]
        if half_rest:
            at = chunk * peers + core * half_rest
            terms[at : at + half_rest, :] = halves[core][LANES : LANES + half_rest]
    in_ref[...] = terms[0:LANES, :] * coarse_scale
    out_ref[...] = terms[LANES:, :] * coarse_scale
    gain_ref[...] = halves[0][LANES + half_rest : LANES + half_rest + 1] * coarse_scale


def pair_exchange(first, second, peers):
    pairs = [(i, i ^ 1) for i in range(peers)]
    between = [(i, ((i + 1) ^ 1) - 1) for i in range(1, peers - 1)]
    return lax.ppermute(first, "curve", pairs), lax.ppermute(second, "curve", between)


def joined(later, own, there):
    return jnp.where(
        later, jnp.concatenate([there, own], axis=0), jnp.concatenate([own, there], axis=0)
    )


def swapped(values, hops, peers):
    return lax.ppermute(values, "curve", [(i, i ^ hops) for i in range(peers)])


def reduced(sent, half, device, peers, beside):
    hops = 2
    while hops < peers // 4:
        there = swapped(sent, hops, peers)
        own = sent[:half].astype(F32) + there[:half].astype(F32)
        coarse = joined((device & hops) != 0, sent[half:], there[half:])
        sent = jnp.concatenate([own.astype(BF16), coarse], axis=0)
        hops *= 2
    near, far = peers // 4, peers // 2
    parts = [sent] + [swapped(sent, hops, peers) for hops in (near, far, near + far)]
    *parts, beside = lax.optimization_barrier((*parts, beside))
    sums = [part[:half].astype(F32) for part in parts]
    rows = [part[half:] for part in parts]
    own = (sums[0] + sums[1]) + (sums[2] + sums[3])
    later = (device & near) != 0
    coarse = joined(
        (device & far) != 0, joined(later, rows[0], rows[1]), joined(later, rows[2], rows[3])
    )
    return own, coarse, beside


def per_device(
    fine_latent,
    coarse_latent,
    grad_coarse,
    restrict_weights,
    send_rows,
    pair_slots,
    edge_receivers,
    edge_offsets,
    edge_weight,
    node_weight_in,
    node_weight_out,
    node_gain,
):
    peers = lax.axis_size("curve")
    device = lax.axis_index("curve")
    even = (device & 1) == 0
    coarse_count = coarse_latent.shape[0]
    fine_count = fine_latent.shape[0]
    edge_count = edge_receivers.shape[0]
    capacity = send_rows.shape[0] // peers
    rest_rows = term_sizes(peers)[2]
    half = LANES + rest_rows
    payload = capacity + EXTRA
    edge_rows = edge_count // LANES
    window_count = fine_count + 2 * HB
    fine_blocks = fine_count // SPAN
    params = pltpu.CompilerParams(vmem_limit_bytes=64 * 1024 * 1024 - 256 * 1024)
    roomy = pltpu.CompilerParams(vmem_limit_bytes=62 * 1024 * 1024)
    anywhere = pl.BlockSpec(memory_space=pl.ANY)

    scalar = pl.BlockSpec(memory_space=pltpu.SMEM)

    head, end = fine_latent[:HB], fine_latent[fine_count - HB :]
    halos = pair_exchange(jnp.where(even, end, head), jnp.where(even, head, end), peers)

    sent, rest = pl.pallas_call(
        functools.partial(coarse_kernel, peers),
        out_shape=(
            jax.ShapeDtypeStruct((peers, payload, LANES), BF16),
            jax.ShapeDtypeStruct((2 * rest_rows, LANES), F32),
        ),
        in_specs=[anywhere] * 7,
        scratch_shapes=[
            pltpu.VMEM((SPAN, coarse_count), BF16),
            pltpu.VMEM((2 * LANES, LANES), F32),
            pltpu.VMEM((coarse_count, LANES), BF16),
            pltpu.VMEM((coarse_count, LANES), BF16),
            pltpu.VMEM((2, coarse_count), BF16),
            pltpu.VMEM((peers * capacity // LANES, LANES), jnp.int32),
            pltpu.VMEM((LANES, LANES), BF16),
            pltpu.VMEM((LANES, LANES), BF16),
            pltpu.VMEM((1, LANES), F32),
            pltpu.SemaphoreType.DMA((7,)),
        ],
        compiler_params=params,
        cost_estimate=pl.CostEstimate(
            flops=2_000_000_000, bytes_accessed=2_000_000, transcendentals=400_000
        ),
        name="coarse_block",
    )(
        coarse_latent,
        grad_coarse,
        restrict_weights,
        send_rows.reshape(-1, LANES),
        node_weight_in,
        node_weight_out,
        node_gain.reshape(1, LANES),
    )
    arrived = lax.all_to_all(sent, "curve", split_axis=0, concat_axis=0, tiled=True)

    pair_count = fine_count // 2
    in_vmem = pl.BlockSpec(memory_space=pltpu.VMEM)
    slope, hot, block, window, slope_sum, ordered, stats, slot_hot, slot_block = pl.pallas_call(
        slope_kernel,
        out_shape=(
            jax.ShapeDtypeStruct((edge_count, LANES), F32),
            jax.ShapeDtypeStruct((edge_count, SPAN), BF16),
            jax.ShapeDtypeStruct((edge_count, LANES), BF16),
            jax.ShapeDtypeStruct((window_count, LANES), BF16),
            jax.ShapeDtypeStruct((fine_count, LANES), F32),
            jax.ShapeDtypeStruct((2, edge_rows, LANES), jnp.int32),
            jax.ShapeDtypeStruct((edge_rows, LANES), jnp.int32),
            jax.ShapeDtypeStruct((pair_count, SPAN), BF16),
            jax.ShapeDtypeStruct((pair_count, LANES), jnp.int32),
        ),
        in_specs=[anywhere] * 7,
        out_specs=[anywhere] * 4 + [in_vmem] * 5,
        scratch_shapes=[
            pltpu.VMEM((edge_rows, LANES), jnp.int32),
            pltpu.VMEM((edge_rows, LANES), jnp.int32),
            pltpu.VMEM((pair_count // LANES, LANES), jnp.int32),
            pltpu.VMEM((window_count, LANES), BF16),
            pltpu.VMEM((2 * LANES, LANES), BF16),
            pltpu.VMEM((2, HB, LANES), BF16),
            pltpu.VMEM((edge_count, LANES), F32),
            pltpu.VMEM((edge_count, SPAN), BF16),
            pltpu.VMEM((edge_count, LANES), BF16),
            pltpu.SMEM((edge_rows, LANES), jnp.int32),
            pltpu.SemaphoreType.DMA((7,)),
            pltpu.SemaphoreType.DMA,
            pltpu.SemaphoreType.DMA((3, edge_count // TILE)),
            pltpu.SemaphoreType.DMA,
        ],
        compiler_params=params,
        cost_estimate=pl.CostEstimate(
            flops=16_000_000_000, bytes_accessed=5_000_000, transcendentals=800_000
        ),
        name="edge_slope",
    )(
        edge_receivers.reshape(-1, LANES),
        edge_offsets.reshape(-1, LANES),
        pair_slots.reshape(-1, LANES),
        fine_latent,
        edge_weight,
        *halos,
    )

    coarse_scale = 1.0 / math.sqrt(coarse_count * peers)
    edge_scale = 1.0 / math.sqrt(edge_count * peers)
    grad_rows, send_sum, first, second, keep = pl.pallas_call(
        edge_kernel,
        out_shape=(
            jax.ShapeDtypeStruct((fine_count, LANES), BF16),
            jax.ShapeDtypeStruct((window_count, LANES), F32),
            pltpu.VMEM((half + HB, LANES), BF16),
            pltpu.VMEM((HB, LANES), BF16),
            pltpu.VMEM((half + EXTRA, LANES), F32),
        ),
        in_specs=[scalar] + [anywhere] * 11,
        scratch_shapes=[
            pltpu.VMEM((SPAN, peers * capacity), BF16),
            pltpu.VMEM((fine_count, LANES), F32),
            pltpu.VMEM((peers, payload, LANES), BF16),
            pltpu.VMEM((pair_count, SPAN), BF16),
            pltpu.VMEM((pair_count, LANES), jnp.int32),
            pltpu.VMEM((edge_count, SPAN), BF16),
            pltpu.VMEM((edge_count, LANES), F32),
            pltpu.VMEM((edge_count, LANES), BF16),
            pltpu.VMEM((2, edge_rows, LANES), jnp.int32),
            pltpu.VMEM((window_count, LANES), BF16),
            pltpu.VMEM((fine_count, LANES), F32),
            pltpu.VMEM((2 * LANES, LANES), BF16),
            pltpu.VMEM((2 * rest_rows, LANES), F32),
            pltpu.SemaphoreType.DMA((11,)),
        ],
        compiler_params=roomy,
        cost_estimate=pl.CostEstimate(
            flops=24_000_000_000, bytes_accessed=8_000_000, transcendentals=0
        ),
        name="edge_back",
    )(
        stats,
        arrived,
        slot_hot,
        slot_block,
        hot,
        slope,
        block,
        ordered,
        window,
        slope_sum,
        edge_weight,
        rest,
    )
    one, two = pair_exchange(first, second, peers)
    sent = keep + jnp.pad(one[:half].astype(F32), ((0, EXTRA), (0, 0)))
    sent = sent.astype(BF16)
    grad_fine = pl.pallas_call(
        fine_kernel,
        out_shape=jax.ShapeDtypeStruct((fine_count, LANES), BF16),
        in_specs=[anywhere] * 6,
        out_specs=anywhere,
        scratch_shapes=[
            pltpu.VMEM((fine_count, LANES), BF16),
            pltpu.VMEM((window_count, LANES), F32),
            pltpu.VMEM((fine_count, LANES), F32),
            pltpu.VMEM((2 * LANES, LANES), BF16),
            pltpu.VMEM((half + HB, LANES), BF16),
            pltpu.VMEM((HB, LANES), BF16),
            pltpu.VMEM((fine_count, LANES), BF16),
            pltpu.SemaphoreType.DMA((6,)),
            pltpu.SemaphoreType.DMA((fine_blocks,)),
        ],
        compiler_params=pltpu.CompilerParams(vmem_limit_bytes=64 * 1024 * 1024 - 1536 * 1024),
        cost_estimate=pl.CostEstimate(
            flops=1_000_000_000, bytes_accessed=4_000_000, transcendentals=0
        ),
        name="fine_sums",
    )(grad_rows, send_sum, slope_sum, edge_weight, one, two)
    own, coarse, grad_fine = reduced(sent, half, device, peers, grad_fine)
    there = swapped(jnp.concatenate([own, coarse.astype(F32)], axis=0), 1, peers)
    edge_terms, term_in, term_out, term_gain = pl.pallas_call(
        functools.partial(last_kernel, edge_scale, coarse_scale, peers),
        out_shape=(
            jax.ShapeDtypeStruct((2 * LANES, LANES), F32),
            jax.ShapeDtypeStruct((LANES, LANES), F32),
            jax.ShapeDtypeStruct((LANES, LANES), F32),
            jax.ShapeDtypeStruct((1, LANES), F32),
        ),
        scratch_shapes=[pltpu.VMEM((2 * LANES, LANES), F32)],
        compiler_params=pltpu.CompilerParams(vmem_limit_bytes=4 * 1024 * 1024),
        name="last_terms",
    )(own, coarse, there)
    return grad_fine, edge_terms, term_in, term_out, term_gain.reshape(LANES)


def solution(mesh):
    placed = (
        P(("groups", "curve"), None),
        P(("groups", "curve"), None),
        P(("groups", "curve"), None),
        P(None, ("groups", "curve")),
        P(("groups", "curve")),
        P(("groups", "curve")),
        P(("groups", "curve")),
        P(("groups", "curve")),
        P(),
        P(),
        P(),
        P(),
    )
    return jax.shard_map(
        per_device,
        mesh=mesh,
        in_specs=placed,
        out_specs=(
            P(("groups", "curve"), None),
            P("groups", None),
            P("groups", None),
            P("groups", None),
            P("groups"),
        ),
        check_vma=False,
    )
```
